32 devices in a mesh: dp: 4 (over x, core), expert: 2 (over y), tensor: 4 (over z).
Axes of the slice: x: 2, y: 2, z: 4, core: 2. Of those that a mesh axis runs over, the one named last changes fastest.
Arguments:
- images: bfloat16 [32, 197, 768], P(('dp', 'expert')), may hold values from -6 to 6
- images_held: int32 [8], P(('dp', 'expert')), may hold values from 2 to 4, as said below
- routes: int32 [32, 197, 2], P(('dp', 'expert')), may hold values from 0 to 31, as said below
- slot_index: int32 [32, 197, 2], P(('dp', 'expert')), may hold values from 0 to 64, as said below
- first_gain: bfloat16 [768], P('dp'), may hold values from 0.5 to 1.5
- first_shift: bfloat16 [768], P('dp'), may hold values from -1 to 1
- w_qkv: bfloat16 [3, 768, 768], P(None, 'dp', 'tensor'), may hold values from -0.21875 to 0.21875
- qv_bias: bfloat16 [2, 768], P(None, 'tensor'), may hold values from -1 to 1
- w_out: bfloat16 [768, 768], P('tensor', 'dp'), may hold values from -0.875 to 0.875
- out_bias: bfloat16 [768], P('dp'), may hold values from -1 to 1
- second_gain: bfloat16 [768], P('dp'), may hold values from 0.5 to 1.5
- second_shift: bfloat16 [768], P('dp'), may hold values from -1 to 1
- w_router: bfloat16 [768, 32], P('dp'), may hold values from -0.15625 to 0.15625
- w_in: bfloat16 [32, 768, 3072], P('expert', 'dp', 'tensor'), may hold values from -0.21875 to 0.21875
- in_bias: bfloat16 [32, 3072], P('expert', 'tensor'), may hold values from -1 to 1
- w_back: bfloat16 [32, 3072, 768], P('expert', 'tensor', 'dp'), may hold values from -1.75 to 1.75
- back_bias: bfloat16 [32, 768], P('expert', 'dp'), may hold values from -5 to 5
- cotangent: bfloat16 [32, 197, 768], P(('dp', 'expert')), may hold values from -6 to 6
Outputs:
- output: bfloat16 [32, 197, 768], P(('dp', 'expert'))
- grad_images: float32 [32, 197, 768], P(('dp', 'expert'))
- grad_first_gain: float32 [768], P('dp')
- grad_first_shift: float32 [768], P('dp')
- grad_w_qkv: float32 [3, 768, 768], P(None, 'dp', 'tensor')
- grad_qv_bias: float32 [2, 768], P(None, 'tensor')
- grad_w_out: float32 [768, 768], P('tensor', 'dp')
- grad_out_bias: float32 [768], P('dp')
- grad_second_gain: float32 [768], P('dp')
- grad_second_shift: float32 [768], P('dp')
- grad_w_router: float32 [768, 32], P('dp')
- grad_w_in: float32 [32, 768, 3072], P('expert', 'dp', 'tensor')
- grad_in_bias: float32 [32, 3072], P('expert', 'tensor')
- grad_w_back: float32 [32, 3072, 768], P('expert', 'tensor', 'dp')
- grad_back_bias: float32 [32, 768], P('expert', 'dp')
The draws below stay inside these ranges and needn't reach their ends.
Inputs may be any that keep to these rules, and one draw needn't show every extreme that they name: `images_held`: the first images of a group are the real ones; some group is full. `routes`: a token names two different experts. `slot_index`: within one group the kept choices of one expert take the slots 0 to n - 1 once each, in the order of tokens and choices; 64 marks a dropped choice, and every choice of a token of an image past the group's count is dropped; some expert takes all 64 slots in every group.
All inputs are finite; a program needn't handle non-finite values.
Results may differ from the reference program's by a relative error of at most 0.013.
Values may be sent and summed in bfloat16 or wider, within the bound.
No kernel may reach another device: no remote copies, remote signals or barrier semaphores. Data moves between devices by JAX's collectives and lax.ppermute only.
A program may use at most 256 MiB of HBM per device.

```python
import jax
import jax.numpy as jnp
from jax import lax

D = 768
HEADS = 12
HEAD_DIM = 64
FF = 3072
EXPERTS = 32
S = 197
TOPK = 2
IMG_DEV = 4
CAP = 64
GROUPS = 8
IMAGES = 32


def routing(key):
    keys_list = jax.random.split(key, 8)
    token_count = IMG_DEV * S
    expert_order = jax.random.permutation(keys_list[0], EXPERTS)
    coin_flip = jax.random.randint(keys_list[1], (GROUPS, token_count), 0, 2)
    spread_pick = jax.random.randint(keys_list[2], (GROUPS, token_count), 0, EXPERTS)
    narrow_pick = jax.random.randint(keys_list[3], (GROUPS, token_count), 0, max(EXPERTS // 4, 1))
    favoured = jax.random.randint(keys_list[4], (), 0, EXPERTS)
    position = jnp.arange(token_count, dtype=jnp.int32)
    common = expert_order[jnp.where(coin_flip == 1, spread_pick, narrow_pick)]
    first_pick = jnp.where(position[None, :] <= CAP, favoured, common)
    offset = jax.random.randint(keys_list[5], (GROUPS, token_count), 1, EXPERTS)
    second_pick = (first_pick + offset) % EXPERTS
    held_count = jax.random.randint(keys_list[6], (GROUPS,), (IMG_DEV + 1) // 2, IMG_DEV + 1)
    full_group = jax.random.randint(keys_list[7], (), 0, GROUPS)
    held_count = jnp.where(jnp.arange(GROUPS, dtype=jnp.int32) == full_group, IMG_DEV, held_count).astype(jnp.int32)
    pair_picks = jnp.stack([first_pick, second_pick], axis=-1).reshape(GROUPS, token_count * TOPK)
    alive_rows = jnp.repeat((position // S)[None, :] < held_count[:, None], TOPK, axis=1).astype(jnp.int32)
    onehot = (pair_picks[:, :, None] == jnp.arange(EXPERTS, dtype=jnp.int32)[None, None, :]).astype(jnp.int32)
    onehot = onehot * alive_rows[:, :, None]
    earlier = jnp.cumsum(onehot, axis=1) - onehot
    position_in = jnp.sum(earlier * onehot, axis=-1)
    slot_rows = jnp.where((alive_rows == 1) & (position_in < CAP), position_in, CAP).astype(jnp.int32)
    return (pair_picks.reshape(IMAGES, S, TOPK).astype(jnp.int32), slot_rows.reshape(IMAGES, S, TOPK), held_count)


def draw_images_held(key, part):
    picks, slot_rows, held_count = routing(key)
    return held_count


def draw_routes(key, part):
    picks, slot_rows, held_count = routing(key)
    return picks


def draw_slot_index(key, part):
    picks, slot_rows, held_count = routing(key)
    return slot_rows


def levels(own_key, extent, pieces, smallest, high):
    level, own = 1.0, jax.random.fold_in(own_key, 6)
    for dim, shards_of in pieces:
        heights = jnp.exp(jax.random.uniform(jax.random.fold_in(own, dim), (shards_of,), jnp.float32, smallest / len(pieces), high / len(pieces)))
        level = level * jnp.repeat(heights, extent[dim] // shards_of).reshape([-1 if axis == dim else 1 for axis in range(len(extent))])
    return level


def normal_values(key, extent, scale, most, cuts=(), kind=jnp.bfloat16):
    loudness = levels(key, extent, cuts, -0.22, 0.18) if cuts else 1.0
    entries = jax.random.normal(key, extent, jnp.float32) * scale * loudness
    return jnp.minimum(jnp.maximum(entries, -most), most).astype(kind)


def setup_inputs(seed: int = 0) -> dict:
    key_of = jax.random.split(jax.random.key(seed), 19)
    images = normal_values(key_of[0], (IMAGES, S, D), 1.0, 6.0, ((0, 8),))
    images_held = draw_images_held(jax.random.fold_in(key_of[18], 71), 0)
    routes = draw_routes(jax.random.fold_in(key_of[18], 71), 0)
    slot_index = draw_slot_index(jax.random.fold_in(key_of[18], 71), 0)
    first_gain = jnp.clip(1.0 + 0.1 * jax.random.normal(key_of[4], (D,), jnp.float32), 0.5, 1.5).astype(jnp.bfloat16)
    first_shift = normal_values(key_of[5], (D,), 0.2, 1.0, ((0, 4),))
    w_qkv = normal_values(key_of[6], (3, D, D), D ** -0.5, 0.21875, ((1, 4), (2, 4)))
    qv_bias = normal_values(key_of[7], (2, D), 0.2, 1.0, ((1, 4),))
    w_out = normal_values(key_of[8], (D, D), (D // 16) ** -0.5, 0.875, ((0, 4), (1, 4)))
    out_bias = normal_values(key_of[9], (D,), 0.2, 1.0, ((0, 4),))
    second_gain = jnp.clip(1.0 + 0.1 * jax.random.normal(key_of[10], (D,), jnp.float32), 0.5, 1.5).astype(jnp.bfloat16)
    second_shift = normal_values(key_of[11], (D,), 0.2, 1.0, ((0, 4),))
    w_router = normal_values(key_of[12], (D, EXPERTS), (2 * D) ** -0.5, 0.15625, ((0, 4),))
    w_in = normal_values(key_of[13], (EXPERTS, D, FF), D ** -0.5, 0.21875, ((0, 2), (1, 4), (2, 4)))
    in_bias = normal_values(key_of[14], (EXPERTS, FF), 0.2, 1.0, ((0, 2), (1, 4)))
    w_back = normal_values(key_of[15], (EXPERTS, FF, D), (max(FF // 256, 1)) ** -0.5, 1.75, ((0, 2), (1, 4), (2, 4)))
    back_bias = normal_values(key_of[16], (EXPERTS, D), 1.0, 5.0, ((0, 2), (1, 4)))
    cotangent = normal_values(key_of[17], (IMAGES, S, D), 1.0, 6.0, ((0, 8),))
    return {"images": images, "images_held": images_held, "routes": routes, "slot_index": slot_index, "first_gain": first_gain, "first_shift": first_shift, "w_qkv": w_qkv, "qv_bias": qv_bias, "w_out": w_out, "out_bias": out_bias, "second_gain": second_gain, "second_shift": second_shift, "w_router": w_router, "w_in": w_in, "in_bias": in_bias, "w_back": w_back, "back_bias": back_bias, "cotangent": cotangent}


EPS = 1e-06
HI = lax.Precision.HIGHEST

@jax.custom_vjp
def low(v):
    return lax.optimization_barrier(v.astype(jnp.bfloat16)).astype(jnp.float32)

@jax.custom_vjp
def low_back(v):
    return v

def low_keep(v):
    return (low(v), None)

def low_pass(kept, grad):
    return (grad,)

def back_keep(v):
    return (v, None)

def back_low(kept, grad):
    return (low(grad),)
low.defvjp(low_keep, low_pass)
low_back.defvjp(back_keep, back_low)

def layer_norm(values, norm_gain, norm_shift):
    average = lax.optimization_barrier(jnp.mean(values, axis=-1, keepdims=True))
    centred = values - average
    spread = lax.optimization_barrier(jnp.mean(centred * centred, axis=-1, keepdims=True))
    return centred * lax.rsqrt(spread + EPS) * norm_gain + norm_shift

def image_attention(triple):
    queries, key_rows, value_rows = triple
    scores = low_back(jnp.einsum('qhd,khd->hqk', queries, key_rows, precision=HI) * HEAD_DIM ** (-0.5))
    weights = low(jax.nn.softmax(scores, axis=-1))
    return jnp.einsum('hqk,khd->qhd', weights, value_rows, precision=HI)

def forward(params, live_rows, target, routes):
    images, first_gain, first_shift, w_qkv, qv_bias, w_out, out_bias, second_gain, second_shift, w_router, w_in, in_bias, w_back, back_bias = params
    normed = low(layer_norm(images, first_gain, first_shift))
    queries = low(low_back(jnp.einsum('isd,de->ise', normed, w_qkv[0], precision=HI)) + qv_bias[0])
    key_rows = low(low_back(jnp.einsum('isd,de->ise', normed, w_qkv[1], precision=HI)))
    value_rows = low(low_back(jnp.einsum('isd,de->ise', normed, w_qkv[2], precision=HI)) + qv_bias[1])
    head_shape = (IMAGES, S, HEADS, HEAD_DIM)
    attended = lax.map(jax.checkpoint(image_attention), (queries.reshape(head_shape), key_rows.reshape(head_shape), value_rows.reshape(head_shape)))
    attended = low(low_back(attended.reshape(IMAGES, S, D)))
    mixed = images + low_back(jnp.einsum('isd,de->ise', attended, w_out, precision=HI)) + out_bias
    routed = low(layer_norm(mixed, second_gain, second_shift))
    logits = low_back(jnp.einsum('isd,de->ise', routed, w_router, precision=HI))
    probs = jax.nn.softmax(logits, axis=-1)
    gates = jnp.take_along_axis(probs, routes, axis=-1)
    pair_rows = jnp.broadcast_to(routed[:, :, None, :], (IMAGES, S, TOPK, D)).reshape(GROUPS, IMG_DEV * S * TOPK, D)
    flat_target = target.reshape(GROUPS, IMG_DEV * S * TOPK)

    def fill_group(group_rows, group_target):
        empty = jnp.zeros((EXPERTS * CAP + 1, D), jnp.float32)
        return empty.at[group_target].set(group_rows)[:EXPERTS * CAP]
    buffers = low_back(jax.vmap(fill_group)(pair_rows, flat_target).reshape(GROUPS, EXPERTS, CAP, D))
    hidden_pre = low_back(jnp.einsum('gecd,edf->gecf', buffers, w_in, precision=HI)) + in_bias[None, :, None, :]
    hidden = low(jax.nn.gelu(hidden_pre))
    returned = low(low_back(jnp.einsum('gecf,efd->gecd', hidden, w_back, precision=HI) + back_bias[None, :, None, :]))
    padded = jnp.concatenate([returned.reshape(GROUPS, EXPERTS * CAP, D), jnp.zeros((GROUPS, 1, D), jnp.float32)], axis=1)
    picked = jnp.take_along_axis(padded, flat_target[:, :, None], axis=1).reshape(IMAGES, S, TOPK, D)
    expert_mix = lax.optimization_barrier(jnp.sum(gates[..., None] * picked, axis=2))
    return live_rows * (mixed + expert_mix)

def reference(images, images_held, routes, slot_index, first_gain, first_shift, w_qkv, qv_bias, w_out, out_bias, second_gain, second_shift, w_router, w_in, in_bias, w_back, back_bias, cotangent):
    params = tuple((array.astype(jnp.float32) for array in (images, first_gain, first_shift, w_qkv, qv_bias, w_out, out_bias, second_gain, second_shift, w_router, w_in, in_bias, w_back, back_bias)))
    image_live = jnp.arange(IMAGES, dtype=jnp.int32) % IMG_DEV < jnp.repeat(images_held, IMG_DEV)
    live_rows = image_live.astype(jnp.float32)[:, None, None]
    target = jnp.where(slot_index < CAP, routes * CAP + slot_index, EXPERTS * CAP).astype(jnp.int32)

    def run_block(*weights):
        return forward(weights, live_rows, target, routes)
    result, pullback = jax.vjp(run_block, *params)
    grads = pullback(cotangent.astype(jnp.float32))
    return (result.astype(jnp.bfloat16), grads[0], grads[1], grads[2], grads[3], grads[4], grads[5], grads[6], grads[7], grads[8], grads[9], grads[10], grads[11], grads[12], grads[13])
```

```python
import jax
import jax.numpy as jnp
from jax import lax
from jax.sharding import Mesh
from jax.sharding import PartitionSpec as P

HEAD_DIM = 64
EXPERTS = 32
TOPK = 2
CAP = 64
FF_PAIR = 2


EPS = 1e-06


def norm_parts(values, norm_gain, norm_shift):
    average = jnp.mean(values, axis=-1, keepdims=True)
    centred = values - average
    spread = jnp.mean(centred * centred, axis=-1, keepdims=True)
    inv_std = lax.rsqrt(spread + EPS)
    scaled = centred * inv_std
    return (scaled * norm_gain + norm_shift, scaled, inv_std)


def norm_back(grad_out, scaled, inv_std, norm_gain):
    grad_scaled = grad_out * norm_gain
    inner = grad_scaled - jnp.mean(grad_scaled, axis=-1, keepdims=True)
    inner = inner - scaled * jnp.mean(grad_scaled * scaled, axis=-1, keepdims=True)
    return (inner * inv_std, jnp.sum(grad_out * scaled, axis=0), jnp.sum(grad_out, axis=0))


def attention_forward(queries, key_rows, value_rows, scale):
    scores = (
        jnp.einsum("iqhd,ikhd->ihqk", queries, key_rows, preferred_element_type=jnp.float32) * scale
    )
    row_peak = jnp.max(scores, axis=-1, keepdims=True)
    log_total = row_peak + jnp.log(jnp.sum(jnp.exp(scores - row_peak), axis=-1, keepdims=True))
    weights = jnp.exp(scores - log_total).astype(jnp.bfloat16)
    attended = jnp.einsum(
        "ihqk,ikhd->iqhd", weights, value_rows, preferred_element_type=jnp.float32
    )
    return (attended, log_total)


def attention_backward(queries, key_rows, value_rows, log_total, grad_low, scale):
    scores = (
        jnp.einsum("iqhd,ikhd->ihqk", queries, key_rows, preferred_element_type=jnp.float32) * scale
    )
    probs = jnp.exp(scores - log_total)
    weights = probs.astype(jnp.bfloat16)
    grad_values = jnp.einsum(
        "ihqk,iqhd->ikhd", weights, grad_low, preferred_element_type=jnp.float32
    )
    grad_weights = jnp.einsum(
        "iqhd,ikhd->ihqk", grad_low, value_rows, preferred_element_type=jnp.float32
    )
    grad_scores = probs * (grad_weights - jnp.sum(probs * grad_weights, axis=-1, keepdims=True))
    scores_low = grad_scores.astype(jnp.bfloat16)
    grad_queries = (
        jnp.einsum("ihqk,ikhd->iqhd", scores_low, key_rows, preferred_element_type=jnp.float32)
        * scale
    )
    grad_keys = (
        jnp.einsum("ihqk,iqhd->ikhd", scores_low, queries, preferred_element_type=jnp.float32)
        * scale
    )
    return (grad_queries, grad_keys, grad_values)


def gathered_plan(
    images,
    images_held,
    routes,
    slot_index,
    first_gain,
    first_shift,
    w_qkv,
    qv_bias,
    w_out,
    out_bias,
    second_gain,
    second_shift,
    w_router,
    w_in,
    in_bias,
    w_back,
    back_bias,
    cotangent,
):
    image_count, seq_len, width = images.shape
    rows_total = image_count * seq_len
    experts_here = w_in.shape[0]
    (
        gain_first,
        shift_first,
        qkv_full,
        out_full,
        bias_out_full,
        gain_second,
        shift_second,
        router_full,
        in_full,
        back_full,
        back_bias_full,
    ) = (
        lax.all_gather(first_gain, "dp", axis=0, tiled=True),
        lax.all_gather(first_shift, "dp", axis=0, tiled=True),
        lax.all_gather(w_qkv, "dp", axis=1, tiled=True),
        lax.all_gather(w_out, "dp", axis=1, tiled=True),
        lax.all_gather(out_bias, "dp", axis=0, tiled=True),
        lax.all_gather(second_gain, "dp", axis=0, tiled=True),
        lax.all_gather(second_shift, "dp", axis=0, tiled=True),
        lax.all_gather(w_router, "dp", axis=0, tiled=True),
        lax.all_gather(w_in, "dp", axis=1, tiled=True),
        lax.all_gather(w_back, "dp", axis=2, tiled=True),
        lax.all_gather(back_bias, "dp", axis=1, tiled=True),
    )
    gain_first = gain_first.astype(jnp.float32)
    gain_second = gain_second.astype(jnp.float32)
    inputs = images.reshape(rows_total, width).astype(jnp.float32)
    live_image = (jnp.arange(image_count, dtype=jnp.int32) < images_held[0]).astype(jnp.float32)
    live_rows = jnp.repeat(live_image, seq_len)[:, None]
    normed, scaled_first, inv_first = norm_parts(
        inputs, gain_first, shift_first.astype(jnp.float32)
    )
    normed_low = normed.astype(jnp.bfloat16)
    projected = jnp.einsum("td,cde->cte", normed_low, qkv_full, preferred_element_type=jnp.float32)
    local_width = projected.shape[2]
    head_count = local_width // HEAD_DIM
    head_shape = (image_count, seq_len, head_count, HEAD_DIM)
    bias_pair = qv_bias.astype(jnp.float32)
    queries = (projected[0] + bias_pair[0]).astype(jnp.bfloat16).reshape(head_shape)
    key_rows = projected[1].astype(jnp.bfloat16).reshape(head_shape)
    value_rows = (projected[2] + bias_pair[1]).astype(jnp.bfloat16).reshape(head_shape)
    scale = HEAD_DIM ** (-0.5)
    attended, log_total = attention_forward(queries, key_rows, value_rows, scale)
    attended_low = attended.reshape(rows_total, local_width).astype(jnp.bfloat16)
    head_part = jnp.dot(attended_low, out_full, preferred_element_type=jnp.float32)
    mixed = inputs + lax.psum(head_part, "tensor") + bias_out_full.astype(jnp.float32)
    routed, scaled_second, inv_second = norm_parts(
        mixed, gain_second, shift_second.astype(jnp.float32)
    )
    routed_low = routed.astype(jnp.bfloat16)
    logits = jnp.dot(routed_low, router_full, preferred_element_type=jnp.float32)
    probs = jax.nn.softmax(logits, axis=-1)
    pair_routes = routes.reshape(rows_total, TOPK)
    pair_slots = slot_index.reshape(rows_total, TOPK)
    target = jnp.where(pair_slots < CAP, pair_routes * CAP + pair_slots, EXPERTS * CAP).reshape(
        rows_total * TOPK
    )
    gates = jnp.take_along_axis(probs, pair_routes, axis=1)
    pair_rows = jnp.repeat(routed_low, TOPK, axis=0)
    outgoing = (
        jnp.zeros((EXPERTS * CAP + 1, width), jnp.bfloat16)
        .at[target]
        .set(pair_rows)[: EXPERTS * CAP]
    )
    outgoing = outgoing.reshape(EXPERTS, 1, CAP, width)
    arrived = lax.all_to_all(outgoing, "expert", split_axis=0, concat_axis=1, tiled=True)
    sources = arrived.shape[1]
    expert_rows = arrived.reshape(experts_here, sources * CAP, width)
    hidden_pre = jnp.einsum(
        "erd,edf->erf", expert_rows, in_full, preferred_element_type=jnp.float32
    )
    hidden_pre = hidden_pre + in_bias.astype(jnp.float32)[:, None, :]
    hidden_value, gelu_pull = jax.vjp(jax.nn.gelu, hidden_pre)
    hidden_low = hidden_value.astype(jnp.bfloat16)
    expert_part = jnp.einsum(
        "erf,efd->erd", hidden_low, back_full, preferred_element_type=jnp.float32
    )
    bias_back = back_bias_full.astype(jnp.float32)[:, None, :]
    shares = lax.psum_scatter(
        expert_part.reshape(experts_here, sources, CAP, width),
        "tensor",
        scatter_dimension=2,
        tiled=True,
    )
    share_low = (shares + bias_back[:, None]).astype(jnp.bfloat16)
    pieces = lax.all_to_all(share_low, "expert", split_axis=1, concat_axis=0, tiled=True)
    returned = lax.all_gather(pieces, "tensor", axis=2, tiled=True)
    padded = jnp.concatenate(
        [returned.reshape(EXPERTS * CAP, width), jnp.zeros((1, width), jnp.bfloat16)], axis=0
    )
    picked = padded[target].astype(jnp.float32).reshape(rows_total, TOPK, width)
    expert_mix = jnp.sum(gates[:, :, None] * picked, axis=1)
    output = (live_rows * (mixed + expert_mix)).astype(jnp.bfloat16).reshape(images.shape)
    grad_rows = cotangent.reshape(rows_total, width).astype(jnp.float32) * live_rows
    grad_gates = jnp.sum(grad_rows[:, None, :] * picked, axis=-1)
    grad_picked = (
        (gates[:, :, None] * grad_rows[:, None, :])
        .astype(jnp.bfloat16)
        .reshape(rows_total * TOPK, width)
    )
    grad_outgoing = (
        jnp.zeros((EXPERTS * CAP + 1, width), jnp.bfloat16)
        .at[target]
        .set(grad_picked)[: EXPERTS * CAP]
    )
    grad_outgoing = grad_outgoing.reshape(EXPERTS, 1, CAP, width)
    grad_arrived = lax.all_to_all(grad_outgoing, "expert", split_axis=0, concat_axis=1, tiled=True)
    grad_arrived = grad_arrived.reshape(experts_here, sources * CAP, width)
    grad_back_bias = jnp.sum(grad_arrived.astype(jnp.float32), axis=1)
    grad_back_w = jnp.einsum(
        "erf,erd->efd", hidden_low, grad_arrived, preferred_element_type=jnp.float32
    )
    grad_hidden = jnp.einsum(
        "erd,efd->erf", grad_arrived, back_full, preferred_element_type=jnp.float32
    )
    grad_pre = gelu_pull(grad_hidden)[0]
    grad_in_bias_local = jnp.sum(grad_pre, axis=1)
    grad_pre_low = grad_pre.astype(jnp.bfloat16)
    grad_in_w = jnp.einsum(
        "erd,erf->edf", expert_rows, grad_pre_low, preferred_element_type=jnp.float32
    )
    grad_rows_part = jnp.einsum(
        "erf,edf->erd", grad_pre_low, in_full, preferred_element_type=jnp.float32
    )
    grad_shares = lax.psum_scatter(
        grad_rows_part.reshape(experts_here, sources, CAP, width),
        "tensor",
        scatter_dimension=2,
        tiled=True,
    ).astype(jnp.bfloat16)
    grad_pieces = lax.all_to_all(grad_shares, "expert", split_axis=1, concat_axis=0, tiled=True)
    grad_returned = lax.all_gather(grad_pieces, "tensor", axis=2, tiled=True)
    grad_padded = jnp.concatenate(
        [grad_returned.reshape(EXPERTS * CAP, width), jnp.zeros((1, width), jnp.bfloat16)], axis=0
    )
    grad_routed = jnp.sum(
        grad_padded[target].astype(jnp.float32).reshape(rows_total, TOPK, width), axis=1
    )
    expert_match = (
        pair_routes[:, :, None] == jnp.arange(EXPERTS, dtype=jnp.int32)[None, None, :]
    ).astype(jnp.float32)
    grad_probs = jnp.sum(expert_match * grad_gates[:, :, None], axis=1)
    grad_logits = probs * (grad_probs - jnp.sum(probs * grad_probs, axis=-1, keepdims=True))
    grad_logits_low = grad_logits.astype(jnp.bfloat16)
    grad_router = jnp.einsum(
        "td,te->de", routed_low, grad_logits_low, preferred_element_type=jnp.float32
    )
    grad_routed = grad_routed + jnp.einsum(
        "te,de->td", grad_logits_low, router_full, preferred_element_type=jnp.float32
    )
    grad_from_norm, grad_gain_second, grad_shift_second = norm_back(
        grad_routed, scaled_second, inv_second, gain_second
    )
    grad_mixed = grad_rows + grad_from_norm
    grad_bias_out = jnp.sum(grad_mixed, axis=0)
    grad_mixed_low = grad_mixed.astype(jnp.bfloat16)
    grad_out_w = jnp.einsum(
        "te,td->ed", attended_low, grad_mixed_low, preferred_element_type=jnp.float32
    )
    grad_attended = jnp.einsum(
        "td,ed->te", grad_mixed_low, out_full, preferred_element_type=jnp.float32
    )
    grad_attended = grad_attended.astype(jnp.bfloat16).reshape(head_shape)
    grad_queries, grad_keys, grad_values = attention_backward(
        queries, key_rows, value_rows, log_total, grad_attended, scale
    )
    grad_queries = grad_queries.reshape(rows_total, local_width)
    grad_keys = grad_keys.reshape(rows_total, local_width)
    grad_values = grad_values.reshape(rows_total, local_width)
    grad_pair_bias = jnp.stack([jnp.sum(grad_queries, axis=0), jnp.sum(grad_values, axis=0)])
    grad_proj_low = jnp.stack([grad_queries, grad_keys, grad_values]).astype(jnp.bfloat16)
    grad_qkv = jnp.einsum(
        "td,cte->cde", normed_low, grad_proj_low, preferred_element_type=jnp.float32
    )
    grad_normed_part = jnp.einsum(
        "cte,cde->td", grad_proj_low, qkv_full, preferred_element_type=jnp.float32
    )
    grad_normed = lax.psum(grad_normed_part, "tensor")
    grad_from_first, grad_gain_first, grad_shift_first = norm_back(
        grad_normed, scaled_first, inv_first, gain_first
    )
    grad_images = (grad_mixed + grad_from_first).reshape(images.shape)
    expert_start = lax.axis_index("expert") * experts_here
    full_in_bias = lax.dynamic_update_slice(
        jnp.zeros((EXPERTS, grad_in_bias_local.shape[1]), jnp.float32),
        grad_in_bias_local,
        (expert_start, jnp.zeros((), jnp.int32)),
    )
    summed = lax.psum(
        (
            grad_gain_first,
            grad_shift_first,
            grad_qkv,
            grad_pair_bias,
            grad_out_w,
            grad_bias_out,
            grad_gain_second,
            grad_shift_second,
            grad_router,
            full_in_bias,
        ),
        ("dp", "expert"),
    )
    shard_width = width // lax.axis_size("dp")
    shard_start = lax.axis_index("dp") * shard_width
    grad_first_gain = lax.dynamic_slice_in_dim(summed[0], shard_start, shard_width, 0)
    grad_first_shift = lax.dynamic_slice_in_dim(summed[1], shard_start, shard_width, 0)
    grad_w_qkv = lax.dynamic_slice_in_dim(summed[2], shard_start, shard_width, 1)
    grad_qv_bias = summed[3]
    grad_w_out = lax.dynamic_slice_in_dim(summed[4], shard_start, shard_width, 1)
    grad_out_bias = lax.dynamic_slice_in_dim(summed[5], shard_start, shard_width, 0)
    grad_second_gain = lax.dynamic_slice_in_dim(summed[6], shard_start, shard_width, 0)
    grad_second_shift = lax.dynamic_slice_in_dim(summed[7], shard_start, shard_width, 0)
    grad_w_router = lax.dynamic_slice_in_dim(summed[8], shard_start, shard_width, 0)
    grad_in_bias = lax.dynamic_slice_in_dim(summed[9], expert_start, experts_here, 0)
    grad_w_in, grad_w_back, grad_back_shard = (
        lax.psum_scatter(grad_in_w, "dp", scatter_dimension=1, tiled=True),
        lax.psum_scatter(grad_back_w, "dp", scatter_dimension=2, tiled=True),
        lax.psum_scatter(grad_back_bias, "dp", scatter_dimension=1, tiled=True),
    )
    return (
        output,
        grad_images,
        grad_first_gain,
        grad_first_shift,
        grad_w_qkv,
        grad_qv_bias,
        grad_w_out,
        grad_out_bias,
        grad_second_gain,
        grad_second_shift,
        grad_w_router,
        grad_w_in,
        grad_in_bias,
        grad_w_back,
        grad_back_shard,
    )


def swap(values, axes):
    return lax.all_to_all(values, axes, split_axis=0, concat_axis=0, tiled=True)


def high_low(values):
    high = lax.reduce_precision(values, 8, 7)
    return high.astype(jnp.bfloat16), (values - high).astype(jnp.bfloat16)


def moved_plan(
    images,
    images_held,
    routes,
    slot_index,
    first_gain,
    first_shift,
    w_qkv,
    qv_bias,
    w_out,
    out_bias,
    second_gain,
    second_shift,
    w_router,
    w_in,
    in_bias,
    w_back,
    back_bias,
    cotangent,
):
    f32, bf16 = jnp.float32, jnp.bfloat16
    image_count, seq_len, width = images.shape
    rows_total = image_count * seq_len
    experts_here, shard_width, ff_here = w_in.shape
    data, sources = lax.axis_size("dp"), lax.axis_size("expert")
    outer, inner = lax.axis_size("outer"), lax.axis_size("inner")
    tensor = outer * inner
    tensor_axes = ("outer", "inner")
    groups = data * sources
    owners = data * inner
    mine = experts_here // owners
    slots = EXPERTS * CAP
    slots_plane = slots // inner
    dp_at = lax.axis_index("dp")
    inner_at = lax.axis_index("inner")
    tensor_at = lax.axis_index(tensor_axes)
    owner_at = dp_at * inner + inner_at
    local_width = w_out.shape[0]
    slice_width = width // tensor

    def collect(shard):
        parts = swap(shard, ("dp", "inner"))
        parts = parts.reshape(data, inner, mine, shard_width, ff_here)
        return parts.transpose(2, 0, 3, 1, 4).reshape(mine, width, inner * ff_here)

    in_mine = collect(w_in)
    back_mine = collect(w_back.transpose(0, 2, 1))

    packed = jnp.concatenate(
        [
            w_qkv.transpose(1, 0, 2).reshape(shard_width, 3 * local_width),
            w_out.T,
            w_router,
            back_bias.T,
            jnp.stack([first_gain, first_shift, out_bias, second_gain, second_shift], axis=1),
        ],
        axis=1,
    )
    packed = lax.all_gather(packed, "dp", axis=0, tiled=True)
    cuts = [3 * local_width, local_width, EXPERTS, experts_here]
    qkv_full, out_turned, router_full, back_bias_turned, vectors = jnp.split(
        packed, [sum(cuts[: i + 1]) for i in range(4)], axis=1
    )
    gain_first, shift_first, bias_out_full, gain_second, shift_second = (
        vectors[:, i].astype(f32) for i in range(5)
    )
    out_whole = lax.all_gather(out_turned, tensor_axes, axis=1, tiled=True)
    in_bias_all = lax.all_gather(in_bias, "inner", axis=1, tiled=True)
    in_bias_mine = lax.dynamic_slice_in_dim(in_bias_all, owner_at * mine, mine, 0)

    pair_routes = routes.reshape(rows_total, TOPK)
    pair_slots = slot_index.reshape(rows_total, TOPK)
    home, within = pair_routes // experts_here, pair_routes % experts_here
    owner, nth = within // mine, within % mine
    place = ((owner % inner) * data + owner // inner) * sources + home
    target = jnp.where(pair_slots < CAP, (place * mine + nth) * CAP + pair_slots, slots)
    plane_slots = inner_at * slots_plane + jnp.arange(slots_plane, dtype=jnp.int32)
    takes = [plane_slots[:, None] == target[None, :, k] for k in range(TOPK)]
    fill = jnp.logical_or(takes[0], takes[1]).astype(bf16)

    live_image = (jnp.arange(image_count, dtype=jnp.int32) < images_held[0]).astype(f32)
    live_rows = jnp.repeat(live_image, seq_len)[:, None]
    grad_rows = cotangent.reshape(rows_total, width).astype(f32) * live_rows

    def dispatch(rows):
        return jnp.dot(fill, rows, preferred_element_type=f32).astype(bf16)

    cot_out = dispatch(grad_rows.astype(bf16)).reshape(groups, mine * CAP, width)
    cot_rows = swap(cot_out, ("dp", "expert")).reshape(groups, mine, CAP, width)

    inputs = images.reshape(rows_total, width).astype(f32)
    normed, scaled_first, inv_first = norm_parts(inputs, gain_first, shift_first)
    normed_low = normed.astype(bf16)
    projected = jnp.dot(normed_low, qkv_full, preferred_element_type=f32)
    head_count = local_width // HEAD_DIM
    head_shape = (image_count, seq_len, head_count, HEAD_DIM)
    bias_pair = qv_bias.astype(f32)
    queries, key_rows, value_rows = (
        projected[:, i * local_width : (i + 1) * local_width] for i in range(3)
    )
    queries = (queries + bias_pair[0]).astype(bf16).reshape(head_shape)
    key_rows = key_rows.astype(bf16).reshape(head_shape)
    value_rows = (value_rows + bias_pair[1]).astype(bf16).reshape(head_shape)
    scale = HEAD_DIM ** (-0.5)
    attended, log_total = attention_forward(queries, key_rows, value_rows, scale)
    attended_low = attended.reshape(rows_total, local_width).astype(bf16)
    attended_all = lax.all_gather(attended_low, tensor_axes, axis=1, tiled=True)
    mixed = inputs + bias_out_full
    mixed = mixed + jnp.einsum("te,de->td", attended_all, out_whole, preferred_element_type=f32)
    routed, scaled_second, inv_second = norm_parts(mixed, gain_second, shift_second)
    routed_low = routed.astype(bf16)
    logits = jnp.dot(routed_low, router_full, preferred_element_type=f32)
    probs = jax.nn.softmax(logits, axis=-1)
    expert_ids = jnp.arange(EXPERTS, dtype=jnp.int32)
    matches = [(pair_routes[:, k : k + 1] == expert_ids).astype(f32) for k in range(TOPK)]
    gates = [jnp.sum(match * probs, axis=1) for match in matches]

    gate_slots = sum(
        jnp.sum(jnp.where(take, gate[None, :], 0.0), axis=1) for take, gate in zip(takes, gates)
    )
    gate_parts = jnp.stack(high_low(gate_slots.reshape(groups, mine * CAP)), axis=1)
    gate_rows = jnp.pad(gate_parts, ((0, 0), (0, 14), (0, width - mine * CAP)))
    sent = jnp.concatenate([dispatch(routed_low).reshape(groups, mine * CAP, width), gate_rows], axis=1)
    arrived = swap(sent, ("dp", "expert"))
    expert_rows = arrived[:, : mine * CAP].reshape(groups, mine, CAP, width)
    gate_here = jnp.sum(arrived[:, mine * CAP : mine * CAP + 2, : mine * CAP].astype(f32), axis=1)
    gate_here = gate_here.reshape(groups, mine, CAP, 1)
    to_experts = lambda rows: rows.transpose(1, 0, 2, 3).reshape(mine, groups * CAP, -1)
    expert_rows = to_experts(expert_rows)
    grad_returned = to_experts((gate_here * cot_rows.astype(f32)).astype(bf16))

    hidden_pre = jnp.einsum("erd,edf->erf", expert_rows, in_mine, preferred_element_type=f32)
    hidden_pre = hidden_pre + in_bias_mine.astype(f32)[:, None, :]
    hidden_value, gelu_pull = jax.vjp(jax.nn.gelu, hidden_pre)
    hidden_low = hidden_value.astype(bf16)
    expert_part = jnp.einsum("erf,edf->erd", hidden_low, back_mine, preferred_element_type=f32)
    grad_hidden = jnp.einsum("erd,edf->erf", grad_returned, back_mine, preferred_element_type=f32)
    grad_pre = gelu_pull(grad_hidden)[0]
    grad_in_bias_mine = jnp.sum(grad_pre, axis=1)
    grad_pre_low = grad_pre.astype(bf16)
    grad_rows_part = jnp.einsum("erf,edf->erd", grad_pre_low, in_mine, preferred_element_type=f32)
    grad_back_mine = jnp.einsum("erd,erf->edf", grad_returned, hidden_low, preferred_element_type=f32)
    grad_in_mine = jnp.einsum("erd,erf->edf", expert_rows, grad_pre_low, preferred_element_type=f32)
    grad_back_bias_mine = jnp.sum(grad_returned.astype(f32), axis=1)

    bias_here = lax.dynamic_slice(
        back_bias_turned, (lax.axis_index("outer") * (width // outer), owner_at * mine), (width // outer, mine)
    )
    bias_here = bias_here.T.astype(f32)[:, None, :]

    def bring(part, bias):
        share = lax.psum_scatter(part.astype(bf16), "outer", scatter_dimension=2, tiled=True)
        if bias is not None:
            share = (share.astype(f32) + bias).astype(bf16)
        share = share.reshape(mine, groups, CAP, width // outer).transpose(1, 0, 2, 3)
        rows = swap(share, ("dp", "expert")).reshape(slots_plane, width // outer)
        if inner > 1:
            rows = lax.all_to_all(rows, "inner", split_axis=1, concat_axis=0, tiled=True)
        return rows

    returned = bring(expert_part, bias_here)
    grad_buffers = bring(grad_rows_part, None)
    all_slots = jnp.arange(slots, dtype=jnp.int32)
    finds = [(target[:, k : k + 1] == all_slots).astype(bf16) for k in range(TOPK)]
    picked = [jnp.dot(find, returned, preferred_element_type=f32) for find in finds]
    cut = lambda rows: lax.dynamic_slice_in_dim(rows, tensor_at * slice_width, slice_width, 1)
    grad_rows_cut = cut(grad_rows)
    grad_routed_cut = jnp.dot(finds[0] + finds[1], grad_buffers, preferred_element_type=f32)
    gate_terms = jnp.stack([jnp.sum(grad_rows_cut * rows, axis=1) for rows in picked], axis=1)
    gate_high, gate_low = high_low(gate_terms)
    back = jnp.concatenate([grad_routed_cut.astype(bf16), gate_high, gate_low], axis=1)
    back = lax.all_gather(back, tensor_axes, axis=0, tiled=False)
    grad_gates = jnp.sum(back[:, :, slice_width:].astype(f32), axis=0)
    grad_gates = grad_gates[:, :TOPK] + grad_gates[:, TOPK:]
    grad_routed = back[:, :, :slice_width].transpose(1, 0, 2).reshape(rows_total, width).astype(f32)
    expert_mix = gates[0][:, None] * picked[0] + gates[1][:, None] * picked[1]
    output_cut = (live_rows * (cut(mixed) + expert_mix)).astype(bf16)
    output = lax.all_gather(output_cut, tensor_axes, axis=1, tiled=True).reshape(images.shape)

    grad_probs = sum(match * grad_gates[:, k : k + 1] for k, match in enumerate(matches))
    grad_logits = probs * (grad_probs - jnp.sum(probs * grad_probs, axis=-1, keepdims=True))
    grad_logits_low = grad_logits.astype(bf16)
    grad_router = jnp.einsum("td,te->de", routed_low, grad_logits_low, preferred_element_type=f32)
    grad_routed = grad_routed + jnp.einsum(
        "te,de->td", grad_logits_low, router_full, preferred_element_type=f32
    )
    grad_from_norm, grad_gain_second, grad_shift_second = norm_back(
        grad_routed, scaled_second, inv_second, gain_second
    )
    grad_mixed = grad_rows + grad_from_norm
    grad_bias_out = jnp.sum(grad_mixed, axis=0)
    grad_mixed_low = grad_mixed.astype(bf16)
    grad_out_turned = jnp.einsum("td,te->de", grad_mixed_low, attended_low, preferred_element_type=f32)
    grad_attended = jnp.dot(grad_mixed_low, out_turned, preferred_element_type=f32)
    grad_attended = grad_attended.astype(bf16).reshape(head_shape)
    grad_queries, grad_keys, grad_values = (
        grads.reshape(rows_total, local_width)
        for grads in attention_backward(
            queries, key_rows, value_rows, log_total, grad_attended, scale
        )
    )
    grad_pair_bias = jnp.stack([jnp.sum(grad_queries, axis=0), jnp.sum(grad_values, axis=0)])
    grad_proj_low = jnp.concatenate([grad_queries, grad_keys, grad_values], axis=1).astype(bf16)
    grad_qkv = jnp.einsum("td,te->de", normed_low, grad_proj_low, preferred_element_type=f32)
    grad_normed_part = jnp.einsum("te,de->td", grad_proj_low, qkv_full, preferred_element_type=f32)
    grad_normed = lax.psum(grad_normed_part.astype(bf16), tensor_axes).astype(f32)
    grad_from_first, grad_gain_first, grad_shift_first = norm_back(
        grad_normed, scaled_first, inv_first, gain_first
    )
    grad_images = (grad_mixed + grad_from_first).reshape(images.shape)

    def spread(grads):
        parts = grads.astype(bf16).reshape(mine, data, shard_width, inner, ff_here)
        parts = parts.transpose(1, 3, 0, 2, 4).reshape(experts_here, shard_width, ff_here)
        return swap(parts, ("dp", "inner")).astype(f32)

    grad_w_back = spread(grad_back_mine).transpose(0, 2, 1)
    grad_w_in = spread(grad_in_mine)
    bias_grads = jnp.concatenate([grad_in_bias_mine, grad_back_bias_mine], axis=1)
    bias_grads = lax.all_gather(bias_grads, ("dp", "inner"), axis=0, tiled=True)
    grad_in_bias = lax.dynamic_slice_in_dim(bias_grads, inner_at * ff_here, ff_here, 1)
    grad_back_shard = lax.dynamic_slice_in_dim(
        bias_grads, inner * ff_here + dp_at * shard_width, shard_width, 1
    )
    early = jnp.concatenate(
        [
            grad_qkv,
            grad_out_turned,
            grad_router,
            jnp.stack([grad_bias_out, grad_gain_second, grad_shift_second], axis=1),
        ],
        axis=1,
    )
    early = lax.psum(lax.psum_scatter(early, "dp", scatter_dimension=0, tiled=True), "expert")
    grad_w_qkv = early[:, : 3 * local_width].reshape(shard_width, 3, local_width).transpose(1, 0, 2)
    grad_w_out = early[:, 3 * local_width : 4 * local_width].T
    grad_w_router = early[:, 4 * local_width : 4 * local_width + EXPERTS]
    grad_out_bias, grad_second_gain, grad_second_shift = (
        early[:, 4 * local_width + EXPERTS + i] for i in range(3)
    )
    grad_qv_bias, grad_first_norm = lax.psum(
        (grad_pair_bias, jnp.stack([grad_gain_first, grad_shift_first])), ("dp", "expert")
    )
    grad_first_norm = lax.dynamic_slice_in_dim(grad_first_norm, dp_at * shard_width, shard_width, 1)
    return (
        output,
        grad_images,
        grad_first_norm[0],
        grad_first_norm[1],
        grad_w_qkv,
        grad_qv_bias,
        grad_w_out,
        grad_out_bias,
        grad_second_gain,
        grad_second_shift,
        grad_w_router,
        grad_w_in,
        grad_in_bias,
        grad_w_back,
        grad_back_shard,
    )


def solution(mesh):
    data, expert, tensor = (mesh.shape[name] for name in ("dp", "expert", "tensor"))
    experts_here = EXPERTS // expert
    inner = FF_PAIR if tensor % FF_PAIR == 0 else 1
    if experts_here % (data * inner):
        return jax.shard_map(
            gathered_plan,
            mesh=mesh,
            in_specs=(
                P(("dp", "expert"), None, None),
                P(("dp", "expert")),
                P(("dp", "expert"), None, None),
                P(("dp", "expert"), None, None),
                P("dp"),
                P("dp"),
                P(None, "dp", "tensor"),
                P(None, "tensor"),
                P("tensor", "dp"),
                P("dp"),
                P("dp"),
                P("dp"),
                P("dp", None),
                P("expert", "dp", "tensor"),
                P("expert", "tensor"),
                P("expert", "tensor", "dp"),
                P("expert", "dp"),
                P(("dp", "expert"), None, None),
            ),
            out_specs=(
                P(("dp", "expert"), None, None),
                P(("dp", "expert"), None, None),
                P("dp"),
                P("dp"),
                P(None, "dp", "tensor"),
                P(None, "tensor"),
                P("tensor", "dp"),
                P("dp"),
                P("dp"),
                P("dp"),
                P("dp", None),
                P("expert", "dp", "tensor"),
                P("expert", "tensor"),
                P("expert", "tensor", "dp"),
                P("expert", "dp"),
            ),
            check_vma=False,
        )
    devices = mesh.devices.reshape(data, expert, tensor // inner, inner)
    split_mesh = Mesh(devices, ("dp", "expert", "outer", "inner"))
    return jax.shard_map(
        moved_plan,
        mesh=split_mesh,
        in_specs=(
            P(("dp", "expert"), None, None),
            P(("dp", "expert")),
            P(("dp", "expert"), None, None),
            P(("dp", "expert"), None, None),
            P("dp"),
            P("dp"),
            P(None, "dp", ("outer", "inner")),
            P(None, ("outer", "inner")),
            P(("outer", "inner"), "dp"),
            P("dp"),
            P("dp"),
            P("dp"),
            P("dp", None),
            P("expert", "dp", ("outer", "inner")),
            P("expert", ("outer", "inner")),
            P("expert", ("outer", "inner"), "dp"),
            P("expert", "dp"),
            P(("dp", "expert"), None, None),
        ),
        out_specs=(
            P(("dp", "expert"), None, None),
            P(("dp", "expert"), None, None),
            P("dp"),
            P("dp"),
            P(None, "dp", ("outer", "inner")),
            P(None, ("outer", "inner")),
            P(("outer", "inner"), "dp"),
            P("dp"),
            P("dp"),
            P("dp"),
            P("dp", None),
            P("expert", "dp", ("outer", "inner")),
            P("expert", ("outer", "inner")),
            P("expert", ("outer", "inner"), "dp"),
            P("expert", "dp"),
        ),
        check_vma=False,
    )
```

```python
import functools
import math

import jax
import jax.numpy as jnp
from jax import lax
from jax.experimental import pallas as pl
from jax.experimental.pallas import tpu as pltpu
from jax.sharding import Mesh
from jax.sharding import PartitionSpec as P

HEAD_DIM = 64
EXPERTS = 32
TOPK = 2
CAP = 64
FF_PAIR = 2
VMEM_LIMIT = 56 * 1024 * 1024
GELU_SCALE = (2.0 / math.pi) ** 0.5
GELU_CUBE = 0.044715

DP = "dp"
EXPERT = "expert"
TENSOR = "tensor"
OUTER = "outer"
INNER = "inner"


EPS = 1e-06


def norm_parts(values, norm_gain, norm_shift):
    average = jnp.mean(values, axis=-1, keepdims=True)
    centred = values - average
    spread = jnp.mean(centred * centred, axis=-1, keepdims=True)
    inv_std = lax.rsqrt(spread + EPS)
    scaled = centred * inv_std
    return (scaled * norm_gain + norm_shift, scaled, inv_std)


def norm_back(grad_out, scaled, inv_std, norm_gain):
    grad_scaled = grad_out * norm_gain
    inner = grad_scaled - jnp.mean(grad_scaled, axis=-1, keepdims=True)
    inner = inner - scaled * jnp.mean(grad_scaled * scaled, axis=-1, keepdims=True)
    return (inner * inv_std, jnp.sum(grad_out * scaled, axis=0), jnp.sum(grad_out, axis=0))


def attention_forward(queries, key_rows, value_rows, scale):
    scores = (
        jnp.einsum("iqhd,ikhd->ihqk", queries, key_rows, preferred_element_type=jnp.float32) * scale
    )
    row_peak = jnp.max(scores, axis=-1, keepdims=True)
    log_total = row_peak + jnp.log(jnp.sum(jnp.exp(scores - row_peak), axis=-1, keepdims=True))
    weights = jnp.exp(scores - log_total).astype(jnp.bfloat16)
    attended = jnp.einsum(
        "ihqk,ikhd->iqhd", weights, value_rows, preferred_element_type=jnp.float32
    )
    return (attended, log_total)


def attention_backward(queries, key_rows, value_rows, log_total, grad_low, scale):
    scores = (
        jnp.einsum("iqhd,ikhd->ihqk", queries, key_rows, preferred_element_type=jnp.float32) * scale
    )
    probs = jnp.exp(scores - log_total)
    weights = probs.astype(jnp.bfloat16)
    grad_values = jnp.einsum(
        "ihqk,iqhd->ikhd", weights, grad_low, preferred_element_type=jnp.float32
    )
    grad_weights = jnp.einsum(
        "iqhd,ikhd->ihqk", grad_low, value_rows, preferred_element_type=jnp.float32
    )
    grad_scores = probs * (grad_weights - jnp.sum(probs * grad_weights, axis=-1, keepdims=True))
    scores_low = grad_scores.astype(jnp.bfloat16)
    grad_queries = (
        jnp.einsum("ihqk,ikhd->iqhd", scores_low, key_rows, preferred_element_type=jnp.float32)
        * scale
    )
    grad_keys = (
        jnp.einsum("ihqk,iqhd->ikhd", scores_low, queries, preferred_element_type=jnp.float32)
        * scale
    )
    return (grad_queries, grad_keys, grad_values)


def gathered_plan(
    images,
    images_held,
    routes,
    slot_index,
    first_gain,
    first_shift,
    w_qkv,
    qv_bias,
    w_out,
    out_bias,
    second_gain,
    second_shift,
    w_router,
    w_in,
    in_bias,
    w_back,
    back_bias,
    cotangent,
):
    image_count, seq_len, width = images.shape
    rows_total = image_count * seq_len
    experts_here = w_in.shape[0]
    (
        gain_first,
        shift_first,
        qkv_full,
        out_full,
        bias_out_full,
        gain_second,
        shift_second,
        router_full,
        in_full,
        back_full,
        back_bias_full,
    ) = (
        lax.all_gather(first_gain, DP, axis=0, tiled=True),
        lax.all_gather(first_shift, DP, axis=0, tiled=True),
        lax.all_gather(w_qkv, DP, axis=1, tiled=True),
        lax.all_gather(w_out, DP, axis=1, tiled=True),
        lax.all_gather(out_bias, DP, axis=0, tiled=True),
        lax.all_gather(second_gain, DP, axis=0, tiled=True),
        lax.all_gather(second_shift, DP, axis=0, tiled=True),
        lax.all_gather(w_router, DP, axis=0, tiled=True),
        lax.all_gather(w_in, DP, axis=1, tiled=True),
        lax.all_gather(w_back, DP, axis=2, tiled=True),
        lax.all_gather(back_bias, DP, axis=1, tiled=True),
    )
    gain_first = gain_first.astype(jnp.float32)
    gain_second = gain_second.astype(jnp.float32)
    inputs = images.reshape(rows_total, width).astype(jnp.float32)
    live_image = (jnp.arange(image_count, dtype=jnp.int32) < images_held[0]).astype(jnp.float32)
    live_rows = jnp.repeat(live_image, seq_len)[:, None]
    normed, scaled_first, inv_first = norm_parts(
        inputs, gain_first, shift_first.astype(jnp.float32)
    )
    normed_low = normed.astype(jnp.bfloat16)
    projected = jnp.einsum("td,cde->cte", normed_low, qkv_full, preferred_element_type=jnp.float32)
    local_width = projected.shape[2]
    head_count = local_width // HEAD_DIM
    head_shape = (image_count, seq_len, head_count, HEAD_DIM)
    bias_pair = qv_bias.astype(jnp.float32)
    queries = (projected[0] + bias_pair[0]).astype(jnp.bfloat16).reshape(head_shape)
    key_rows = projected[1].astype(jnp.bfloat16).reshape(head_shape)
    value_rows = (projected[2] + bias_pair[1]).astype(jnp.bfloat16).reshape(head_shape)
    scale = HEAD_DIM ** (-0.5)
    attended, log_total = attention_forward(queries, key_rows, value_rows, scale)
    attended_low = attended.reshape(rows_total, local_width).astype(jnp.bfloat16)
    head_part = jnp.dot(attended_low, out_full, preferred_element_type=jnp.float32)
    mixed = inputs + lax.psum(head_part, TENSOR) + bias_out_full.astype(jnp.float32)
    routed, scaled_second, inv_second = norm_parts(
        mixed, gain_second, shift_second.astype(jnp.float32)
    )
    routed_low = routed.astype(jnp.bfloat16)
    logits = jnp.dot(routed_low, router_full, preferred_element_type=jnp.float32)
    probs = jax.nn.softmax(logits, axis=-1)
    pair_routes = routes.reshape(rows_total, TOPK)
    pair_slots = slot_index.reshape(rows_total, TOPK)
    target = jnp.where(pair_slots < CAP, pair_routes * CAP + pair_slots, EXPERTS * CAP).reshape(
        rows_total * TOPK
    )
    gates = jnp.take_along_axis(probs, pair_routes, axis=1)
    pair_rows = jnp.repeat(routed_low, TOPK, axis=0)
    outgoing = (
        jnp.zeros((EXPERTS * CAP + 1, width), jnp.bfloat16)
        .at[target]
        .set(pair_rows)[: EXPERTS * CAP]
    )
    outgoing = outgoing.reshape(EXPERTS, 1, CAP, width)
    arrived = lax.all_to_all(outgoing, EXPERT, split_axis=0, concat_axis=1, tiled=True)
    sources = arrived.shape[1]
    expert_rows = arrived.reshape(experts_here, sources * CAP, width)
    hidden_pre = jnp.einsum(
        "erd,edf->erf", expert_rows, in_full, preferred_element_type=jnp.float32
    )
    hidden_pre = hidden_pre + in_bias.astype(jnp.float32)[:, None, :]
    hidden_value, gelu_pull = jax.vjp(jax.nn.gelu, hidden_pre)
    hidden_low = hidden_value.astype(jnp.bfloat16)
    expert_part = jnp.einsum(
        "erf,efd->erd", hidden_low, back_full, preferred_element_type=jnp.float32
    )
    bias_back = back_bias_full.astype(jnp.float32)[:, None, :]
    shares = lax.psum_scatter(
        expert_part.reshape(experts_here, sources, CAP, width),
        TENSOR,
        scatter_dimension=2,
        tiled=True,
    )
    share_low = (shares + bias_back[:, None]).astype(jnp.bfloat16)
    pieces = lax.all_to_all(share_low, EXPERT, split_axis=1, concat_axis=0, tiled=True)
    returned = lax.all_gather(pieces, TENSOR, axis=2, tiled=True)
    padded = jnp.concatenate(
        [returned.reshape(EXPERTS * CAP, width), jnp.zeros((1, width), jnp.bfloat16)], axis=0
    )
    picked = padded[target].astype(jnp.float32).reshape(rows_total, TOPK, width)
    expert_mix = jnp.sum(gates[:, :, None] * picked, axis=1)
    output = (live_rows * (mixed + expert_mix)).astype(jnp.bfloat16).reshape(images.shape)
    grad_rows = cotangent.reshape(rows_total, width).astype(jnp.float32) * live_rows
    grad_gates = jnp.sum(grad_rows[:, None, :] * picked, axis=-1)
    grad_picked = (
        (gates[:, :, None] * grad_rows[:, None, :])
        .astype(jnp.bfloat16)
        .reshape(rows_total * TOPK, width)
    )
    grad_outgoing = (
        jnp.zeros((EXPERTS * CAP + 1, width), jnp.bfloat16)
        .at[target]
        .set(grad_picked)[: EXPERTS * CAP]
    )
    grad_outgoing = grad_outgoing.reshape(EXPERTS, 1, CAP, width)
    grad_arrived = lax.all_to_all(grad_outgoing, EXPERT, split_axis=0, concat_axis=1, tiled=True)
    grad_arrived = grad_arrived.reshape(experts_here, sources * CAP, width)
    grad_back_bias = jnp.sum(grad_arrived.astype(jnp.float32), axis=1)
    grad_back_w = jnp.einsum(
        "erf,erd->efd", hidden_low, grad_arrived, preferred_element_type=jnp.float32
    )
    grad_hidden = jnp.einsum(
        "erd,efd->erf", grad_arrived, back_full, preferred_element_type=jnp.float32
    )
    grad_pre = gelu_pull(grad_hidden)[0]
    grad_in_bias_local = jnp.sum(grad_pre, axis=1)
    grad_pre_low = grad_pre.astype(jnp.bfloat16)
    grad_in_w = jnp.einsum(
        "erd,erf->edf", expert_rows, grad_pre_low, preferred_element_type=jnp.float32
    )
    grad_rows_part = jnp.einsum(
        "erf,edf->erd", grad_pre_low, in_full, preferred_element_type=jnp.float32
    )
    grad_shares = lax.psum_scatter(
        grad_rows_part.reshape(experts_here, sources, CAP, width),
        TENSOR,
        scatter_dimension=2,
        tiled=True,
    ).astype(jnp.bfloat16)
    grad_pieces = lax.all_to_all(grad_shares, EXPERT, split_axis=1, concat_axis=0, tiled=True)
    grad_returned = lax.all_gather(grad_pieces, TENSOR, axis=2, tiled=True)
    grad_padded = jnp.concatenate(
        [grad_returned.reshape(EXPERTS * CAP, width), jnp.zeros((1, width), jnp.bfloat16)], axis=0
    )
    grad_routed = jnp.sum(
        grad_padded[target].astype(jnp.float32).reshape(rows_total, TOPK, width), axis=1
    )
    expert_match = (
        pair_routes[:, :, None] == jnp.arange(EXPERTS, dtype=jnp.int32)[None, None, :]
    ).astype(jnp.float32)
    grad_probs = jnp.sum(expert_match * grad_gates[:, :, None], axis=1)
    grad_logits = probs * (grad_probs - jnp.sum(probs * grad_probs, axis=-1, keepdims=True))
    grad_logits_low = grad_logits.astype(jnp.bfloat16)
    grad_router = jnp.einsum(
        "td,te->de", routed_low, grad_logits_low, preferred_element_type=jnp.float32
    )
    grad_routed = grad_routed + jnp.einsum(
        "te,de->td", grad_logits_low, router_full, preferred_element_type=jnp.float32
    )
    grad_from_norm, grad_gain_second, grad_shift_second = norm_back(
        grad_routed, scaled_second, inv_second, gain_second
    )
    grad_mixed = grad_rows + grad_from_norm
    grad_bias_out = jnp.sum(grad_mixed, axis=0)
    grad_mixed_low = grad_mixed.astype(jnp.bfloat16)
    grad_out_w = jnp.einsum(
        "te,td->ed", attended_low, grad_mixed_low, preferred_element_type=jnp.float32
    )
    grad_attended = jnp.einsum(
        "td,ed->te", grad_mixed_low, out_full, preferred_element_type=jnp.float32
    )
    grad_attended = grad_attended.astype(jnp.bfloat16).reshape(head_shape)
    grad_queries, grad_keys, grad_values = attention_backward(
        queries, key_rows, value_rows, log_total, grad_attended, scale
    )
    grad_queries = grad_queries.reshape(rows_total, local_width)
    grad_keys = grad_keys.reshape(rows_total, local_width)
    grad_values = grad_values.reshape(rows_total, local_width)
    grad_pair_bias = jnp.stack([jnp.sum(grad_queries, axis=0), jnp.sum(grad_values, axis=0)])
    grad_proj_low = jnp.stack([grad_queries, grad_keys, grad_values]).astype(jnp.bfloat16)
    grad_qkv = jnp.einsum(
        "td,cte->cde", normed_low, grad_proj_low, preferred_element_type=jnp.float32
    )
    grad_normed_part = jnp.einsum(
        "cte,cde->td", grad_proj_low, qkv_full, preferred_element_type=jnp.float32
    )
    grad_normed = lax.psum(grad_normed_part, TENSOR)
    grad_from_first, grad_gain_first, grad_shift_first = norm_back(
        grad_normed, scaled_first, inv_first, gain_first
    )
    grad_images = (grad_mixed + grad_from_first).reshape(images.shape)
    expert_start = lax.axis_index(EXPERT) * experts_here
    full_in_bias = lax.dynamic_update_slice(
        jnp.zeros((EXPERTS, grad_in_bias_local.shape[1]), jnp.float32),
        grad_in_bias_local,
        (expert_start, jnp.zeros((), jnp.int32)),
    )
    summed = lax.psum(
        (
            grad_gain_first,
            grad_shift_first,
            grad_qkv,
            grad_pair_bias,
            grad_out_w,
            grad_bias_out,
            grad_gain_second,
            grad_shift_second,
            grad_router,
            full_in_bias,
        ),
        (DP, EXPERT),
    )
    shard_width = width // lax.axis_size(DP)
    shard_start = lax.axis_index(DP) * shard_width
    grad_first_gain = lax.dynamic_slice_in_dim(summed[0], shard_start, shard_width, 0)
    grad_first_shift = lax.dynamic_slice_in_dim(summed[1], shard_start, shard_width, 0)
    grad_w_qkv = lax.dynamic_slice_in_dim(summed[2], shard_start, shard_width, 1)
    grad_qv_bias = summed[3]
    grad_w_out = lax.dynamic_slice_in_dim(summed[4], shard_start, shard_width, 1)
    grad_out_bias = lax.dynamic_slice_in_dim(summed[5], shard_start, shard_width, 0)
    grad_second_gain = lax.dynamic_slice_in_dim(summed[6], shard_start, shard_width, 0)
    grad_second_shift = lax.dynamic_slice_in_dim(summed[7], shard_start, shard_width, 0)
    grad_w_router = lax.dynamic_slice_in_dim(summed[8], shard_start, shard_width, 0)
    grad_in_bias = lax.dynamic_slice_in_dim(summed[9], expert_start, experts_here, 0)
    grad_w_in, grad_w_back, grad_back_shard = (
        lax.psum_scatter(grad_in_w, DP, scatter_dimension=1, tiled=True),
        lax.psum_scatter(grad_back_w, DP, scatter_dimension=2, tiled=True),
        lax.psum_scatter(grad_back_bias, DP, scatter_dimension=1, tiled=True),
    )
    return (
        output,
        grad_images,
        grad_first_gain,
        grad_first_shift,
        grad_w_qkv,
        grad_qv_bias,
        grad_w_out,
        grad_out_bias,
        grad_second_gain,
        grad_second_shift,
        grad_w_router,
        grad_w_in,
        grad_in_bias,
        grad_w_back,
        grad_back_shard,
    )


def swap(values, axes):
    return lax.all_to_all(values, axes, split_axis=0, concat_axis=0, tiled=True)


def high_low(values):
    high = lax.reduce_precision(values, 8, 7)
    return high.astype(jnp.bfloat16), (values - high).astype(jnp.bfloat16)


def turned_dot(left, right, left_dim, right_dim):
    return lax.dot_general(
        left, right, (((left_dim,), (right_dim,)), ((), ())), preferred_element_type=jnp.float32
    )


def expert_kernel(
    inner,
    rows_ref,
    gate_ref,
    cot_ref,
    in_ref,
    back_ref,
    in_bias_ref,
    back_bias_ref,
    returned_ref,
    grads_ref,
    hidden_ref,
    grad_pre_ref,
    grad_turned_ref,
    grad_in_bias_ref,
    grad_back_bias_ref,
):
    f32, bf16 = jnp.float32, jnp.bfloat16
    groups, cap, width = rows_ref.shape
    chunks = in_ref.shape[0]
    data = chunks // inner
    tensor, slice_width = returned_ref.shape[1:3]
    mine = back_bias_ref.shape[1]
    total = groups * cap
    at = pl.program_id(0)
    rows = rows_ref[...].reshape(total, width)
    cot_turned = cot_ref[...].reshape(total, width).T.astype(f32)
    pair = gate_ref[:, 0:1, :].astype(f32) + gate_ref[:, 1:2, :].astype(f32)
    pair = pair.reshape(groups, pair.shape[-1])
    gate = jnp.zeros((groups, cap), f32)
    for j in range(mine):
        gate = jnp.where(at == j, pair[:, j * cap : (j + 1) * cap], gate)
    gate = jnp.concatenate([gate[g : g + 1, :] for g in range(groups)], axis=1)
    grad_turned = (cot_turned * gate).astype(bf16)
    grad_turned_ref[0] = grad_turned
    grad_returned = grad_turned.T
    grad_back_bias_ref[0] = jnp.sum(grad_returned.astype(f32), axis=0, keepdims=True)
    bias_columns = back_bias_ref[...]
    bias = jnp.zeros((width, 1), f32)
    for j in range(mine):
        bias = jnp.where(at == j, bias_columns[:, j : j + 1], bias)
    part = jnp.broadcast_to(bias, (width, total))
    back = jnp.zeros((width, total), f32)
    for t in range(inner):
        w_in = jnp.concatenate([in_ref[d * inner + t, 0] for d in range(data)], axis=0)
        w_back = jnp.concatenate([back_ref[d * inner + t, 0] for d in range(data)], axis=0)
        pre = jnp.dot(rows, w_in, preferred_element_type=f32) + in_bias_ref[0, t : t + 1, :]
        square = pre * pre
        bent = jnp.tanh(GELU_SCALE * pre * (1.0 + GELU_CUBE * square))
        half = 0.5 * (1.0 + bent)
        hidden = (pre * half).astype(bf16)
        slope = half + (0.5 * GELU_SCALE) * pre * (1.0 - bent * bent) * (
            1.0 + (3.0 * GELU_CUBE) * square
        )
        hidden_ref[0, t] = hidden
        grad_pre = jnp.dot(grad_returned, w_back, preferred_element_type=f32) * slope
        grad_in_bias_ref[0, t : t + 1, :] = jnp.sum(grad_pre, axis=0, keepdims=True)
        grad_pre = grad_pre.astype(bf16)
        grad_pre_ref[0, t] = grad_pre
        part = part + turned_dot(w_back, hidden, 1, 1)
        back = back + turned_dot(w_in, grad_pre, 1, 1)
    gate_terms = jnp.sum(part * cot_turned, axis=0, keepdims=True)
    high = gate_terms.astype(bf16)
    low = (gate_terms - high.astype(f32)).astype(bf16)
    extra = grads_ref.shape[2] - slice_width
    tail = jnp.concatenate([high, low, jnp.zeros((extra - 2, total), bf16)], axis=0)
    part = part.astype(bf16)
    back = back.astype(bf16)
    for j in range(mine):

        @pl.when(at == j)
        def _():
            lanes = slice(j * cap, (j + 1) * cap)
            for g in range(groups):
                mine_lanes = slice(g * cap, (g + 1) * cap)
                for z in range(tensor):
                    features = slice(z * slice_width, (z + 1) * slice_width)
                    returned_ref[g, z, :, lanes] = part[features, mine_lanes]
                    grads_ref[g, z, :slice_width, lanes] = back[features, mine_lanes]
                    grads_ref[g, z, slice_width:, lanes] = tail[:, mine_lanes]


def run_experts(arrived, cot_rows, in_raw, back_raw, in_bias, back_bias, mine, inner, tensor):
    f32, bf16 = jnp.float32, jnp.bfloat16
    groups, _, width = cot_rows.shape
    chunks, _, depth, ff = in_raw.shape
    total = groups * CAP
    slice_width = width // tensor
    gate_at = mine * CAP // 16
    outs = [
        ((groups, tensor, slice_width, mine * CAP), bf16, lambda j: (0, 0, 0, 0), None),
        ((groups, tensor, slice_width + 16, mine * CAP), bf16, lambda j: (0, 0, 0, 0), None),
        ((mine, inner, total, ff), bf16, lambda j: (j, 0, 0, 0), 1),
        ((mine, inner, total, ff), bf16, lambda j: (j, 0, 0, 0), 1),
        ((mine, width, total), bf16, lambda j: (j, 0, 0), 1),
        ((mine, inner, ff), f32, lambda j: (j, 0, 0), 1),
        ((mine, 1, width), f32, lambda j: (j, 0, 0), 1),
    ]
    return pl.pallas_call(
        functools.partial(expert_kernel, inner),
        grid=(mine,),
        in_specs=[
            pl.BlockSpec((groups, CAP, width), lambda j: (0, j, 0)),
            pl.BlockSpec((groups, 16, mine * CAP), lambda j: (0, gate_at, 0)),
            pl.BlockSpec((groups, CAP, width), lambda j: (0, j, 0)),
            pl.BlockSpec((chunks, 1, depth, ff), lambda j: (0, j, 0, 0)),
            pl.BlockSpec((chunks, 1, depth, ff), lambda j: (0, j, 0, 0)),
            pl.BlockSpec((1, inner, ff), lambda j: (j, 0, 0)),
            pl.BlockSpec((width, mine), lambda j: (0, 0)),
        ],
        out_specs=[
            pl.BlockSpec(shape if lead is None else (lead, *shape[1:]), index)
            for shape, _, index, lead in outs
        ],
        out_shape=[jax.ShapeDtypeStruct(shape, dtype) for shape, dtype, _, _ in outs],
        compiler_params=pltpu.CompilerParams(vmem_limit_bytes=VMEM_LIMIT),
        cost_estimate=pl.CostEstimate(
            flops=8 * mine * total * width * inner * ff,
            bytes_accessed=4 * chunks * mine * depth * ff + 12 * mine * total * inner * ff,
            transcendentals=mine * total * inner * ff,
        ),
    )(arrived, arrived, cot_rows, in_raw, back_raw, in_bias, back_bias)


def weight_kernel(rows_ref, grad_pre_ref, grad_turned_ref, hidden_ref, grad_in_ref, grad_back_ref):
    groups, cap, width = rows_ref.shape
    shape = grad_in_ref.shape
    rows = rows_ref[...].reshape(groups * cap, width)
    grad_in = turned_dot(rows, grad_pre_ref[0, 0], 0, 0)
    grad_in_ref[...] = grad_in.astype(jnp.bfloat16).reshape(shape)
    grad_back = jnp.dot(grad_turned_ref[0], hidden_ref[0, 0], preferred_element_type=jnp.float32)
    grad_back_ref[...] = grad_back.astype(jnp.bfloat16).reshape(shape)


def weight_grads(arrived, grad_pre, grad_turned, hidden, data):
    mine, inner, total, ff = hidden.shape
    groups, _, width = arrived.shape
    depth = width // data
    out = (data, inner, mine, depth, ff)
    kept = pl.BlockSpec((1, 1, total, ff), lambda j, t: (j, t, 0, 0))
    given = pl.BlockSpec((data, 1, 1, depth, ff), lambda j, t: (0, t, j, 0, 0))
    return pl.pallas_call(
        weight_kernel,
        grid=(mine, inner),
        in_specs=[
            pl.BlockSpec((groups, CAP, width), lambda j, t: (0, j, 0)),
            kept,
            pl.BlockSpec((1, width, total), lambda j, t: (j, 0, 0)),
            kept,
        ],
        out_specs=[given, given],
        out_shape=[jax.ShapeDtypeStruct(out, jnp.bfloat16)] * 2,
        compiler_params=pltpu.CompilerParams(vmem_limit_bytes=VMEM_LIMIT),
        cost_estimate=pl.CostEstimate(
            flops=4 * mine * total * width * inner * ff,
            bytes_accessed=4 * mine * inner * (total + width) * ff,
            transcendentals=0,
        ),
    )(arrived, grad_pre, grad_turned, hidden)


def moved_plan(
    images,
    images_held,
    routes,
    slot_index,
    first_gain,
    first_shift,
    w_qkv,
    qv_bias,
    w_out,
    out_bias,
    second_gain,
    second_shift,
    w_router,
    w_in,
    in_bias,
    w_back,
    back_bias,
    cotangent,
):
    f32, bf16 = jnp.float32, jnp.bfloat16
    image_count, seq_len, width = images.shape
    rows_total = image_count * seq_len
    experts_here, shard_width, ff_here = w_in.shape
    data, sources = lax.axis_size(DP), lax.axis_size(EXPERT)
    outer, inner = lax.axis_size(OUTER), lax.axis_size(INNER)
    tensor = outer * inner
    tensor_axes = (OUTER, INNER)
    groups = data * sources
    owners = data * inner
    mine = experts_here // owners
    slots = EXPERTS * CAP
    slots_plane = slots // inner
    dp_at = lax.axis_index(DP)
    inner_at = lax.axis_index(INNER)
    tensor_at = lax.axis_index(tensor_axes)
    owner_at = dp_at * inner + inner_at
    local_width = w_out.shape[0]
    slice_width = width // tensor

    chunk_shape = (owners, mine, shard_width, ff_here)
    in_raw = swap(w_in, (DP, INNER)).reshape(chunk_shape)
    back_raw = swap(w_back.transpose(0, 2, 1), (DP, INNER)).reshape(chunk_shape)

    packed = jnp.concatenate(
        [
            w_qkv.transpose(1, 0, 2).reshape(shard_width, 3 * local_width),
            w_out.T,
            w_router,
            back_bias.T,
            jnp.stack([first_gain, first_shift, out_bias, second_gain, second_shift], axis=1),
        ],
        axis=1,
    )
    packed = lax.all_gather(packed, DP, axis=0, tiled=True)
    cuts = [3 * local_width, local_width, EXPERTS, experts_here]
    qkv_full, out_turned, router_full, back_bias_turned, vectors = jnp.split(
        packed, [sum(cuts[: i + 1]) for i in range(4)], axis=1
    )
    gain_first, shift_first, bias_out_full, gain_second, shift_second = (
        vectors[:, i].astype(f32) for i in range(5)
    )
    out_whole = lax.all_gather(out_turned, tensor_axes, axis=1, tiled=True)
    in_bias_all = jnp.stack(
        [
            lax.ppermute(in_bias, INNER, [(i, (i + s) % inner) for i in range(inner)])
            for s in range(inner)
        ]
    )
    in_bias_all = jnp.take(in_bias_all, (inner_at - jnp.arange(inner)) % inner, axis=0)
    in_bias_mine = lax.dynamic_slice_in_dim(in_bias_all, owner_at * mine, mine, 1)
    in_bias_mine = in_bias_mine.transpose(1, 0, 2).astype(f32)

    pair_routes = routes.reshape(rows_total, TOPK)
    pair_slots = slot_index.reshape(rows_total, TOPK)
    home, within = pair_routes // experts_here, pair_routes % experts_here
    owner, nth = within // mine, within % mine
    place = ((owner // inner) * sources + home) * inner + owner % inner
    target = jnp.where(pair_slots < CAP, (place * mine + nth) * CAP + pair_slots, slots)
    plane_slots = jnp.arange(slots, dtype=jnp.int32).reshape(groups, inner, mine * CAP)
    plane_slots = lax.dynamic_slice_in_dim(plane_slots, inner_at, 1, 1).reshape(slots_plane)
    takes = [plane_slots[:, None] == target[None, :, k] for k in range(TOPK)]
    fill = jnp.logical_or(takes[0], takes[1]).astype(bf16)

    live_image = (jnp.arange(image_count, dtype=jnp.int32) < images_held[0]).astype(f32)
    live_rows = jnp.repeat(live_image, seq_len)[:, None]
    grad_rows = cotangent.reshape(rows_total, width).astype(f32) * live_rows

    def dispatch(rows):
        return jnp.dot(fill, rows, preferred_element_type=f32).astype(bf16)

    cot_out = dispatch(grad_rows.astype(bf16)).reshape(groups, mine * CAP, width)
    cot_rows = swap(cot_out, (DP, EXPERT))

    inputs = images.reshape(rows_total, width).astype(f32)
    normed, scaled_first, inv_first = norm_parts(inputs, gain_first, shift_first)
    normed_low = normed.astype(bf16)
    projected = jnp.dot(normed_low, qkv_full, preferred_element_type=f32)
    head_count = local_width // HEAD_DIM
    head_shape = (image_count, seq_len, head_count, HEAD_DIM)
    bias_pair = qv_bias.astype(f32)
    queries, key_rows, value_rows = (
        projected[:, i * local_width : (i + 1) * local_width] for i in range(3)
    )
    queries = (queries + bias_pair[0]).astype(bf16).reshape(head_shape)
    key_rows = key_rows.astype(bf16).reshape(head_shape)
    value_rows = (value_rows + bias_pair[1]).astype(bf16).reshape(head_shape)
    scale = HEAD_DIM ** (-0.5)
    attended, log_total = attention_forward(queries, key_rows, value_rows, scale)
    attended_low = attended.reshape(rows_total, local_width).astype(bf16)
    attended_all = lax.all_gather(attended_low, tensor_axes, axis=1, tiled=True)
    attended_all, in_raw = lax.optimization_barrier((attended_all, in_raw))
    mixed = inputs + bias_out_full
    mixed = mixed + jnp.einsum("te,de->td", attended_all, out_whole, preferred_element_type=f32)
    routed, scaled_second, inv_second = norm_parts(mixed, gain_second, shift_second)
    routed_low = routed.astype(bf16)
    logits = jnp.dot(routed_low, router_full, preferred_element_type=f32)
    probs = jax.nn.softmax(logits, axis=-1)
    expert_ids = jnp.arange(EXPERTS, dtype=jnp.int32)
    matches = [(pair_routes[:, k : k + 1] == expert_ids).astype(f32) for k in range(TOPK)]
    gates = [jnp.sum(match * probs, axis=1) for match in matches]

    gate_slots = sum(
        jnp.sum(jnp.where(take, gate[None, :], 0.0), axis=1) for take, gate in zip(takes, gates)
    )
    gate_parts = jnp.stack(high_low(gate_slots.reshape(groups, mine * CAP)), axis=1)
    gate_rows = jnp.pad(gate_parts, ((0, 0), (0, 14), (0, width - mine * CAP)))
    sent = jnp.concatenate([dispatch(routed_low).reshape(groups, mine * CAP, width), gate_rows], axis=1)
    sent, back_raw = lax.optimization_barrier((sent, back_raw))
    arrived = swap(sent, (DP, EXPERT))
    back_bias_mine = lax.dynamic_slice_in_dim(back_bias_turned, owner_at * mine, mine, 1)
    back_bias_mine = jnp.where(lax.axis_index(OUTER) == 0, back_bias_mine.astype(f32), 0.0)
    (
        returned_out,
        grads_out,
        hidden_low,
        grad_pre_low,
        grad_turned,
        grad_in_bias_mine,
        grad_back_bias_mine,
    ) = run_experts(
        arrived, cot_rows, in_raw, back_raw, in_bias_mine, back_bias_mine, mine, inner, tensor
    )

    everywhere = (DP, EXPERT, OUTER, INNER)

    def bring(parts):
        parts = parts.reshape(groups * tensor, *parts.shape[2:])
        parts = swap(parts, everywhere).astype(f32)
        parts = jnp.sum(parts.reshape(groups, outer, inner, *parts.shape[1:]), axis=1)
        return parts.reshape(groups * inner, *parts.shape[2:])

    def in_line(parts):
        return parts.transpose(1, 0, 2).reshape(parts.shape[1], slots)

    grad_parts = bring(grads_out)
    grad_slots = in_line(grad_parts[:, :slice_width]).astype(bf16)
    gate_slots_back = in_line(grad_parts[:, slice_width : slice_width + 2])
    gate_slots_back = gate_slots_back[0] + gate_slots_back[1]
    all_slots = jnp.arange(slots, dtype=jnp.int32)
    found = [target[None, :, k] == all_slots[:, None] for k in range(TOPK)]
    finds = [hit.astype(bf16) for hit in found]
    both = jnp.logical_or(found[0], found[1]).astype(bf16)
    grad_gates = jnp.stack(
        [jnp.sum(jnp.where(hit, gate_slots_back[:, None], 0.0), axis=0) for hit in found], axis=1
    )
    grad_routed_cut = jnp.dot(grad_slots, both, preferred_element_type=f32).astype(bf16)
    grad_routed = lax.all_gather(grad_routed_cut, tensor_axes, axis=0, tiled=True).T.astype(f32)

    grad_in_out, grad_back_out = weight_grads(arrived, grad_pre_low, grad_turned, hidden_low, data)
    returned = in_line(bring(returned_out)).astype(bf16)
    picked = [jnp.dot(returned, find, preferred_element_type=f32) for find in finds]
    mixed_cut = lax.dynamic_slice_in_dim(mixed, tensor_at * slice_width, slice_width, 1)
    expert_mix = gates[0][None, :] * picked[0] + gates[1][None, :] * picked[1]
    output_cut = (live_rows * (mixed_cut + expert_mix.T)).astype(bf16)
    output = lax.all_gather(output_cut, tensor_axes, axis=1, tiled=True).reshape(images.shape)

    grad_probs = sum(match * grad_gates[:, k : k + 1] for k, match in enumerate(matches))
    grad_logits = probs * (grad_probs - jnp.sum(probs * grad_probs, axis=-1, keepdims=True))
    grad_logits_low = grad_logits.astype(bf16)
    grad_router = jnp.einsum("td,te->de", routed_low, grad_logits_low, preferred_element_type=f32)
    grad_routed = grad_routed + jnp.einsum(
        "te,de->td", grad_logits_low, router_full, preferred_element_type=f32
    )
    grad_from_norm, grad_gain_second, grad_shift_second = norm_back(
        grad_routed, scaled_second, inv_second, gain_second
    )
    grad_mixed = grad_rows + grad_from_norm
    grad_bias_out = jnp.sum(grad_mixed, axis=0)
    grad_mixed_low = grad_mixed.astype(bf16)
    grad_out_turned = jnp.einsum("td,te->de", grad_mixed_low, attended_low, preferred_element_type=f32)
    grad_attended = jnp.dot(grad_mixed_low, out_turned, preferred_element_type=f32)
    grad_attended = grad_attended.astype(bf16).reshape(head_shape)
    grad_queries, grad_keys, grad_values = (
        grads.reshape(rows_total, local_width)
        for grads in attention_backward(
            queries, key_rows, value_rows, log_total, grad_attended, scale
        )
    )
    grad_pair_bias = jnp.stack([jnp.sum(grad_queries, axis=0), jnp.sum(grad_values, axis=0)])
    grad_proj_low = jnp.concatenate([grad_queries, grad_keys, grad_values], axis=1).astype(bf16)
    grad_qkv = jnp.einsum("td,te->de", normed_low, grad_proj_low, preferred_element_type=f32)
    grad_normed_part = jnp.einsum("te,de->td", grad_proj_low, qkv_full, preferred_element_type=f32)
    grad_normed = lax.psum(grad_normed_part.astype(bf16), tensor_axes).astype(f32)
    grad_from_first, _, _ = norm_back(grad_normed, scaled_first, inv_first, gain_first)
    first_terms = jnp.stack(
        [jnp.sum(grad_normed_part * scaled_first, axis=0), jnp.sum(grad_normed_part, axis=0)]
    )
    grad_images = (grad_mixed + grad_from_first).reshape(images.shape)

    def spread(parts):
        parts = parts.reshape(experts_here, shard_width, ff_here)
        return swap(parts, (DP, INNER)).astype(f32)

    grad_w_back = spread(grad_back_out).transpose(0, 2, 1)
    grad_w_in = spread(grad_in_out)
    bias_grads = jnp.concatenate(
        [grad_in_bias_mine.reshape(mine, inner * ff_here), grad_back_bias_mine[:, 0]], axis=1
    )
    bias_grads = lax.all_gather(bias_grads, (DP, INNER), axis=0, tiled=True)
    grad_in_bias = lax.dynamic_slice_in_dim(bias_grads, inner_at * ff_here, ff_here, 1)
    grad_back_shard = lax.dynamic_slice_in_dim(
        bias_grads, inner * ff_here + dp_at * shard_width, shard_width, 1
    )
    early = jnp.concatenate(
        [
            grad_qkv,
            grad_out_turned,
            grad_router,
            jnp.stack([grad_bias_out, grad_gain_second, grad_shift_second], axis=1),
        ],
        axis=1,
    )
    early = lax.psum(lax.psum_scatter(early, DP, scatter_dimension=0, tiled=True), EXPERT)
    grad_w_qkv = early[:, : 3 * local_width].reshape(shard_width, 3, local_width).transpose(1, 0, 2)
    grad_w_out = early[:, 3 * local_width : 4 * local_width].T
    grad_w_router = early[:, 4 * local_width : 4 * local_width + EXPERTS]
    grad_out_bias, grad_second_gain, grad_second_shift = (
        early[:, 4 * local_width + EXPERTS + i] for i in range(3)
    )
    grad_qv_bias = lax.psum(grad_pair_bias, (DP, EXPERT))
    grad_first_norm = lax.psum(first_terms, everywhere)
    grad_first_norm = lax.dynamic_slice_in_dim(grad_first_norm, dp_at * shard_width, shard_width, 1)
    return (
        output,
        grad_images,
        grad_first_norm[0],
        grad_first_norm[1],
        grad_w_qkv,
        grad_qv_bias,
        grad_w_out,
        grad_out_bias,
        grad_second_gain,
        grad_second_shift,
        grad_w_router,
        grad_w_in,
        grad_in_bias,
        grad_w_back,
        grad_back_shard,
    )


def specs(tensor):
    rows = P((DP, EXPERT), None, None)
    vector, square = P(DP), P(tensor, DP)
    qkv, pair, router = P(None, DP, tensor), P(None, tensor), P(DP, None)
    inward, outward = P(EXPERT, DP, tensor), P(EXPERT, tensor, DP)
    params = (vector, vector, qkv, pair, square, vector, vector, vector, router)
    experts = (inward, P(EXPERT, tensor), outward, P(EXPERT, DP))
    taken = (rows, P((DP, EXPERT)), rows, rows, *params, *experts, rows)
    given = (rows, rows, *params, *experts)
    return taken, given


def solution(mesh):
    data, expert, tensor = (mesh.shape[name] for name in (DP, EXPERT, TENSOR))
    inner = FF_PAIR if tensor % FF_PAIR == 0 else 1
    if (EXPERTS // expert) % (data * inner):
        taken, given = specs(TENSOR)
        return jax.shard_map(
            gathered_plan, mesh=mesh, in_specs=taken, out_specs=given, check_vma=False
        )
    devices = mesh.devices.reshape(data, expert, tensor // inner, inner)
    split_mesh = Mesh(devices, (DP, EXPERT, OUTER, INNER))
    taken, given = specs((OUTER, INNER))
    return jax.shard_map(
        moved_plan, mesh=split_mesh, in_specs=taken, out_specs=given, check_vma=False
    )
```

```python
import functools
import math

import jax
import jax.numpy as jnp
from jax import lax
from jax.experimental import pallas as pl
from jax.experimental.pallas import tpu as pltpu
from jax.sharding import Mesh
from jax.sharding import PartitionSpec as P

HEAD_DIM = 64
EXPERTS = 32
TOPK = 2
CAP = 64
FF_PAIR = 2
EXTRA = 16
VMEM_LIMIT = 56 * 1024 * 1024
GELU_SCALE = (2.0 / math.pi) ** 0.5
GELU_CUBE = 0.044715

DP = "dp"
EXPERT = "expert"
TENSOR = "tensor"
OUTER = "outer"
INNER = "inner"


EPS = 1e-06


def norm_parts(values, norm_gain, norm_shift):
    average = jnp.mean(values, axis=-1, keepdims=True)
    centred = values - average
    spread = jnp.mean(centred * centred, axis=-1, keepdims=True)
    inv_std = lax.rsqrt(spread + EPS)
    scaled = centred * inv_std
    return (scaled * norm_gain + norm_shift, scaled, inv_std)


def norm_back(grad_out, scaled, inv_std, norm_gain):
    grad_scaled = grad_out * norm_gain
    inner = grad_scaled - jnp.mean(grad_scaled, axis=-1, keepdims=True)
    inner = inner - scaled * jnp.mean(grad_scaled * scaled, axis=-1, keepdims=True)
    return (inner * inv_std, jnp.sum(grad_out * scaled, axis=0), jnp.sum(grad_out, axis=0))


def attention_forward(queries, key_rows, value_rows, scale):
    scores = (
        jnp.einsum("iqhd,ikhd->ihqk", queries, key_rows, preferred_element_type=jnp.float32) * scale
    )
    row_peak = jnp.max(scores, axis=-1, keepdims=True)
    log_total = row_peak + jnp.log(jnp.sum(jnp.exp(scores - row_peak), axis=-1, keepdims=True))
    weights = jnp.exp(scores - log_total).astype(jnp.bfloat16)
    attended = jnp.einsum(
        "ihqk,ikhd->iqhd", weights, value_rows, preferred_element_type=jnp.float32
    )
    return (attended, log_total)


def attention_backward(queries, key_rows, value_rows, log_total, grad_low, scale):
    scores = (
        jnp.einsum("iqhd,ikhd->ihqk", queries, key_rows, preferred_element_type=jnp.float32) * scale
    )
    probs = jnp.exp(scores - log_total)
    weights = probs.astype(jnp.bfloat16)
    grad_values = jnp.einsum(
        "ihqk,iqhd->ikhd", weights, grad_low, preferred_element_type=jnp.float32
    )
    grad_weights = jnp.einsum(
        "iqhd,ikhd->ihqk", grad_low, value_rows, preferred_element_type=jnp.float32
    )
    grad_scores = probs * (grad_weights - jnp.sum(probs * grad_weights, axis=-1, keepdims=True))
    scores_low = grad_scores.astype(jnp.bfloat16)
    grad_queries = (
        jnp.einsum("ihqk,ikhd->iqhd", scores_low, key_rows, preferred_element_type=jnp.float32)
        * scale
    )
    grad_keys = (
        jnp.einsum("ihqk,iqhd->ikhd", scores_low, queries, preferred_element_type=jnp.float32)
        * scale
    )
    return (grad_queries, grad_keys, grad_values)


def gathered_plan(
    images,
    images_held,
    routes,
    slot_index,
    first_gain,
    first_shift,
    w_qkv,
    qv_bias,
    w_out,
    out_bias,
    second_gain,
    second_shift,
    w_router,
    w_in,
    in_bias,
    w_back,
    back_bias,
    cotangent,
):
    image_count, seq_len, width = images.shape
    rows_total = image_count * seq_len
    experts_here = w_in.shape[0]
    (
        gain_first,
        shift_first,
        qkv_full,
        out_full,
        bias_out_full,
        gain_second,
        shift_second,
        router_full,
        in_full,
        back_full,
        back_bias_full,
    ) = (
        lax.all_gather(first_gain, DP, axis=0, tiled=True),
        lax.all_gather(first_shift, DP, axis=0, tiled=True),
        lax.all_gather(w_qkv, DP, axis=1, tiled=True),
        lax.all_gather(w_out, DP, axis=1, tiled=True),
        lax.all_gather(out_bias, DP, axis=0, tiled=True),
        lax.all_gather(second_gain, DP, axis=0, tiled=True),
        lax.all_gather(second_shift, DP, axis=0, tiled=True),
        lax.all_gather(w_router, DP, axis=0, tiled=True),
        lax.all_gather(w_in, DP, axis=1, tiled=True),
        lax.all_gather(w_back, DP, axis=2, tiled=True),
        lax.all_gather(back_bias, DP, axis=1, tiled=True),
    )
    gain_first = gain_first.astype(jnp.float32)
    gain_second = gain_second.astype(jnp.float32)
    inputs = images.reshape(rows_total, width).astype(jnp.float32)
    live_image = (jnp.arange(image_count, dtype=jnp.int32) < images_held[0]).astype(jnp.float32)
    live_rows = jnp.repeat(live_image, seq_len)[:, None]
    normed, scaled_first, inv_first = norm_parts(
        inputs, gain_first, shift_first.astype(jnp.float32)
    )
    normed_low = normed.astype(jnp.bfloat16)
    projected = jnp.einsum("td,cde->cte", normed_low, qkv_full, preferred_element_type=jnp.float32)
    local_width = projected.shape[2]
    head_count = local_width // HEAD_DIM
    head_shape = (image_count, seq_len, head_count, HEAD_DIM)
    bias_pair = qv_bias.astype(jnp.float32)
    queries = (projected[0] + bias_pair[0]).astype(jnp.bfloat16).reshape(head_shape)
    key_rows = projected[1].astype(jnp.bfloat16).reshape(head_shape)
    value_rows = (projected[2] + bias_pair[1]).astype(jnp.bfloat16).reshape(head_shape)
    scale = HEAD_DIM ** (-0.5)
    attended, log_total = attention_forward(queries, key_rows, value_rows, scale)
    attended_low = attended.reshape(rows_total, local_width).astype(jnp.bfloat16)
    head_part = jnp.dot(attended_low, out_full, preferred_element_type=jnp.float32)
    mixed = inputs + lax.psum(head_part, TENSOR) + bias_out_full.astype(jnp.float32)
    routed, scaled_second, inv_second = norm_parts(
        mixed, gain_second, shift_second.astype(jnp.float32)
    )
    routed_low = routed.astype(jnp.bfloat16)
    logits = jnp.dot(routed_low, router_full, preferred_element_type=jnp.float32)
    probs = jax.nn.softmax(logits, axis=-1)
    pair_routes = routes.reshape(rows_total, TOPK)
    pair_slots = slot_index.reshape(rows_total, TOPK)
    target = jnp.where(pair_slots < CAP, pair_routes * CAP + pair_slots, EXPERTS * CAP).reshape(
        rows_total * TOPK
    )
    gates = jnp.take_along_axis(probs, pair_routes, axis=1)
    pair_rows = jnp.repeat(routed_low, TOPK, axis=0)
    outgoing = (
        jnp.zeros((EXPERTS * CAP + 1, width), jnp.bfloat16)
        .at[target]
        .set(pair_rows)[: EXPERTS * CAP]
    )
    outgoing = outgoing.reshape(EXPERTS, 1, CAP, width)
    arrived = lax.all_to_all(outgoing, EXPERT, split_axis=0, concat_axis=1, tiled=True)
    sources = arrived.shape[1]
    expert_rows = arrived.reshape(experts_here, sources * CAP, width)
    hidden_pre = jnp.einsum(
        "erd,edf->erf", expert_rows, in_full, preferred_element_type=jnp.float32
    )
    hidden_pre = hidden_pre + in_bias.astype(jnp.float32)[:, None, :]
    hidden_value, gelu_pull = jax.vjp(jax.nn.gelu, hidden_pre)
    hidden_low = hidden_value.astype(jnp.bfloat16)
    expert_part = jnp.einsum(
        "erf,efd->erd", hidden_low, back_full, preferred_element_type=jnp.float32
    )
    bias_back = back_bias_full.astype(jnp.float32)[:, None, :]
    shares = lax.psum_scatter(
        expert_part.reshape(experts_here, sources, CAP, width),
        TENSOR,
        scatter_dimension=2,
        tiled=True,
    )
    share_low = (shares + bias_back[:, None]).astype(jnp.bfloat16)
    pieces = lax.all_to_all(share_low, EXPERT, split_axis=1, concat_axis=0, tiled=True)
    returned = lax.all_gather(pieces, TENSOR, axis=2, tiled=True)
    padded = jnp.concatenate(
        [returned.reshape(EXPERTS * CAP, width), jnp.zeros((1, width), jnp.bfloat16)], axis=0
    )
    picked = padded[target].astype(jnp.float32).reshape(rows_total, TOPK, width)
    expert_mix = jnp.sum(gates[:, :, None] * picked, axis=1)
    output = (live_rows * (mixed + expert_mix)).astype(jnp.bfloat16).reshape(images.shape)
    grad_rows = cotangent.reshape(rows_total, width).astype(jnp.float32) * live_rows
    grad_gates = jnp.sum(grad_rows[:, None, :] * picked, axis=-1)
    grad_picked = (
        (gates[:, :, None] * grad_rows[:, None, :])
        .astype(jnp.bfloat16)
        .reshape(rows_total * TOPK, width)
    )
    grad_outgoing = (
        jnp.zeros((EXPERTS * CAP + 1, width), jnp.bfloat16)
        .at[target]
        .set(grad_picked)[: EXPERTS * CAP]
    )
    grad_outgoing = grad_outgoing.reshape(EXPERTS, 1, CAP, width)
    grad_arrived = lax.all_to_all(grad_outgoing, EXPERT, split_axis=0, concat_axis=1, tiled=True)
    grad_arrived = grad_arrived.reshape(experts_here, sources * CAP, width)
    grad_back_bias = jnp.sum(grad_arrived.astype(jnp.float32), axis=1)
    grad_back_w = jnp.einsum(
        "erf,erd->efd", hidden_low, grad_arrived, preferred_element_type=jnp.float32
    )
    grad_hidden = jnp.einsum(
        "erd,efd->erf", grad_arrived, back_full, preferred_element_type=jnp.float32
    )
    grad_pre = gelu_pull(grad_hidden)[0]
    grad_in_bias_local = jnp.sum(grad_pre, axis=1)
    grad_pre_low = grad_pre.astype(jnp.bfloat16)
    grad_in_w = jnp.einsum(
        "erd,erf->edf", expert_rows, grad_pre_low, preferred_element_type=jnp.float32
    )
    grad_rows_part = jnp.einsum(
        "erf,edf->erd", grad_pre_low, in_full, preferred_element_type=jnp.float32
    )
    grad_shares = lax.psum_scatter(
        grad_rows_part.reshape(experts_here, sources, CAP, width),
        TENSOR,
        scatter_dimension=2,
        tiled=True,
    ).astype(jnp.bfloat16)
    grad_pieces = lax.all_to_all(grad_shares, EXPERT, split_axis=1, concat_axis=0, tiled=True)
    grad_returned = lax.all_gather(grad_pieces, TENSOR, axis=2, tiled=True)
    grad_padded = jnp.concatenate(
        [grad_returned.reshape(EXPERTS * CAP, width), jnp.zeros((1, width), jnp.bfloat16)], axis=0
    )
    grad_routed = jnp.sum(
        grad_padded[target].astype(jnp.float32).reshape(rows_total, TOPK, width), axis=1
    )
    expert_match = (
        pair_routes[:, :, None] == jnp.arange(EXPERTS, dtype=jnp.int32)[None, None, :]
    ).astype(jnp.float32)
    grad_probs = jnp.sum(expert_match * grad_gates[:, :, None], axis=1)
    grad_logits = probs * (grad_probs - jnp.sum(probs * grad_probs, axis=-1, keepdims=True))
    grad_logits_low = grad_logits.astype(jnp.bfloat16)
    grad_router = jnp.einsum(
        "td,te->de", routed_low, grad_logits_low, preferred_element_type=jnp.float32
    )
    grad_routed = grad_routed + jnp.einsum(
        "te,de->td", grad_logits_low, router_full, preferred_element_type=jnp.float32
    )
    grad_from_norm, grad_gain_second, grad_shift_second = norm_back(
        grad_routed, scaled_second, inv_second, gain_second
    )
    grad_mixed = grad_rows + grad_from_norm
    grad_bias_out = jnp.sum(grad_mixed, axis=0)
    grad_mixed_low = grad_mixed.astype(jnp.bfloat16)
    grad_out_w = jnp.einsum(
        "te,td->ed", attended_low, grad_mixed_low, preferred_element_type=jnp.float32
    )
    grad_attended = jnp.einsum(
        "td,ed->te", grad_mixed_low, out_full, preferred_element_type=jnp.float32
    )
    grad_attended = grad_attended.astype(jnp.bfloat16).reshape(head_shape)
    grad_queries, grad_keys, grad_values = attention_backward(
        queries, key_rows, value_rows, log_total, grad_attended, scale
    )
    grad_queries = grad_queries.reshape(rows_total, local_width)
    grad_keys = grad_keys.reshape(rows_total, local_width)
    grad_values = grad_values.reshape(rows_total, local_width)
    grad_pair_bias = jnp.stack([jnp.sum(grad_queries, axis=0), jnp.sum(grad_values, axis=0)])
    grad_proj_low = jnp.stack([grad_queries, grad_keys, grad_values]).astype(jnp.bfloat16)
    grad_qkv = jnp.einsum(
        "td,cte->cde", normed_low, grad_proj_low, preferred_element_type=jnp.float32
    )
    grad_normed_part = jnp.einsum(
        "cte,cde->td", grad_proj_low, qkv_full, preferred_element_type=jnp.float32
    )
    grad_normed = lax.psum(grad_normed_part, TENSOR)
    grad_from_first, grad_gain_first, grad_shift_first = norm_back(
        grad_normed, scaled_first, inv_first, gain_first
    )
    grad_images = (grad_mixed + grad_from_first).reshape(images.shape)
    expert_start = lax.axis_index(EXPERT) * experts_here
    full_in_bias = lax.dynamic_update_slice(
        jnp.zeros((EXPERTS, grad_in_bias_local.shape[1]), jnp.float32),
        grad_in_bias_local,
        (expert_start, jnp.zeros((), jnp.int32)),
    )
    summed = lax.psum(
        (
            grad_gain_first,
            grad_shift_first,
            grad_qkv,
            grad_pair_bias,
            grad_out_w,
            grad_bias_out,
            grad_gain_second,
            grad_shift_second,
            grad_router,
            full_in_bias,
        ),
        (DP, EXPERT),
    )
    shard_width = width // lax.axis_size(DP)
    shard_start = lax.axis_index(DP) * shard_width
    grad_first_gain = lax.dynamic_slice_in_dim(summed[0], shard_start, shard_width, 0)
    grad_first_shift = lax.dynamic_slice_in_dim(summed[1], shard_start, shard_width, 0)
    grad_w_qkv = lax.dynamic_slice_in_dim(summed[2], shard_start, shard_width, 1)
    grad_qv_bias = summed[3]
    grad_w_out = lax.dynamic_slice_in_dim(summed[4], shard_start, shard_width, 1)
    grad_out_bias = lax.dynamic_slice_in_dim(summed[5], shard_start, shard_width, 0)
    grad_second_gain = lax.dynamic_slice_in_dim(summed[6], shard_start, shard_width, 0)
    grad_second_shift = lax.dynamic_slice_in_dim(summed[7], shard_start, shard_width, 0)
    grad_w_router = lax.dynamic_slice_in_dim(summed[8], shard_start, shard_width, 0)
    grad_in_bias = lax.dynamic_slice_in_dim(summed[9], expert_start, experts_here, 0)
    grad_w_in, grad_w_back, grad_back_shard = (
        lax.psum_scatter(grad_in_w, DP, scatter_dimension=1, tiled=True),
        lax.psum_scatter(grad_back_w, DP, scatter_dimension=2, tiled=True),
        lax.psum_scatter(grad_back_bias, DP, scatter_dimension=1, tiled=True),
    )
    return (
        output,
        grad_images,
        grad_first_gain,
        grad_first_shift,
        grad_w_qkv,
        grad_qv_bias,
        grad_w_out,
        grad_out_bias,
        grad_second_gain,
        grad_second_shift,
        grad_w_router,
        grad_w_in,
        grad_in_bias,
        grad_w_back,
        grad_back_shard,
    )


def swap(values, axes):
    return lax.all_to_all(values, axes, split_axis=0, concat_axis=0, tiled=True)


def hop_gather(values, axes):
    count, at = lax.axis_size(axes), lax.axis_index(axes)
    hops = [values]
    for s in range(1, count):
        hops.append(lax.ppermute(values, axes, [(i, (i + s) % count) for i in range(count)]))
    order = (at - jnp.arange(count, dtype=jnp.int32)) % count
    return jnp.take(jnp.stack(hops), order, axis=0)


def high_low(values):
    high = lax.reduce_precision(values, 8, 7)
    return high.astype(jnp.bfloat16), (values - high).astype(jnp.bfloat16)


def turned_dot(left, right, left_dim, right_dim):
    return lax.dot_general(
        left, right, (((left_dim,), (right_dim,)), ((), ())), preferred_element_type=jnp.float32
    )


def expert_kernel(
    inner,
    rows_ref,
    gate_ref,
    cot_ref,
    in_ref,
    back_ref,
    in_bias_ref,
    back_bias_ref,
    returned_ref,
    grads_ref,
    hidden_ref,
    grad_pre_ref,
    grad_turned_ref,
    grad_in_bias_ref,
    grad_back_bias_ref,
):
    f32, bf16 = jnp.float32, jnp.bfloat16
    groups, cap, width = rows_ref.shape
    chunks = in_ref.shape[0]
    data = chunks // inner
    tensor, slice_width = returned_ref.shape[1:3]
    mine = back_bias_ref.shape[1]
    total = groups * cap
    at = pl.program_id(0)
    rows = rows_ref[...].reshape(total, width)
    cot_turned = cot_ref[...].reshape(total, width).T.astype(f32)
    pair = gate_ref[:, 0:1, :].astype(f32) + gate_ref[:, 1:2, :].astype(f32)
    pair = pair.reshape(groups, pair.shape[-1])
    gate = jnp.zeros((groups, cap), f32)
    for j in range(mine):
        gate = jnp.where(at == j, pair[:, j * cap : (j + 1) * cap], gate)
    gate = jnp.concatenate([gate[g : g + 1, :] for g in range(groups)], axis=1)
    grad_turned = (cot_turned * gate).astype(bf16)
    grad_turned_ref[0] = grad_turned
    grad_returned = grad_turned.T
    grad_back_bias_ref[0] = jnp.sum(grad_returned.astype(f32), axis=0, keepdims=True)
    bias_columns = back_bias_ref[...]
    bias = jnp.zeros((width, 1), f32)
    for j in range(mine):
        bias = jnp.where(at == j, bias_columns[:, j : j + 1], bias)
    part = jnp.broadcast_to(bias, (width, total))
    back = jnp.zeros((width, total), f32)
    for t in range(inner):
        w_in = jnp.concatenate([in_ref[d * inner + t, 0] for d in range(data)], axis=0)
        w_back = jnp.concatenate([back_ref[d * inner + t, 0] for d in range(data)], axis=0)
        pre = jnp.dot(rows, w_in, preferred_element_type=f32) + in_bias_ref[0, t : t + 1, :]
        square = pre * pre
        bent = jnp.tanh(GELU_SCALE * pre * (1.0 + GELU_CUBE * square))
        half = 0.5 * (1.0 + bent)
        hidden = (pre * half).astype(bf16)
        slope = half + (0.5 * GELU_SCALE) * pre * (1.0 - bent * bent) * (
            1.0 + (3.0 * GELU_CUBE) * square
        )
        hidden_ref[0, t] = hidden
        grad_pre = jnp.dot(grad_returned, w_back, preferred_element_type=f32) * slope
        grad_in_bias_ref[0, t : t + 1, :] = jnp.sum(grad_pre, axis=0, keepdims=True)
        grad_pre = grad_pre.astype(bf16)
        grad_pre_ref[0, t] = grad_pre
        part = part + turned_dot(w_back, hidden, 1, 1)
        back = back + turned_dot(w_in, grad_pre, 1, 1)
    gate_terms = jnp.sum(part * cot_turned, axis=0, keepdims=True)
    high = gate_terms.astype(bf16)
    low = (gate_terms - high.astype(f32)).astype(bf16)
    extra = grads_ref.shape[2] - slice_width
    tail = jnp.concatenate([high, low, jnp.zeros((extra - 2, total), bf16)], axis=0)
    part = part.astype(bf16)
    back = back.astype(bf16)
    for j in range(mine):

        @pl.when(at == j)
        def _():
            lanes = slice(j * cap, (j + 1) * cap)
            for g in range(groups):
                mine_lanes = slice(g * cap, (g + 1) * cap)
                for z in range(tensor):
                    features = slice(z * slice_width, (z + 1) * slice_width)
                    returned_ref[g, z, :, lanes] = part[features, mine_lanes]
                    grads_ref[g, z, :slice_width, lanes] = back[features, mine_lanes]
                    grads_ref[g, z, slice_width:, lanes] = tail[:, mine_lanes]


def run_experts(arrived, cot_rows, in_raw, back_raw, in_bias, back_bias, mine, inner, tensor):
    f32, bf16 = jnp.float32, jnp.bfloat16
    groups, _, width = cot_rows.shape
    chunks, _, depth, ff = in_raw.shape
    total = groups * CAP
    slice_width = width // tensor
    gate_at = mine * CAP // 16
    outs = [
        ((groups, tensor, slice_width, mine * CAP), bf16, lambda j: (0, 0, 0, 0), None),
        ((groups, tensor, slice_width + 16, mine * CAP), bf16, lambda j: (0, 0, 0, 0), None),
        ((mine, inner, total, ff), bf16, lambda j: (j, 0, 0, 0), 1),
        ((mine, inner, total, ff), bf16, lambda j: (j, 0, 0, 0), 1),
        ((mine, width, total), bf16, lambda j: (j, 0, 0), 1),
        ((mine, inner, ff), f32, lambda j: (j, 0, 0), 1),
        ((mine, 1, width), f32, lambda j: (j, 0, 0), 1),
    ]
    return pl.pallas_call(
        functools.partial(expert_kernel, inner),
        grid=(mine,),
        in_specs=[
            pl.BlockSpec((groups, CAP, width), lambda j: (0, j, 0)),
            pl.BlockSpec((groups, 16, mine * CAP), lambda j: (0, gate_at, 0)),
            pl.BlockSpec((groups, CAP, width), lambda j: (0, j, 0)),
            pl.BlockSpec((chunks, 1, depth, ff), lambda j: (0, j, 0, 0)),
            pl.BlockSpec((chunks, 1, depth, ff), lambda j: (0, j, 0, 0)),
            pl.BlockSpec((1, inner, ff), lambda j: (j, 0, 0)),
            pl.BlockSpec((width, mine), lambda j: (0, 0)),
        ],
        out_specs=[
            pl.BlockSpec(shape if lead is None else (lead, *shape[1:]), index)
            for shape, _, index, lead in outs
        ],
        out_shape=[jax.ShapeDtypeStruct(shape, dtype) for shape, dtype, _, _ in outs],
        compiler_params=pltpu.CompilerParams(vmem_limit_bytes=VMEM_LIMIT),
        cost_estimate=pl.CostEstimate(
            flops=8 * mine * total * width * inner * ff,
            bytes_accessed=4 * chunks * mine * depth * ff + 12 * mine * total * inner * ff,
            transcendentals=mine * total * inner * ff,
        ),
    )(arrived, arrived, cot_rows, in_raw, back_raw, in_bias, back_bias)


def weight_kernel(
    rows_ref,
    grad_pre_ref,
    grad_turned_ref,
    hidden_ref,
    in_bias_ref,
    back_bias_ref,
    grad_in_ref,
    grad_back_ref,
):
    f32, bf16 = jnp.float32, jnp.bfloat16
    groups, cap, width = rows_ref.shape
    data, ff = grad_in_ref.shape[0], grad_in_ref.shape[-1]
    depth = width // data
    mine = back_bias_ref.shape[0]
    at = pl.program_id(1)
    rows = rows_ref[...].reshape(groups * cap, width)
    grad_in = turned_dot(rows, grad_pre_ref[0, 0], 0, 0).astype(bf16)
    grad_back = jnp.dot(grad_turned_ref[0], hidden_ref[0, 0], preferred_element_type=f32)
    grad_back = grad_back.astype(bf16)
    for j in range(mine):

        @pl.when(at == j)
        def _():
            for d in range(data):
                block = slice(j * depth, (j + 1) * depth)
                grad_in_ref[d, 0, block] = grad_in[d * depth : (d + 1) * depth]
                grad_back_ref[d, 0, block] = grad_back[d * depth : (d + 1) * depth]

    @pl.when(at == mine - 1)
    def _():
        pairs = []
        for j in range(mine):
            values = in_bias_ref[j, 0]
            high = values.astype(bf16).astype(f32)
            pairs += [high, values - high]
        for d in range(data):
            lines = list(pairs)
            for j in range(mine):
                values = back_bias_ref[j, :, d * depth : (d + 1) * depth]
                high = values.astype(bf16).astype(f32)
                gap = jnp.zeros((1, ff // 2 - depth), f32)
                lines.append(jnp.concatenate([high, gap, values - high, gap], axis=1))
            lines.append(jnp.zeros((EXTRA - len(lines), ff), f32))
            grad_in_ref[d, 0, mine * depth :] = jnp.concatenate(lines, axis=0).astype(bf16)


def weight_grads(arrived, grad_pre, grad_turned, hidden, grad_in_bias, grad_back_bias, data):
    mine, inner, total, ff = hidden.shape
    groups, _, width = arrived.shape
    depth = width // data
    kept = pl.BlockSpec((1, 1, total, ff), lambda t, j: (j, t, 0, 0))
    lines = (mine * depth + EXTRA, mine * depth)
    return pl.pallas_call(
        weight_kernel,
        grid=(inner, mine),
        in_specs=[
            pl.BlockSpec((groups, CAP, width), lambda t, j: (0, j, 0)),
            kept,
            pl.BlockSpec((1, width, total), lambda t, j: (j, 0, 0)),
            kept,
            pl.BlockSpec((mine, 1, 1, ff), lambda t, j: (0, t, 0, 0)),
            pl.BlockSpec((mine, 1, width), lambda t, j: (0, 0, 0)),
        ],
        out_specs=[pl.BlockSpec((data, 1, n, ff), lambda t, j: (0, t, 0, 0)) for n in lines],
        out_shape=[jax.ShapeDtypeStruct((data, inner, n, ff), jnp.bfloat16) for n in lines],
        compiler_params=pltpu.CompilerParams(vmem_limit_bytes=VMEM_LIMIT),
        cost_estimate=pl.CostEstimate(
            flops=4 * mine * total * width * inner * ff,
            bytes_accessed=4 * mine * inner * (total + width) * ff,
            transcendentals=0,
        ),
    )(arrived, grad_pre, grad_turned, hidden, grad_in_bias[:, :, None], grad_back_bias)


def moved_plan(
    images,
    images_held,
    routes,
    slot_index,
    first_gain,
    first_shift,
    w_qkv,
    qv_bias,
    w_out,
    out_bias,
    second_gain,
    second_shift,
    w_router,
    w_in,
    in_bias,
    w_back,
    back_bias,
    cotangent,
):
    f32, bf16 = jnp.float32, jnp.bfloat16
    image_count, seq_len, width = images.shape
    rows_total = image_count * seq_len
    experts_here, shard_width, ff_here = w_in.shape
    data, sources = lax.axis_size(DP), lax.axis_size(EXPERT)
    outer, inner = lax.axis_size(OUTER), lax.axis_size(INNER)
    tensor = outer * inner
    tensor_axes = (OUTER, INNER)
    groups = data * sources
    owners = data * inner
    mine = experts_here // owners
    slots = EXPERTS * CAP
    slots_plane = slots // inner
    dp_at = lax.axis_index(DP)
    inner_at = lax.axis_index(INNER)
    tensor_at = lax.axis_index(tensor_axes)
    owner_at = dp_at * inner + inner_at
    local_width = w_out.shape[0]
    slice_width = width // tensor

    chunk_shape = (owners, mine, shard_width, ff_here)
    in_raw = swap(w_in, (DP, INNER)).reshape(chunk_shape)
    back_raw = swap(w_back.transpose(0, 2, 1), (DP, INNER)).reshape(chunk_shape)

    packed = jnp.concatenate(
        [
            w_qkv.transpose(1, 0, 2).reshape(shard_width, 3 * local_width),
            w_out.T,
            w_router,
            back_bias.T,
            jnp.stack([first_gain, first_shift, out_bias, second_gain, second_shift], axis=1),
        ],
        axis=1,
    )
    packed = lax.all_gather(packed, DP, axis=0, tiled=True)
    packed, in_raw = lax.optimization_barrier((packed, in_raw))
    cuts = [3 * local_width, local_width, EXPERTS, experts_here]
    qkv_full, out_turned, router_full, back_bias_turned, vectors = jnp.split(
        packed, [sum(cuts[: i + 1]) for i in range(4)], axis=1
    )
    gain_first, shift_first, bias_out_full, gain_second, shift_second = (
        vectors[:, i].astype(f32) for i in range(5)
    )
    out_whole = hop_gather(out_turned, tensor_axes)
    out_whole = out_whole.transpose(1, 0, 2).reshape(width, width)
    in_bias_all = hop_gather(in_bias, INNER)
    in_bias_mine = lax.dynamic_slice_in_dim(in_bias_all, owner_at * mine, mine, 1)
    in_bias_mine = in_bias_mine.transpose(1, 0, 2).astype(f32)

    pair_routes = routes.reshape(rows_total, TOPK)
    pair_slots = slot_index.reshape(rows_total, TOPK)
    home, within = pair_routes // experts_here, pair_routes % experts_here
    owner, nth = within // mine, within % mine
    place = ((owner // inner) * sources + home) * inner + owner % inner
    target = jnp.where(pair_slots < CAP, (place * mine + nth) * CAP + pair_slots, slots)
    plane_slots = jnp.arange(slots, dtype=jnp.int32).reshape(groups, inner, mine * CAP)
    plane_slots = lax.dynamic_slice_in_dim(plane_slots, inner_at, 1, 1).reshape(slots_plane)
    takes = [plane_slots[:, None] == target[None, :, k] for k in range(TOPK)]
    fill = jnp.logical_or(takes[0], takes[1]).astype(bf16)

    live_image = (jnp.arange(image_count, dtype=jnp.int32) < images_held[0]).astype(f32)
    live_rows = jnp.repeat(live_image, seq_len)[:, None]
    grad_rows = cotangent.reshape(rows_total, width).astype(f32) * live_rows

    def dispatch(rows):
        return jnp.dot(fill, rows, preferred_element_type=f32).astype(bf16)

    cot_out = dispatch(grad_rows.astype(bf16)).reshape(groups, mine * CAP, width)
    cot_rows = swap(cot_out, (DP, EXPERT))

    inputs = images.reshape(rows_total, width).astype(f32)
    normed, scaled_first, inv_first = norm_parts(inputs, gain_first, shift_first)
    normed_low = normed.astype(bf16)
    projected = jnp.dot(normed_low, qkv_full, preferred_element_type=f32)
    head_count = local_width // HEAD_DIM
    head_shape = (image_count, seq_len, head_count, HEAD_DIM)
    bias_pair = qv_bias.astype(f32)
    queries, key_rows, value_rows = (
        projected[:, i * local_width : (i + 1) * local_width] for i in range(3)
    )
    queries = (queries + bias_pair[0]).astype(bf16).reshape(head_shape)
    key_rows = key_rows.astype(bf16).reshape(head_shape)
    value_rows = (value_rows + bias_pair[1]).astype(bf16).reshape(head_shape)
    scale = HEAD_DIM ** (-0.5)
    attended, log_total = attention_forward(queries, key_rows, value_rows, scale)
    attended_low = attended.reshape(rows_total, local_width).astype(bf16)
    attended_all = lax.all_gather(attended_low, tensor_axes, axis=1, tiled=True)
    attended_all, back_raw = lax.optimization_barrier((attended_all, back_raw))
    mixed = inputs + bias_out_full
    mixed = mixed + jnp.einsum("te,de->td", attended_all, out_whole, preferred_element_type=f32)
    routed, scaled_second, inv_second = norm_parts(mixed, gain_second, shift_second)
    routed_low = routed.astype(bf16)
    logits = jnp.dot(routed_low, router_full, preferred_element_type=f32)
    probs = jax.nn.softmax(logits, axis=-1)
    expert_ids = jnp.arange(EXPERTS, dtype=jnp.int32)
    matches = [(pair_routes[:, k : k + 1] == expert_ids).astype(f32) for k in range(TOPK)]
    gates = [jnp.sum(match * probs, axis=1) for match in matches]

    gate_slots = sum(
        jnp.sum(jnp.where(take, gate[None, :], 0.0), axis=1) for take, gate in zip(takes, gates)
    )
    gate_parts = jnp.stack(high_low(gate_slots.reshape(groups, mine * CAP)), axis=1)
    gate_rows = jnp.pad(gate_parts, ((0, 0), (0, 14), (0, width - mine * CAP)))
    sent = jnp.concatenate([dispatch(routed_low).reshape(groups, mine * CAP, width), gate_rows], axis=1)
    sent, cot_rows = lax.optimization_barrier((sent, cot_rows))
    arrived = swap(sent, (DP, EXPERT))
    back_bias_mine = lax.dynamic_slice_in_dim(back_bias_turned, owner_at * mine, mine, 1)
    back_bias_mine = jnp.where(lax.axis_index(OUTER) == 0, back_bias_mine.astype(f32), 0.0)
    (
        returned_out,
        grads_out,
        hidden_low,
        grad_pre_low,
        grad_turned,
        grad_in_bias_mine,
        grad_back_bias_mine,
    ) = run_experts(
        arrived, cot_rows, in_raw, back_raw, in_bias_mine, back_bias_mine, mine, inner, tensor
    )

    everywhere = (DP, EXPERT, OUTER, INNER)

    def bring(parts):
        parts = parts.reshape(groups * tensor, *parts.shape[2:])
        parts = swap(parts, everywhere).astype(f32)
        parts = jnp.sum(parts.reshape(groups, outer, inner, *parts.shape[1:]), axis=1)
        return parts.reshape(groups * inner, *parts.shape[2:])

    def in_line(parts):
        return parts.transpose(1, 0, 2).reshape(parts.shape[1], slots)

    grad_parts = bring(grads_out)
    grad_slots = in_line(grad_parts[:, :slice_width]).astype(bf16)
    gate_slots_back = in_line(grad_parts[:, slice_width : slice_width + 2])
    gate_slots_back = gate_slots_back[0] + gate_slots_back[1]
    all_slots = jnp.arange(slots, dtype=jnp.int32)
    found = [target[None, :, k] == all_slots[:, None] for k in range(TOPK)]
    finds = [hit.astype(bf16) for hit in found]
    both = jnp.logical_or(found[0], found[1]).astype(bf16)
    grad_gates = jnp.stack(
        [jnp.sum(jnp.where(hit, gate_slots_back[:, None], 0.0), axis=0) for hit in found], axis=1
    )
    grad_routed_cut = jnp.dot(grad_slots, both, preferred_element_type=f32).astype(bf16)
    grad_in_out, grad_back_out = weight_grads(
        arrived, grad_pre_low, grad_turned, hidden_low, grad_in_bias_mine, grad_back_bias_mine, data
    )
    grad_routed_cut, returned_out, grad_in_out, grad_back_out = lax.optimization_barrier(
        (grad_routed_cut, returned_out, grad_in_out, grad_back_out)
    )
    grad_routed = lax.all_gather(grad_routed_cut, tensor_axes, axis=0, tiled=True).T.astype(f32)
    returned = in_line(bring(returned_out)).astype(bf16)
    picked = [jnp.dot(returned, find, preferred_element_type=f32) for find in finds]
    mixed_cut = lax.dynamic_slice_in_dim(mixed, tensor_at * slice_width, slice_width, 1)
    expert_mix = gates[0][None, :] * picked[0] + gates[1][None, :] * picked[1]
    output_cut = (live_rows * (mixed_cut + expert_mix.T)).astype(bf16)
    output = lax.all_gather(output_cut, tensor_axes, axis=1, tiled=True).reshape(images.shape)

    grad_probs = sum(match * grad_gates[:, k : k + 1] for k, match in enumerate(matches))
    grad_logits = probs * (grad_probs - jnp.sum(probs * grad_probs, axis=-1, keepdims=True))
    grad_logits_low = grad_logits.astype(bf16)
    grad_router = jnp.einsum("td,te->de", routed_low, grad_logits_low, preferred_element_type=f32)
    grad_routed = grad_routed + jnp.einsum(
        "te,de->td", grad_logits_low, router_full, preferred_element_type=f32
    )
    grad_from_norm, grad_gain_second, grad_shift_second = norm_back(
        grad_routed, scaled_second, inv_second, gain_second
    )
    grad_mixed = grad_rows + grad_from_norm
    grad_bias_out = jnp.sum(grad_mixed, axis=0)
    grad_mixed_low = grad_mixed.astype(bf16)
    grad_out_turned = jnp.einsum("td,te->de", grad_mixed_low, attended_low, preferred_element_type=f32)
    grad_attended = jnp.dot(grad_mixed_low, out_turned, preferred_element_type=f32)
    grad_attended = grad_attended.astype(bf16).reshape(head_shape)
    grad_queries, grad_keys, grad_values = (
        grads.reshape(rows_total, local_width)
        for grads in attention_backward(
            queries, key_rows, value_rows, log_total, grad_attended, scale
        )
    )
    grad_pair_bias = jnp.stack([jnp.sum(grad_queries, axis=0), jnp.sum(grad_values, axis=0)])
    grad_proj_low = jnp.concatenate([grad_queries, grad_keys, grad_values], axis=1).astype(bf16)
    grad_qkv = jnp.einsum("td,te->de", normed_low, grad_proj_low, preferred_element_type=f32)
    grad_normed_part = jnp.einsum("te,de->td", grad_proj_low, qkv_full, preferred_element_type=f32)
    grad_normed = lax.psum(grad_normed_part.astype(bf16), tensor_axes).astype(f32)
    grad_from_first, _, _ = norm_back(grad_normed, scaled_first, inv_first, gain_first)
    first_terms = jnp.stack(
        [jnp.sum(grad_normed_part * scaled_first, axis=0), jnp.sum(grad_normed_part, axis=0)]
    )
    grad_images = (grad_mixed + grad_from_first).reshape(images.shape)

    def spread(parts):
        return swap(parts.reshape(owners, *parts.shape[2:]), (DP, INNER)).astype(f32)

    experts_shape = (experts_here, shard_width, ff_here)
    grad_in_parts = spread(grad_in_out)
    grad_w_in = grad_in_parts[:, : mine * shard_width].reshape(experts_shape)
    lines = grad_in_parts[:, mine * shard_width :]
    grad_in_bias = lines[:, : 2 * mine].reshape(owners, mine, 2, ff_here)
    grad_in_bias = jnp.sum(grad_in_bias, axis=2).reshape(experts_here, ff_here)
    lines = lines[:, 2 * mine : 3 * mine].reshape(experts_here, 2, ff_here // 2)
    grad_back_shard = jnp.sum(lines[:, :, :shard_width], axis=1)
    early = jnp.concatenate(
        [grad_qkv.astype(bf16), grad_out_turned.astype(bf16), grad_router.astype(bf16)], axis=1
    )
    early, grad_back_out = lax.optimization_barrier((early, grad_back_out))
    early = swap(early.reshape(groups, shard_width // sources, -1), (DP, EXPERT))
    early, grad_back_out = lax.optimization_barrier((early, grad_back_out))
    grad_w_back = spread(grad_back_out).reshape(experts_shape).transpose(0, 2, 1)
    early = jnp.sum(early.astype(f32), axis=0)
    early = hop_gather(early, EXPERT).reshape(shard_width, -1)
    grad_w_qkv = early[:, : 3 * local_width].reshape(shard_width, 3, local_width).transpose(1, 0, 2)
    grad_w_out = early[:, 3 * local_width : 4 * local_width].T
    grad_w_router = early[:, 4 * local_width :]
    once = (tensor_at == 0).astype(f32)
    pair_bias = lax.dynamic_update_slice(
        jnp.zeros((2, width), f32), grad_pair_bias, (0, tensor_at * local_width)
    )
    vectors = [grad_bias_out, grad_gain_second, grad_shift_second]
    vectors = jnp.concatenate([first_terms, pair_bias, once * jnp.stack(vectors)], axis=0)
    vectors = lax.psum(vectors, everywhere)
    grad_qv_bias = lax.dynamic_slice_in_dim(vectors[2:4], tensor_at * local_width, local_width, 1)
    vectors = lax.dynamic_slice_in_dim(vectors, dp_at * shard_width, shard_width, 1)
    grad_first_gain, grad_first_shift, _, _, grad_out_bias, grad_second_gain, grad_second_shift = vectors
    return (
        output,
        grad_images,
        grad_first_gain,
        grad_first_shift,
        grad_w_qkv,
        grad_qv_bias,
        grad_w_out,
        grad_out_bias,
        grad_second_gain,
        grad_second_shift,
        grad_w_router,
        grad_w_in,
        grad_in_bias,
        grad_w_back,
        grad_back_shard,
    )


def specs(tensor):
    rows = P((DP, EXPERT), None, None)
    vector, square = P(DP), P(tensor, DP)
    qkv, pair, router = P(None, DP, tensor), P(None, tensor), P(DP, None)
    inward, outward = P(EXPERT, DP, tensor), P(EXPERT, tensor, DP)
    params = (vector, vector, qkv, pair, square, vector, vector, vector, router)
    experts = (inward, P(EXPERT, tensor), outward, P(EXPERT, DP))
    taken = (rows, P((DP, EXPERT)), rows, rows, *params, *experts, rows)
    given = (rows, rows, *params, *experts)
    return taken, given


def solution(mesh):
    data, expert, tensor = (mesh.shape[name] for name in (DP, EXPERT, TENSOR))
    inner = FF_PAIR if tensor % FF_PAIR == 0 else 1
    if (EXPERTS // expert) % (data * inner):
        taken, given = specs(TENSOR)
        return jax.shard_map(
            gathered_plan, mesh=mesh, in_specs=taken, out_specs=given, check_vma=False
        )
    devices = mesh.devices.reshape(data, expert, tensor // inner, inner)
    split_mesh = Mesh(devices, (DP, EXPERT, OUTER, INNER))
    taken, given = specs((OUTER, INNER))
    return jax.shard_map(
        moved_plan, mesh=split_mesh, in_specs=taken, out_specs=given, check_vma=False
    )
```

```python
import functools
import math

import jax
import jax.numpy as jnp
from jax import lax
from jax.experimental import pallas as pl
from jax.experimental.pallas import tpu as pltpu
from jax.sharding import Mesh
from jax.sharding import PartitionSpec as P

HEAD_DIM = 64
EXPERTS = 32
TOPK = 2
CAP = 64
FF_PAIR = 1
EXTRA = 16
VMEM_LIMIT = 56 * 1024 * 1024
GELU_SCALE = (2.0 / math.pi) ** 0.5
GELU_CUBE = 0.044715

DP = "dp"
EXPERT = "expert"
TENSOR = "tensor"
OUTER = "outer"
INNER = "inner"


EPS = 1e-06


def norm_parts(values, norm_gain, norm_shift):
    average = jnp.mean(values, axis=-1, keepdims=True)
    centred = values - average
    spread = jnp.mean(centred * centred, axis=-1, keepdims=True)
    inv_std = lax.rsqrt(spread + EPS)
    scaled = centred * inv_std
    return (scaled * norm_gain + norm_shift, scaled, inv_std)


def norm_back(grad_out, scaled, inv_std, norm_gain):
    grad_scaled = grad_out * norm_gain
    inner = grad_scaled - jnp.mean(grad_scaled, axis=-1, keepdims=True)
    inner = inner - scaled * jnp.mean(grad_scaled * scaled, axis=-1, keepdims=True)
    return (inner * inv_std, jnp.sum(grad_out * scaled, axis=0), jnp.sum(grad_out, axis=0))


def attention_forward(queries, key_rows, value_rows, scale):
    scores = (
        jnp.einsum("iqhd,ikhd->ihqk", queries, key_rows, preferred_element_type=jnp.float32) * scale
    )
    row_peak = jnp.max(scores, axis=-1, keepdims=True)
    log_total = row_peak + jnp.log(jnp.sum(jnp.exp(scores - row_peak), axis=-1, keepdims=True))
    weights = jnp.exp(scores - log_total).astype(jnp.bfloat16)
    attended = jnp.einsum(
        "ihqk,ikhd->iqhd", weights, value_rows, preferred_element_type=jnp.float32
    )
    return (attended, log_total)


def attention_backward(queries, key_rows, value_rows, log_total, grad_low, scale):
    scores = (
        jnp.einsum("iqhd,ikhd->ihqk", queries, key_rows, preferred_element_type=jnp.float32) * scale
    )
    probs = jnp.exp(scores - log_total)
    weights = probs.astype(jnp.bfloat16)
    grad_values = jnp.einsum(
        "ihqk,iqhd->ikhd", weights, grad_low, preferred_element_type=jnp.float32
    )
    grad_weights = jnp.einsum(
        "iqhd,ikhd->ihqk", grad_low, value_rows, preferred_element_type=jnp.float32
    )
    grad_scores = probs * (grad_weights - jnp.sum(probs * grad_weights, axis=-1, keepdims=True))
    scores_low = grad_scores.astype(jnp.bfloat16)
    grad_queries = (
        jnp.einsum("ihqk,ikhd->iqhd", scores_low, key_rows, preferred_element_type=jnp.float32)
        * scale
    )
    grad_keys = (
        jnp.einsum("ihqk,iqhd->ikhd", scores_low, queries, preferred_element_type=jnp.float32)
        * scale
    )
    return (grad_queries, grad_keys, grad_values)


def gathered_plan(
    images,
    images_held,
    routes,
    slot_index,
    first_gain,
    first_shift,
    w_qkv,
    qv_bias,
    w_out,
    out_bias,
    second_gain,
    second_shift,
    w_router,
    w_in,
    in_bias,
    w_back,
    back_bias,
    cotangent,
):
    image_count, seq_len, width = images.shape
    rows_total = image_count * seq_len
    experts_here = w_in.shape[0]
    (
        gain_first,
        shift_first,
        qkv_full,
        out_full,
        bias_out_full,
        gain_second,
        shift_second,
        router_full,
        in_full,
        back_full,
        back_bias_full,
    ) = (
        lax.all_gather(first_gain, DP, axis=0, tiled=True),
        lax.all_gather(first_shift, DP, axis=0, tiled=True),
        lax.all_gather(w_qkv, DP, axis=1, tiled=True),
        lax.all_gather(w_out, DP, axis=1, tiled=True),
        lax.all_gather(out_bias, DP, axis=0, tiled=True),
        lax.all_gather(second_gain, DP, axis=0, tiled=True),
        lax.all_gather(second_shift, DP, axis=0, tiled=True),
        lax.all_gather(w_router, DP, axis=0, tiled=True),
        lax.all_gather(w_in, DP, axis=1, tiled=True),
        lax.all_gather(w_back, DP, axis=2, tiled=True),
        lax.all_gather(back_bias, DP, axis=1, tiled=True),
    )
    gain_first = gain_first.astype(jnp.float32)
    gain_second = gain_second.astype(jnp.float32)
    inputs = images.reshape(rows_total, width).astype(jnp.float32)
    live_image = (jnp.arange(image_count, dtype=jnp.int32) < images_held[0]).astype(jnp.float32)
    live_rows = jnp.repeat(live_image, seq_len)[:, None]
    normed, scaled_first, inv_first = norm_parts(
        inputs, gain_first, shift_first.astype(jnp.float32)
    )
    normed_low = normed.astype(jnp.bfloat16)
    projected = jnp.einsum("td,cde->cte", normed_low, qkv_full, preferred_element_type=jnp.float32)
    local_width = projected.shape[2]
    head_count = local_width // HEAD_DIM
    head_shape = (image_count, seq_len, head_count, HEAD_DIM)
    bias_pair = qv_bias.astype(jnp.float32)
    queries = (projected[0] + bias_pair[0]).astype(jnp.bfloat16).reshape(head_shape)
    key_rows = projected[1].astype(jnp.bfloat16).reshape(head_shape)
    value_rows = (projected[2] + bias_pair[1]).astype(jnp.bfloat16).reshape(head_shape)
    scale = HEAD_DIM ** (-0.5)
    attended, log_total = attention_forward(queries, key_rows, value_rows, scale)
    attended_low = attended.reshape(rows_total, local_width).astype(jnp.bfloat16)
    head_part = jnp.dot(attended_low, out_full, preferred_element_type=jnp.float32)
    mixed = inputs + lax.psum(head_part, TENSOR) + bias_out_full.astype(jnp.float32)
    routed, scaled_second, inv_second = norm_parts(
        mixed, gain_second, shift_second.astype(jnp.float32)
    )
    routed_low = routed.astype(jnp.bfloat16)
    logits = jnp.dot(routed_low, router_full, preferred_element_type=jnp.float32)
    probs = jax.nn.softmax(logits, axis=-1)
    pair_routes = routes.reshape(rows_total, TOPK)
    pair_slots = slot_index.reshape(rows_total, TOPK)
    target = jnp.where(pair_slots < CAP, pair_routes * CAP + pair_slots, EXPERTS * CAP).reshape(
        rows_total * TOPK
    )
    gates = jnp.take_along_axis(probs, pair_routes, axis=1)
    pair_rows = jnp.repeat(routed_low, TOPK, axis=0)
    outgoing = (
        jnp.zeros((EXPERTS * CAP + 1, width), jnp.bfloat16)
        .at[target]
        .set(pair_rows)[: EXPERTS * CAP]
    )
    outgoing = outgoing.reshape(EXPERTS, 1, CAP, width)
    arrived = lax.all_to_all(outgoing, EXPERT, split_axis=0, concat_axis=1, tiled=True)
    sources = arrived.shape[1]
    expert_rows = arrived.reshape(experts_here, sources * CAP, width)
    hidden_pre = jnp.einsum(
        "erd,edf->erf", expert_rows, in_full, preferred_element_type=jnp.float32
    )
    hidden_pre = hidden_pre + in_bias.astype(jnp.float32)[:, None, :]
    hidden_value, gelu_pull = jax.vjp(jax.nn.gelu, hidden_pre)
    hidden_low = hidden_value.astype(jnp.bfloat16)
    expert_part = jnp.einsum(
        "erf,efd->erd", hidden_low, back_full, preferred_element_type=jnp.float32
    )
    bias_back = back_bias_full.astype(jnp.float32)[:, None, :]
    shares = lax.psum_scatter(
        expert_part.reshape(experts_here, sources, CAP, width),
        TENSOR,
        scatter_dimension=2,
        tiled=True,
    )
    share_low = (shares + bias_back[:, None]).astype(jnp.bfloat16)
    pieces = lax.all_to_all(share_low, EXPERT, split_axis=1, concat_axis=0, tiled=True)
    returned = lax.all_gather(pieces, TENSOR, axis=2, tiled=True)
    padded = jnp.concatenate(
        [returned.reshape(EXPERTS * CAP, width), jnp.zeros((1, width), jnp.bfloat16)], axis=0
    )
    picked = padded[target].astype(jnp.float32).reshape(rows_total, TOPK, width)
    expert_mix = jnp.sum(gates[:, :, None] * picked, axis=1)
    output = (live_rows * (mixed + expert_mix)).astype(jnp.bfloat16).reshape(images.shape)
    grad_rows = cotangent.reshape(rows_total, width).astype(jnp.float32) * live_rows
    grad_gates = jnp.sum(grad_rows[:, None, :] * picked, axis=-1)
    grad_picked = (
        (gates[:, :, None] * grad_rows[:, None, :])
        .astype(jnp.bfloat16)
        .reshape(rows_total * TOPK, width)
    )
    grad_outgoing = (
        jnp.zeros((EXPERTS * CAP + 1, width), jnp.bfloat16)
        .at[target]
        .set(grad_picked)[: EXPERTS * CAP]
    )
    grad_outgoing = grad_outgoing.reshape(EXPERTS, 1, CAP, width)
    grad_arrived = lax.all_to_all(grad_outgoing, EXPERT, split_axis=0, concat_axis=1, tiled=True)
    grad_arrived = grad_arrived.reshape(experts_here, sources * CAP, width)
    grad_back_bias = jnp.sum(grad_arrived.astype(jnp.float32), axis=1)
    grad_back_w = jnp.einsum(
        "erf,erd->efd", hidden_low, grad_arrived, preferred_element_type=jnp.float32
    )
    grad_hidden = jnp.einsum(
        "erd,efd->erf", grad_arrived, back_full, preferred_element_type=jnp.float32
    )
    grad_pre = gelu_pull(grad_hidden)[0]
    grad_in_bias_local = jnp.sum(grad_pre, axis=1)
    grad_pre_low = grad_pre.astype(jnp.bfloat16)
    grad_in_w = jnp.einsum(
        "erd,erf->edf", expert_rows, grad_pre_low, preferred_element_type=jnp.float32
    )
    grad_rows_part = jnp.einsum(
        "erf,edf->erd", grad_pre_low, in_full, preferred_element_type=jnp.float32
    )
    grad_shares = lax.psum_scatter(
        grad_rows_part.reshape(experts_here, sources, CAP, width),
        TENSOR,
        scatter_dimension=2,
        tiled=True,
    ).astype(jnp.bfloat16)
    grad_pieces = lax.all_to_all(grad_shares, EXPERT, split_axis=1, concat_axis=0, tiled=True)
    grad_returned = lax.all_gather(grad_pieces, TENSOR, axis=2, tiled=True)
    grad_padded = jnp.concatenate(
        [grad_returned.reshape(EXPERTS * CAP, width), jnp.zeros((1, width), jnp.bfloat16)], axis=0
    )
    grad_routed = jnp.sum(
        grad_padded[target].astype(jnp.float32).reshape(rows_total, TOPK, width), axis=1
    )
    expert_match = (
        pair_routes[:, :, None] == jnp.arange(EXPERTS, dtype=jnp.int32)[None, None, :]
    ).astype(jnp.float32)
    grad_probs = jnp.sum(expert_match * grad_gates[:, :, None], axis=1)
    grad_logits = probs * (grad_probs - jnp.sum(probs * grad_probs, axis=-1, keepdims=True))
    grad_logits_low = grad_logits.astype(jnp.bfloat16)
    grad_router = jnp.einsum(
        "td,te->de", routed_low, grad_logits_low, preferred_element_type=jnp.float32
    )
    grad_routed = grad_routed + jnp.einsum(
        "te,de->td", grad_logits_low, router_full, preferred_element_type=jnp.float32
    )
    grad_from_norm, grad_gain_second, grad_shift_second = norm_back(
        grad_routed, scaled_second, inv_second, gain_second
    )
    grad_mixed = grad_rows + grad_from_norm
    grad_bias_out = jnp.sum(grad_mixed, axis=0)
    grad_mixed_low = grad_mixed.astype(jnp.bfloat16)
    grad_out_w = jnp.einsum(
        "te,td->ed", attended_low, grad_mixed_low, preferred_element_type=jnp.float32
    )
    grad_attended = jnp.einsum(
        "td,ed->te", grad_mixed_low, out_full, preferred_element_type=jnp.float32
    )
    grad_attended = grad_attended.astype(jnp.bfloat16).reshape(head_shape)
    grad_queries, grad_keys, grad_values = attention_backward(
        queries, key_rows, value_rows, log_total, grad_attended, scale
    )
    grad_queries = grad_queries.reshape(rows_total, local_width)
    grad_keys = grad_keys.reshape(rows_total, local_width)
    grad_values = grad_values.reshape(rows_total, local_width)
    grad_pair_bias = jnp.stack([jnp.sum(grad_queries, axis=0), jnp.sum(grad_values, axis=0)])
    grad_proj_low = jnp.stack([grad_queries, grad_keys, grad_values]).astype(jnp.bfloat16)
    grad_qkv = jnp.einsum(
        "td,cte->cde", normed_low, grad_proj_low, preferred_element_type=jnp.float32
    )
    grad_normed_part = jnp.einsum(
        "cte,cde->td", grad_proj_low, qkv_full, preferred_element_type=jnp.float32
    )
    grad_normed = lax.psum(grad_normed_part, TENSOR)
    grad_from_first, grad_gain_first, grad_shift_first = norm_back(
        grad_normed, scaled_first, inv_first, gain_first
    )
    grad_images = (grad_mixed + grad_from_first).reshape(images.shape)
    expert_start = lax.axis_index(EXPERT) * experts_here
    full_in_bias = lax.dynamic_update_slice(
        jnp.zeros((EXPERTS, grad_in_bias_local.shape[1]), jnp.float32),
        grad_in_bias_local,
        (expert_start, jnp.zeros((), jnp.int32)),
    )
    summed = lax.psum(
        (
            grad_gain_first,
            grad_shift_first,
            grad_qkv,
            grad_pair_bias,
            grad_out_w,
            grad_bias_out,
            grad_gain_second,
            grad_shift_second,
            grad_router,
            full_in_bias,
        ),
        (DP, EXPERT),
    )
    shard_width = width // lax.axis_size(DP)
    shard_start = lax.axis_index(DP) * shard_width
    grad_first_gain = lax.dynamic_slice_in_dim(summed[0], shard_start, shard_width, 0)
    grad_first_shift = lax.dynamic_slice_in_dim(summed[1], shard_start, shard_width, 0)
    grad_w_qkv = lax.dynamic_slice_in_dim(summed[2], shard_start, shard_width, 1)
    grad_qv_bias = summed[3]
    grad_w_out = lax.dynamic_slice_in_dim(summed[4], shard_start, shard_width, 1)
    grad_out_bias = lax.dynamic_slice_in_dim(summed[5], shard_start, shard_width, 0)
    grad_second_gain = lax.dynamic_slice_in_dim(summed[6], shard_start, shard_width, 0)
    grad_second_shift = lax.dynamic_slice_in_dim(summed[7], shard_start, shard_width, 0)
    grad_w_router = lax.dynamic_slice_in_dim(summed[8], shard_start, shard_width, 0)
    grad_in_bias = lax.dynamic_slice_in_dim(summed[9], expert_start, experts_here, 0)
    grad_w_in, grad_w_back, grad_back_shard = (
        lax.psum_scatter(grad_in_w, DP, scatter_dimension=1, tiled=True),
        lax.psum_scatter(grad_back_w, DP, scatter_dimension=2, tiled=True),
        lax.psum_scatter(grad_back_bias, DP, scatter_dimension=1, tiled=True),
    )
    return (
        output,
        grad_images,
        grad_first_gain,
        grad_first_shift,
        grad_w_qkv,
        grad_qv_bias,
        grad_w_out,
        grad_out_bias,
        grad_second_gain,
        grad_second_shift,
        grad_w_router,
        grad_w_in,
        grad_in_bias,
        grad_w_back,
        grad_back_shard,
    )


def swap(values, axes):
    return lax.all_to_all(values, axes, split_axis=0, concat_axis=0, tiled=True)


def hop_gather(values, axes):
    count, at = lax.axis_size(axes), lax.axis_index(axes)
    hops = [values]
    for s in range(1, count):
        hops.append(lax.ppermute(values, axes, [(i, (i + s) % count) for i in range(count)]))
    order = (at - jnp.arange(count, dtype=jnp.int32)) % count
    return jnp.take(jnp.stack(hops), order, axis=0)


def cross(values, s):
    count = lax.axis_size((DP, INNER))
    return lax.ppermute(values, (DP, INNER), [(i, i ^ s) for i in range(count)]) if s else values


def high_low(values):
    high = lax.reduce_precision(values, 8, 7)
    return high.astype(jnp.bfloat16), (values - high).astype(jnp.bfloat16)


def turned_dot(left, right, left_dim, right_dim):
    return lax.dot_general(
        left, right, (((left_dim,), (right_dim,)), ((), ())), preferred_element_type=jnp.float32
    )


def expert_kernel(inner, owners, at_ref, rows_ref, gate_ref, cot_ref, in_bias_ref, back_bias_ref, *refs):
    piece_refs, refs = refs[:owners], refs[owners:]
    returned_ref, grads_ref, hidden_ref, grad_pre_ref, grad_turned_ref = refs[:5]
    grad_in_bias_ref, grad_back_bias_ref, weight_ref = refs[5:]
    f32, bf16 = jnp.float32, jnp.bfloat16
    groups, cap, width = rows_ref.shape
    depth = piece_refs[0].shape[2]
    for s, piece_ref in enumerate(piece_refs):
        source = at_ref[0] ^ s
        place = pl.ds(pl.multiple_of((source // inner) * depth, depth), depth)
        for k in range(2):
            weight_ref[k, source % inner, place] = piece_ref[k, 0]
    tensor, slice_width = returned_ref.shape[1:3]
    mine = back_bias_ref.shape[1]
    total = groups * cap
    at = pl.program_id(0)
    rows = rows_ref[...].reshape(total, width)
    cot_turned = cot_ref[...].reshape(total, width).T.astype(f32)
    pair = gate_ref[:, 0:1, :].astype(f32) + gate_ref[:, 1:2, :].astype(f32)
    pair = pair.reshape(groups, pair.shape[-1])
    gate = jnp.zeros((groups, cap), f32)
    for j in range(mine):
        gate = jnp.where(at == j, pair[:, j * cap : (j + 1) * cap], gate)
    gate = jnp.concatenate([gate[g : g + 1, :] for g in range(groups)], axis=1)
    grad_turned = (cot_turned * gate).astype(bf16)
    grad_turned_ref[0] = grad_turned
    grad_returned = grad_turned.T
    grad_back_bias_ref[0] = jnp.sum(grad_returned.astype(f32), axis=0, keepdims=True)
    bias_columns = back_bias_ref[...]
    bias = jnp.zeros((width, 1), f32)
    for j in range(mine):
        bias = jnp.where(at == j, bias_columns[:, j : j + 1], bias)
    part = jnp.broadcast_to(bias, (width, total))
    back = jnp.zeros((width, total), f32)
    for t in range(inner):
        w_in, w_back = weight_ref[0, t], weight_ref[1, t]
        pre = jnp.dot(rows, w_in, preferred_element_type=f32) + in_bias_ref[0, t : t + 1, :]
        square = pre * pre
        bent = jnp.tanh(GELU_SCALE * pre * (1.0 + GELU_CUBE * square))
        half = 0.5 * (1.0 + bent)
        hidden = (pre * half).astype(bf16)
        slope = half + (0.5 * GELU_SCALE) * pre * (1.0 - bent * bent) * (
            1.0 + (3.0 * GELU_CUBE) * square
        )
        hidden_ref[0, t] = hidden
        grad_pre = jnp.dot(grad_returned, w_back, preferred_element_type=f32) * slope
        grad_in_bias_ref[0, t : t + 1, :] = jnp.sum(grad_pre, axis=0, keepdims=True)
        grad_pre = grad_pre.astype(bf16)
        grad_pre_ref[0, t] = grad_pre
        part = part + turned_dot(w_back, hidden, 1, 1)
        back = back + turned_dot(w_in, grad_pre, 1, 1)
    gate_terms = jnp.sum(part * cot_turned, axis=0, keepdims=True)
    high = gate_terms.astype(bf16)
    low = (gate_terms - high.astype(f32)).astype(bf16)
    extra = grads_ref.shape[2] - slice_width
    tail = jnp.concatenate([high, low, jnp.zeros((extra - 2, total), bf16)], axis=0)
    part = part.astype(bf16)
    back = back.astype(bf16)
    for j in range(mine):

        @pl.when(at == j)
        def _():
            lanes = slice(j * cap, (j + 1) * cap)
            for g in range(groups):
                mine_lanes = slice(g * cap, (g + 1) * cap)
                for z in range(tensor):
                    features = slice(z * slice_width, (z + 1) * slice_width)
                    returned_ref[g, z, :, lanes] = part[features, mine_lanes]
                    grads_ref[g, z, :slice_width, lanes] = back[features, mine_lanes]
                    grads_ref[g, z, slice_width:, lanes] = tail[:, mine_lanes]


def run_experts(owner_at, arrived, cot_rows, pieces, in_bias, back_bias, inner, tensor):
    f32, bf16 = jnp.float32, jnp.bfloat16
    groups, _, width = cot_rows.shape
    owners = len(pieces)
    _, mine, depth, ff = pieces[0].shape
    total = groups * CAP
    slice_width = width // tensor
    gate_at = mine * CAP // EXTRA
    outs = [
        ((groups, tensor, slice_width, mine * CAP), bf16, lambda j: (0, 0, 0, 0), None),
        ((groups, tensor, slice_width + EXTRA, mine * CAP), bf16, lambda j: (0, 0, 0, 0), None),
        ((mine, inner, total, ff), bf16, lambda j: (j, 0, 0, 0), 1),
        ((mine, inner, total, ff), bf16, lambda j: (j, 0, 0, 0), 1),
        ((mine, width, total), bf16, lambda j: (j, 0, 0), 1),
        ((mine, inner, ff), f32, lambda j: (j, 0, 0), 1),
        ((mine, 1, width), f32, lambda j: (j, 0, 0), 1),
    ]
    return pl.pallas_call(
        functools.partial(expert_kernel, inner, owners),
        grid=(mine,),
        in_specs=[
            pl.BlockSpec(memory_space=pltpu.SMEM),
            pl.BlockSpec((groups, CAP, width), lambda j: (0, j, 0)),
            pl.BlockSpec((groups, EXTRA, mine * CAP), lambda j: (0, gate_at, 0)),
            pl.BlockSpec((groups, CAP, width), lambda j: (0, j, 0)),
            pl.BlockSpec((1, inner, ff), lambda j: (j, 0, 0)),
            pl.BlockSpec((width, mine), lambda j: (0, 0)),
        ]
        + [pl.BlockSpec((2, 1, depth, ff), lambda j: (0, j, 0, 0))] * owners,
        out_specs=[
            pl.BlockSpec(shape if lead is None else (lead, *shape[1:]), index)
            for shape, _, index, lead in outs
        ],
        out_shape=[jax.ShapeDtypeStruct(shape, dtype) for shape, dtype, _, _ in outs],
        scratch_shapes=[pltpu.VMEM((2, inner, width, ff), bf16)],
        compiler_params=pltpu.CompilerParams(vmem_limit_bytes=VMEM_LIMIT),
        cost_estimate=pl.CostEstimate(
            flops=8 * mine * total * width * inner * ff,
            bytes_accessed=4 * owners * mine * depth * ff + 12 * mine * total * inner * ff,
            transcendentals=mine * total * inner * ff,
        ),
    )(owner_at.reshape(1), arrived, arrived, cot_rows, in_bias, back_bias, *pieces)


def weight_kernel(
    inner,
    at_ref,
    rows_ref,
    grad_pre_ref,
    grad_turned_ref,
    hidden_ref,
    in_bias_ref,
    back_bias_ref,
    *refs,
):
    f32, bf16 = jnp.float32, jnp.bfloat16
    out_refs, sums_ref, tail_ref = refs[:-2], refs[-2], refs[-1]
    groups, cap, width = rows_ref.shape
    mine = back_bias_ref.shape[0]
    ff = sums_ref.shape[-1]
    depth = width * inner // len(out_refs)
    data = width // depth
    part, at = pl.program_id(0), pl.program_id(1)
    rows = rows_ref[...].reshape(groups * cap, width)
    sums_ref[0] = turned_dot(rows, grad_pre_ref[0, 0], 0, 0).astype(bf16)
    grad_back = jnp.dot(grad_turned_ref[0], hidden_ref[0, 0], preferred_element_type=f32)
    sums_ref[1] = grad_back.astype(bf16)

    @pl.when(at == mine - 1)
    def _():
        pairs = []
        for j in range(mine):
            values = in_bias_ref[j, 0]
            high = values.astype(bf16).astype(f32)
            pairs += [high, values - high]
        for d in range(data):
            lines = list(pairs)
            for j in range(mine):
                values = back_bias_ref[j, :, d * depth : (d + 1) * depth]
                high = values.astype(bf16).astype(f32)
                gap = jnp.zeros((1, ff // 2 - depth), f32)
                lines.append(jnp.concatenate([high, gap, values - high, gap], axis=1))
            lines.append(jnp.zeros((EXTRA - len(lines), ff), f32))
            tail_ref[d] = jnp.concatenate(lines, axis=0).astype(bf16)

    for s, out_ref in enumerate(out_refs):
        owner = at_ref[0] ^ s
        d = owner // inner
        place = pl.ds(pl.multiple_of(d * depth, depth), depth)

        @pl.when(owner % inner == part)
        def _():
            for k in range(2):
                line = pl.multiple_of((k * mine + at) * depth, depth)
                out_ref[pl.ds(line, depth)] = sums_ref[k, place]

            @pl.when(at == mine - 1)
            def _():
                out_ref[2 * mine * depth :] = tail_ref[d]


def weight_grads(
    owner_at, arrived, grad_pre, grad_turned, hidden, grad_in_bias, grad_back_bias, owners
):
    mine, inner, total, ff = hidden.shape
    groups, _, width = arrived.shape
    depth = width * inner // owners
    kept = pl.BlockSpec((1, 1, total, ff), lambda t, j: (j, t, 0, 0))
    out = (2 * mine * depth + EXTRA, ff)
    return pl.pallas_call(
        functools.partial(weight_kernel, inner),
        grid=(inner, mine),
        in_specs=[
            pl.BlockSpec(memory_space=pltpu.SMEM),
            pl.BlockSpec((groups, CAP, width), lambda t, j: (0, j, 0)),
            kept,
            pl.BlockSpec((1, width, total), lambda t, j: (j, 0, 0)),
            kept,
            pl.BlockSpec((mine, 1, 1, ff), lambda t, j: (0, t, 0, 0)),
            pl.BlockSpec((mine, 1, width), lambda t, j: (0, 0, 0)),
        ],
        out_specs=[pl.BlockSpec(out, lambda t, j: (0, 0))] * owners,
        out_shape=[jax.ShapeDtypeStruct(out, jnp.bfloat16)] * owners,
        scratch_shapes=[
            pltpu.VMEM((2, width, ff), jnp.bfloat16),
            pltpu.VMEM((width // depth, EXTRA, ff), jnp.bfloat16),
        ],
        compiler_params=pltpu.CompilerParams(vmem_limit_bytes=VMEM_LIMIT),
        cost_estimate=pl.CostEstimate(
            flops=4 * mine * total * width * inner * ff,
            bytes_accessed=4 * mine * inner * (total + width) * ff,
            transcendentals=0,
        ),
    )(
        owner_at.reshape(1),
        arrived,
        grad_pre,
        grad_turned,
        hidden,
        grad_in_bias[:, :, None],
        grad_back_bias,
    )


def moved_plan(
    images,
    images_held,
    routes,
    slot_index,
    first_gain,
    first_shift,
    w_qkv,
    qv_bias,
    w_out,
    out_bias,
    second_gain,
    second_shift,
    w_router,
    w_in,
    in_bias,
    w_back,
    back_bias,
    cotangent,
):
    f32, bf16 = jnp.float32, jnp.bfloat16
    image_count, seq_len, width = images.shape
    rows_total = image_count * seq_len
    experts_here, shard_width, ff_here = w_in.shape
    data, sources = lax.axis_size(DP), lax.axis_size(EXPERT)
    outer, inner = lax.axis_size(OUTER), lax.axis_size(INNER)
    tensor = outer * inner
    tensor_axes = (OUTER, INNER)
    groups = data * sources
    owners = data * inner
    mine = experts_here // owners
    slots = EXPERTS * CAP
    slots_plane = slots // inner
    dp_at = lax.axis_index(DP)
    inner_at = lax.axis_index(INNER)
    tensor_at = lax.axis_index(tensor_axes)
    owner_at = dp_at * inner + inner_at
    local_width = w_out.shape[0]
    slice_width = width // tensor

    packed = jnp.concatenate(
        [
            w_qkv.transpose(1, 0, 2).reshape(shard_width, 3 * local_width),
            w_out.T,
            w_router,
            back_bias.T,
            jnp.stack([first_gain, first_shift, out_bias, second_gain, second_shift], axis=1),
        ],
        axis=1,
    )
    packed = lax.all_gather(packed, DP, axis=0, tiled=True)

    back_turned = w_back.transpose(0, 2, 1)
    pieces = []
    for s in range(owners):
        start = (owner_at ^ s) * mine
        piece = [lax.dynamic_slice_in_dim(shard, start, mine, 0) for shard in (w_in, back_turned)]
        pieces.append(jnp.stack(piece))
    near = owners // 2
    packed, *pieces[near:] = lax.optimization_barrier((packed, *pieces[near:]))
    pieces = [cross(piece, s) for s, piece in enumerate(pieces)]
    cuts = [3 * local_width, local_width, EXPERTS, experts_here]
    qkv_full, out_turned, router_full, back_bias_turned, vectors = jnp.split(
        packed, [sum(cuts[: i + 1]) for i in range(4)], axis=1
    )
    gain_first, shift_first, bias_out_full, gain_second, shift_second = (
        vectors[:, i].astype(f32) for i in range(5)
    )
    out_whole = hop_gather(out_turned, tensor_axes)
    out_whole = out_whole.transpose(1, 0, 2).reshape(width, width)
    in_bias_all = hop_gather(in_bias, INNER)
    in_bias_mine = lax.dynamic_slice_in_dim(in_bias_all, owner_at * mine, mine, 1)
    in_bias_mine = in_bias_mine.transpose(1, 0, 2).astype(f32)

    pair_routes = routes.reshape(rows_total, TOPK)
    pair_slots = slot_index.reshape(rows_total, TOPK)
    home, within = pair_routes // experts_here, pair_routes % experts_here
    owner, nth = within // mine, within % mine
    place = ((owner // inner) * sources + home) * inner + owner % inner
    target = jnp.where(pair_slots < CAP, (place * mine + nth) * CAP + pair_slots, slots)
    plane_slots = jnp.arange(slots, dtype=jnp.int32).reshape(groups, inner, mine * CAP)
    plane_slots = lax.dynamic_slice_in_dim(plane_slots, inner_at, 1, 1).reshape(slots_plane)
    takes = [plane_slots[:, None] == target[None, :, k] for k in range(TOPK)]
    fill = jnp.logical_or(takes[0], takes[1]).astype(bf16)

    live_image = (jnp.arange(image_count, dtype=jnp.int32) < images_held[0]).astype(f32)
    live_rows = jnp.repeat(live_image, seq_len)[:, None]
    grad_rows = cotangent.reshape(rows_total, width).astype(f32) * live_rows

    def dispatch(rows):
        return jnp.dot(fill, rows, preferred_element_type=f32).astype(bf16)

    cot_out = dispatch(grad_rows.astype(bf16)).reshape(groups, mine * CAP, width)
    cot_rows = swap(cot_out, (DP, EXPERT))

    inputs = images.reshape(rows_total, width).astype(f32)
    normed, scaled_first, inv_first = norm_parts(inputs, gain_first, shift_first)
    normed_low = normed.astype(bf16)
    projected = jnp.dot(normed_low, qkv_full, preferred_element_type=f32)
    head_count = local_width // HEAD_DIM
    head_shape = (image_count, seq_len, head_count, HEAD_DIM)
    bias_pair = qv_bias.astype(f32)
    queries, key_rows, value_rows = (
        projected[:, i * local_width : (i + 1) * local_width] for i in range(3)
    )
    queries = (queries + bias_pair[0]).astype(bf16).reshape(head_shape)
    key_rows = key_rows.astype(bf16).reshape(head_shape)
    value_rows = (value_rows + bias_pair[1]).astype(bf16).reshape(head_shape)
    scale = HEAD_DIM ** (-0.5)
    attended, log_total = attention_forward(queries, key_rows, value_rows, scale)
    attended_low = attended.reshape(rows_total, local_width).astype(bf16)
    attended_all = lax.all_gather(attended_low, tensor_axes, axis=1, tiled=True)
    mixed = inputs + bias_out_full
    mixed = mixed + jnp.einsum("te,de->td", attended_all, out_whole, preferred_element_type=f32)
    routed, scaled_second, inv_second = norm_parts(mixed, gain_second, shift_second)
    routed_low = routed.astype(bf16)
    logits = jnp.dot(routed_low, router_full, preferred_element_type=f32)
    probs = jax.nn.softmax(logits, axis=-1)
    expert_ids = jnp.arange(EXPERTS, dtype=jnp.int32)
    matches = [(pair_routes[:, k : k + 1] == expert_ids).astype(f32) for k in range(TOPK)]
    gates = [jnp.sum(match * probs, axis=1) for match in matches]

    gate_slots = sum(
        jnp.sum(jnp.where(take, gate[None, :], 0.0), axis=1) for take, gate in zip(takes, gates)
    )
    gate_parts = jnp.stack(high_low(gate_slots.reshape(groups, mine * CAP)), axis=1)
    gate_rows = jnp.pad(gate_parts, ((0, 0), (0, 14), (0, width - mine * CAP)))
    sent = jnp.concatenate([dispatch(routed_low).reshape(groups, mine * CAP, width), gate_rows], axis=1)
    sent, cot_rows = lax.optimization_barrier((sent, cot_rows))
    arrived = swap(sent, (DP, EXPERT))
    back_bias_mine = lax.dynamic_slice_in_dim(back_bias_turned, owner_at * mine, mine, 1)
    back_bias_mine = jnp.where(lax.axis_index(OUTER) == 0, back_bias_mine.astype(f32), 0.0)
    (
        returned_out,
        grads_out,
        hidden_low,
        grad_pre_low,
        grad_turned,
        grad_in_bias_mine,
        grad_back_bias_mine,
    ) = run_experts(
        owner_at, arrived, cot_rows, pieces, in_bias_mine, back_bias_mine, inner, tensor
    )

    everywhere = (DP, EXPERT, OUTER, INNER)

    def bring(parts):
        parts = parts.reshape(groups * tensor, *parts.shape[2:])
        parts = swap(parts, everywhere).astype(f32)
        parts = jnp.sum(parts.reshape(groups, outer, inner, *parts.shape[1:]), axis=1)
        return parts.reshape(groups * inner, *parts.shape[2:])

    def in_line(parts):
        return parts.transpose(1, 0, 2).reshape(parts.shape[1], slots)

    grad_parts = bring(grads_out)
    grad_slots = in_line(grad_parts[:, :slice_width]).astype(bf16)
    gate_slots_back = in_line(grad_parts[:, slice_width : slice_width + 2])
    gate_slots_back = gate_slots_back[0] + gate_slots_back[1]
    all_slots = jnp.arange(slots, dtype=jnp.int32)
    found = [target[None, :, k] == all_slots[:, None] for k in range(TOPK)]
    finds = [hit.astype(bf16) for hit in found]
    both = jnp.logical_or(found[0], found[1]).astype(bf16)
    grad_gates = jnp.stack(
        [jnp.sum(jnp.where(hit, gate_slots_back[:, None], 0.0), axis=0) for hit in found], axis=1
    )
    grad_routed_cut = jnp.dot(grad_slots, both, preferred_element_type=f32).astype(bf16)
    weight_out = weight_grads(
        owner_at,
        arrived,
        grad_pre_low,
        grad_turned,
        hidden_low,
        grad_in_bias_mine,
        grad_back_bias_mine,
        owners,
    )
    grad_routed_cut, returned_out, *weight_out = lax.optimization_barrier(
        (grad_routed_cut, returned_out, *weight_out)
    )
    grad_routed = lax.all_gather(grad_routed_cut, tensor_axes, axis=0, tiled=True).T.astype(f32)
    returned = in_line(bring(returned_out)).astype(bf16)
    picked = [jnp.dot(returned, find, preferred_element_type=f32) for find in finds]
    mixed_cut = lax.dynamic_slice_in_dim(mixed, tensor_at * slice_width, slice_width, 1)
    expert_mix = gates[0][None, :] * picked[0] + gates[1][None, :] * picked[1]
    output_cut = (live_rows * (mixed_cut + expert_mix.T)).astype(bf16)
    output = lax.all_gather(output_cut, tensor_axes, axis=1, tiled=True).reshape(images.shape)

    grad_probs = sum(match * grad_gates[:, k : k + 1] for k, match in enumerate(matches))
    grad_logits = probs * (grad_probs - jnp.sum(probs * grad_probs, axis=-1, keepdims=True))
    grad_logits_low = grad_logits.astype(bf16)
    grad_router = jnp.einsum("td,te->de", routed_low, grad_logits_low, preferred_element_type=f32)
    grad_routed = grad_routed + jnp.einsum(
        "te,de->td", grad_logits_low, router_full, preferred_element_type=f32
    )
    grad_from_norm, grad_gain_second, grad_shift_second = norm_back(
        grad_routed, scaled_second, inv_second, gain_second
    )
    grad_mixed = grad_rows + grad_from_norm
    grad_bias_out = jnp.sum(grad_mixed, axis=0)
    grad_mixed_low = grad_mixed.astype(bf16)
    grad_out_turned = jnp.einsum("td,te->de", grad_mixed_low, attended_low, preferred_element_type=f32)
    grad_attended = jnp.dot(grad_mixed_low, out_turned, preferred_element_type=f32)
    grad_attended = grad_attended.astype(bf16).reshape(head_shape)
    grad_queries, grad_keys, grad_values = (
        grads.reshape(rows_total, local_width)
        for grads in attention_backward(
            queries, key_rows, value_rows, log_total, grad_attended, scale
        )
    )
    grad_pair_bias = jnp.stack([jnp.sum(grad_queries, axis=0), jnp.sum(grad_values, axis=0)])
    grad_proj_low = jnp.concatenate([grad_queries, grad_keys, grad_values], axis=1).astype(bf16)
    grad_qkv = jnp.einsum("td,te->de", normed_low, grad_proj_low, preferred_element_type=f32)
    grad_normed_part = jnp.einsum("te,de->td", grad_proj_low, qkv_full, preferred_element_type=f32)
    grad_normed = lax.psum(grad_normed_part.astype(bf16), tensor_axes).astype(f32)
    grad_from_first, _, _ = norm_back(grad_normed, scaled_first, inv_first, gain_first)
    first_terms = jnp.stack(
        [jnp.sum(grad_normed_part * scaled_first, axis=0), jnp.sum(grad_normed_part, axis=0)]
    )
    grad_images = (grad_mixed + grad_from_first).reshape(images.shape)

    experts_shape = (experts_here, shard_width, ff_here)
    grad_w_in, grad_w_back = jnp.zeros(experts_shape, f32), jnp.zeros(experts_shape, f32)
    grad_in_bias = jnp.zeros((experts_here, ff_here), f32)
    grad_back_shard = jnp.zeros((experts_here, shard_width), f32)
    for s in range(owners):
        piece = cross(weight_out[s], s).astype(f32)
        start = (owner_at ^ s) * mine
        two = piece[: 2 * mine * shard_width].reshape(2, mine, shard_width, ff_here)
        grad_w_in = lax.dynamic_update_slice_in_dim(grad_w_in, two[0], start, 0)
        grad_w_back = lax.dynamic_update_slice_in_dim(grad_w_back, two[1], start, 0)
        lines = piece[2 * mine * shard_width :]
        line = jnp.sum(lines[: 2 * mine].reshape(mine, 2, ff_here), axis=1)
        grad_in_bias = lax.dynamic_update_slice_in_dim(grad_in_bias, line, start, 0)
        line = lines[2 * mine : 3 * mine]
        line = line[:, :shard_width] + line[:, ff_here // 2 : ff_here // 2 + shard_width]
        grad_back_shard = lax.dynamic_update_slice_in_dim(grad_back_shard, line, start, 0)
    grad_w_back = grad_w_back.transpose(0, 2, 1)
    early = jnp.concatenate(
        [grad_qkv.astype(bf16), grad_out_turned.astype(bf16), grad_router.astype(bf16)], axis=1
    )
    early = swap(early.reshape(groups, shard_width // sources, -1), (DP, EXPERT))
    early = jnp.sum(early.astype(f32), axis=0)
    early = hop_gather(early, EXPERT).reshape(shard_width, -1)
    grad_w_qkv = early[:, : 3 * local_width].reshape(shard_width, 3, local_width).transpose(1, 0, 2)
    grad_w_out = early[:, 3 * local_width : 4 * local_width].T
    grad_w_router = early[:, 4 * local_width :]
    once = (tensor_at == 0).astype(f32)
    pair_bias = lax.dynamic_update_slice(
        jnp.zeros((2, width), f32), grad_pair_bias, (0, tensor_at * local_width)
    )
    vectors = [grad_bias_out, grad_gain_second, grad_shift_second]
    vectors = jnp.concatenate([first_terms, pair_bias, once * jnp.stack(vectors)], axis=0)
    vectors = lax.psum(vectors, everywhere)
    grad_qv_bias = lax.dynamic_slice_in_dim(vectors[2:4], tensor_at * local_width, local_width, 1)
    vectors = lax.dynamic_slice_in_dim(vectors, dp_at * shard_width, shard_width, 1)
    grad_first_gain, grad_first_shift, _, _, grad_out_bias, grad_second_gain, grad_second_shift = vectors
    return (
        output,
        grad_images,
        grad_first_gain,
        grad_first_shift,
        grad_w_qkv,
        grad_qv_bias,
        grad_w_out,
        grad_out_bias,
        grad_second_gain,
        grad_second_shift,
        grad_w_router,
        grad_w_in,
        grad_in_bias,
        grad_w_back,
        grad_back_shard,
    )


def specs(tensor):
    rows = P((DP, EXPERT), None, None)
    vector, square = P(DP), P(tensor, DP)
    qkv, pair, router = P(None, DP, tensor), P(None, tensor), P(DP, None)
    inward, outward = P(EXPERT, DP, tensor), P(EXPERT, tensor, DP)
    params = (vector, vector, qkv, pair, square, vector, vector, vector, router)
    experts = (inward, P(EXPERT, tensor), outward, P(EXPERT, DP))
    taken = (rows, P((DP, EXPERT)), rows, rows, *params, *experts, rows)
    given = (rows, rows, *params, *experts)
    return taken, given


def solution(mesh):
    data, expert, tensor = (mesh.shape[name] for name in (DP, EXPERT, TENSOR))
    inner = FF_PAIR if tensor % FF_PAIR == 0 else 1
    owners = data * inner
    if (EXPERTS // expert) % owners or owners & (owners - 1):
        taken, given = specs(TENSOR)
        return jax.shard_map(
            gathered_plan, mesh=mesh, in_specs=taken, out_specs=given, check_vma=False
        )
    devices = mesh.devices.reshape(data, expert, tensor // inner, inner)
    split_mesh = Mesh(devices, (DP, EXPERT, OUTER, INNER))
    taken, given = specs((OUTER, INNER))
    return jax.shard_map(
        moved_plan, mesh=split_mesh, in_specs=taken, out_specs=given, check_vma=False
    )
```

```python
import functools
import math

import jax
import jax.numpy as jnp
from jax import lax
from jax.experimental import pallas as pl
from jax.experimental.pallas import tpu as pltpu
from jax.sharding import Mesh
from jax.sharding import PartitionSpec as P

HEAD_DIM = 64
EXPERTS = 32
TOPK = 2
CAP = 64
FF_PAIR = 2
PAIR = 2
EXTRA = 16
VMEM_LIMIT = 56 * 1024 * 1024
GELU_SCALE = (2.0 / math.pi) ** 0.5
GELU_CUBE = 0.044715

DP = "dp"
EXPERT = "expert"
TENSOR = "tensor"
OUTER = "outer"
INNER = "inner"


EPS = 1e-06


def norm_parts(values, norm_gain, norm_shift):
    average = jnp.mean(values, axis=-1, keepdims=True)
    centred = values - average
    spread = jnp.mean(centred * centred, axis=-1, keepdims=True)
    inv_std = lax.rsqrt(spread + EPS)
    scaled = centred * inv_std
    return (scaled * norm_gain + norm_shift, scaled, inv_std)


def norm_back(grad_out, scaled, inv_std, norm_gain):
    grad_scaled = grad_out * norm_gain
    inner = grad_scaled - jnp.mean(grad_scaled, axis=-1, keepdims=True)
    inner = inner - scaled * jnp.mean(grad_scaled * scaled, axis=-1, keepdims=True)
    return (inner * inv_std, jnp.sum(grad_out * scaled, axis=0), jnp.sum(grad_out, axis=0))


def attention_forward(queries, key_rows, value_rows, scale):
    scores = (
        jnp.einsum("iqhd,ikhd->ihqk", queries, key_rows, preferred_element_type=jnp.float32) * scale
    )
    row_peak = jnp.max(scores, axis=-1, keepdims=True)
    log_total = row_peak + jnp.log(jnp.sum(jnp.exp(scores - row_peak), axis=-1, keepdims=True))
    weights = jnp.exp(scores - log_total).astype(jnp.bfloat16)
    attended = jnp.einsum(
        "ihqk,ikhd->iqhd", weights, value_rows, preferred_element_type=jnp.float32
    )
    return (attended, log_total)


def attention_backward(queries, key_rows, value_rows, log_total, grad_low, scale):
    scores = (
        jnp.einsum("iqhd,ikhd->ihqk", queries, key_rows, preferred_element_type=jnp.float32) * scale
    )
    probs = jnp.exp(scores - log_total)
    weights = probs.astype(jnp.bfloat16)
    grad_values = jnp.einsum(
        "ihqk,iqhd->ikhd", weights, grad_low, preferred_element_type=jnp.float32
    )
    grad_weights = jnp.einsum(
        "iqhd,ikhd->ihqk", grad_low, value_rows, preferred_element_type=jnp.float32
    )
    grad_scores = probs * (grad_weights - jnp.sum(probs * grad_weights, axis=-1, keepdims=True))
    scores_low = grad_scores.astype(jnp.bfloat16)
    grad_queries = (
        jnp.einsum("ihqk,ikhd->iqhd", scores_low, key_rows, preferred_element_type=jnp.float32)
        * scale
    )
    grad_keys = (
        jnp.einsum("ihqk,iqhd->ikhd", scores_low, queries, preferred_element_type=jnp.float32)
        * scale
    )
    return (grad_queries, grad_keys, grad_values)


def gathered_plan(
    images,
    images_held,
    routes,
    slot_index,
    first_gain,
    first_shift,
    w_qkv,
    qv_bias,
    w_out,
    out_bias,
    second_gain,
    second_shift,
    w_router,
    w_in,
    in_bias,
    w_back,
    back_bias,
    cotangent,
):
    image_count, seq_len, width = images.shape
    rows_total = image_count * seq_len
    experts_here = w_in.shape[0]
    (
        gain_first,
        shift_first,
        qkv_full,
        out_full,
        bias_out_full,
        gain_second,
        shift_second,
        router_full,
        in_full,
        back_full,
        back_bias_full,
    ) = (
        lax.all_gather(first_gain, DP, axis=0, tiled=True),
        lax.all_gather(first_shift, DP, axis=0, tiled=True),
        lax.all_gather(w_qkv, DP, axis=1, tiled=True),
        lax.all_gather(w_out, DP, axis=1, tiled=True),
        lax.all_gather(out_bias, DP, axis=0, tiled=True),
        lax.all_gather(second_gain, DP, axis=0, tiled=True),
        lax.all_gather(second_shift, DP, axis=0, tiled=True),
        lax.all_gather(w_router, DP, axis=0, tiled=True),
        lax.all_gather(w_in, DP, axis=1, tiled=True),
        lax.all_gather(w_back, DP, axis=2, tiled=True),
        lax.all_gather(back_bias, DP, axis=1, tiled=True),
    )
    gain_first = gain_first.astype(jnp.float32)
    gain_second = gain_second.astype(jnp.float32)
    inputs = images.reshape(rows_total, width).astype(jnp.float32)
    live_image = (jnp.arange(image_count, dtype=jnp.int32) < images_held[0]).astype(jnp.float32)
    live_rows = jnp.repeat(live_image, seq_len)[:, None]
    normed, scaled_first, inv_first = norm_parts(
        inputs, gain_first, shift_first.astype(jnp.float32)
    )
    normed_low = normed.astype(jnp.bfloat16)
    projected = jnp.einsum("td,cde->cte", normed_low, qkv_full, preferred_element_type=jnp.float32)
    local_width = projected.shape[2]
    head_count = local_width // HEAD_DIM
    head_shape = (image_count, seq_len, head_count, HEAD_DIM)
    bias_pair = qv_bias.astype(jnp.float32)
    queries = (projected[0] + bias_pair[0]).astype(jnp.bfloat16).reshape(head_shape)
    key_rows = projected[1].astype(jnp.bfloat16).reshape(head_shape)
    value_rows = (projected[2] + bias_pair[1]).astype(jnp.bfloat16).reshape(head_shape)
    scale = HEAD_DIM ** (-0.5)
    attended, log_total = attention_forward(queries, key_rows, value_rows, scale)
    attended_low = attended.reshape(rows_total, local_width).astype(jnp.bfloat16)
    head_part = jnp.dot(attended_low, out_full, preferred_element_type=jnp.float32)
    mixed = inputs + lax.psum(head_part, TENSOR) + bias_out_full.astype(jnp.float32)
    routed, scaled_second, inv_second = norm_parts(
        mixed, gain_second, shift_second.astype(jnp.float32)
    )
    routed_low = routed.astype(jnp.bfloat16)
    logits = jnp.dot(routed_low, router_full, preferred_element_type=jnp.float32)
    probs = jax.nn.softmax(logits, axis=-1)
    pair_routes = routes.reshape(rows_total, TOPK)
    pair_slots = slot_index.reshape(rows_total, TOPK)
    target = jnp.where(pair_slots < CAP, pair_routes * CAP + pair_slots, EXPERTS * CAP).reshape(
        rows_total * TOPK
    )
    gates = jnp.take_along_axis(probs, pair_routes, axis=1)
    pair_rows = jnp.repeat(routed_low, TOPK, axis=0)
    outgoing = (
        jnp.zeros((EXPERTS * CAP + 1, width), jnp.bfloat16)
        .at[target]
        .set(pair_rows)[: EXPERTS * CAP]
    )
    outgoing = outgoing.reshape(EXPERTS, 1, CAP, width)
    arrived = lax.all_to_all(outgoing, EXPERT, split_axis=0, concat_axis=1, tiled=True)
    sources = arrived.shape[1]
    expert_rows = arrived.reshape(experts_here, sources * CAP, width)
    hidden_pre = jnp.einsum(
        "erd,edf->erf", expert_rows, in_full, preferred_element_type=jnp.float32
    )
    hidden_pre = hidden_pre + in_bias.astype(jnp.float32)[:, None, :]
    hidden_value, gelu_pull = jax.vjp(jax.nn.gelu, hidden_pre)
    hidden_low = hidden_value.astype(jnp.bfloat16)
    expert_part = jnp.einsum(
        "erf,efd->erd", hidden_low, back_full, preferred_element_type=jnp.float32
    )
    bias_back = back_bias_full.astype(jnp.float32)[:, None, :]
    shares = lax.psum_scatter(
        expert_part.reshape(experts_here, sources, CAP, width),
        TENSOR,
        scatter_dimension=2,
        tiled=True,
    )
    share_low = (shares + bias_back[:, None]).astype(jnp.bfloat16)
    pieces = lax.all_to_all(share_low, EXPERT, split_axis=1, concat_axis=0, tiled=True)
    returned = lax.all_gather(pieces, TENSOR, axis=2, tiled=True)
    padded = jnp.concatenate(
        [returned.reshape(EXPERTS * CAP, width), jnp.zeros((1, width), jnp.bfloat16)], axis=0
    )
    picked = padded[target].astype(jnp.float32).reshape(rows_total, TOPK, width)
    expert_mix = jnp.sum(gates[:, :, None] * picked, axis=1)
    output = (live_rows * (mixed + expert_mix)).astype(jnp.bfloat16).reshape(images.shape)
    grad_rows = cotangent.reshape(rows_total, width).astype(jnp.float32) * live_rows
    grad_gates = jnp.sum(grad_rows[:, None, :] * picked, axis=-1)
    grad_picked = (
        (gates[:, :, None] * grad_rows[:, None, :])
        .astype(jnp.bfloat16)
        .reshape(rows_total * TOPK, width)
    )
    grad_outgoing = (
        jnp.zeros((EXPERTS * CAP + 1, width), jnp.bfloat16)
        .at[target]
        .set(grad_picked)[: EXPERTS * CAP]
    )
    grad_outgoing = grad_outgoing.reshape(EXPERTS, 1, CAP, width)
    grad_arrived = lax.all_to_all(grad_outgoing, EXPERT, split_axis=0, concat_axis=1, tiled=True)
    grad_arrived = grad_arrived.reshape(experts_here, sources * CAP, width)
    grad_back_bias = jnp.sum(grad_arrived.astype(jnp.float32), axis=1)
    grad_back_w = jnp.einsum(
        "erf,erd->efd", hidden_low, grad_arrived, preferred_element_type=jnp.float32
    )
    grad_hidden = jnp.einsum(
        "erd,efd->erf", grad_arrived, back_full, preferred_element_type=jnp.float32
    )
    grad_pre = gelu_pull(grad_hidden)[0]
    grad_in_bias_local = jnp.sum(grad_pre, axis=1)
    grad_pre_low = grad_pre.astype(jnp.bfloat16)
    grad_in_w = jnp.einsum(
        "erd,erf->edf", expert_rows, grad_pre_low, preferred_element_type=jnp.float32
    )
    grad_rows_part = jnp.einsum(
        "erf,edf->erd", grad_pre_low, in_full, preferred_element_type=jnp.float32
    )
    grad_shares = lax.psum_scatter(
        grad_rows_part.reshape(experts_here, sources, CAP, width),
        TENSOR,
        scatter_dimension=2,
        tiled=True,
    ).astype(jnp.bfloat16)
    grad_pieces = lax.all_to_all(grad_shares, EXPERT, split_axis=1, concat_axis=0, tiled=True)
    grad_returned = lax.all_gather(grad_pieces, TENSOR, axis=2, tiled=True)
    grad_padded = jnp.concatenate(
        [grad_returned.reshape(EXPERTS * CAP, width), jnp.zeros((1, width), jnp.bfloat16)], axis=0
    )
    grad_routed = jnp.sum(
        grad_padded[target].astype(jnp.float32).reshape(rows_total, TOPK, width), axis=1
    )
    expert_match = (
        pair_routes[:, :, None] == jnp.arange(EXPERTS, dtype=jnp.int32)[None, None, :]
    ).astype(jnp.float32)
    grad_probs = jnp.sum(expert_match * grad_gates[:, :, None], axis=1)
    grad_logits = probs * (grad_probs - jnp.sum(probs * grad_probs, axis=-1, keepdims=True))
    grad_logits_low = grad_logits.astype(jnp.bfloat16)
    grad_router = jnp.einsum(
        "td,te->de", routed_low, grad_logits_low, preferred_element_type=jnp.float32
    )
    grad_routed = grad_routed + jnp.einsum(
        "te,de->td", grad_logits_low, router_full, preferred_element_type=jnp.float32
    )
    grad_from_norm, grad_gain_second, grad_shift_second = norm_back(
        grad_routed, scaled_second, inv_second, gain_second
    )
    grad_mixed = grad_rows + grad_from_norm
    grad_bias_out = jnp.sum(grad_mixed, axis=0)
    grad_mixed_low = grad_mixed.astype(jnp.bfloat16)
    grad_out_w = jnp.einsum(
        "te,td->ed", attended_low, grad_mixed_low, preferred_element_type=jnp.float32
    )
    grad_attended = jnp.einsum(
        "td,ed->te", grad_mixed_low, out_full, preferred_element_type=jnp.float32
    )
    grad_attended = grad_attended.astype(jnp.bfloat16).reshape(head_shape)
    grad_queries, grad_keys, grad_values = attention_backward(
        queries, key_rows, value_rows, log_total, grad_attended, scale
    )
    grad_queries = grad_queries.reshape(rows_total, local_width)
    grad_keys = grad_keys.reshape(rows_total, local_width)
    grad_values = grad_values.reshape(rows_total, local_width)
    grad_pair_bias = jnp.stack([jnp.sum(grad_queries, axis=0), jnp.sum(grad_values, axis=0)])
    grad_proj_low = jnp.stack([grad_queries, grad_keys, grad_values]).astype(jnp.bfloat16)
    grad_qkv = jnp.einsum(
        "td,cte->cde", normed_low, grad_proj_low, preferred_element_type=jnp.float32
    )
    grad_normed_part = jnp.einsum(
        "cte,cde->td", grad_proj_low, qkv_full, preferred_element_type=jnp.float32
    )
    grad_normed = lax.psum(grad_normed_part, TENSOR)
    grad_from_first, grad_gain_first, grad_shift_first = norm_back(
        grad_normed, scaled_first, inv_first, gain_first
    )
    grad_images = (grad_mixed + grad_from_first).reshape(images.shape)
    expert_start = lax.axis_index(EXPERT) * experts_here
    full_in_bias = lax.dynamic_update_slice(
        jnp.zeros((EXPERTS, grad_in_bias_local.shape[1]), jnp.float32),
        grad_in_bias_local,
        (expert_start, jnp.zeros((), jnp.int32)),
    )
    summed = lax.psum(
        (
            grad_gain_first,
            grad_shift_first,
            grad_qkv,
            grad_pair_bias,
            grad_out_w,
            grad_bias_out,
            grad_gain_second,
            grad_shift_second,
            grad_router,
            full_in_bias,
        ),
        (DP, EXPERT),
    )
    shard_width = width // lax.axis_size(DP)
    shard_start = lax.axis_index(DP) * shard_width
    grad_first_gain = lax.dynamic_slice_in_dim(summed[0], shard_start, shard_width, 0)
    grad_first_shift = lax.dynamic_slice_in_dim(summed[1], shard_start, shard_width, 0)
    grad_w_qkv = lax.dynamic_slice_in_dim(summed[2], shard_start, shard_width, 1)
    grad_qv_bias = summed[3]
    grad_w_out = lax.dynamic_slice_in_dim(summed[4], shard_start, shard_width, 1)
    grad_out_bias = lax.dynamic_slice_in_dim(summed[5], shard_start, shard_width, 0)
    grad_second_gain = lax.dynamic_slice_in_dim(summed[6], shard_start, shard_width, 0)
    grad_second_shift = lax.dynamic_slice_in_dim(summed[7], shard_start, shard_width, 0)
    grad_w_router = lax.dynamic_slice_in_dim(summed[8], shard_start, shard_width, 0)
    grad_in_bias = lax.dynamic_slice_in_dim(summed[9], expert_start, experts_here, 0)
    grad_w_in, grad_w_back, grad_back_shard = (
        lax.psum_scatter(grad_in_w, DP, scatter_dimension=1, tiled=True),
        lax.psum_scatter(grad_back_w, DP, scatter_dimension=2, tiled=True),
        lax.psum_scatter(grad_back_bias, DP, scatter_dimension=1, tiled=True),
    )
    return (
        output,
        grad_images,
        grad_first_gain,
        grad_first_shift,
        grad_w_qkv,
        grad_qv_bias,
        grad_w_out,
        grad_out_bias,
        grad_second_gain,
        grad_second_shift,
        grad_w_router,
        grad_w_in,
        grad_in_bias,
        grad_w_back,
        grad_back_shard,
    )


def swap(values, axes):
    return lax.all_to_all(values, axes, split_axis=0, concat_axis=0, tiled=True)


def hop_gather(values, axes):
    count, at = lax.axis_size(axes), lax.axis_index(axes)
    gathered = jnp.zeros((count, *values.shape), values.dtype)
    for s in range(count):
        hop = values
        if s:
            hop = lax.ppermute(values, axes, [(i, (i + s) % count) for i in range(count)])
        gathered = lax.dynamic_update_slice_in_dim(gathered, hop[None], (at - s) % count, 0)
    return gathered


def turned_dot(left, right, left_dim, right_dim):
    return lax.dot_general(
        left, right, (((left_dim,), (right_dim,)), ((), ())), preferred_element_type=jnp.float32
    )


def expert_kernel(
    inner,
    rows_ref,
    gate_ref,
    cot_ref,
    in_ref,
    back_ref,
    in_bias_ref,
    back_bias_ref,
    returned_ref,
    grads_ref,
    hidden_ref,
    grad_pre_ref,
    grad_turned_ref,
    grad_in_bias_ref,
    grad_back_bias_ref,
):
    f32, bf16 = jnp.float32, jnp.bfloat16
    groups, cap, width = rows_ref.shape
    chunks = in_ref.shape[0]
    data = chunks // inner
    tensor, slice_width = returned_ref.shape[1:3]
    mine = back_bias_ref.shape[1]
    total = groups * cap
    at = pl.program_id(0)
    rows = rows_ref[...].reshape(total, width)
    cot_turned = cot_ref[...].reshape(total, width).T.astype(f32)
    pair = gate_ref[:, 0:1, :].astype(f32) + gate_ref[:, 1:2, :].astype(f32)
    pair = pair.reshape(groups, pair.shape[-1])
    gate = jnp.zeros((groups, cap), f32)
    for j in range(mine):
        gate = jnp.where(at == j, pair[:, j * cap : (j + 1) * cap], gate)
    gate = jnp.concatenate([gate[g : g + 1, :] for g in range(groups)], axis=1)
    grad_turned = (cot_turned * gate).astype(bf16)
    grad_turned_ref[0] = grad_turned
    grad_returned = grad_turned.T
    grad_back_bias_ref[0] = jnp.sum(grad_returned.astype(f32), axis=0, keepdims=True)
    bias_columns = back_bias_ref[...]
    bias = jnp.zeros((width, 1), f32)
    for j in range(mine):
        bias = jnp.where(at == j, bias_columns[:, j : j + 1], bias)
    part = jnp.broadcast_to(bias, (width, total))
    back = jnp.zeros((width, total), f32)
    for t in range(inner):
        w_in = jnp.concatenate([in_ref[d * inner + t, 0] for d in range(data)], axis=0)
        w_back = jnp.concatenate([back_ref[d * inner + t, 0] for d in range(data)], axis=0)
        pre = jnp.dot(rows, w_in, preferred_element_type=f32) + in_bias_ref[0, t : t + 1, :]
        square = pre * pre
        bent = jnp.tanh(GELU_SCALE * pre * (1.0 + GELU_CUBE * square))
        half = 0.5 * (1.0 + bent)
        hidden = (pre * half).astype(bf16)
        slope = half + (0.5 * GELU_SCALE) * pre * (1.0 - bent * bent) * (
            1.0 + (3.0 * GELU_CUBE) * square
        )
        hidden_ref[0, t] = hidden
        grad_pre = jnp.dot(grad_returned, w_back, preferred_element_type=f32) * slope
        grad_in_bias_ref[0, t : t + 1, :] = jnp.sum(grad_pre, axis=0, keepdims=True)
        grad_pre = grad_pre.astype(bf16)
        grad_pre_ref[0, t] = grad_pre
        part = part + turned_dot(w_back, hidden, 1, 1)
        back = back + turned_dot(w_in, grad_pre, 1, 1)
    gate_terms = jnp.sum(part * cot_turned, axis=0, keepdims=True)
    high = gate_terms.astype(bf16)
    low = (gate_terms - high.astype(f32)).astype(bf16)
    extra = grads_ref.shape[2] - slice_width
    tail = jnp.concatenate([high, low, jnp.zeros((extra - 2, total), bf16)], axis=0)
    part = part.astype(bf16)
    back = back.astype(bf16)
    for j in range(mine):

        @pl.when(at == j)
        def _():
            lanes = slice(j * cap, (j + 1) * cap)
            for g in range(groups):
                mine_lanes = slice(g * cap, (g + 1) * cap)
                for z in range(tensor):
                    features = slice(z * slice_width, (z + 1) * slice_width)
                    returned_ref[g, z, :, lanes] = part[features, mine_lanes]
                    grads_ref[g, z, :slice_width, lanes] = back[features, mine_lanes]
                    grads_ref[g, z, slice_width:, lanes] = tail[:, mine_lanes]


def run_experts(arrived, cot_rows, in_raw, back_raw, in_bias, back_bias, mine, inner, tensor):
    f32, bf16 = jnp.float32, jnp.bfloat16
    groups, _, width = cot_rows.shape
    chunks, _, depth, ff = in_raw.shape
    total = groups * CAP
    slice_width = width // tensor
    gate_at = mine * CAP // 16
    outs = [
        ((groups, tensor, slice_width, mine * CAP), bf16, lambda j: (0, 0, 0, 0), None),
        ((groups, tensor, slice_width + 16, mine * CAP), bf16, lambda j: (0, 0, 0, 0), None),
        ((mine, inner, total, ff), bf16, lambda j: (j, 0, 0, 0), 1),
        ((mine, inner, total, ff), bf16, lambda j: (j, 0, 0, 0), 1),
        ((mine, width, total), bf16, lambda j: (j, 0, 0), 1),
        ((mine, inner, ff), f32, lambda j: (j, 0, 0), 1),
        ((mine, 1, width), f32, lambda j: (j, 0, 0), 1),
    ]
    return pl.pallas_call(
        functools.partial(expert_kernel, inner),
        grid=(mine,),
        in_specs=[
            pl.BlockSpec((groups, CAP, width), lambda j: (0, j, 0)),
            pl.BlockSpec((groups, 16, mine * CAP), lambda j: (0, gate_at, 0)),
            pl.BlockSpec((groups, CAP, width), lambda j: (0, j, 0)),
            pl.BlockSpec((chunks, 1, depth, ff), lambda j: (0, j, 0, 0)),
            pl.BlockSpec((chunks, 1, depth, ff), lambda j: (0, j, 0, 0)),
            pl.BlockSpec((1, inner, ff), lambda j: (j, 0, 0)),
            pl.BlockSpec((width, mine), lambda j: (0, 0)),
        ],
        out_specs=[
            pl.BlockSpec(shape if lead is None else (lead, *shape[1:]), index)
            for shape, _, index, lead in outs
        ],
        out_shape=[jax.ShapeDtypeStruct(shape, dtype) for shape, dtype, _, _ in outs],
        compiler_params=pltpu.CompilerParams(vmem_limit_bytes=VMEM_LIMIT),
        cost_estimate=pl.CostEstimate(
            flops=8 * mine * total * width * inner * ff,
            bytes_accessed=4 * chunks * mine * depth * ff + 12 * mine * total * inner * ff,
            transcendentals=mine * total * inner * ff,
        ),
    )(arrived, arrived, cot_rows, in_raw, back_raw, in_bias, back_bias)


def weight_kernel(
    rows_ref,
    grad_pre_ref,
    grad_turned_ref,
    hidden_ref,
    in_bias_ref,
    back_bias_ref,
    grad_in_ref,
    grad_back_ref,
):
    f32, bf16 = jnp.float32, jnp.bfloat16
    groups, cap, width = rows_ref.shape
    data, ff = grad_in_ref.shape[0], grad_in_ref.shape[-1]
    depth = width // data
    mine = back_bias_ref.shape[0]
    at = pl.program_id(1)
    rows = rows_ref[...].reshape(groups * cap, width)
    grad_in = turned_dot(rows, grad_pre_ref[0, 0], 0, 0).astype(bf16)
    grad_back = jnp.dot(grad_turned_ref[0], hidden_ref[0, 0], preferred_element_type=f32)
    grad_back = grad_back.astype(bf16)
    for j in range(mine):

        @pl.when(at == j)
        def _():
            for d in range(data):
                block = slice(j * depth, (j + 1) * depth)
                grad_in_ref[d, 0, block] = grad_in[d * depth : (d + 1) * depth]
                grad_back_ref[d, 0, block] = grad_back[d * depth : (d + 1) * depth]

    @pl.when(at == mine - 1)
    def _():
        pairs = []
        for j in range(mine):
            values = in_bias_ref[j, 0]
            high = values.astype(bf16).astype(f32)
            pairs += [high, values - high]
        for d in range(data):
            lines = list(pairs)
            for j in range(mine):
                values = back_bias_ref[j, :, d * depth : (d + 1) * depth]
                high = values.astype(bf16).astype(f32)
                gap = jnp.zeros((1, ff // 2 - depth), f32)
                lines.append(jnp.concatenate([high, gap, values - high, gap], axis=1))
            lines.append(jnp.zeros((EXTRA - len(lines), ff), f32))
            grad_in_ref[d, 0, mine * depth :] = jnp.concatenate(lines, axis=0).astype(bf16)


def weight_grads(arrived, grad_pre, grad_turned, hidden, grad_in_bias, grad_back_bias, data):
    mine, inner, total, ff = hidden.shape
    groups, _, width = arrived.shape
    depth = width // data
    kept = pl.BlockSpec((1, 1, total, ff), lambda t, j: (j, t, 0, 0))
    lines = (mine * depth + EXTRA, mine * depth)
    return pl.pallas_call(
        weight_kernel,
        grid=(inner, mine),
        in_specs=[
            pl.BlockSpec((groups, CAP, width), lambda t, j: (0, j, 0)),
            kept,
            pl.BlockSpec((1, width, total), lambda t, j: (j, 0, 0)),
            kept,
            pl.BlockSpec((mine, 1, 1, ff), lambda t, j: (0, t, 0, 0)),
            pl.BlockSpec((mine, 1, width), lambda t, j: (0, 0, 0)),
        ],
        out_specs=[pl.BlockSpec((data, 1, n, ff), lambda t, j: (0, t, 0, 0)) for n in lines],
        out_shape=[jax.ShapeDtypeStruct((data, inner, n, ff), jnp.bfloat16) for n in lines],
        compiler_params=pltpu.CompilerParams(vmem_limit_bytes=VMEM_LIMIT),
        cost_estimate=pl.CostEstimate(
            flops=4 * mine * total * width * inner * ff,
            bytes_accessed=4 * mine * inner * (total + width) * ff,
            transcendentals=0,
        ),
    )(arrived, grad_pre, grad_turned, hidden, grad_in_bias[:, :, None], grad_back_bias)


def norm_rows(values):
    average = jnp.mean(values, axis=-1, keepdims=True)
    centred = values - average
    spread = jnp.mean(centred * centred, axis=-1, keepdims=True)
    inv_std = lax.rsqrt(spread + EPS)
    return centred * inv_std, inv_std


def norm_rows_back(grad_out, scaled, inv_std, norm_gain):
    grad_scaled = grad_out * norm_gain
    inner = grad_scaled - jnp.mean(grad_scaled, axis=-1, keepdims=True)
    inner = inner - scaled * jnp.mean(grad_scaled * scaled, axis=-1, keepdims=True)
    return inner * inv_std


def call_kernel(kernel, grid, inputs, outputs, scratch=(), flops=0):
    smem = pl.BlockSpec(memory_space=pltpu.SMEM)
    return pl.pallas_call(
        kernel,
        grid=grid,
        in_specs=[smem if b is None else pl.BlockSpec(b, i) for _, b, i in inputs],
        out_specs=[pl.BlockSpec(b, i) for _, _, b, i in outputs],
        out_shape=[jax.ShapeDtypeStruct(shape, dtype) for shape, dtype, _, _ in outputs],
        scratch_shapes=list(scratch),
        compiler_params=pltpu.CompilerParams(vmem_limit_bytes=VMEM_LIMIT),
        cost_estimate=pl.CostEstimate(
            flops=flops,
            bytes_accessed=sum(a.size * a.dtype.itemsize for a, _, _ in inputs),
            transcendentals=0,
        ),
    )(*(a for a, _, _ in inputs))


def whole(array):
    return array, array.shape, lambda p: (0,) * array.ndim


def by_step(array, lead):
    return array, (lead, *array.shape[1:]), lambda p: (p,) + (0,) * (array.ndim - 1)


def attend_kernel(images_ref, packed_ref, vector_ref, bias_ref, attended_ref, proj_ref):
    f32, bf16 = jnp.float32, jnp.bfloat16
    local = bias_ref.shape[1]
    weight = packed_ref[:, : 3 * local]
    for h in range(images_ref.shape[0]):
        scaled, _ = norm_rows(images_ref[h].astype(f32))
        normed = (scaled * vector_ref[0:1] + vector_ref[1:2]).astype(bf16)
        proj = jnp.dot(normed, weight, preferred_element_type=f32)
        queries = (proj[:, :local] + bias_ref[0:1]).astype(bf16)
        keys = proj[:, local : 2 * local].astype(bf16)
        values = (proj[:, 2 * local :] + bias_ref[1:2]).astype(bf16)
        proj_ref[h] = jnp.concatenate([queries, keys, values], axis=1)
        parts = []
        for n in range(0, local, HEAD_DIM):
            head = slice(n, n + HEAD_DIM)
            scores = turned_dot(queries[:, head], keys[:, head], 1, 1) * HEAD_DIM**-0.5
            scores = jnp.exp(scores - jnp.max(scores, axis=-1, keepdims=True))
            weights = scores / jnp.sum(scores, axis=-1, keepdims=True)
            parts.append(
                jnp.dot(weights.astype(bf16), values[:, head], preferred_element_type=f32)
            )
        attended_ref[0, :, h * local : (h + 1) * local] = jnp.concatenate(parts, axis=1).astype(bf16)


def run_attend(images, packed, vectors, qv_bias):
    count, length, width = images.shape
    local = qv_bias.shape[1]
    return call_kernel(
        attend_kernel,
        (count // PAIR,),
        [by_step(images, PAIR), whole(packed), whole(vectors), whole(qv_bias)],
        [
            ((count // PAIR, length, PAIR * local), jnp.bfloat16, (1, length, PAIR * local), lambda p: (p, 0, 0)),
            ((count, length, 3 * local), jnp.bfloat16, (PAIR, length, 3 * local), lambda p: (p, 0, 0)),
        ],
        flops=2 * count * length * local * (3 * width + 4 * length),
    )


def slot_hits(target_row, count):
    return lax.broadcasted_iota(jnp.int32, (count, target_row.shape[1]), 0) == target_row


def send_kernel(rows_ref, target_ref, out_ref, sum_ref):
    f32, bf16 = jnp.float32, jnp.bfloat16
    slots = sum_ref.shape[0]
    at = pl.program_id(0)

    @pl.when(at == 0)
    def _():
        sum_ref[...] = jnp.zeros_like(sum_ref)

    for h in range(rows_ref.shape[0]):
        hits = [slot_hits(target_ref[h, k : k + 1], slots) for k in range(TOPK)]
        fill = jnp.logical_or(hits[0], hits[1]).astype(f32).astype(bf16)
        sum_ref[...] += jnp.dot(fill, rows_ref[h], preferred_element_type=f32)

    @pl.when(at == pl.num_programs(0) - 1)
    def _():
        out_ref[...] = sum_ref[...].astype(bf16).reshape(out_ref.shape)


def run_send(rows, plane_target, groups, slots_plane):
    count, length, width = rows.shape
    out = (groups, slots_plane // groups, width)
    return call_kernel(
        send_kernel,
        (count // PAIR,),
        [by_step(rows, PAIR), by_step(plane_target, PAIR)],
        [(out, jnp.bfloat16, out, lambda p: (0, 0, 0))],
        [pltpu.VMEM((slots_plane, width), jnp.float32)],
        flops=2 * count * length * width * slots_plane,
    )[0]


def route_kernel(
    router_at,
    images_ref,
    attended_ref,
    out_ref,
    packed_ref,
    vector_ref,
    routes_ref,
    target_ref,
    mixed_ref,
    probs_ref,
    sent_ref,
    sum_ref,
    gate_ref,
):
    f32, bf16 = jnp.float32, jnp.bfloat16
    slots = sum_ref.shape[0]
    tensor, local = attended_ref.shape[0], attended_ref.shape[3] // images_ref.shape[0]
    at = pl.program_id(0)

    @pl.when(at == 0)
    def _():
        sum_ref[...] = jnp.zeros_like(sum_ref)
        gate_ref[...] = jnp.zeros_like(gate_ref)

    router = packed_ref[:, router_at : router_at + EXPERTS]
    for h in range(images_ref.shape[0]):
        mixed = images_ref[h].astype(f32) + vector_ref[2:3]
        for z in range(tensor):
            part = attended_ref[z, 0, :, h * local : (h + 1) * local]
            weight = out_ref[z * local : (z + 1) * local]
            mixed = mixed + jnp.dot(part, weight, preferred_element_type=f32)
        mixed_ref[h] = mixed
        scaled, _ = norm_rows(mixed)
        routed = (scaled * vector_ref[3:4] + vector_ref[4:5]).astype(bf16)
        logits = jnp.dot(routed, router, preferred_element_type=f32)
        logits = jnp.exp(logits - jnp.max(logits, axis=-1, keepdims=True))
        probs = logits / jnp.sum(logits, axis=-1, keepdims=True)
        probs_ref[h] = probs
        experts = lax.broadcasted_iota(jnp.int32, probs.shape, 1)
        fill = jnp.zeros((slots, probs.shape[0]), f32)
        for k in range(TOPK):
            match = experts == routes_ref[h, :, k : k + 1]
            gate = jnp.sum(jnp.where(match, probs, 0.0), axis=1, keepdims=True)
            high = gate.astype(bf16)
            low = (gate - high.astype(f32)).astype(bf16)
            pair = jnp.concatenate([high, low, jnp.zeros((gate.shape[0], 6), bf16)], axis=1)
            hit = slot_hits(target_ref[h, k : k + 1], slots).astype(f32)
            fill = fill + hit
            gate_ref[...] += turned_dot(pair, hit.astype(bf16), 0, 1)
        sum_ref[...] += jnp.dot(fill.astype(bf16), routed, preferred_element_type=f32)

    @pl.when(at == pl.num_programs(0) - 1)
    def _():
        groups, lines, width = sent_ref.shape
        here = slots // groups
        for g in range(groups):
            lanes = slice(g * here, (g + 1) * here)
            sent_ref[g, :here] = sum_ref[lanes].astype(bf16)
            gates = jnp.concatenate([gate_ref[:, lanes], jnp.zeros((8, width - here), f32)], axis=1)
            gates = jnp.concatenate([gates, jnp.zeros((lines - here - 8, width), f32)], axis=0)
            sent_ref[g, here:] = gates.astype(bf16)


def run_route(images, attended_all, out_whole, packed, vectors, routes, plane_target, groups, slots_plane, router_at):
    f32, bf16 = jnp.float32, jnp.bfloat16
    count, length, width = images.shape
    tensor = attended_all.shape[0]
    sent = (groups, slots_plane // groups + EXTRA, width)
    return call_kernel(
        functools.partial(route_kernel, router_at),
        (count // PAIR,),
        [
            by_step(images, PAIR),
            (attended_all, (tensor, 1, *attended_all.shape[2:]), lambda p: (0, p, 0, 0)),
            whole(out_whole),
            whole(packed),
            whole(vectors),
            by_step(routes, PAIR),
            by_step(plane_target, PAIR),
        ],
        [
            ((count, length, width), f32, (PAIR, length, width), lambda p: (p, 0, 0)),
            ((count, length, EXPERTS), f32, (PAIR, length, EXPERTS), lambda p: (p, 0, 0)),
            (sent, bf16, sent, lambda p: (0, 0, 0)),
        ],
        [pltpu.VMEM((slots_plane, width), f32), pltpu.VMEM((8, slots_plane), f32)],
        flops=2 * count * length * width * (width + slots_plane),
    )


def slot_blocks(parts_ref, slots_ref, outer, inner):
    here = parts_ref.shape[2]
    for b in range(slots_ref.shape[1] // here):
        first = (b // inner) * outer * inner + b % inner
        total = parts_ref[first].astype(jnp.float32)
        for o in range(1, outer):
            total = total + parts_ref[first + o * inner].astype(jnp.float32)
        slots_ref[:, b * here : (b + 1) * here] = total


def token_hits(target_column, count):
    return lax.broadcasted_iota(jnp.int32, (target_column.shape[0], count), 1) == target_column


def take_grads_kernel(outer, inner, parts_ref, target_ref, rows_ref, gates_ref, slots_ref):
    f32, bf16 = jnp.float32, jnp.bfloat16
    slots = slots_ref.shape[1]
    local = rows_ref.shape[2] // target_ref.shape[0]

    @pl.when(pl.program_id(0) == 0)
    def _():
        slot_blocks(parts_ref, slots_ref, outer, inner)

    grads = slots_ref[:local].astype(bf16)
    gate_terms = slots_ref[local : local + 1] + slots_ref[local + 1 : local + 2]
    for h in range(target_ref.shape[0]):
        hits = [token_hits(target_ref[h, :, k : k + 1], slots) for k in range(TOPK)]
        find = jnp.logical_or(hits[0], hits[1]).astype(f32).astype(bf16)
        rows_ref[0, :, h * local : (h + 1) * local] = turned_dot(find, grads, 1, 1).astype(bf16)
        terms = [
            jnp.sum(jnp.where(hit, gate_terms, 0.0), axis=1, keepdims=True) for hit in hits
        ]
        gates_ref[h] = jnp.concatenate(terms, axis=1)


def run_take_grads(parts, target, local, outer, inner, slots):
    count, length, _ = target.shape
    return call_kernel(
        functools.partial(take_grads_kernel, outer, inner),
        (count // PAIR,),
        [whole(parts), by_step(target, PAIR)],
        [
            ((count // PAIR, length, PAIR * local), jnp.bfloat16, (1, length, PAIR * local), lambda p: (p, 0, 0)),
            ((count, length, TOPK), jnp.float32, (PAIR, length, TOPK), lambda p: (p, 0, 0)),
        ],
        [pltpu.VMEM((parts.shape[1], slots), jnp.float32)],
        flops=2 * count * length * slots * local,
    )


def take_rows_kernel(
    outer, inner, held_ref, parts_ref, target_ref, probs_ref, routes_ref, mixed_ref, out_ref, slots_ref
):
    f32, bf16 = jnp.float32, jnp.bfloat16
    slots = slots_ref.shape[1]
    pair = target_ref.shape[0]
    local = out_ref.shape[2] // pair
    at = pl.program_id(0)

    @pl.when(at == 0)
    def _():
        slot_blocks(parts_ref, slots_ref, outer, inner)

    returned = slots_ref[...].astype(bf16)
    for h in range(pair):
        probs = probs_ref[h]
        experts = lax.broadcasted_iota(jnp.int32, probs.shape, 1)
        rows = mixed_ref[h]
        for k in range(TOPK):
            match = experts == routes_ref[h, :, k : k + 1]
            gate = jnp.sum(jnp.where(match, probs, 0.0), axis=1, keepdims=True)
            find = token_hits(target_ref[h, :, k : k + 1], slots).astype(f32).astype(bf16)
            rows = rows + gate * turned_dot(find, returned, 1, 1)
        live = (at * pair + h < held_ref[0]).astype(f32)
        out_ref[0, :, h * local : (h + 1) * local] = (live * rows).astype(bf16)


def run_take_rows(held, parts, target, probs, routes, mixed_cut, outer, inner, slots):
    count, length, local = mixed_cut.shape
    return call_kernel(
        functools.partial(take_rows_kernel, outer, inner),
        (count // PAIR,),
        [
            (held, None, None),
            whole(parts),
            by_step(target, PAIR),
            by_step(probs, PAIR),
            by_step(routes, PAIR),
            by_step(mixed_cut, PAIR),
        ],
        [((count // PAIR, length, PAIR * local), jnp.bfloat16, (1, length, PAIR * local), lambda p: (p, 0, 0))],
        [pltpu.VMEM((parts.shape[1], slots), jnp.float32)],
        flops=4 * count * length * slots * local,
    )[0]


def pull_kernel(
    router_at,
    held_ref,
    images_ref,
    cot_ref,
    mixed_ref,
    probs_ref,
    routes_ref,
    gates_ref,
    rows_ref,
    attended_ref,
    proj_ref,
    packed_ref,
    vector_ref,
    grad_mixed_ref,
    normed_ref,
    matrix_ref,
    sums_ref,
    matrix_sum_ref,
):
    f32, bf16 = jnp.float32, jnp.bfloat16
    pair = images_ref.shape[0]
    tensor = rows_ref.shape[0]
    local = attended_ref.shape[2] // pair
    width = images_ref.shape[2]
    at = pl.program_id(0)

    @pl.when(at == 0)
    def _():
        sums_ref[...] = jnp.zeros_like(sums_ref)
        matrix_sum_ref[...] = jnp.zeros_like(matrix_sum_ref)

    qkv = packed_ref[:, : 3 * local]
    out_turned = packed_ref[:, 3 * local : 4 * local]
    router = packed_ref[:, router_at : router_at + EXPERTS]
    scale = HEAD_DIM**-0.5
    for h in range(pair):
        lanes = slice(h * local, (h + 1) * local)
        live = (at * pair + h < held_ref[0]).astype(f32)
        cot = cot_ref[h].astype(f32) * live
        scaled, inv_std = norm_rows(mixed_ref[h])
        routed = (scaled * vector_ref[3:4] + vector_ref[4:5]).astype(bf16)
        probs = probs_ref[h]
        experts = lax.broadcasted_iota(jnp.int32, probs.shape, 1)
        grad_probs = jnp.zeros(probs.shape, f32)
        for k in range(TOPK):
            match = experts == routes_ref[h, :, k : k + 1]
            grad_probs = grad_probs + jnp.where(match, gates_ref[h, :, k : k + 1], 0.0)
        grad_logits = probs * (grad_probs - jnp.sum(probs * grad_probs, axis=-1, keepdims=True))
        grad_logits = grad_logits.astype(bf16)
        grad_routed = jnp.concatenate([rows_ref[z, 0, :, lanes] for z in range(tensor)], axis=1)
        grad_routed = grad_routed.astype(f32) + turned_dot(grad_logits, router, 1, 1)
        grad_mixed = cot + norm_rows_back(grad_routed, scaled, inv_std, vector_ref[3:4])
        grad_mixed_ref[h] = grad_mixed
        low = grad_mixed.astype(bf16)
        grad_attended = jnp.dot(low, out_turned, preferred_element_type=f32).astype(bf16)
        proj = proj_ref[h]
        grads = [[], [], []]
        for n in range(0, local, HEAD_DIM):
            queries = proj[:, n : n + HEAD_DIM]
            keys = proj[:, local + n : local + n + HEAD_DIM]
            values = proj[:, 2 * local + n : 2 * local + n + HEAD_DIM]
            grad_head = grad_attended[:, n : n + HEAD_DIM]
            scores = turned_dot(queries, keys, 1, 1) * scale
            scores = jnp.exp(scores - jnp.max(scores, axis=-1, keepdims=True))
            weights = scores / jnp.sum(scores, axis=-1, keepdims=True)
            grads[2].append(turned_dot(weights.astype(bf16), grad_head, 0, 0))
            grad_weights = turned_dot(grad_head, values, 1, 1)
            inner = jnp.sum(weights * grad_weights, axis=-1, keepdims=True)
            grad_scores = (weights * (grad_weights - inner)).astype(bf16)
            grads[0].append(jnp.dot(grad_scores, keys, preferred_element_type=f32) * scale)
            grads[1].append(turned_dot(grad_scores, queries, 0, 0) * scale)
        grad_proj = jnp.concatenate(grads[0] + grads[1] + grads[2], axis=1)
        proj_sum = jnp.sum(grad_proj, axis=0, keepdims=True)
        grad_proj = grad_proj.astype(bf16)
        first, _ = norm_rows(images_ref[h].astype(f32))
        normed = (first * vector_ref[0:1] + vector_ref[1:2]).astype(bf16)
        grad_normed = turned_dot(grad_proj, qkv, 1, 1)
        normed_ref[h] = grad_normed.astype(bf16)
        attended = attended_ref[0, :, lanes]
        matrix = jnp.concatenate(
            [
                turned_dot(normed, grad_proj, 0, 0),
                turned_dot(low, attended, 0, 0),
                turned_dot(routed, grad_logits, 0, 0),
            ],
            axis=1,
        )
        matrix_sum_ref[...] += matrix
        column = lambda values: jnp.sum(values, axis=0, keepdims=True)
        sums_ref[0:1] += column(grad_normed * first)
        sums_ref[1:2] += column(grad_normed)
        sums_ref[2:3] += column(grad_mixed)
        sums_ref[3:4] += column(grad_routed * scaled)
        sums_ref[4:5] += column(grad_routed)
        sums_ref[5:6, : 3 * local] += proj_sum

    @pl.when(at == pl.num_programs(0) - 1)
    def _():
        matrix_ref[...] = matrix_sum_ref[...].astype(bf16)


def run_pull(held, images, cot, mixed, probs, routes, gates, rows_all, attended, proj, packed, vectors, router_at):
    f32, bf16 = jnp.float32, jnp.bfloat16
    count, length, width = images.shape
    tensor = rows_all.shape[0]
    local = proj.shape[2] // 3
    tokens = (count, length, width)
    block = (PAIR, length, width)
    step = lambda p: (p, 0, 0)
    still = lambda p: (0, 0)
    matrix = (width, 4 * local + EXPERTS)
    return call_kernel(
        functools.partial(pull_kernel, router_at),
        (count // PAIR,),
        [
            (held, None, None),
            by_step(images, PAIR),
            by_step(cot, PAIR),
            by_step(mixed, PAIR),
            by_step(probs, PAIR),
            by_step(routes, PAIR),
            by_step(gates, PAIR),
            (rows_all, (tensor, 1, *rows_all.shape[2:]), lambda p: (0, p, 0, 0)),
            by_step(attended, 1),
            by_step(proj, PAIR),
            whole(packed),
            whole(vectors),
        ],
        [
            (tokens, f32, block, step),
            (tokens, bf16, block, step),
            (matrix, bf16, matrix, still),
            ((8, width), f32, (8, width), still),
        ],
        [pltpu.VMEM(matrix, f32)],
        flops=2 * count * length * (width * 12 * local + 14 * length * local),
    )


def last_kernel(images_ref, normed_ref, mixed_ref, vector_ref, out_ref):
    for h in range(images_ref.shape[0]):
        scaled, inv_std = norm_rows(images_ref[h].astype(jnp.float32))
        grad = normed_ref[h].astype(jnp.float32)
        out_ref[h] = mixed_ref[h] + norm_rows_back(grad, scaled, inv_std, vector_ref[0:1])


def run_last(images, grad_normed, grad_mixed, vectors):
    return call_kernel(
        last_kernel,
        (images.shape[0],),
        [by_step(images, 1), by_step(grad_normed, 1), by_step(grad_mixed, 1), whole(vectors)],
        [(images.shape, jnp.float32, (1, *images.shape[1:]), lambda p: (p, 0, 0))],
    )[0]


def moved_plan(
    images,
    images_held,
    routes,
    slot_index,
    first_gain,
    first_shift,
    w_qkv,
    qv_bias,
    w_out,
    out_bias,
    second_gain,
    second_shift,
    w_router,
    w_in,
    in_bias,
    w_back,
    back_bias,
    cotangent,
):
    f32, bf16 = jnp.float32, jnp.bfloat16
    image_count, seq_len, width = images.shape
    experts_here, shard_width, ff_here = w_in.shape
    data, sources = lax.axis_size(DP), lax.axis_size(EXPERT)
    outer, inner = lax.axis_size(OUTER), lax.axis_size(INNER)
    tensor = outer * inner
    tensor_axes = (OUTER, INNER)
    everywhere = (DP, EXPERT, OUTER, INNER)
    groups = data * sources
    owners = data * inner
    mine = experts_here // owners
    slots = EXPERTS * CAP
    dp_at = lax.axis_index(DP)
    inner_at = lax.axis_index(INNER)
    tensor_at = lax.axis_index(tensor_axes)
    owner_at = dp_at * inner + inner_at
    local_width = w_out.shape[0]
    slice_width = width // tensor
    router_at = 4 * local_width

    chunk_shape = (owners, mine, shard_width, ff_here)
    in_raw = swap(w_in, (DP, INNER)).reshape(chunk_shape)
    back_raw = swap(w_back.transpose(0, 2, 1), (DP, INNER)).reshape(chunk_shape)

    packed = jnp.concatenate(
        [
            w_qkv.transpose(1, 0, 2).reshape(shard_width, 3 * local_width),
            w_out.T,
            w_router,
            back_bias.T,
            jnp.stack([first_gain, first_shift, out_bias, second_gain, second_shift], axis=1),
        ],
        axis=1,
    )
    packed = lax.all_gather(packed, DP, axis=0, tiled=True)
    vectors = packed[:, router_at + EXPERTS + experts_here :].T.astype(f32)
    out_whole = hop_gather(w_out, tensor_axes).reshape(width, shard_width)
    out_whole = hop_gather(out_whole, DP).transpose(1, 0, 2).reshape(width, width)
    in_bias_all = hop_gather(in_bias, INNER)
    in_bias_mine = lax.dynamic_slice_in_dim(in_bias_all, owner_at * mine, mine, 1)
    in_bias_mine = in_bias_mine.transpose(1, 0, 2).astype(f32)

    home, within = routes // experts_here, routes % experts_here
    owner, nth = within // mine, within % mine
    kept = slot_index < CAP
    group_place = (owner // inner) * sources + home
    target = ((group_place * inner + owner % inner) * mine + nth) * CAP + slot_index
    target = jnp.where(kept, target, slots)
    plane_target = (group_place * mine + nth) * CAP + slot_index
    plane_target = jnp.where(jnp.logical_and(kept, owner % inner == inner_at), plane_target, -1)
    plane_target = plane_target.transpose(0, 2, 1)
    cot_out = run_send(cotangent, plane_target, groups, slots // inner)
    cot_rows = swap(cot_out, (DP, EXPERT))

    attended, proj = run_attend(images, packed, vectors, qv_bias.astype(f32))
    attended_all = lax.all_gather(attended, tensor_axes)
    attended_all, in_raw = lax.optimization_barrier((attended_all, in_raw))
    mixed, probs, sent = run_route(
        images,
        attended_all,
        out_whole,
        packed,
        vectors,
        routes,
        plane_target,
        groups,
        slots // inner,
        router_at,
    )
    sent, back_raw = lax.optimization_barrier((sent, back_raw))
    arrived = swap(sent, (DP, EXPERT))
    back_bias_mine = lax.dynamic_slice_in_dim(packed, router_at + EXPERTS + owner_at * mine, mine, 1)
    back_bias_mine = jnp.where(lax.axis_index(OUTER) == 0, back_bias_mine.astype(f32), 0.0)
    (
        returned_out,
        grads_out,
        hidden_low,
        grad_pre_low,
        grad_turned,
        grad_in_bias_mine,
        grad_back_bias_mine,
    ) = run_experts(
        arrived, cot_rows, in_raw, back_raw, in_bias_mine, back_bias_mine, mine, inner, tensor
    )

    def bring(parts):
        return swap(parts.reshape(groups * tensor, *parts.shape[2:]), everywhere)

    def spread(parts):
        return swap(parts.reshape(owners, *parts.shape[2:]), (DP, INNER))

    grad_parts = bring(grads_out)
    rows_cut, grad_gates = run_take_grads(grad_parts, target, slice_width, outer, inner, slots)
    rows_all = lax.all_gather(rows_cut, tensor_axes)
    grad_in_out, grad_back_out = weight_grads(
        arrived, grad_pre_low, grad_turned, hidden_low, grad_in_bias_mine, grad_back_bias_mine, data
    )
    rows_cut, grad_in_out = lax.optimization_barrier((rows_cut, grad_in_out))
    grad_in_parts = spread(grad_in_out)
    rows_all, grad_in_parts = lax.optimization_barrier((rows_all, grad_in_parts))
    grad_mixed, normed_part, matrix, sums = run_pull(
        images_held,
        images,
        cotangent,
        mixed,
        probs,
        routes,
        grad_gates,
        rows_all,
        attended,
        proj,
        packed,
        vectors,
        router_at,
    )
    grad_normed = lax.psum(normed_part, tensor_axes)
    grad_images = run_last(images, grad_normed, grad_mixed, vectors)

    normed_part, returned_out = lax.optimization_barrier((normed_part, returned_out))
    returned = bring(returned_out)
    mixed_cut = lax.dynamic_slice_in_dim(mixed, tensor_at * slice_width, slice_width, 2)
    output_cut = run_take_rows(
        images_held, returned, target, probs, routes, mixed_cut, outer, inner, slots
    )
    output = lax.all_gather(output_cut, tensor_axes)
    output = output.reshape(tensor, image_count // PAIR, seq_len, PAIR, slice_width)
    output = output.transpose(1, 3, 2, 0, 4).reshape(images.shape)

    matrix, returned = lax.optimization_barrier((matrix, returned))
    early = swap(matrix.reshape(groups, shard_width // sources, -1), (DP, EXPERT))
    early, grad_back_out = lax.optimization_barrier((early, grad_back_out))
    grad_back_parts = spread(grad_back_out)
    early = jnp.sum(early.astype(f32), axis=0)
    early = hop_gather(early, EXPERT).reshape(shard_width, -1)
    grad_w_qkv = early[:, : 3 * local_width].reshape(shard_width, 3, local_width).transpose(1, 0, 2)
    grad_w_out = early[:, 3 * local_width : 4 * local_width].T
    grad_w_router = early[:, 4 * local_width :]
    experts_shape = (experts_here, shard_width, ff_here)
    grad_w_in = grad_in_parts[:, : mine * shard_width].astype(f32).reshape(experts_shape)
    grad_w_back = grad_back_parts.astype(f32).reshape(experts_shape).transpose(0, 2, 1)
    lines = grad_in_parts[:, mine * shard_width :].astype(f32)
    grad_in_bias = lines[:, : 2 * mine].reshape(owners, mine, 2, ff_here)
    grad_in_bias = jnp.sum(grad_in_bias, axis=2).reshape(experts_here, ff_here)
    lines = lines[:, 2 * mine : 3 * mine].reshape(experts_here, 2, ff_here // 2)
    grad_back_shard = jnp.sum(lines[:, :, :shard_width], axis=1)
    once = (tensor_at == 0).astype(f32)
    pair_bias = jnp.stack([sums[5, :local_width], sums[5, 2 * local_width : 3 * local_width]])
    pair_bias = lax.dynamic_update_slice(
        jnp.zeros((2, width), f32), pair_bias, (0, tensor_at * local_width)
    )
    totals = jnp.concatenate([sums[0:2], pair_bias, once * sums[2:5]], axis=0)
    totals = lax.psum(totals, everywhere)
    grad_qv_bias = lax.dynamic_slice_in_dim(totals[2:4], tensor_at * local_width, local_width, 1)
    totals = lax.dynamic_slice_in_dim(totals, dp_at * shard_width, shard_width, 1)
    return (
        output,
        grad_images,
        totals[0],
        totals[1],
        grad_w_qkv,
        grad_qv_bias,
        grad_w_out,
        totals[4],
        totals[5],
        totals[6],
        grad_w_router,
        grad_w_in,
        grad_in_bias,
        grad_w_back,
        grad_back_shard,
    )


def specs(tensor):
    rows = P((DP, EXPERT), None, None)
    vector, square = P(DP), P(tensor, DP)
    qkv, pair, router = P(None, DP, tensor), P(None, tensor), P(DP, None)
    inward, outward = P(EXPERT, DP, tensor), P(EXPERT, tensor, DP)
    params = (vector, vector, qkv, pair, square, vector, vector, vector, router)
    experts = (inward, P(EXPERT, tensor), outward, P(EXPERT, DP))
    taken = (rows, P((DP, EXPERT)), rows, rows, *params, *experts, rows)
    given = (rows, rows, *params, *experts)
    return taken, given


def solution(mesh):
    data, expert, tensor = (mesh.shape[name] for name in (DP, EXPERT, TENSOR))
    inner = FF_PAIR if tensor % FF_PAIR == 0 else 1
    owners = data * inner
    if (EXPERTS // expert) % owners or owners & (owners - 1):
        taken, given = specs(TENSOR)
        return jax.shard_map(
            gathered_plan, mesh=mesh, in_specs=taken, out_specs=given, check_vma=False
        )
    devices = mesh.devices.reshape(data, expert, tensor // inner, inner)
    split_mesh = Mesh(devices, (DP, EXPERT, OUTER, INNER))
    taken, given = specs((OUTER, INNER))
    return jax.shard_map(
        moved_plan, mesh=split_mesh, in_specs=taken, out_specs=given, check_vma=False
    )
```

```python
import functools
import math

import jax
import jax.numpy as jnp
from jax import lax
from jax.experimental import pallas as pl
from jax.experimental.pallas import tpu as pltpu
from jax.sharding import Mesh
from jax.sharding import PartitionSpec as P

HEAD_DIM = 64
EXPERTS = 32
TOPK = 2
CAP = 64
FF_PAIR = 2
PAIR = 2
EXTRA = 16
VMEM_LIMIT = 56 * 1024 * 1024
GELU_SCALE = (2.0 / math.pi) ** 0.5
GELU_CUBE = 0.044715

DP = "dp"
EXPERT = "expert"
TENSOR = "tensor"
OUTER = "outer"
INNER = "inner"


EPS = 1e-06


def norm_parts(values, norm_gain, norm_shift):
    average = jnp.mean(values, axis=-1, keepdims=True)
    centred = values - average
    spread = jnp.mean(centred * centred, axis=-1, keepdims=True)
    inv_std = lax.rsqrt(spread + EPS)
    scaled = centred * inv_std
    return (scaled * norm_gain + norm_shift, scaled, inv_std)


def norm_back(grad_out, scaled, inv_std, norm_gain):
    grad_scaled = grad_out * norm_gain
    inner = grad_scaled - jnp.mean(grad_scaled, axis=-1, keepdims=True)
    inner = inner - scaled * jnp.mean(grad_scaled * scaled, axis=-1, keepdims=True)
    return (inner * inv_std, jnp.sum(grad_out * scaled, axis=0), jnp.sum(grad_out, axis=0))


def attention_forward(queries, key_rows, value_rows, scale):
    scores = (
        jnp.einsum("iqhd,ikhd->ihqk", queries, key_rows, preferred_element_type=jnp.float32) * scale
    )
    row_peak = jnp.max(scores, axis=-1, keepdims=True)
    log_total = row_peak + jnp.log(jnp.sum(jnp.exp(scores - row_peak), axis=-1, keepdims=True))
    weights = jnp.exp(scores - log_total).astype(jnp.bfloat16)
    attended = jnp.einsum(
        "ihqk,ikhd->iqhd", weights, value_rows, preferred_element_type=jnp.float32
    )
    return (attended, log_total)


def attention_backward(queries, key_rows, value_rows, log_total, grad_low, scale):
    scores = (
        jnp.einsum("iqhd,ikhd->ihqk", queries, key_rows, preferred_element_type=jnp.float32) * scale
    )
    probs = jnp.exp(scores - log_total)
    weights = probs.astype(jnp.bfloat16)
    grad_values = jnp.einsum(
        "ihqk,iqhd->ikhd", weights, grad_low, preferred_element_type=jnp.float32
    )
    grad_weights = jnp.einsum(
        "iqhd,ikhd->ihqk", grad_low, value_rows, preferred_element_type=jnp.float32
    )
    grad_scores = probs * (grad_weights - jnp.sum(probs * grad_weights, axis=-1, keepdims=True))
    scores_low = grad_scores.astype(jnp.bfloat16)
    grad_queries = (
        jnp.einsum("ihqk,ikhd->iqhd", scores_low, key_rows, preferred_element_type=jnp.float32)
        * scale
    )
    grad_keys = (
        jnp.einsum("ihqk,iqhd->ikhd", scores_low, queries, preferred_element_type=jnp.float32)
        * scale
    )
    return (grad_queries, grad_keys, grad_values)


def gathered_plan(
    images,
    images_held,
    routes,
    slot_index,
    first_gain,
    first_shift,
    w_qkv,
    qv_bias,
    w_out,
    out_bias,
    second_gain,
    second_shift,
    w_router,
    w_in,
    in_bias,
    w_back,
    back_bias,
    cotangent,
):
    image_count, seq_len, width = images.shape
    rows_total = image_count * seq_len
    experts_here = w_in.shape[0]
    (
        gain_first,
        shift_first,
        qkv_full,
        out_full,
        bias_out_full,
        gain_second,
        shift_second,
        router_full,
        in_full,
        back_full,
        back_bias_full,
    ) = (
        lax.all_gather(first_gain, DP, axis=0, tiled=True),
        lax.all_gather(first_shift, DP, axis=0, tiled=True),
        lax.all_gather(w_qkv, DP, axis=1, tiled=True),
        lax.all_gather(w_out, DP, axis=1, tiled=True),
        lax.all_gather(out_bias, DP, axis=0, tiled=True),
        lax.all_gather(second_gain, DP, axis=0, tiled=True),
        lax.all_gather(second_shift, DP, axis=0, tiled=True),
        lax.all_gather(w_router, DP, axis=0, tiled=True),
        lax.all_gather(w_in, DP, axis=1, tiled=True),
        lax.all_gather(w_back, DP, axis=2, tiled=True),
        lax.all_gather(back_bias, DP, axis=1, tiled=True),
    )
    gain_first = gain_first.astype(jnp.float32)
    gain_second = gain_second.astype(jnp.float32)
    inputs = images.reshape(rows_total, width).astype(jnp.float32)
    live_image = (jnp.arange(image_count, dtype=jnp.int32) < images_held[0]).astype(jnp.float32)
    live_rows = jnp.repeat(live_image, seq_len)[:, None]
    normed, scaled_first, inv_first = norm_parts(
        inputs, gain_first, shift_first.astype(jnp.float32)
    )
    normed_low = normed.astype(jnp.bfloat16)
    projected = jnp.einsum("td,cde->cte", normed_low, qkv_full, preferred_element_type=jnp.float32)
    local_width = projected.shape[2]
    head_count = local_width // HEAD_DIM
    head_shape = (image_count, seq_len, head_count, HEAD_DIM)
    bias_pair = qv_bias.astype(jnp.float32)
    queries = (projected[0] + bias_pair[0]).astype(jnp.bfloat16).reshape(head_shape)
    key_rows = projected[1].astype(jnp.bfloat16).reshape(head_shape)
    value_rows = (projected[2] + bias_pair[1]).astype(jnp.bfloat16).reshape(head_shape)
    scale = HEAD_DIM ** (-0.5)
    attended, log_total = attention_forward(queries, key_rows, value_rows, scale)
    attended_low = attended.reshape(rows_total, local_width).astype(jnp.bfloat16)
    head_part = jnp.dot(attended_low, out_full, preferred_element_type=jnp.float32)
    mixed = inputs + lax.psum(head_part, TENSOR) + bias_out_full.astype(jnp.float32)
    routed, scaled_second, inv_second = norm_parts(
        mixed, gain_second, shift_second.astype(jnp.float32)
    )
    routed_low = routed.astype(jnp.bfloat16)
    logits = jnp.dot(routed_low, router_full, preferred_element_type=jnp.float32)
    probs = jax.nn.softmax(logits, axis=-1)
    pair_routes = routes.reshape(rows_total, TOPK)
    pair_slots = slot_index.reshape(rows_total, TOPK)
    target = jnp.where(pair_slots < CAP, pair_routes * CAP + pair_slots, EXPERTS * CAP).reshape(
        rows_total * TOPK
    )
    gates = jnp.take_along_axis(probs, pair_routes, axis=1)
    pair_rows = jnp.repeat(routed_low, TOPK, axis=0)
    outgoing = (
        jnp.zeros((EXPERTS * CAP + 1, width), jnp.bfloat16)
        .at[target]
        .set(pair_rows)[: EXPERTS * CAP]
    )
    outgoing = outgoing.reshape(EXPERTS, 1, CAP, width)
    arrived = lax.all_to_all(outgoing, EXPERT, split_axis=0, concat_axis=1, tiled=True)
    sources = arrived.shape[1]
    expert_rows = arrived.reshape(experts_here, sources * CAP, width)
    hidden_pre = jnp.einsum(
        "erd,edf->erf", expert_rows, in_full, preferred_element_type=jnp.float32
    )
    hidden_pre = hidden_pre + in_bias.astype(jnp.float32)[:, None, :]
    hidden_value, gelu_pull = jax.vjp(jax.nn.gelu, hidden_pre)
    hidden_low = hidden_value.astype(jnp.bfloat16)
    expert_part = jnp.einsum(
        "erf,efd->erd", hidden_low, back_full, preferred_element_type=jnp.float32
    )
    bias_back = back_bias_full.astype(jnp.float32)[:, None, :]
    shares = lax.psum_scatter(
        expert_part.reshape(experts_here, sources, CAP, width),
        TENSOR,
        scatter_dimension=2,
        tiled=True,
    )
    share_low = (shares + bias_back[:, None]).astype(jnp.bfloat16)
    pieces = lax.all_to_all(share_low, EXPERT, split_axis=1, concat_axis=0, tiled=True)
    returned = lax.all_gather(pieces, TENSOR, axis=2, tiled=True)
    padded = jnp.concatenate(
        [returned.reshape(EXPERTS * CAP, width), jnp.zeros((1, width), jnp.bfloat16)], axis=0
    )
    picked = padded[target].astype(jnp.float32).reshape(rows_total, TOPK, width)
    expert_mix = jnp.sum(gates[:, :, None] * picked, axis=1)
    output = (live_rows * (mixed + expert_mix)).astype(jnp.bfloat16).reshape(images.shape)
    grad_rows = cotangent.reshape(rows_total, width).astype(jnp.float32) * live_rows
    grad_gates = jnp.sum(grad_rows[:, None, :] * picked, axis=-1)
    grad_picked = (
        (gates[:, :, None] * grad_rows[:, None, :])
        .astype(jnp.bfloat16)
        .reshape(rows_total * TOPK, width)
    )
    grad_outgoing = (
        jnp.zeros((EXPERTS * CAP + 1, width), jnp.bfloat16)
        .at[target]
        .set(grad_picked)[: EXPERTS * CAP]
    )
    grad_outgoing = grad_outgoing.reshape(EXPERTS, 1, CAP, width)
    grad_arrived = lax.all_to_all(grad_outgoing, EXPERT, split_axis=0, concat_axis=1, tiled=True)
    grad_arrived = grad_arrived.reshape(experts_here, sources * CAP, width)
    grad_back_bias = jnp.sum(grad_arrived.astype(jnp.float32), axis=1)
    grad_back_w = jnp.einsum(
        "erf,erd->efd", hidden_low, grad_arrived, preferred_element_type=jnp.float32
    )
    grad_hidden = jnp.einsum(
        "erd,efd->erf", grad_arrived, back_full, preferred_element_type=jnp.float32
    )
    grad_pre = gelu_pull(grad_hidden)[0]
    grad_in_bias_local = jnp.sum(grad_pre, axis=1)
    grad_pre_low = grad_pre.astype(jnp.bfloat16)
    grad_in_w = jnp.einsum(
        "erd,erf->edf", expert_rows, grad_pre_low, preferred_element_type=jnp.float32
    )
    grad_rows_part = jnp.einsum(
        "erf,edf->erd", grad_pre_low, in_full, preferred_element_type=jnp.float32
    )
    grad_shares = lax.psum_scatter(
        grad_rows_part.reshape(experts_here, sources, CAP, width),
        TENSOR,
        scatter_dimension=2,
        tiled=True,
    ).astype(jnp.bfloat16)
    grad_pieces = lax.all_to_all(grad_shares, EXPERT, split_axis=1, concat_axis=0, tiled=True)
    grad_returned = lax.all_gather(grad_pieces, TENSOR, axis=2, tiled=True)
    grad_padded = jnp.concatenate(
        [grad_returned.reshape(EXPERTS * CAP, width), jnp.zeros((1, width), jnp.bfloat16)], axis=0
    )
    grad_routed = jnp.sum(
        grad_padded[target].astype(jnp.float32).reshape(rows_total, TOPK, width), axis=1
    )
    expert_match = (
        pair_routes[:, :, None] == jnp.arange(EXPERTS, dtype=jnp.int32)[None, None, :]
    ).astype(jnp.float32)
    grad_probs = jnp.sum(expert_match * grad_gates[:, :, None], axis=1)
    grad_logits = probs * (grad_probs - jnp.sum(probs * grad_probs, axis=-1, keepdims=True))
    grad_logits_low = grad_logits.astype(jnp.bfloat16)
    grad_router = jnp.einsum(
        "td,te->de", routed_low, grad_logits_low, preferred_element_type=jnp.float32
    )
    grad_routed = grad_routed + jnp.einsum(
        "te,de->td", grad_logits_low, router_full, preferred_element_type=jnp.float32
    )
    grad_from_norm, grad_gain_second, grad_shift_second = norm_back(
        grad_routed, scaled_second, inv_second, gain_second
    )
    grad_mixed = grad_rows + grad_from_norm
    grad_bias_out = jnp.sum(grad_mixed, axis=0)
    grad_mixed_low = grad_mixed.astype(jnp.bfloat16)
    grad_out_w = jnp.einsum(
        "te,td->ed", attended_low, grad_mixed_low, preferred_element_type=jnp.float32
    )
    grad_attended = jnp.einsum(
        "td,ed->te", grad_mixed_low, out_full, preferred_element_type=jnp.float32
    )
    grad_attended = grad_attended.astype(jnp.bfloat16).reshape(head_shape)
    grad_queries, grad_keys, grad_values = attention_backward(
        queries, key_rows, value_rows, log_total, grad_attended, scale
    )
    grad_queries = grad_queries.reshape(rows_total, local_width)
    grad_keys = grad_keys.reshape(rows_total, local_width)
    grad_values = grad_values.reshape(rows_total, local_width)
    grad_pair_bias = jnp.stack([jnp.sum(grad_queries, axis=0), jnp.sum(grad_values, axis=0)])
    grad_proj_low = jnp.stack([grad_queries, grad_keys, grad_values]).astype(jnp.bfloat16)
    grad_qkv = jnp.einsum(
        "td,cte->cde", normed_low, grad_proj_low, preferred_element_type=jnp.float32
    )
    grad_normed_part = jnp.einsum(
        "cte,cde->td", grad_proj_low, qkv_full, preferred_element_type=jnp.float32
    )
    grad_normed = lax.psum(grad_normed_part, TENSOR)
    grad_from_first, grad_gain_first, grad_shift_first = norm_back(
        grad_normed, scaled_first, inv_first, gain_first
    )
    grad_images = (grad_mixed + grad_from_first).reshape(images.shape)
    expert_start = lax.axis_index(EXPERT) * experts_here
    full_in_bias = lax.dynamic_update_slice(
        jnp.zeros((EXPERTS, grad_in_bias_local.shape[1]), jnp.float32),
        grad_in_bias_local,
        (expert_start, jnp.zeros((), jnp.int32)),
    )
    summed = lax.psum(
        (
            grad_gain_first,
            grad_shift_first,
            grad_qkv,
            grad_pair_bias,
            grad_out_w,
            grad_bias_out,
            grad_gain_second,
            grad_shift_second,
            grad_router,
            full_in_bias,
        ),
        (DP, EXPERT),
    )
    shard_width = width // lax.axis_size(DP)
    shard_start = lax.axis_index(DP) * shard_width
    grad_first_gain = lax.dynamic_slice_in_dim(summed[0], shard_start, shard_width, 0)
    grad_first_shift = lax.dynamic_slice_in_dim(summed[1], shard_start, shard_width, 0)
    grad_w_qkv = lax.dynamic_slice_in_dim(summed[2], shard_start, shard_width, 1)
    grad_qv_bias = summed[3]
    grad_w_out = lax.dynamic_slice_in_dim(summed[4], shard_start, shard_width, 1)
    grad_out_bias = lax.dynamic_slice_in_dim(summed[5], shard_start, shard_width, 0)
    grad_second_gain = lax.dynamic_slice_in_dim(summed[6], shard_start, shard_width, 0)
    grad_second_shift = lax.dynamic_slice_in_dim(summed[7], shard_start, shard_width, 0)
    grad_w_router = lax.dynamic_slice_in_dim(summed[8], shard_start, shard_width, 0)
    grad_in_bias = lax.dynamic_slice_in_dim(summed[9], expert_start, experts_here, 0)
    grad_w_in, grad_w_back, grad_back_shard = (
        lax.psum_scatter(grad_in_w, DP, scatter_dimension=1, tiled=True),
        lax.psum_scatter(grad_back_w, DP, scatter_dimension=2, tiled=True),
        lax.psum_scatter(grad_back_bias, DP, scatter_dimension=1, tiled=True),
    )
    return (
        output,
        grad_images,
        grad_first_gain,
        grad_first_shift,
        grad_w_qkv,
        grad_qv_bias,
        grad_w_out,
        grad_out_bias,
        grad_second_gain,
        grad_second_shift,
        grad_w_router,
        grad_w_in,
        grad_in_bias,
        grad_w_back,
        grad_back_shard,
    )


def swap(values, axes):
    return lax.all_to_all(values, axes, split_axis=0, concat_axis=0, tiled=True)


def hop_gather(values, axes):
    count, at = lax.axis_size(axes), lax.axis_index(axes)
    hops = [values]
    for s in range(1, count):
        hops.append(lax.ppermute(values, axes, [(i, i ^ s) for i in range(count)]))
    gathered = []
    for i in range(count):
        found = hops[0]
        for s in range(1, count):
            found = jnp.where(at ^ i == s, hops[s], found)
        gathered.append(found)
    return gathered


def high_low(values):
    high = lax.reduce_precision(values, 8, 7)
    return high.astype(jnp.bfloat16), (values - high).astype(jnp.bfloat16)


def turned_dot(left, right, left_dim, right_dim):
    return lax.dot_general(
        left, right, (((left_dim,), (right_dim,)), ((), ())), preferred_element_type=jnp.float32
    )


def expert_kernel(
    inner,
    rows_ref,
    gate_ref,
    cot_ref,
    in_ref,
    back_ref,
    in_bias_ref,
    back_bias_ref,
    returned_ref,
    grads_ref,
    hidden_ref,
    grad_pre_ref,
    grad_turned_ref,
    grad_in_bias_ref,
    grad_back_bias_ref,
):
    f32, bf16 = jnp.float32, jnp.bfloat16
    groups, cap, width = rows_ref.shape
    chunks = in_ref.shape[0]
    data = chunks // inner
    tensor, slice_width = returned_ref.shape[1:3]
    mine = back_bias_ref.shape[1]
    total = groups * cap
    at = pl.program_id(0)
    rows = rows_ref[...].reshape(total, width)
    cot_turned = cot_ref[...].reshape(total, width).T.astype(f32)
    pair = gate_ref[:, 0:1, :].astype(f32) + gate_ref[:, 1:2, :].astype(f32)
    pair = pair.reshape(groups, pair.shape[-1])
    gate = jnp.zeros((groups, cap), f32)
    for j in range(mine):
        gate = jnp.where(at == j, pair[:, j * cap : (j + 1) * cap], gate)
    gate = jnp.concatenate([gate[g : g + 1, :] for g in range(groups)], axis=1)
    grad_turned = (cot_turned * gate).astype(bf16)
    grad_turned_ref[0] = grad_turned
    grad_returned = grad_turned.T
    grad_back_bias_ref[0] = jnp.sum(grad_returned.astype(f32), axis=0, keepdims=True)
    bias_columns = back_bias_ref[...]
    bias = jnp.zeros((width, 1), f32)
    for j in range(mine):
        bias = jnp.where(at == j, bias_columns[:, j : j + 1], bias)
    part = jnp.broadcast_to(bias, (width, total))
    back = jnp.zeros((width, total), f32)
    for t in range(inner):
        w_in = jnp.concatenate([in_ref[d * inner + t, 0] for d in range(data)], axis=0)
        w_back = jnp.concatenate([back_ref[d * inner + t, 0] for d in range(data)], axis=0)
        pre = jnp.dot(rows, w_in, preferred_element_type=f32) + in_bias_ref[0, t : t + 1, :]
        square = pre * pre
        bent = jnp.tanh(GELU_SCALE * pre * (1.0 + GELU_CUBE * square))
        half = 0.5 * (1.0 + bent)
        hidden = (pre * half).astype(bf16)
        slope = half + (0.5 * GELU_SCALE) * pre * (1.0 - bent * bent) * (
            1.0 + (3.0 * GELU_CUBE) * square
        )
        hidden_ref[0, t] = hidden
        grad_pre = jnp.dot(grad_returned, w_back, preferred_element_type=f32) * slope
        grad_in_bias_ref[0, t : t + 1, :] = jnp.sum(grad_pre, axis=0, keepdims=True)
        grad_pre = grad_pre.astype(bf16)
        grad_pre_ref[0, t] = grad_pre
        part = part + turned_dot(w_back, hidden, 1, 1)
        back = back + turned_dot(w_in, grad_pre, 1, 1)
    gate_terms = jnp.sum(part * cot_turned, axis=0, keepdims=True)
    high = gate_terms.astype(bf16)
    low = (gate_terms - high.astype(f32)).astype(bf16)
    extra = grads_ref.shape[2] - slice_width
    tail = jnp.concatenate([high, low, jnp.zeros((extra - 2, total), bf16)], axis=0)
    part = part.astype(bf16)
    back = back.astype(bf16)
    for j in range(mine):

        @pl.when(at == j)
        def _():
            lanes = slice(j * cap, (j + 1) * cap)
            for g in range(groups):
                mine_lanes = slice(g * cap, (g + 1) * cap)
                for z in range(tensor):
                    features = slice(z * slice_width, (z + 1) * slice_width)
                    returned_ref[g, z, :, lanes] = part[features, mine_lanes]
                    grads_ref[g, z, :slice_width, lanes] = back[features, mine_lanes]
                    grads_ref[g, z, slice_width:, lanes] = tail[:, mine_lanes]


def run_experts(arrived, in_raw, back_raw, in_bias, back_bias, inner, tensor):
    f32, bf16 = jnp.float32, jnp.bfloat16
    groups, _, width = arrived.shape
    chunks, mine, depth, ff = in_raw.shape
    total = groups * CAP
    slice_width = width // tensor
    gate_at = 2 * mine * CAP // EXTRA
    outs = [
        ((groups, tensor, slice_width, mine * CAP), bf16, lambda j: (0, 0, 0, 0), None),
        ((groups, tensor, slice_width + EXTRA, mine * CAP), bf16, lambda j: (0, 0, 0, 0), None),
        ((mine, inner, total, ff), bf16, lambda j: (j, 0, 0, 0), 1),
        ((mine, inner, total, ff), bf16, lambda j: (j, 0, 0, 0), 1),
        ((mine, width, total), bf16, lambda j: (j, 0, 0), 1),
        ((mine, inner, ff), f32, lambda j: (j, 0, 0), 1),
        ((mine, 1, width), f32, lambda j: (j, 0, 0), 1),
    ]
    return pl.pallas_call(
        functools.partial(expert_kernel, inner),
        grid=(mine,),
        in_specs=[
            pl.BlockSpec((groups, CAP, width), lambda j: (0, j, 0)),
            pl.BlockSpec((groups, EXTRA, mine * CAP), lambda j: (0, gate_at, 0)),
            pl.BlockSpec((groups, CAP, width), lambda j: (0, mine + j, 0)),
            pl.BlockSpec((chunks, 1, depth, ff), lambda j: (0, j, 0, 0)),
            pl.BlockSpec((chunks, 1, depth, ff), lambda j: (0, j, 0, 0)),
            pl.BlockSpec((1, inner, ff), lambda j: (j, 0, 0)),
            pl.BlockSpec((width, mine), lambda j: (0, 0)),
        ],
        out_specs=[
            pl.BlockSpec(shape if lead is None else (lead, *shape[1:]), index)
            for shape, _, index, lead in outs
        ],
        out_shape=[jax.ShapeDtypeStruct(shape, dtype) for shape, dtype, _, _ in outs],
        compiler_params=pltpu.CompilerParams(vmem_limit_bytes=VMEM_LIMIT),
        cost_estimate=pl.CostEstimate(
            flops=8 * mine * total * width * inner * ff,
            bytes_accessed=4 * chunks * mine * depth * ff + 12 * mine * total * inner * ff,
            transcendentals=mine * total * inner * ff,
        ),
    )(arrived, arrived, arrived, in_raw, back_raw, in_bias, back_bias)


def weight_kernel(
    rows_ref,
    grad_pre_ref,
    grad_turned_ref,
    hidden_ref,
    in_bias_ref,
    back_bias_ref,
    out_ref,
):
    f32, bf16 = jnp.float32, jnp.bfloat16
    groups, cap, width = rows_ref.shape
    data, ff = out_ref.shape[0], out_ref.shape[-1]
    depth = width // data
    mine = back_bias_ref.shape[0]
    at = pl.program_id(1)
    rows = rows_ref[...].reshape(groups * cap, width)
    grad_in = turned_dot(rows, grad_pre_ref[0, 0], 0, 0).astype(bf16)
    grad_back = jnp.dot(grad_turned_ref[0], hidden_ref[0, 0], preferred_element_type=f32)
    grad_back = grad_back.astype(bf16)
    for j in range(mine):

        @pl.when(at == j)
        def _():
            for d in range(data):
                lines = slice(d * depth, (d + 1) * depth)
                out_ref[d, 0, j * depth : (j + 1) * depth] = grad_in[lines]
                out_ref[d, 0, (mine + j) * depth : (mine + j + 1) * depth] = grad_back[lines]

    @pl.when(at == mine - 1)
    def _():
        pairs = []
        for j in range(mine):
            values = in_bias_ref[j, 0]
            high = values.astype(bf16).astype(f32)
            pairs += [high, values - high]
        for d in range(data):
            lines = list(pairs)
            for j in range(mine):
                values = back_bias_ref[j, :, d * depth : (d + 1) * depth]
                high = values.astype(bf16).astype(f32)
                gap = jnp.zeros((1, ff // 2 - depth), f32)
                lines.append(jnp.concatenate([high, gap, values - high, gap], axis=1))
            lines.append(jnp.zeros((EXTRA - len(lines), ff), f32))
            out_ref[d, 0, 2 * mine * depth :] = jnp.concatenate(lines, axis=0).astype(bf16)


def weight_grads(arrived, grad_pre, grad_turned, hidden, grad_in_bias, grad_back_bias, data):
    mine, inner, total, ff = hidden.shape
    groups, _, width = arrived.shape
    depth = width // data
    kept = pl.BlockSpec((1, 1, total, ff), lambda t, j: (j, t, 0, 0))
    out = (data, inner, 2 * mine * depth + EXTRA, ff)
    return pl.pallas_call(
        weight_kernel,
        grid=(inner, mine),
        in_specs=[
            pl.BlockSpec((groups, CAP, width), lambda t, j: (0, j, 0)),
            kept,
            pl.BlockSpec((1, width, total), lambda t, j: (j, 0, 0)),
            kept,
            pl.BlockSpec((mine, 1, 1, ff), lambda t, j: (0, t, 0, 0)),
            pl.BlockSpec((mine, 1, width), lambda t, j: (0, 0, 0)),
        ],
        out_specs=pl.BlockSpec((data, 1, *out[2:]), lambda t, j: (0, t, 0, 0)),
        out_shape=jax.ShapeDtypeStruct(out, jnp.bfloat16),
        compiler_params=pltpu.CompilerParams(vmem_limit_bytes=VMEM_LIMIT),
        cost_estimate=pl.CostEstimate(
            flops=4 * mine * total * width * inner * ff,
            bytes_accessed=4 * mine * inner * (total + width) * ff,
            transcendentals=0,
        ),
    )(arrived, grad_pre, grad_turned, hidden, grad_in_bias[:, :, None], grad_back_bias)


def widen_kernel(parts_ref, in_ref, back_ref):
    mine, depth, ff = in_ref.shape
    rows = mine * depth
    in_ref[...] = parts_ref[0, :rows].astype(jnp.float32).reshape(mine, depth, ff)
    back_ref[...] = parts_ref[0, rows : 2 * rows].astype(jnp.float32).reshape(mine, depth, ff)


def run_widen(parts, mine, depth):
    owners, _, ff = parts.shape
    out = ((owners * mine, depth, ff), jnp.float32, (mine, depth, ff), lambda p: (p, 0, 0))
    return call_kernel(widen_kernel, (owners,), [by_step(parts, 1)], [out, out])


def norm_rows(values):
    average = jnp.mean(values, axis=-1, keepdims=True)
    centred = values - average
    spread = jnp.mean(centred * centred, axis=-1, keepdims=True)
    inv_std = lax.rsqrt(spread + EPS)
    return centred * inv_std, inv_std


def norm_rows_back(grad_out, scaled, inv_std, norm_gain):
    grad_scaled = grad_out * norm_gain
    inner = grad_scaled - jnp.mean(grad_scaled, axis=-1, keepdims=True)
    inner = inner - scaled * jnp.mean(grad_scaled * scaled, axis=-1, keepdims=True)
    return inner * inv_std


def call_kernel(kernel, grid, inputs, outputs, scratch=(), flops=0):
    smem = pl.BlockSpec(memory_space=pltpu.SMEM)
    return pl.pallas_call(
        kernel,
        grid=grid,
        in_specs=[smem if b is None else pl.BlockSpec(b, i) for _, b, i in inputs],
        out_specs=[pl.BlockSpec(b, i) for _, _, b, i in outputs],
        out_shape=[jax.ShapeDtypeStruct(shape, dtype) for shape, dtype, _, _ in outputs],
        scratch_shapes=list(scratch),
        compiler_params=pltpu.CompilerParams(vmem_limit_bytes=VMEM_LIMIT),
        cost_estimate=pl.CostEstimate(
            flops=flops,
            bytes_accessed=sum(a.size * a.dtype.itemsize for a, _, _ in inputs),
            transcendentals=0,
        ),
    )(*(a for a, _, _ in inputs))


def whole(array):
    return array, array.shape, lambda p: (0,) * array.ndim


def by_step(array, lead):
    return array, (lead, *array.shape[1:]), lambda p: (p,) + (0,) * (array.ndim - 1)


def attend_kernel(images_ref, packed_ref, vector_ref, bias_ref, attended_ref, proj_ref):
    f32, bf16 = jnp.float32, jnp.bfloat16
    local = bias_ref.shape[1]
    weight = packed_ref[:, : 3 * local]
    for h in range(images_ref.shape[0]):
        scaled, _ = norm_rows(images_ref[h].astype(f32))
        normed = (scaled * vector_ref[0:1] + vector_ref[1:2]).astype(bf16)
        proj = jnp.dot(normed, weight, preferred_element_type=f32)
        queries = (proj[:, :local] + bias_ref[0:1]).astype(bf16)
        keys = proj[:, local : 2 * local].astype(bf16)
        values = (proj[:, 2 * local :] + bias_ref[1:2]).astype(bf16)
        proj_ref[h] = jnp.concatenate([queries, keys, values], axis=1)
        parts = []
        for n in range(0, local, HEAD_DIM):
            head = slice(n, n + HEAD_DIM)
            scores = turned_dot(queries[:, head], keys[:, head], 1, 1) * HEAD_DIM**-0.5
            scores = jnp.exp(scores - jnp.max(scores, axis=-1, keepdims=True))
            weights = scores / jnp.sum(scores, axis=-1, keepdims=True)
            parts.append(
                jnp.dot(weights.astype(bf16), values[:, head], preferred_element_type=f32)
            )
        attended_ref[0, :, h * local : (h + 1) * local] = jnp.concatenate(parts, axis=1).astype(bf16)


def run_attend(images, packed, vectors, qv_bias):
    count, length, width = images.shape
    local = qv_bias.shape[1]
    return call_kernel(
        attend_kernel,
        (count // PAIR,),
        [by_step(images, PAIR), whole(packed), whole(vectors), whole(qv_bias)],
        [
            ((count // PAIR, length, PAIR * local), jnp.bfloat16, (1, length, PAIR * local), lambda p: (p, 0, 0)),
            ((count, length, 3 * local), jnp.bfloat16, (PAIR, length, 3 * local), lambda p: (p, 0, 0)),
        ],
        flops=2 * count * length * local * (3 * width + 4 * length),
    )


def slot_hits(target_row, count):
    return lax.broadcasted_iota(jnp.int32, (count, target_row.shape[1]), 0) == target_row


def route_kernel(
    router_at,
    images_ref,
    cot_ref,
    attended_ref,
    out_ref,
    packed_ref,
    vector_ref,
    routes_ref,
    target_ref,
    mixed_ref,
    probs_ref,
    sent_ref,
    sum_ref,
    gate_ref,
):
    f32, bf16 = jnp.float32, jnp.bfloat16
    slots = sum_ref.shape[1]
    tensor, local = attended_ref.shape[0], attended_ref.shape[3] // images_ref.shape[0]
    at = pl.program_id(0)

    @pl.when(at == 0)
    def _():
        sum_ref[...] = jnp.zeros_like(sum_ref)
        gate_ref[...] = jnp.zeros_like(gate_ref)

    router = packed_ref[:, router_at : router_at + EXPERTS]
    for h in range(images_ref.shape[0]):
        mixed = images_ref[h].astype(f32) + vector_ref[2:3]
        for z in range(tensor):
            part = attended_ref[z, 0, :, h * local : (h + 1) * local]
            weight = out_ref[z * local : (z + 1) * local]
            mixed = mixed + jnp.dot(part, weight, preferred_element_type=f32)
        mixed_ref[h] = mixed
        scaled, _ = norm_rows(mixed)
        routed = (scaled * vector_ref[3:4] + vector_ref[4:5]).astype(bf16)
        logits = jnp.dot(routed, router, preferred_element_type=f32)
        logits = jnp.exp(logits - jnp.max(logits, axis=-1, keepdims=True))
        probs = logits / jnp.sum(logits, axis=-1, keepdims=True)
        probs_ref[h] = probs
        experts = lax.broadcasted_iota(jnp.int32, probs.shape, 1)
        fill = jnp.zeros((slots, probs.shape[0]), f32)
        for k in range(TOPK):
            match = experts == routes_ref[h, :, k : k + 1]
            gate = jnp.sum(jnp.where(match, probs, 0.0), axis=1, keepdims=True)
            high = gate.astype(bf16)
            low = (gate - high.astype(f32)).astype(bf16)
            pair = jnp.concatenate([high, low, jnp.zeros((gate.shape[0], 6), bf16)], axis=1)
            hit = slot_hits(target_ref[h, k : k + 1], slots).astype(f32)
            fill = fill + hit
            gate_ref[...] += turned_dot(pair, hit.astype(bf16), 0, 1)
        fill = fill.astype(bf16)
        sum_ref[0] += jnp.dot(fill, routed, preferred_element_type=f32)
        sum_ref[1] += jnp.dot(fill, cot_ref[h], preferred_element_type=f32)

    @pl.when(at == pl.num_programs(0) - 1)
    def _():
        groups, lines, width = sent_ref.shape
        here = slots // groups
        for g in range(groups):
            lanes = slice(g * here, (g + 1) * here)
            sent_ref[g, :here] = sum_ref[0, lanes].astype(bf16)
            sent_ref[g, here : 2 * here] = sum_ref[1, lanes].astype(bf16)
            gates = jnp.concatenate([gate_ref[:, lanes], jnp.zeros((8, width - here), f32)], axis=1)
            gates = jnp.concatenate([gates, jnp.zeros((lines - 2 * here - 8, width), f32)], axis=0)
            sent_ref[g, 2 * here :] = gates.astype(bf16)


def run_route(
    images, cot, attended_all, out_whole, packed, vectors, routes, plane_target, groups, slots_plane
):
    f32, bf16 = jnp.float32, jnp.bfloat16
    count, length, width = images.shape
    tensor = attended_all.shape[0]
    sent = (groups, 2 * slots_plane // groups + EXTRA, width)
    return call_kernel(
        functools.partial(route_kernel, tensor * attended_all.shape[3] // PAIR),
        (count // PAIR,),
        [
            by_step(images, PAIR),
            by_step(cot, PAIR),
            (attended_all, (tensor, 1, *attended_all.shape[2:]), lambda p: (0, p, 0, 0)),
            whole(out_whole),
            whole(packed),
            whole(vectors),
            by_step(routes, PAIR),
            by_step(plane_target, PAIR),
        ],
        [
            ((count, length, width), f32, (PAIR, length, width), lambda p: (p, 0, 0)),
            ((count, length, EXPERTS), f32, (PAIR, length, EXPERTS), lambda p: (p, 0, 0)),
            (sent, bf16, sent, lambda p: (0, 0, 0)),
        ],
        [pltpu.VMEM((2, slots_plane, width), f32), pltpu.VMEM((8, slots_plane), f32)],
        flops=2 * count * length * width * (width + 2 * slots_plane),
    )


def slot_blocks(parts_ref, slots_ref, outer, inner):
    here = parts_ref.shape[2]
    for b in range(slots_ref.shape[1] // here):
        first = (b // inner) * outer * inner + b % inner
        total = parts_ref[first].astype(jnp.float32)
        for o in range(1, outer):
            total = total + parts_ref[first + o * inner].astype(jnp.float32)
        slots_ref[:, b * here : (b + 1) * here] = total


def token_hits(target_column, count):
    return lax.broadcasted_iota(jnp.int32, (target_column.shape[0], count), 1) == target_column


def take_grads_kernel(outer, inner, parts_ref, target_ref, rows_ref, gates_ref, slots_ref):
    f32, bf16 = jnp.float32, jnp.bfloat16
    slots = slots_ref.shape[1]
    local = rows_ref.shape[2] // target_ref.shape[0]

    @pl.when(pl.program_id(0) == 0)
    def _():
        slot_blocks(parts_ref, slots_ref, outer, inner)

    grads = slots_ref[:local].astype(bf16)
    gate_terms = slots_ref[local : local + 1] + slots_ref[local + 1 : local + 2]
    for h in range(target_ref.shape[0]):
        hits = [token_hits(target_ref[h, :, k : k + 1], slots) for k in range(TOPK)]
        find = jnp.logical_or(hits[0], hits[1]).astype(f32).astype(bf16)
        rows_ref[0, :, h * local : (h + 1) * local] = turned_dot(find, grads, 1, 1).astype(bf16)
        terms = [
            jnp.sum(jnp.where(hit, gate_terms, 0.0), axis=1, keepdims=True) for hit in hits
        ]
        gates_ref[h] = jnp.concatenate(terms, axis=1)


def run_take_grads(parts, target, local, outer, inner, slots):
    count, length, _ = target.shape
    return call_kernel(
        functools.partial(take_grads_kernel, outer, inner),
        (count // PAIR,),
        [whole(parts), by_step(target, PAIR)],
        [
            ((count // PAIR, length, PAIR * local), jnp.bfloat16, (1, length, PAIR * local), lambda p: (p, 0, 0)),
            ((count, length, TOPK), jnp.float32, (PAIR, length, TOPK), lambda p: (p, 0, 0)),
        ],
        [pltpu.VMEM((parts.shape[1], slots), jnp.float32)],
        flops=2 * count * length * slots * local,
    )


def take_rows_kernel(
    outer, inner, held_ref, parts_ref, target_ref, probs_ref, routes_ref, mixed_ref, out_ref, slots_ref
):
    f32, bf16 = jnp.float32, jnp.bfloat16
    slots = slots_ref.shape[1]
    pair = target_ref.shape[0]
    local = out_ref.shape[2] // pair
    at = pl.program_id(0)

    @pl.when(at == 0)
    def _():
        slot_blocks(parts_ref, slots_ref, outer, inner)

    returned = slots_ref[...].astype(bf16)
    for h in range(pair):
        probs = probs_ref[h]
        experts = lax.broadcasted_iota(jnp.int32, probs.shape, 1)
        rows = mixed_ref[h]
        for k in range(TOPK):
            match = experts == routes_ref[h, :, k : k + 1]
            gate = jnp.sum(jnp.where(match, probs, 0.0), axis=1, keepdims=True)
            find = token_hits(target_ref[h, :, k : k + 1], slots).astype(f32).astype(bf16)
            rows = rows + gate * turned_dot(find, returned, 1, 1)
        live = (at * pair + h < held_ref[0]).astype(f32)
        out_ref[0, :, h * local : (h + 1) * local] = (live * rows).astype(bf16)


def run_take_rows(held, parts, target, probs, routes, mixed_cut, outer, inner, slots):
    count, length, local = mixed_cut.shape
    return call_kernel(
        functools.partial(take_rows_kernel, outer, inner),
        (count // PAIR,),
        [
            (held, None, None),
            whole(parts),
            by_step(target, PAIR),
            by_step(probs, PAIR),
            by_step(routes, PAIR),
            by_step(mixed_cut, PAIR),
        ],
        [((count // PAIR, length, PAIR * local), jnp.bfloat16, (1, length, PAIR * local), lambda p: (p, 0, 0))],
        [pltpu.VMEM((parts.shape[1], slots), jnp.float32)],
        flops=4 * count * length * slots * local,
    )[0]


def pull_kernel(
    router_at,
    held_ref,
    images_ref,
    cot_ref,
    mixed_ref,
    probs_ref,
    routes_ref,
    gates_ref,
    rows_ref,
    attended_ref,
    proj_ref,
    packed_ref,
    vector_ref,
    grad_mixed_ref,
    normed_ref,
    matrix_ref,
    sums_ref,
    matrix_sum_ref,
):
    f32, bf16 = jnp.float32, jnp.bfloat16
    pair = images_ref.shape[0]
    tensor = rows_ref.shape[0]
    local = attended_ref.shape[2] // pair
    width = images_ref.shape[2]
    at = pl.program_id(0)

    @pl.when(at == 0)
    def _():
        sums_ref[...] = jnp.zeros_like(sums_ref)
        matrix_sum_ref[...] = jnp.zeros_like(matrix_sum_ref)

    qkv = packed_ref[:, : 3 * local]
    out_turned = packed_ref[:, 3 * local : 4 * local]
    router = packed_ref[:, router_at : router_at + EXPERTS]
    scale = HEAD_DIM**-0.5
    for h in range(pair):
        lanes = slice(h * local, (h + 1) * local)
        live = (at * pair + h < held_ref[0]).astype(f32)
        cot = cot_ref[h].astype(f32) * live
        scaled, inv_std = norm_rows(mixed_ref[h])
        routed = (scaled * vector_ref[3:4] + vector_ref[4:5]).astype(bf16)
        probs = probs_ref[h]
        experts = lax.broadcasted_iota(jnp.int32, probs.shape, 1)
        grad_probs = jnp.zeros(probs.shape, f32)
        for k in range(TOPK):
            match = experts == routes_ref[h, :, k : k + 1]
            grad_probs = grad_probs + jnp.where(match, gates_ref[h, :, k : k + 1], 0.0)
        grad_logits = probs * (grad_probs - jnp.sum(probs * grad_probs, axis=-1, keepdims=True))
        grad_logits = grad_logits.astype(bf16)
        grad_routed = jnp.concatenate([rows_ref[z, 0, :, lanes] for z in range(tensor)], axis=1)
        grad_routed = grad_routed.astype(f32) + turned_dot(grad_logits, router, 1, 1)
        grad_mixed = cot + norm_rows_back(grad_routed, scaled, inv_std, vector_ref[3:4])
        grad_mixed_ref[h] = grad_mixed
        low = grad_mixed.astype(bf16)
        grad_attended = jnp.dot(low, out_turned, preferred_element_type=f32).astype(bf16)
        proj = proj_ref[h]
        grads = [[], [], []]
        for n in range(0, local, HEAD_DIM):
            queries = proj[:, n : n + HEAD_DIM]
            keys = proj[:, local + n : local + n + HEAD_DIM]
            values = proj[:, 2 * local + n : 2 * local + n + HEAD_DIM]
            grad_head = grad_attended[:, n : n + HEAD_DIM]
            scores = turned_dot(queries, keys, 1, 1) * scale
            scores = jnp.exp(scores - jnp.max(scores, axis=-1, keepdims=True))
            weights = scores / jnp.sum(scores, axis=-1, keepdims=True)
            grads[2].append(turned_dot(weights.astype(bf16), grad_head, 0, 0))
            grad_weights = turned_dot(grad_head, values, 1, 1)
            inner = jnp.sum(weights * grad_weights, axis=-1, keepdims=True)
            grad_scores = (weights * (grad_weights - inner)).astype(bf16)
            grads[0].append(jnp.dot(grad_scores, keys, preferred_element_type=f32) * scale)
            grads[1].append(turned_dot(grad_scores, queries, 0, 0) * scale)
        grad_proj = jnp.concatenate(grads[0] + grads[1] + grads[2], axis=1)
        proj_sum = jnp.sum(grad_proj, axis=0, keepdims=True)
        grad_proj = grad_proj.astype(bf16)
        first, _ = norm_rows(images_ref[h].astype(f32))
        normed = (first * vector_ref[0:1] + vector_ref[1:2]).astype(bf16)
        grad_normed = turned_dot(grad_proj, qkv, 1, 1)
        normed_ref[h] = grad_normed.astype(bf16)
        attended = attended_ref[0, :, lanes]
        matrix = jnp.concatenate(
            [
                turned_dot(normed, grad_proj, 0, 0),
                turned_dot(low, attended, 0, 0),
                turned_dot(routed, grad_logits, 0, 0),
            ],
            axis=1,
        )
        matrix_sum_ref[...] += matrix
        column = lambda values: jnp.sum(values, axis=0, keepdims=True)
        sums_ref[2:3] += column(grad_mixed)
        sums_ref[3:4] += column(grad_routed * scaled)
        sums_ref[4:5] += column(grad_routed)
        sums_ref[5:6, : 3 * local] += proj_sum

    @pl.when(at == pl.num_programs(0) - 1)
    def _():
        matrix_ref[...] = matrix_sum_ref[...].astype(bf16)


def run_pull(held, images, cot, mixed, probs, routes, gates, rows_all, attended, proj, packed, vectors, router_at):
    f32, bf16 = jnp.float32, jnp.bfloat16
    count, length, width = images.shape
    tensor = rows_all.shape[0]
    local = proj.shape[2] // 3
    tokens = (count, length, width)
    block = (PAIR, length, width)
    step = lambda p: (p, 0, 0)
    still = lambda p: (0, 0)
    matrix = (width, 4 * local + EXPERTS)
    return call_kernel(
        functools.partial(pull_kernel, router_at),
        (count // PAIR,),
        [
            (held, None, None),
            by_step(images, PAIR),
            by_step(cot, PAIR),
            by_step(mixed, PAIR),
            by_step(probs, PAIR),
            by_step(routes, PAIR),
            by_step(gates, PAIR),
            (rows_all, (tensor, 1, *rows_all.shape[2:]), lambda p: (0, p, 0, 0)),
            by_step(attended, 1),
            by_step(proj, PAIR),
            whole(packed),
            whole(vectors),
        ],
        [
            (tokens, f32, block, step),
            (tokens, bf16, block, step),
            (matrix, bf16, matrix, still),
            ((8, width), f32, (8, width), still),
        ],
        [pltpu.VMEM(matrix, f32)],
        flops=2 * count * length * (width * 12 * local + 14 * length * local),
    )


def last_kernel(images_ref, normed_ref, mixed_ref, vector_ref, out_ref, sums_ref):
    @pl.when(pl.program_id(0) == 0)
    def _():
        sums_ref[...] = jnp.zeros_like(sums_ref)

    for h in range(images_ref.shape[0]):
        scaled, inv_std = norm_rows(images_ref[h].astype(jnp.float32))
        grad = normed_ref[h].astype(jnp.float32)
        out_ref[h] = mixed_ref[h] + norm_rows_back(grad, scaled, inv_std, vector_ref[0:1])
        sums_ref[0:1] += jnp.sum(grad * scaled, axis=0, keepdims=True)
        sums_ref[1:2] += jnp.sum(grad, axis=0, keepdims=True)


def run_last(images, grad_normed, grad_mixed, vectors):
    width = images.shape[2]
    return call_kernel(
        last_kernel,
        (images.shape[0],),
        [by_step(images, 1), by_step(grad_normed, 1), by_step(grad_mixed, 1), whole(vectors)],
        [
            (images.shape, jnp.float32, (1, *images.shape[1:]), lambda p: (p, 0, 0)),
            ((8, width), jnp.float32, (8, width), lambda p: (0, 0)),
        ],
    )


def moved_plan(
    images,
    images_held,
    routes,
    slot_index,
    first_gain,
    first_shift,
    w_qkv,
    qv_bias,
    w_out,
    out_bias,
    second_gain,
    second_shift,
    w_router,
    w_in,
    in_bias,
    w_back,
    back_bias,
    cotangent,
):
    f32, bf16 = jnp.float32, jnp.bfloat16
    image_count, seq_len, width = images.shape
    experts_here, shard_width, ff_here = w_in.shape
    data, sources = lax.axis_size(DP), lax.axis_size(EXPERT)
    outer, inner = lax.axis_size(OUTER), lax.axis_size(INNER)
    tensor = outer * inner
    tensor_axes = (OUTER, INNER)
    everywhere = (DP, EXPERT, OUTER, INNER)
    groups = data * sources
    owners = data * inner
    mine = experts_here // owners
    slots = EXPERTS * CAP
    dp_at = lax.axis_index(DP)
    inner_at = lax.axis_index(INNER)
    tensor_at = lax.axis_index(tensor_axes)
    owner_at = dp_at * inner + inner_at
    local_width = w_out.shape[0]
    slice_width = width // tensor
    router_at = 4 * local_width

    packed = jnp.concatenate(
        [
            w_qkv.transpose(1, 0, 2).reshape(shard_width, 3 * local_width),
            w_out.T,
            w_router,
            back_bias.T,
            jnp.stack([first_gain, first_shift, out_bias, second_gain, second_shift], axis=1),
        ],
        axis=1,
    )
    packed = swap(jnp.broadcast_to(packed[None], (data, *packed.shape)), DP).reshape(width, -1)
    out_rows = jnp.concatenate(hop_gather(w_out, tensor_axes), axis=0)
    in_bias_all = jnp.stack(hop_gather(in_bias, INNER))
    packed, out_rows, in_bias_all, w_in = lax.optimization_barrier(
        (packed, out_rows, in_bias_all, w_in)
    )
    vectors = packed[:, router_at + EXPERTS + experts_here :].T.astype(f32)
    out_whole = jnp.concatenate(hop_gather(out_rows, DP), axis=1)
    in_bias_mine = lax.dynamic_slice_in_dim(in_bias_all, owner_at * mine, mine, 1)
    in_bias_mine = in_bias_mine.transpose(1, 0, 2).astype(f32)

    chunk_shape = (owners, mine, shard_width, ff_here)
    in_raw, w_back = lax.optimization_barrier((swap(w_in, (DP, INNER)), w_back))
    in_raw = in_raw.reshape(chunk_shape)
    back_raw = swap(w_back.transpose(0, 2, 1), (DP, INNER)).reshape(chunk_shape)

    home, within = routes // experts_here, routes % experts_here
    owner, nth = within // mine, within % mine
    kept = slot_index < CAP
    group_place = (owner // inner) * sources + home
    target = ((group_place * inner + owner % inner) * mine + nth) * CAP + slot_index
    target = jnp.where(kept, target, slots)
    plane_target = (group_place * mine + nth) * CAP + slot_index
    plane_target = jnp.where(jnp.logical_and(kept, owner % inner == inner_at), plane_target, -1)
    plane_target = plane_target.transpose(0, 2, 1)

    attended, proj = run_attend(images, packed, vectors, qv_bias.astype(f32))
    attended_all = lax.all_gather(attended, tensor_axes)
    attended_all, in_raw = lax.optimization_barrier((attended_all, in_raw))
    mixed, probs, sent = run_route(
        images,
        cotangent,
        attended_all,
        out_whole,
        packed,
        vectors,
        routes,
        plane_target,
        groups,
        slots // inner,
    )
    sent, back_raw = lax.optimization_barrier((sent, back_raw))
    arrived = swap(sent, (DP, EXPERT))
    back_bias_mine = lax.dynamic_slice_in_dim(packed, router_at + EXPERTS + owner_at * mine, mine, 1)
    back_bias_mine = jnp.where(lax.axis_index(OUTER) == 0, back_bias_mine.astype(f32), 0.0)
    (
        returned_out,
        grads_out,
        hidden_low,
        grad_pre_low,
        grad_turned,
        grad_in_bias_mine,
        grad_back_bias_mine,
    ) = run_experts(
        arrived, in_raw, back_raw, in_bias_mine, back_bias_mine, inner, tensor
    )

    def bring(parts):
        return swap(parts.reshape(groups * tensor, *parts.shape[2:]), everywhere)

    grad_parts = bring(grads_out)
    weight_out = weight_grads(
        arrived, grad_pre_low, grad_turned, hidden_low, grad_in_bias_mine, grad_back_bias_mine, data
    )
    rows_cut, grad_gates = run_take_grads(grad_parts, target, slice_width, outer, inner, slots)
    rows_cut, returned_out = lax.optimization_barrier((rows_cut, returned_out))
    rows_all = lax.all_gather(rows_cut, tensor_axes)
    returned = bring(returned_out)
    rows_all, returned = lax.optimization_barrier((rows_all, returned))
    returned, weight_out = lax.optimization_barrier((returned, weight_out))
    weight_parts = swap(weight_out.reshape(owners, *weight_out.shape[2:]), (DP, INNER))
    grad_mixed, normed_part, matrix, sums = run_pull(
        images_held,
        images,
        cotangent,
        mixed,
        probs,
        routes,
        grad_gates,
        rows_all,
        attended,
        proj,
        packed,
        vectors,
        router_at,
    )
    grad_normed = lax.psum(normed_part, tensor_axes)
    grad_images, first_sums = run_last(images, grad_normed, grad_mixed, vectors)
    mixed_cut = lax.dynamic_slice_in_dim(mixed, tensor_at * slice_width, slice_width, 2)
    output_cut = run_take_rows(
        images_held, returned, target, probs, routes, mixed_cut, outer, inner, slots
    )
    output = lax.all_gather(output_cut, tensor_axes)
    output = output.reshape(tensor, image_count // PAIR, seq_len, PAIR, slice_width)
    output = output.transpose(1, 3, 2, 0, 4).reshape(images.shape)

    pair_sums = [sums[5, :local_width], sums[5, 2 * local_width : 3 * local_width]]
    pair_sums = jnp.tile(jnp.stack(pair_sums), (1, data))
    vector_grads = jnp.concatenate([first_sums[:2], sums[2:5], pair_sums], axis=0)
    high, low = high_low(vector_grads)
    small = jnp.concatenate([matrix, high.T, low.T], axis=1)
    small = swap(small.reshape(groups, shard_width // sources, -1), (DP, EXPERT))
    small = jnp.sum(small.astype(f32), axis=0)
    small = jnp.concatenate(hop_gather(small, EXPERT), axis=0)
    grad_w_qkv = small[:, : 3 * local_width].reshape(shard_width, 3, local_width).transpose(1, 0, 2)
    grad_w_out = small[:, 3 * local_width : router_at].T
    grad_w_router = small[:, router_at : router_at + EXPERTS]
    vector_grads = small[:, router_at + EXPERTS :].T
    vector_grads = vector_grads[:7] + vector_grads[7:]
    grad_w_in, grad_w_back = run_widen(weight_parts, mine, shard_width)
    grad_w_back = grad_w_back.transpose(0, 2, 1)
    lines = weight_parts[:, 2 * mine * shard_width :].astype(f32)
    grad_in_bias = lines[:, : 2 * mine].reshape(owners, mine, 2, ff_here)
    grad_in_bias = jnp.sum(grad_in_bias, axis=2).reshape(experts_here, ff_here)
    lines = lines[:, 2 * mine : 3 * mine].reshape(experts_here, 2, ff_here // 2)
    grad_back_shard = jnp.sum(lines[:, :, :shard_width], axis=1)
    return (
        output,
        grad_images,
        vector_grads[0],
        vector_grads[1],
        grad_w_qkv,
        vector_grads[5:7],
        grad_w_out,
        vector_grads[2],
        vector_grads[3],
        vector_grads[4],
        grad_w_router,
        grad_w_in,
        grad_in_bias,
        grad_w_back,
        grad_back_shard,
    )


def specs(tensor):
    rows = P((DP, EXPERT), None, None)
    vector, square = P(DP), P(tensor, DP)
    qkv, pair, router = P(None, DP, tensor), P(None, tensor), P(DP, None)
    inward, outward = P(EXPERT, DP, tensor), P(EXPERT, tensor, DP)
    params = (vector, vector, qkv, pair, square, vector, vector, vector, router)
    experts = (inward, P(EXPERT, tensor), outward, P(EXPERT, DP))
    taken = (rows, P((DP, EXPERT)), rows, rows, *params, *experts, rows)
    given = (rows, rows, *params, *experts)
    return taken, given


def solution(mesh):
    data, expert, tensor = (mesh.shape[name] for name in (DP, EXPERT, TENSOR))
    inner = FF_PAIR if tensor % FF_PAIR == 0 else 1
    owners = data * inner
    if (EXPERTS // expert) % owners or any(n & (n - 1) for n in (data, expert, tensor)):
        taken, given = specs(TENSOR)
        return jax.shard_map(
            gathered_plan, mesh=mesh, in_specs=taken, out_specs=given, check_vma=False
        )
    devices = mesh.devices.reshape(data, expert, tensor // inner, inner)
    split_mesh = Mesh(devices, (DP, EXPERT, OUTER, INNER))
    taken, given = specs((OUTER, INNER))
    return jax.shard_map(
        moved_plan, mesh=split_mesh, in_specs=taken, out_specs=given, check_vma=False
    )
```

```python
import functools
import math

import jax
import jax.numpy as jnp
from jax import lax
from jax.experimental import pallas as pl
from jax.experimental.pallas import tpu as pltpu
from jax.sharding import Mesh
from jax.sharding import PartitionSpec as P

HEAD_DIM = 64
EXPERTS = 32
TOPK = 2
CAP = 64
FF_PAIR = 2
PAIR = 2
EXTRA = 16
VMEM_LIMIT = 56 * 1024 * 1024
GELU_SCALE = (2.0 / math.pi) ** 0.5
GELU_CUBE = 0.044715

DP = "dp"
EXPERT = "expert"
TENSOR = "tensor"
OUTER = "outer"
INNER = "inner"


EPS = 1e-06


def norm_parts(values, norm_gain, norm_shift):
    average = jnp.mean(values, axis=-1, keepdims=True)
    centred = values - average
    spread = jnp.mean(centred * centred, axis=-1, keepdims=True)
    inv_std = lax.rsqrt(spread + EPS)
    scaled = centred * inv_std
    return (scaled * norm_gain + norm_shift, scaled, inv_std)


def norm_back(grad_out, scaled, inv_std, norm_gain):
    grad_scaled = grad_out * norm_gain
    inner = grad_scaled - jnp.mean(grad_scaled, axis=-1, keepdims=True)
    inner = inner - scaled * jnp.mean(grad_scaled * scaled, axis=-1, keepdims=True)
    return (inner * inv_std, jnp.sum(grad_out * scaled, axis=0), jnp.sum(grad_out, axis=0))


def attention_forward(queries, key_rows, value_rows, scale):
    scores = (
        jnp.einsum("iqhd,ikhd->ihqk", queries, key_rows, preferred_element_type=jnp.float32) * scale
    )
    row_peak = jnp.max(scores, axis=-1, keepdims=True)
    log_total = row_peak + jnp.log(jnp.sum(jnp.exp(scores - row_peak), axis=-1, keepdims=True))
    weights = jnp.exp(scores - log_total).astype(jnp.bfloat16)
    attended = jnp.einsum(
        "ihqk,ikhd->iqhd", weights, value_rows, preferred_element_type=jnp.float32
    )
    return (attended, log_total)


def attention_backward(queries, key_rows, value_rows, log_total, grad_low, scale):
    scores = (
        jnp.einsum("iqhd,ikhd->ihqk", queries, key_rows, preferred_element_type=jnp.float32) * scale
    )
    probs = jnp.exp(scores - log_total)
    weights = probs.astype(jnp.bfloat16)
    grad_values = jnp.einsum(
        "ihqk,iqhd->ikhd", weights, grad_low, preferred_element_type=jnp.float32
    )
    grad_weights = jnp.einsum(
        "iqhd,ikhd->ihqk", grad_low, value_rows, preferred_element_type=jnp.float32
    )
    grad_scores = probs * (grad_weights - jnp.sum(probs * grad_weights, axis=-1, keepdims=True))
    scores_low = grad_scores.astype(jnp.bfloat16)
    grad_queries = (
        jnp.einsum("ihqk,ikhd->iqhd", scores_low, key_rows, preferred_element_type=jnp.float32)
        * scale
    )
    grad_keys = (
        jnp.einsum("ihqk,iqhd->ikhd", scores_low, queries, preferred_element_type=jnp.float32)
        * scale
    )
    return (grad_queries, grad_keys, grad_values)


def gathered_plan(
    images,
    images_held,
    routes,
    slot_index,
    first_gain,
    first_shift,
    w_qkv,
    qv_bias,
    w_out,
    out_bias,
    second_gain,
    second_shift,
    w_router,
    w_in,
    in_bias,
    w_back,
    back_bias,
    cotangent,
):
    image_count, seq_len, width = images.shape
    rows_total = image_count * seq_len
    experts_here = w_in.shape[0]
    (
        gain_first,
        shift_first,
        qkv_full,
        out_full,
        bias_out_full,
        gain_second,
        shift_second,
        router_full,
        in_full,
        back_full,
        back_bias_full,
    ) = (
        lax.all_gather(first_gain, DP, axis=0, tiled=True),
        lax.all_gather(first_shift, DP, axis=0, tiled=True),
        lax.all_gather(w_qkv, DP, axis=1, tiled=True),
        lax.all_gather(w_out, DP, axis=1, tiled=True),
        lax.all_gather(out_bias, DP, axis=0, tiled=True),
        lax.all_gather(second_gain, DP, axis=0, tiled=True),
        lax.all_gather(second_shift, DP, axis=0, tiled=True),
        lax.all_gather(w_router, DP, axis=0, tiled=True),
        lax.all_gather(w_in, DP, axis=1, tiled=True),
        lax.all_gather(w_back, DP, axis=2, tiled=True),
        lax.all_gather(back_bias, DP, axis=1, tiled=True),
    )
    gain_first = gain_first.astype(jnp.float32)
    gain_second = gain_second.astype(jnp.float32)
    inputs = images.reshape(rows_total, width).astype(jnp.float32)
    live_image = (jnp.arange(image_count, dtype=jnp.int32) < images_held[0]).astype(jnp.float32)
    live_rows = jnp.repeat(live_image, seq_len)[:, None]
    normed, scaled_first, inv_first = norm_parts(
        inputs, gain_first, shift_first.astype(jnp.float32)
    )
    normed_low = normed.astype(jnp.bfloat16)
    projected = jnp.einsum("td,cde->cte", normed_low, qkv_full, preferred_element_type=jnp.float32)
    local_width = projected.shape[2]
    head_count = local_width // HEAD_DIM
    head_shape = (image_count, seq_len, head_count, HEAD_DIM)
    bias_pair = qv_bias.astype(jnp.float32)
    queries = (projected[0] + bias_pair[0]).astype(jnp.bfloat16).reshape(head_shape)
    key_rows = projected[1].astype(jnp.bfloat16).reshape(head_shape)
    value_rows = (projected[2] + bias_pair[1]).astype(jnp.bfloat16).reshape(head_shape)
    scale = HEAD_DIM ** (-0.5)
    attended, log_total = attention_forward(queries, key_rows, value_rows, scale)
    attended_low = attended.reshape(rows_total, local_width).astype(jnp.bfloat16)
    head_part = jnp.dot(attended_low, out_full, preferred_element_type=jnp.float32)
    mixed = inputs + lax.psum(head_part, TENSOR) + bias_out_full.astype(jnp.float32)
    routed, scaled_second, inv_second = norm_parts(
        mixed, gain_second, shift_second.astype(jnp.float32)
    )
    routed_low = routed.astype(jnp.bfloat16)
    logits = jnp.dot(routed_low, router_full, preferred_element_type=jnp.float32)
    probs = jax.nn.softmax(logits, axis=-1)
    pair_routes = routes.reshape(rows_total, TOPK)
    pair_slots = slot_index.reshape(rows_total, TOPK)
    target = jnp.where(pair_slots < CAP, pair_routes * CAP + pair_slots, EXPERTS * CAP).reshape(
        rows_total * TOPK
    )
    gates = jnp.take_along_axis(probs, pair_routes, axis=1)
    pair_rows = jnp.repeat(routed_low, TOPK, axis=0)
    outgoing = (
        jnp.zeros((EXPERTS * CAP + 1, width), jnp.bfloat16)
        .at[target]
        .set(pair_rows)[: EXPERTS * CAP]
    )
    outgoing = outgoing.reshape(EXPERTS, 1, CAP, width)
    arrived = lax.all_to_all(outgoing, EXPERT, split_axis=0, concat_axis=1, tiled=True)
    sources = arrived.shape[1]
    expert_rows = arrived.reshape(experts_here, sources * CAP, width)
    hidden_pre = jnp.einsum(
        "erd,edf->erf", expert_rows, in_full, preferred_element_type=jnp.float32
    )
    hidden_pre = hidden_pre + in_bias.astype(jnp.float32)[:, None, :]
    hidden_value, gelu_pull = jax.vjp(jax.nn.gelu, hidden_pre)
    hidden_low = hidden_value.astype(jnp.bfloat16)
    expert_part = jnp.einsum(
        "erf,efd->erd", hidden_low, back_full, preferred_element_type=jnp.float32
    )
    bias_back = back_bias_full.astype(jnp.float32)[:, None, :]
    shares = lax.psum_scatter(
        expert_part.reshape(experts_here, sources, CAP, width),
        TENSOR,
        scatter_dimension=2,
        tiled=True,
    )
    share_low = (shares + bias_back[:, None]).astype(jnp.bfloat16)
    pieces = lax.all_to_all(share_low, EXPERT, split_axis=1, concat_axis=0, tiled=True)
    returned = lax.all_gather(pieces, TENSOR, axis=2, tiled=True)
    padded = jnp.concatenate(
        [returned.reshape(EXPERTS * CAP, width), jnp.zeros((1, width), jnp.bfloat16)], axis=0
    )
    picked = padded[target].astype(jnp.float32).reshape(rows_total, TOPK, width)
    expert_mix = jnp.sum(gates[:, :, None] * picked, axis=1)
    output = (live_rows * (mixed + expert_mix)).astype(jnp.bfloat16).reshape(images.shape)
    grad_rows = cotangent.reshape(rows_total, width).astype(jnp.float32) * live_rows
    grad_gates = jnp.sum(grad_rows[:, None, :] * picked, axis=-1)
    grad_picked = (
        (gates[:, :, None] * grad_rows[:, None, :])
        .astype(jnp.bfloat16)
        .reshape(rows_total * TOPK, width)
    )
    grad_outgoing = (
        jnp.zeros((EXPERTS * CAP + 1, width), jnp.bfloat16)
        .at[target]
        .set(grad_picked)[: EXPERTS * CAP]
    )
    grad_outgoing = grad_outgoing.reshape(EXPERTS, 1, CAP, width)
    grad_arrived = lax.all_to_all(grad_outgoing, EXPERT, split_axis=0, concat_axis=1, tiled=True)
    grad_arrived = grad_arrived.reshape(experts_here, sources * CAP, width)
    grad_back_bias = jnp.sum(grad_arrived.astype(jnp.float32), axis=1)
    grad_back_w = jnp.einsum(
        "erf,erd->efd", hidden_low, grad_arrived, preferred_element_type=jnp.float32
    )
    grad_hidden = jnp.einsum(
        "erd,efd->erf", grad_arrived, back_full, preferred_element_type=jnp.float32
    )
    grad_pre = gelu_pull(grad_hidden)[0]
    grad_in_bias_local = jnp.sum(grad_pre, axis=1)
    grad_pre_low = grad_pre.astype(jnp.bfloat16)
    grad_in_w = jnp.einsum(
        "erd,erf->edf", expert_rows, grad_pre_low, preferred_element_type=jnp.float32
    )
    grad_rows_part = jnp.einsum(
        "erf,edf->erd", grad_pre_low, in_full, preferred_element_type=jnp.float32
    )
    grad_shares = lax.psum_scatter(
        grad_rows_part.reshape(experts_here, sources, CAP, width),
        TENSOR,
        scatter_dimension=2,
        tiled=True,
    ).astype(jnp.bfloat16)
    grad_pieces = lax.all_to_all(grad_shares, EXPERT, split_axis=1, concat_axis=0, tiled=True)
    grad_returned = lax.all_gather(grad_pieces, TENSOR, axis=2, tiled=True)
    grad_padded = jnp.concatenate(
        [grad_returned.reshape(EXPERTS * CAP, width), jnp.zeros((1, width), jnp.bfloat16)], axis=0
    )
    grad_routed = jnp.sum(
        grad_padded[target].astype(jnp.float32).reshape(rows_total, TOPK, width), axis=1
    )
    expert_match = (
        pair_routes[:, :, None] == jnp.arange(EXPERTS, dtype=jnp.int32)[None, None, :]
    ).astype(jnp.float32)
    grad_probs = jnp.sum(expert_match * grad_gates[:, :, None], axis=1)
    grad_logits = probs * (grad_probs - jnp.sum(probs * grad_probs, axis=-1, keepdims=True))
    grad_logits_low = grad_logits.astype(jnp.bfloat16)
    grad_router = jnp.einsum(
        "td,te->de", routed_low, grad_logits_low, preferred_element_type=jnp.float32
    )
    grad_routed = grad_routed + jnp.einsum(
        "te,de->td", grad_logits_low, router_full, preferred_element_type=jnp.float32
    )
    grad_from_norm, grad_gain_second, grad_shift_second = norm_back(
        grad_routed, scaled_second, inv_second, gain_second
    )
    grad_mixed = grad_rows + grad_from_norm
    grad_bias_out = jnp.sum(grad_mixed, axis=0)
    grad_mixed_low = grad_mixed.astype(jnp.bfloat16)
    grad_out_w = jnp.einsum(
        "te,td->ed", attended_low, grad_mixed_low, preferred_element_type=jnp.float32
    )
    grad_attended = jnp.einsum(
        "td,ed->te", grad_mixed_low, out_full, preferred_element_type=jnp.float32
    )
    grad_attended = grad_attended.astype(jnp.bfloat16).reshape(head_shape)
    grad_queries, grad_keys, grad_values = attention_backward(
        queries, key_rows, value_rows, log_total, grad_attended, scale
    )
    grad_queries = grad_queries.reshape(rows_total, local_width)
    grad_keys = grad_keys.reshape(rows_total, local_width)
    grad_values = grad_values.reshape(rows_total, local_width)
    grad_pair_bias = jnp.stack([jnp.sum(grad_queries, axis=0), jnp.sum(grad_values, axis=0)])
    grad_proj_low = jnp.stack([grad_queries, grad_keys, grad_values]).astype(jnp.bfloat16)
    grad_qkv = jnp.einsum(
        "td,cte->cde", normed_low, grad_proj_low, preferred_element_type=jnp.float32
    )
    grad_normed_part = jnp.einsum(
        "cte,cde->td", grad_proj_low, qkv_full, preferred_element_type=jnp.float32
    )
    grad_normed = lax.psum(grad_normed_part, TENSOR)
    grad_from_first, grad_gain_first, grad_shift_first = norm_back(
        grad_normed, scaled_first, inv_first, gain_first
    )
    grad_images = (grad_mixed + grad_from_first).reshape(images.shape)
    expert_start = lax.axis_index(EXPERT) * experts_here
    full_in_bias = lax.dynamic_update_slice(
        jnp.zeros((EXPERTS, grad_in_bias_local.shape[1]), jnp.float32),
        grad_in_bias_local,
        (expert_start, jnp.zeros((), jnp.int32)),
    )
    summed = lax.psum(
        (
            grad_gain_first,
            grad_shift_first,
            grad_qkv,
            grad_pair_bias,
            grad_out_w,
            grad_bias_out,
            grad_gain_second,
            grad_shift_second,
            grad_router,
            full_in_bias,
        ),
        (DP, EXPERT),
    )
    shard_width = width // lax.axis_size(DP)
    shard_start = lax.axis_index(DP) * shard_width
    grad_first_gain = lax.dynamic_slice_in_dim(summed[0], shard_start, shard_width, 0)
    grad_first_shift = lax.dynamic_slice_in_dim(summed[1], shard_start, shard_width, 0)
    grad_w_qkv = lax.dynamic_slice_in_dim(summed[2], shard_start, shard_width, 1)
    grad_qv_bias = summed[3]
    grad_w_out = lax.dynamic_slice_in_dim(summed[4], shard_start, shard_width, 1)
    grad_out_bias = lax.dynamic_slice_in_dim(summed[5], shard_start, shard_width, 0)
    grad_second_gain = lax.dynamic_slice_in_dim(summed[6], shard_start, shard_width, 0)
    grad_second_shift = lax.dynamic_slice_in_dim(summed[7], shard_start, shard_width, 0)
    grad_w_router = lax.dynamic_slice_in_dim(summed[8], shard_start, shard_width, 0)
    grad_in_bias = lax.dynamic_slice_in_dim(summed[9], expert_start, experts_here, 0)
    grad_w_in, grad_w_back, grad_back_shard = (
        lax.psum_scatter(grad_in_w, DP, scatter_dimension=1, tiled=True),
        lax.psum_scatter(grad_back_w, DP, scatter_dimension=2, tiled=True),
        lax.psum_scatter(grad_back_bias, DP, scatter_dimension=1, tiled=True),
    )
    return (
        output,
        grad_images,
        grad_first_gain,
        grad_first_shift,
        grad_w_qkv,
        grad_qv_bias,
        grad_w_out,
        grad_out_bias,
        grad_second_gain,
        grad_second_shift,
        grad_w_router,
        grad_w_in,
        grad_in_bias,
        grad_w_back,
        grad_back_shard,
    )


def swap(values, axes):
    return lax.all_to_all(values, axes, split_axis=0, concat_axis=0, tiled=True)


def hop_gather(values, axes):
    count, at = lax.axis_size(axes), lax.axis_index(axes)
    hops = [values]
    for s in range(1, count):
        hops.append(lax.ppermute(values, axes, [(i, i ^ s) for i in range(count)]))
    gathered = []
    for i in range(count):
        found = hops[0]
        for s in range(1, count):
            found = jnp.where(at ^ i == s, hops[s], found)
        gathered.append(found)
    return gathered


def high_low(values):
    high = lax.reduce_precision(values, 8, 7)
    return high.astype(jnp.bfloat16), (values - high).astype(jnp.bfloat16)


def turned_dot(left, right, left_dim, right_dim):
    return lax.dot_general(
        left, right, (((left_dim,), (right_dim,)), ((), ())), preferred_element_type=jnp.float32
    )


def expert_kernel(
    inner,
    rows_ref,
    gate_ref,
    cot_ref,
    in_ref,
    back_ref,
    in_bias_ref,
    back_bias_ref,
    returned_ref,
    grads_ref,
    hidden_ref,
    grad_pre_ref,
    grad_turned_ref,
    grad_in_bias_ref,
    grad_back_bias_ref,
):
    f32, bf16 = jnp.float32, jnp.bfloat16
    groups, cap, width = rows_ref.shape
    chunks = in_ref.shape[0]
    data = chunks // inner
    tensor, slice_width = returned_ref.shape[1:3]
    mine = back_bias_ref.shape[1]
    total = groups * cap
    at = pl.program_id(0)
    rows = rows_ref[...].reshape(total, width)
    cot_turned = cot_ref[...].reshape(total, width).T.astype(f32)
    pair = gate_ref[:, 0:1, :].astype(f32) + gate_ref[:, 1:2, :].astype(f32)
    pair = pair.reshape(groups, pair.shape[-1])
    gate = jnp.zeros((groups, cap), f32)
    for j in range(mine):
        gate = jnp.where(at == j, pair[:, j * cap : (j + 1) * cap], gate)
    gate = jnp.concatenate([gate[g : g + 1, :] for g in range(groups)], axis=1)
    grad_turned = (cot_turned * gate).astype(bf16)
    grad_turned_ref[0] = grad_turned
    grad_returned = grad_turned.T
    grad_back_bias_ref[0] = jnp.sum(grad_returned.astype(f32), axis=0, keepdims=True)
    bias_columns = back_bias_ref[...]
    bias = jnp.zeros((width, 1), f32)
    for j in range(mine):
        bias = jnp.where(at == j, bias_columns[:, j : j + 1], bias)
    part = jnp.broadcast_to(bias, (width, total))
    back = jnp.zeros((width, total), f32)
    for t in range(inner):
        w_in = jnp.concatenate([in_ref[d * inner + t, 0] for d in range(data)], axis=0)
        w_back = jnp.concatenate([back_ref[d * inner + t, 0] for d in range(data)], axis=0)
        pre = jnp.dot(rows, w_in, preferred_element_type=f32) + in_bias_ref[0, t : t + 1, :]
        square = pre * pre
        bent = jnp.tanh(GELU_SCALE * pre * (1.0 + GELU_CUBE * square))
        half = 0.5 * (1.0 + bent)
        hidden = (pre * half).astype(bf16)
        slope = half + (0.5 * GELU_SCALE) * pre * (1.0 - bent * bent) * (
            1.0 + (3.0 * GELU_CUBE) * square
        )
        hidden_ref[0, t] = hidden
        grad_pre = jnp.dot(grad_returned, w_back, preferred_element_type=f32) * slope
        grad_in_bias_ref[0, t : t + 1, :] = jnp.sum(grad_pre, axis=0, keepdims=True)
        grad_pre = grad_pre.astype(bf16)
        grad_pre_ref[0, t] = grad_pre
        part = part + turned_dot(w_back, hidden, 1, 1)
        back = back + turned_dot(w_in, grad_pre, 1, 1)
    gate_terms = jnp.sum(part * cot_turned, axis=0, keepdims=True)
    high = gate_terms.astype(bf16)
    low = (gate_terms - high.astype(f32)).astype(bf16)
    extra = grads_ref.shape[2] - slice_width
    tail = jnp.concatenate([high, low, jnp.zeros((extra - 2, total), bf16)], axis=0)
    part = part.astype(bf16)
    back = back.astype(bf16)
    for j in range(mine):

        @pl.when(at == j)
        def _():
            lanes = slice(j * cap, (j + 1) * cap)
            for g in range(groups):
                mine_lanes = slice(g * cap, (g + 1) * cap)
                for z in range(tensor):
                    features = slice(z * slice_width, (z + 1) * slice_width)
                    returned_ref[g, z, :, lanes] = part[features, mine_lanes]
                    grads_ref[g, z, :slice_width, lanes] = back[features, mine_lanes]
                    grads_ref[g, z, slice_width:, lanes] = tail[:, mine_lanes]


def run_experts(arrived, in_raw, back_raw, in_bias, back_bias, inner, tensor):
    f32, bf16 = jnp.float32, jnp.bfloat16
    groups, _, width = arrived.shape
    chunks, mine, depth, ff = in_raw.shape
    total = groups * CAP
    slice_width = width // tensor
    gate_at = 2 * mine * CAP // EXTRA
    outs = [
        ((groups, tensor, slice_width, mine * CAP), bf16, lambda j: (0, 0, 0, 0), None),
        ((groups, tensor, slice_width + EXTRA, mine * CAP), bf16, lambda j: (0, 0, 0, 0), None),
        ((mine, inner, total, ff), bf16, lambda j: (j, 0, 0, 0), 1),
        ((mine, inner, total, ff), bf16, lambda j: (j, 0, 0, 0), 1),
        ((mine, width, total), bf16, lambda j: (j, 0, 0), 1),
        ((mine, inner, ff), f32, lambda j: (j, 0, 0), 1),
        ((mine, 1, width), f32, lambda j: (j, 0, 0), 1),
    ]
    return pl.pallas_call(
        functools.partial(expert_kernel, inner),
        grid=(mine,),
        in_specs=[
            pl.BlockSpec((groups, CAP, width), lambda j: (0, j, 0)),
            pl.BlockSpec((groups, EXTRA, mine * CAP), lambda j: (0, gate_at, 0)),
            pl.BlockSpec((groups, CAP, width), lambda j: (0, mine + j, 0)),
            pl.BlockSpec((chunks, 1, depth, ff), lambda j: (0, j, 0, 0)),
            pl.BlockSpec((chunks, 1, depth, ff), lambda j: (0, j, 0, 0)),
            pl.BlockSpec((1, inner, ff), lambda j: (j, 0, 0)),
            pl.BlockSpec((width, mine), lambda j: (0, 0)),
        ],
        out_specs=[
            pl.BlockSpec(shape if lead is None else (lead, *shape[1:]), index)
            for shape, _, index, lead in outs
        ],
        out_shape=[jax.ShapeDtypeStruct(shape, dtype) for shape, dtype, _, _ in outs],
        compiler_params=pltpu.CompilerParams(vmem_limit_bytes=VMEM_LIMIT),
        cost_estimate=pl.CostEstimate(
            flops=8 * mine * total * width * inner * ff,
            bytes_accessed=4 * chunks * mine * depth * ff + 12 * mine * total * inner * ff,
            transcendentals=mine * total * inner * ff,
        ),
    )(arrived, arrived, arrived, in_raw, back_raw, in_bias, back_bias)


def weight_kernel(
    rows_ref,
    grad_pre_ref,
    grad_turned_ref,
    hidden_ref,
    in_bias_ref,
    back_bias_ref,
    out_ref,
):
    f32, bf16 = jnp.float32, jnp.bfloat16
    groups, cap, width = rows_ref.shape
    data, ff = out_ref.shape[0], out_ref.shape[-1]
    depth = width // data
    mine = back_bias_ref.shape[0]
    at = pl.program_id(1)
    rows = rows_ref[...].reshape(groups * cap, width)
    grad_in = turned_dot(rows, grad_pre_ref[0, 0], 0, 0).astype(bf16)
    grad_back = jnp.dot(grad_turned_ref[0], hidden_ref[0, 0], preferred_element_type=f32)
    grad_back = grad_back.astype(bf16)
    for j in range(mine):

        @pl.when(at == j)
        def _():
            for d in range(data):
                lines = slice(d * depth, (d + 1) * depth)
                out_ref[d, 0, j * depth : (j + 1) * depth] = grad_in[lines]
                out_ref[d, 0, (mine + j) * depth : (mine + j + 1) * depth] = grad_back[lines]

    @pl.when(at == mine - 1)
    def _():
        pairs = []
        for j in range(mine):
            values = in_bias_ref[j, 0]
            high = values.astype(bf16).astype(f32)
            pairs += [high, values - high]
        for d in range(data):
            lines = list(pairs)
            for j in range(mine):
                values = back_bias_ref[j, :, d * depth : (d + 1) * depth]
                high = values.astype(bf16).astype(f32)
                gap = jnp.zeros((1, ff // 2 - depth), f32)
                lines.append(jnp.concatenate([high, gap, values - high, gap], axis=1))
            lines.append(jnp.zeros((EXTRA - len(lines), ff), f32))
            out_ref[d, 0, 2 * mine * depth :] = jnp.concatenate(lines, axis=0).astype(bf16)


def weight_grads(arrived, grad_pre, grad_turned, hidden, grad_in_bias, grad_back_bias, data):
    mine, inner, total, ff = hidden.shape
    groups, _, width = arrived.shape
    depth = width // data
    kept = pl.BlockSpec((1, 1, total, ff), lambda t, j: (j, t, 0, 0))
    out = (data, inner, 2 * mine * depth + EXTRA, ff)
    return pl.pallas_call(
        weight_kernel,
        grid=(inner, mine),
        in_specs=[
            pl.BlockSpec((groups, CAP, width), lambda t, j: (0, j, 0)),
            kept,
            pl.BlockSpec((1, width, total), lambda t, j: (j, 0, 0)),
            kept,
            pl.BlockSpec((mine, 1, 1, ff), lambda t, j: (0, t, 0, 0)),
            pl.BlockSpec((mine, 1, width), lambda t, j: (0, 0, 0)),
        ],
        out_specs=pl.BlockSpec((data, 1, *out[2:]), lambda t, j: (0, t, 0, 0)),
        out_shape=jax.ShapeDtypeStruct(out, jnp.bfloat16),
        compiler_params=pltpu.CompilerParams(vmem_limit_bytes=VMEM_LIMIT),
        cost_estimate=pl.CostEstimate(
            flops=4 * mine * total * width * inner * ff,
            bytes_accessed=4 * mine * inner * (total + width) * ff,
            transcendentals=0,
        ),
    )(arrived, grad_pre, grad_turned, hidden, grad_in_bias[:, :, None], grad_back_bias)


def widen_kernel(parts_ref, in_ref, back_ref):
    mine, depth, ff = in_ref.shape
    rows = mine * depth
    in_ref[...] = parts_ref[0, :rows].astype(jnp.float32).reshape(mine, depth, ff)
    back_ref[...] = parts_ref[0, rows : 2 * rows].astype(jnp.float32).reshape(mine, depth, ff)


def run_widen(parts, mine, depth):
    owners, _, ff = parts.shape
    out = ((owners * mine, depth, ff), jnp.float32, (mine, depth, ff), lambda p: (p, 0, 0))
    return call_kernel(widen_kernel, (owners,), [by_step(parts, 1)], [out, out])


def norm_rows(values):
    average = jnp.mean(values, axis=-1, keepdims=True)
    centred = values - average
    spread = jnp.mean(centred * centred, axis=-1, keepdims=True)
    inv_std = lax.rsqrt(spread + EPS)
    return centred * inv_std, inv_std


def norm_rows_back(grad_out, scaled, inv_std, norm_gain):
    grad_scaled = grad_out * norm_gain
    inner = grad_scaled - jnp.mean(grad_scaled, axis=-1, keepdims=True)
    inner = inner - scaled * jnp.mean(grad_scaled * scaled, axis=-1, keepdims=True)
    return inner * inv_std


def call_kernel(kernel, grid, inputs, outputs, scratch=(), flops=0):
    smem = pl.BlockSpec(memory_space=pltpu.SMEM)
    return pl.pallas_call(
        kernel,
        grid=grid,
        in_specs=[smem if b is None else pl.BlockSpec(b, i) for _, b, i in inputs],
        out_specs=[pl.BlockSpec(b, i) for _, _, b, i in outputs],
        out_shape=[jax.ShapeDtypeStruct(shape, dtype) for shape, dtype, _, _ in outputs],
        scratch_shapes=list(scratch),
        compiler_params=pltpu.CompilerParams(vmem_limit_bytes=VMEM_LIMIT),
        cost_estimate=pl.CostEstimate(
            flops=flops,
            bytes_accessed=sum(a.size * a.dtype.itemsize for a, _, _ in inputs),
            transcendentals=0,
        ),
    )(*(a for a, _, _ in inputs))


def whole(array):
    return array, array.shape, lambda p: (0,) * array.ndim


def by_step(array, lead):
    return array, (lead, *array.shape[1:]), lambda p: (p,) + (0,) * (array.ndim - 1)


def attend_kernel(images_ref, packed_ref, vector_ref, bias_ref, attended_ref, proj_ref):
    f32, bf16 = jnp.float32, jnp.bfloat16
    local = bias_ref.shape[1]
    weight = packed_ref[:, : 3 * local]
    for h in range(images_ref.shape[0]):
        scaled, _ = norm_rows(images_ref[h].astype(f32))
        normed = (scaled * vector_ref[0:1] + vector_ref[1:2]).astype(bf16)
        proj = jnp.dot(normed, weight, preferred_element_type=f32)
        queries = (proj[:, :local] + bias_ref[0:1]).astype(bf16)
        keys = proj[:, local : 2 * local].astype(bf16)
        values = (proj[:, 2 * local :] + bias_ref[1:2]).astype(bf16)
        proj_ref[h] = jnp.concatenate([queries, keys, values], axis=1)
        parts = []
        for n in range(0, local, HEAD_DIM):
            head = slice(n, n + HEAD_DIM)
            scores = turned_dot(queries[:, head], keys[:, head], 1, 1) * HEAD_DIM**-0.5
            scores = jnp.exp(scores - jnp.max(scores, axis=-1, keepdims=True))
            weights = scores / jnp.sum(scores, axis=-1, keepdims=True)
            parts.append(
                jnp.dot(weights.astype(bf16), values[:, head], preferred_element_type=f32)
            )
        attended_ref[0, :, h * local : (h + 1) * local] = jnp.concatenate(parts, axis=1).astype(bf16)


def run_attend(images, packed, vectors, qv_bias):
    count, length, width = images.shape
    local = qv_bias.shape[1]
    return call_kernel(
        attend_kernel,
        (count // PAIR,),
        [by_step(images, PAIR), whole(packed), whole(vectors), whole(qv_bias)],
        [
            ((count // PAIR, length, PAIR * local), jnp.bfloat16, (1, length, PAIR * local), lambda p: (p, 0, 0)),
            ((count, length, 3 * local), jnp.bfloat16, (PAIR, length, 3 * local), lambda p: (p, 0, 0)),
        ],
        flops=2 * count * length * local * (3 * width + 4 * length),
    )


def slot_hits(target_row, count):
    return lax.broadcasted_iota(jnp.int32, (count, target_row.shape[1]), 0) == target_row


def route_kernel(
    router_at,
    images_ref,
    cot_ref,
    attended_ref,
    out_ref,
    packed_ref,
    vector_ref,
    routes_ref,
    target_ref,
    mixed_ref,
    probs_ref,
    sent_ref,
    sum_ref,
    gate_ref,
):
    f32, bf16 = jnp.float32, jnp.bfloat16
    slots = sum_ref.shape[1]
    tensor, local = attended_ref.shape[0], attended_ref.shape[3] // images_ref.shape[0]
    at = pl.program_id(0)

    @pl.when(at == 0)
    def _():
        sum_ref[...] = jnp.zeros_like(sum_ref)
        gate_ref[...] = jnp.zeros_like(gate_ref)

    router = packed_ref[:, router_at : router_at + EXPERTS]
    for h in range(images_ref.shape[0]):
        mixed = images_ref[h].astype(f32) + vector_ref[2:3]
        for z in range(tensor):
            part = attended_ref[z, 0, :, h * local : (h + 1) * local]
            weight = out_ref[z * local : (z + 1) * local]
            mixed = mixed + jnp.dot(part, weight, preferred_element_type=f32)
        mixed_ref[h] = mixed
        scaled, _ = norm_rows(mixed)
        routed = (scaled * vector_ref[3:4] + vector_ref[4:5]).astype(bf16)
        logits = jnp.dot(routed, router, preferred_element_type=f32)
        logits = jnp.exp(logits - jnp.max(logits, axis=-1, keepdims=True))
        probs = logits / jnp.sum(logits, axis=-1, keepdims=True)
        probs_ref[h] = probs
        experts = lax.broadcasted_iota(jnp.int32, probs.shape, 1)
        fill = jnp.zeros((slots, probs.shape[0]), f32)
        for k in range(TOPK):
            match = experts == routes_ref[h, :, k : k + 1]
            gate = jnp.sum(jnp.where(match, probs, 0.0), axis=1, keepdims=True)
            high = gate.astype(bf16)
            low = (gate - high.astype(f32)).astype(bf16)
            pair = jnp.concatenate([high, low, jnp.zeros((gate.shape[0], 6), bf16)], axis=1)
            hit = slot_hits(target_ref[h, k : k + 1], slots).astype(f32)
            fill = fill + hit
            gate_ref[...] += turned_dot(pair, hit.astype(bf16), 0, 1)
        fill = fill.astype(bf16)
        sum_ref[0] += jnp.dot(fill, routed, preferred_element_type=f32)
        sum_ref[1] += jnp.dot(fill, cot_ref[h], preferred_element_type=f32)

    @pl.when(at == pl.num_programs(0) - 1)
    def _():
        groups, lines, width = sent_ref.shape
        here = slots // groups
        for g in range(groups):
            lanes = slice(g * here, (g + 1) * here)
            sent_ref[g, :here] = sum_ref[0, lanes].astype(bf16)
            sent_ref[g, here : 2 * here] = sum_ref[1, lanes].astype(bf16)
            gates = jnp.concatenate([gate_ref[:, lanes], jnp.zeros((8, width - here), f32)], axis=1)
            gates = jnp.concatenate([gates, jnp.zeros((lines - 2 * here - 8, width), f32)], axis=0)
            sent_ref[g, 2 * here :] = gates.astype(bf16)


def run_route(
    images, cot, attended_all, out_whole, packed, vectors, routes, plane_target, groups, slots_plane
):
    f32, bf16 = jnp.float32, jnp.bfloat16
    count, length, width = images.shape
    tensor = attended_all.shape[0]
    sent = (groups, 2 * slots_plane // groups + EXTRA, width)
    return call_kernel(
        functools.partial(route_kernel, tensor * attended_all.shape[3] // PAIR),
        (count // PAIR,),
        [
            by_step(images, PAIR),
            by_step(cot, PAIR),
            (attended_all, (tensor, 1, *attended_all.shape[2:]), lambda p: (0, p, 0, 0)),
            whole(out_whole),
            whole(packed),
            whole(vectors),
            by_step(routes, PAIR),
            by_step(plane_target, PAIR),
        ],
        [
            ((count, length, width), f32, (PAIR, length, width), lambda p: (p, 0, 0)),
            ((count, length, EXPERTS), f32, (PAIR, length, EXPERTS), lambda p: (p, 0, 0)),
            (sent, bf16, sent, lambda p: (0, 0, 0)),
        ],
        [pltpu.VMEM((2, slots_plane, width), f32), pltpu.VMEM((8, slots_plane), f32)],
        flops=2 * count * length * width * (width + 2 * slots_plane),
    )


def slot_blocks(parts_ref, slots_ref, outer, inner):
    here = parts_ref.shape[2]
    for b in range(slots_ref.shape[1] // here):
        first = (b // inner) * outer * inner + b % inner
        total = parts_ref[first].astype(jnp.float32)
        for o in range(1, outer):
            total = total + parts_ref[first + o * inner].astype(jnp.float32)
        slots_ref[:, b * here : (b + 1) * here] = total


def token_hits(target_column, count):
    return lax.broadcasted_iota(jnp.int32, (target_column.shape[0], count), 1) == target_column


def take_grads_kernel(outer, inner, parts_ref, target_ref, rows_ref, gates_ref, slots_ref):
    f32, bf16 = jnp.float32, jnp.bfloat16
    slots = slots_ref.shape[1]
    local = rows_ref.shape[2] // target_ref.shape[0]

    @pl.when(pl.program_id(0) == 0)
    def _():
        slot_blocks(parts_ref, slots_ref, outer, inner)

    grads = slots_ref[:local].astype(bf16)
    gate_terms = slots_ref[local : local + 1] + slots_ref[local + 1 : local + 2]
    for h in range(target_ref.shape[0]):
        hits = [token_hits(target_ref[h, :, k : k + 1], slots) for k in range(TOPK)]
        find = jnp.logical_or(hits[0], hits[1]).astype(f32).astype(bf16)
        rows_ref[0, :, h * local : (h + 1) * local] = turned_dot(find, grads, 1, 1).astype(bf16)
        terms = [
            jnp.sum(jnp.where(hit, gate_terms, 0.0), axis=1, keepdims=True) for hit in hits
        ]
        gates_ref[h] = jnp.concatenate(terms, axis=1)


def run_take_grads(parts, target, local, outer, inner, slots):
    count, length, _ = target.shape
    return call_kernel(
        functools.partial(take_grads_kernel, outer, inner),
        (count // PAIR,),
        [whole(parts), by_step(target, PAIR)],
        [
            ((count // PAIR, length, PAIR * local), jnp.bfloat16, (1, length, PAIR * local), lambda p: (p, 0, 0)),
            ((count, length, TOPK), jnp.float32, (PAIR, length, TOPK), lambda p: (p, 0, 0)),
        ],
        [pltpu.VMEM((parts.shape[1], slots), jnp.float32)],
        flops=2 * count * length * slots * local,
    )


def take_rows_kernel(
    outer, inner, held_ref, parts_ref, target_ref, probs_ref, routes_ref, mixed_ref, out_ref, slots_ref
):
    f32, bf16 = jnp.float32, jnp.bfloat16
    slots = slots_ref.shape[1]
    pair = target_ref.shape[0]
    local = out_ref.shape[2] // pair
    at = pl.program_id(0)

    @pl.when(at == 0)
    def _():
        slot_blocks(parts_ref, slots_ref, outer, inner)

    returned = slots_ref[...].astype(bf16)
    for h in range(pair):
        probs = probs_ref[h]
        experts = lax.broadcasted_iota(jnp.int32, probs.shape, 1)
        rows = mixed_ref[h]
        for k in range(TOPK):
            match = experts == routes_ref[h, :, k : k + 1]
            gate = jnp.sum(jnp.where(match, probs, 0.0), axis=1, keepdims=True)
            find = token_hits(target_ref[h, :, k : k + 1], slots).astype(f32).astype(bf16)
            rows = rows + gate * turned_dot(find, returned, 1, 1)
        live = (at * pair + h < held_ref[0]).astype(f32)
        out_ref[0, :, h * local : (h + 1) * local] = (live * rows).astype(bf16)


def run_take_rows(held, parts, target, probs, routes, mixed_cut, outer, inner, slots):
    count, length, local = mixed_cut.shape
    return call_kernel(
        functools.partial(take_rows_kernel, outer, inner),
        (count // PAIR,),
        [
            (held, None, None),
            whole(parts),
            by_step(target, PAIR),
            by_step(probs, PAIR),
            by_step(routes, PAIR),
            by_step(mixed_cut, PAIR),
        ],
        [((count // PAIR, length, PAIR * local), jnp.bfloat16, (1, length, PAIR * local), lambda p: (p, 0, 0))],
        [pltpu.VMEM((parts.shape[1], slots), jnp.float32)],
        flops=4 * count * length * slots * local,
    )[0]


def pull_kernel(
    router_at,
    held_ref,
    images_ref,
    cot_ref,
    mixed_ref,
    probs_ref,
    routes_ref,
    gates_ref,
    rows_ref,
    attended_ref,
    proj_ref,
    packed_ref,
    vector_ref,
    grad_mixed_ref,
    normed_ref,
    matrix_ref,
    sums_ref,
    matrix_sum_ref,
):
    f32, bf16 = jnp.float32, jnp.bfloat16
    pair = images_ref.shape[0]
    tensor = rows_ref.shape[0]
    local = attended_ref.shape[2] // pair
    width = images_ref.shape[2]
    at = pl.program_id(0)

    @pl.when(at == 0)
    def _():
        sums_ref[...] = jnp.zeros_like(sums_ref)
        matrix_sum_ref[...] = jnp.zeros_like(matrix_sum_ref)

    qkv = packed_ref[:, : 3 * local]
    out_turned = packed_ref[:, 3 * local : 4 * local]
    router = packed_ref[:, router_at : router_at + EXPERTS]
    scale = HEAD_DIM**-0.5
    for h in range(pair):
        lanes = slice(h * local, (h + 1) * local)
        live = (at * pair + h < held_ref[0]).astype(f32)
        cot = cot_ref[h].astype(f32) * live
        scaled, inv_std = norm_rows(mixed_ref[h])
        routed = (scaled * vector_ref[3:4] + vector_ref[4:5]).astype(bf16)
        probs = probs_ref[h]
        experts = lax.broadcasted_iota(jnp.int32, probs.shape, 1)
        grad_probs = jnp.zeros(probs.shape, f32)
        for k in range(TOPK):
            match = experts == routes_ref[h, :, k : k + 1]
            grad_probs = grad_probs + jnp.where(match, gates_ref[h, :, k : k + 1], 0.0)
        grad_logits = probs * (grad_probs - jnp.sum(probs * grad_probs, axis=-1, keepdims=True))
        grad_logits = grad_logits.astype(bf16)
        grad_routed = jnp.concatenate([rows_ref[z, 0, :, lanes] for z in range(tensor)], axis=1)
        grad_routed = grad_routed.astype(f32) + turned_dot(grad_logits, router, 1, 1)
        grad_mixed = cot + norm_rows_back(grad_routed, scaled, inv_std, vector_ref[3:4])
        grad_mixed_ref[h] = grad_mixed
        low = grad_mixed.astype(bf16)
        grad_attended = jnp.dot(low, out_turned, preferred_element_type=f32).astype(bf16)
        proj = proj_ref[h]
        grads = [[], [], []]
        for n in range(0, local, HEAD_DIM):
            queries = proj[:, n : n + HEAD_DIM]
            keys = proj[:, local + n : local + n + HEAD_DIM]
            values = proj[:, 2 * local + n : 2 * local + n + HEAD_DIM]
            grad_head = grad_attended[:, n : n + HEAD_DIM]
            scores = turned_dot(queries, keys, 1, 1) * scale
            scores = jnp.exp(scores - jnp.max(scores, axis=-1, keepdims=True))
            weights = scores / jnp.sum(scores, axis=-1, keepdims=True)
            grads[2].append(turned_dot(weights.astype(bf16), grad_head, 0, 0))
            grad_weights = turned_dot(grad_head, values, 1, 1)
            inner = jnp.sum(weights * grad_weights, axis=-1, keepdims=True)
            grad_scores = (weights * (grad_weights - inner)).astype(bf16)
            grads[0].append(jnp.dot(grad_scores, keys, preferred_element_type=f32) * scale)
            grads[1].append(turned_dot(grad_scores, queries, 0, 0) * scale)
        grad_proj = jnp.concatenate(grads[0] + grads[1] + grads[2], axis=1)
        proj_sum = jnp.sum(grad_proj, axis=0, keepdims=True)
        grad_proj = grad_proj.astype(bf16)
        first, _ = norm_rows(images_ref[h].astype(f32))
        normed = (first * vector_ref[0:1] + vector_ref[1:2]).astype(bf16)
        grad_normed = turned_dot(grad_proj, qkv, 1, 1)
        normed_ref[h] = grad_normed.astype(bf16)
        attended = attended_ref[0, :, lanes]
        matrix = jnp.concatenate(
            [
                turned_dot(normed, grad_proj, 0, 0),
                turned_dot(low, attended, 0, 0),
                turned_dot(routed, grad_logits, 0, 0),
            ],
            axis=1,
        )
        matrix_sum_ref[...] += matrix
        column = lambda values: jnp.sum(values, axis=0, keepdims=True)
        sums_ref[2:3] += column(grad_mixed)
        sums_ref[3:4] += column(grad_routed * scaled)
        sums_ref[4:5] += column(grad_routed)
        sums_ref[5:6, : 3 * local] += proj_sum

    @pl.when(at == pl.num_programs(0) - 1)
    def _():
        matrix_ref[...] = matrix_sum_ref[...].astype(bf16)


def run_pull(held, images, cot, mixed, probs, routes, gates, rows_all, attended, proj, packed, vectors, router_at):
    f32, bf16 = jnp.float32, jnp.bfloat16
    count, length, width = images.shape
    tensor = rows_all.shape[0]
    local = proj.shape[2] // 3
    tokens = (count, length, width)
    block = (PAIR, length, width)
    step = lambda p: (p, 0, 0)
    still = lambda p: (0, 0)
    matrix = (width, 4 * local + EXPERTS)
    return call_kernel(
        functools.partial(pull_kernel, router_at),
        (count // PAIR,),
        [
            (held, None, None),
            by_step(images, PAIR),
            by_step(cot, PAIR),
            by_step(mixed, PAIR),
            by_step(probs, PAIR),
            by_step(routes, PAIR),
            by_step(gates, PAIR),
            (rows_all, (tensor, 1, *rows_all.shape[2:]), lambda p: (0, p, 0, 0)),
            by_step(attended, 1),
            by_step(proj, PAIR),
            whole(packed),
            whole(vectors),
        ],
        [
            (tokens, f32, block, step),
            (tokens, bf16, block, step),
            (matrix, bf16, matrix, still),
            ((8, width), f32, (8, width), still),
        ],
        [pltpu.VMEM(matrix, f32)],
        flops=2 * count * length * (width * 12 * local + 14 * length * local),
    )


def last_kernel(images_ref, normed_ref, mixed_ref, vector_ref, out_ref, sums_ref):
    @pl.when(pl.program_id(0) == 0)
    def _():
        sums_ref[...] = jnp.zeros_like(sums_ref)

    for h in range(images_ref.shape[0]):
        scaled, inv_std = norm_rows(images_ref[h].astype(jnp.float32))
        grad = normed_ref[h].astype(jnp.float32)
        out_ref[h] = mixed_ref[h] + norm_rows_back(grad, scaled, inv_std, vector_ref[0:1])
        sums_ref[0:1] += jnp.sum(grad * scaled, axis=0, keepdims=True)
        sums_ref[1:2] += jnp.sum(grad, axis=0, keepdims=True)


def run_last(images, grad_normed, grad_mixed, vectors):
    width = images.shape[2]
    return call_kernel(
        last_kernel,
        (images.shape[0],),
        [by_step(images, 1), by_step(grad_normed, 1), by_step(grad_mixed, 1), whole(vectors)],
        [
            (images.shape, jnp.float32, (1, *images.shape[1:]), lambda p: (p, 0, 0)),
            ((8, width), jnp.float32, (8, width), lambda p: (0, 0)),
        ],
    )


def moved_plan(
    images,
    images_held,
    routes,
    slot_index,
    first_gain,
    first_shift,
    w_qkv,
    qv_bias,
    w_out,
    out_bias,
    second_gain,
    second_shift,
    w_router,
    w_in,
    in_bias,
    w_back,
    back_bias,
    cotangent,
):
    f32, bf16 = jnp.float32, jnp.bfloat16
    image_count, seq_len, width = images.shape
    experts_here, shard_width, ff_here = w_in.shape
    data, sources = lax.axis_size(DP), lax.axis_size(EXPERT)
    outer, inner = lax.axis_size(OUTER), lax.axis_size(INNER)
    tensor = outer * inner
    tensor_axes = (OUTER, INNER)
    everywhere = (DP, EXPERT, OUTER, INNER)
    groups = data * sources
    owners = data * inner
    mine = experts_here // owners
    slots = EXPERTS * CAP
    dp_at = lax.axis_index(DP)
    inner_at = lax.axis_index(INNER)
    tensor_at = lax.axis_index(tensor_axes)
    owner_at = dp_at * inner + inner_at
    local_width = w_out.shape[0]
    slice_width = width // tensor
    router_at = 4 * local_width

    packed = jnp.concatenate(
        [
            w_qkv.transpose(1, 0, 2).reshape(shard_width, 3 * local_width),
            w_out.T,
            w_router,
            back_bias.T,
            jnp.stack([first_gain, first_shift, out_bias, second_gain, second_shift], axis=1),
        ],
        axis=1,
    )
    packed = swap(jnp.broadcast_to(packed[None], (data, *packed.shape)), DP).reshape(width, -1)
    out_rows = jnp.concatenate(hop_gather(w_out, tensor_axes), axis=0)
    in_bias_all = jnp.stack(hop_gather(in_bias, INNER))
    packed, out_rows, in_bias_all = lax.optimization_barrier((packed, out_rows, in_bias_all))
    vectors = packed[:, router_at + EXPERTS + experts_here :].T.astype(f32)
    out_whole = jnp.concatenate(hop_gather(out_rows, DP), axis=1)
    in_bias_mine = lax.dynamic_slice_in_dim(in_bias_all, owner_at * mine, mine, 1)
    in_bias_mine = in_bias_mine.transpose(1, 0, 2).astype(f32)

    home, within = routes // experts_here, routes % experts_here
    owner, nth = within // mine, within % mine
    kept = slot_index < CAP
    group_place = (owner // inner) * sources + home
    target = ((group_place * inner + owner % inner) * mine + nth) * CAP + slot_index
    target = jnp.where(kept, target, slots)
    plane_target = (group_place * mine + nth) * CAP + slot_index
    plane_target = jnp.where(jnp.logical_and(kept, owner % inner == inner_at), plane_target, -1)
    plane_target = plane_target.transpose(0, 2, 1)

    attended, proj = run_attend(images, packed, vectors, qv_bias.astype(f32))

    attended, w_in = lax.optimization_barrier((attended, w_in))
    attended_all = lax.all_gather(attended, tensor_axes)
    in_raw = swap(w_in, (DP, INNER))
    attended_all, in_raw, w_back = lax.optimization_barrier((attended_all, in_raw, w_back))
    back_raw = swap(w_back.transpose(0, 2, 1), (DP, INNER))
    chunk_shape = (owners, mine, shard_width, ff_here)
    in_raw, back_raw = in_raw.reshape(chunk_shape), back_raw.reshape(chunk_shape)
    mixed, probs, sent = run_route(
        images,
        cotangent,
        attended_all,
        out_whole,
        packed,
        vectors,
        routes,
        plane_target,
        groups,
        slots // inner,
    )
    sent, back_raw = lax.optimization_barrier((sent, back_raw))
    arrived = swap(sent, (DP, EXPERT))
    back_bias_mine = lax.dynamic_slice_in_dim(packed, router_at + EXPERTS + owner_at * mine, mine, 1)
    back_bias_mine = jnp.where(lax.axis_index(OUTER) == 0, back_bias_mine.astype(f32), 0.0)
    (
        returned_out,
        grads_out,
        hidden_low,
        grad_pre_low,
        grad_turned,
        grad_in_bias_mine,
        grad_back_bias_mine,
    ) = run_experts(
        arrived, in_raw, back_raw, in_bias_mine, back_bias_mine, inner, tensor
    )

    def bring(parts):
        return swap(parts.reshape(groups * tensor, *parts.shape[2:]), everywhere)

    grad_parts = bring(grads_out)
    weight_out = weight_grads(
        arrived, grad_pre_low, grad_turned, hidden_low, grad_in_bias_mine, grad_back_bias_mine, data
    )
    rows_cut, grad_gates = run_take_grads(grad_parts, target, slice_width, outer, inner, slots)
    rows_cut, returned_out = lax.optimization_barrier((rows_cut, returned_out))
    rows_all = lax.all_gather(rows_cut, tensor_axes)
    returned = bring(returned_out)
    rows_all, returned = lax.optimization_barrier((rows_all, returned))
    returned, weight_out = lax.optimization_barrier((returned, weight_out))
    weight_parts = swap(weight_out.reshape(owners, *weight_out.shape[2:]), (DP, INNER))
    grad_mixed, normed_part, matrix, sums = run_pull(
        images_held,
        images,
        cotangent,
        mixed,
        probs,
        routes,
        grad_gates,
        rows_all,
        attended,
        proj,
        packed,
        vectors,
        router_at,
    )
    grad_normed = lax.psum(normed_part, tensor_axes)
    grad_normed, returned = lax.optimization_barrier((grad_normed, returned))
    grad_images, first_sums = run_last(images, grad_normed, grad_mixed, vectors)
    mixed_cut = lax.dynamic_slice_in_dim(mixed, tensor_at * slice_width, slice_width, 2)
    output_cut = run_take_rows(
        images_held, returned, target, probs, routes, mixed_cut, outer, inner, slots
    )
    output = lax.all_gather(output_cut, tensor_axes)
    output = output.reshape(tensor, image_count // PAIR, seq_len, PAIR, slice_width)
    output = output.transpose(1, 3, 2, 0, 4).reshape(images.shape)

    pair_sums = [sums[5, :local_width], sums[5, 2 * local_width : 3 * local_width]]
    pair_sums = jnp.tile(jnp.stack(pair_sums), (1, data))
    vector_grads = jnp.concatenate([first_sums[:2], sums[2:5], pair_sums], axis=0)
    high, low = high_low(vector_grads)
    small = jnp.concatenate([matrix, high.T, low.T], axis=1)
    small, weight_parts = lax.optimization_barrier((small, weight_parts))
    small = swap(small.reshape(groups, shard_width // sources, -1), (DP, EXPERT))
    small = jnp.sum(small.astype(f32), axis=0)
    small = jnp.concatenate(hop_gather(small, EXPERT), axis=0)
    grad_w_qkv = small[:, : 3 * local_width].reshape(shard_width, 3, local_width).transpose(1, 0, 2)
    grad_w_out = small[:, 3 * local_width : router_at].T
    grad_w_router = small[:, router_at : router_at + EXPERTS]
    vector_grads = small[:, router_at + EXPERTS :].T
    vector_grads = vector_grads[:7] + vector_grads[7:]
    grad_w_in, grad_w_back = run_widen(weight_parts, mine, shard_width)
    grad_w_back = grad_w_back.transpose(0, 2, 1)
    lines = weight_parts[:, 2 * mine * shard_width :].astype(f32)
    grad_in_bias = lines[:, : 2 * mine].reshape(owners, mine, 2, ff_here)
    grad_in_bias = jnp.sum(grad_in_bias, axis=2).reshape(experts_here, ff_here)
    lines = lines[:, 2 * mine : 3 * mine].reshape(experts_here, 2, ff_here // 2)
    grad_back_shard = jnp.sum(lines[:, :, :shard_width], axis=1)
    return (
        output,
        grad_images,
        vector_grads[0],
        vector_grads[1],
        grad_w_qkv,
        vector_grads[5:7],
        grad_w_out,
        vector_grads[2],
        vector_grads[3],
        vector_grads[4],
        grad_w_router,
        grad_w_in,
        grad_in_bias,
        grad_w_back,
        grad_back_shard,
    )


def specs(tensor):
    rows = P((DP, EXPERT), None, None)
    vector, square = P(DP), P(tensor, DP)
    qkv, pair, router = P(None, DP, tensor), P(None, tensor), P(DP, None)
    inward, outward = P(EXPERT, DP, tensor), P(EXPERT, tensor, DP)
    params = (vector, vector, qkv, pair, square, vector, vector, vector, router)
    experts = (inward, P(EXPERT, tensor), outward, P(EXPERT, DP))
    taken = (rows, P((DP, EXPERT)), rows, rows, *params, *experts, rows)
    given = (rows, rows, *params, *experts)
    return taken, given


def solution(mesh):
    data, expert, tensor = (mesh.shape[name] for name in (DP, EXPERT, TENSOR))
    inner = FF_PAIR if tensor % FF_PAIR == 0 else 1
    owners = data * inner
    if (EXPERTS // expert) % owners or any(n & (n - 1) for n in (data, expert, tensor)):
        taken, given = specs(TENSOR)
        return jax.shard_map(
            gathered_plan, mesh=mesh, in_specs=taken, out_specs=given, check_vma=False
        )
    devices = mesh.devices.reshape(data, expert, tensor // inner, inner)
    split_mesh = Mesh(devices, (DP, EXPERT, OUTER, INNER))
    taken, given = specs((OUTER, INNER))
    return jax.shard_map(
        moved_plan, mesh=split_mesh, in_specs=taken, out_specs=given, check_vma=False
    )
```

```python
import functools
import math

import jax
import jax.numpy as jnp
from jax import lax
from jax.experimental import pallas as pl
from jax.experimental.pallas import tpu as pltpu
from jax.sharding import Mesh
from jax.sharding import PartitionSpec as P

HEAD_DIM = 64
EXPERTS = 32
TOPK = 2
CAP = 64
FF_PAIR = 1
PAIR = 2
EXTRA = 16
VMEM_LIMIT = 56 * 1024 * 1024
GELU_SCALE = (2.0 / math.pi) ** 0.5
GELU_CUBE = 0.044715

DP = "dp"
EXPERT = "expert"
TENSOR = "tensor"
OUTER = "outer"
INNER = "inner"


EPS = 1e-06


def norm_parts(values, norm_gain, norm_shift):
    average = jnp.mean(values, axis=-1, keepdims=True)
    centred = values - average
    spread = jnp.mean(centred * centred, axis=-1, keepdims=True)
    inv_std = lax.rsqrt(spread + EPS)
    scaled = centred * inv_std
    return (scaled * norm_gain + norm_shift, scaled, inv_std)


def norm_back(grad_out, scaled, inv_std, norm_gain):
    grad_scaled = grad_out * norm_gain
    inner = grad_scaled - jnp.mean(grad_scaled, axis=-1, keepdims=True)
    inner = inner - scaled * jnp.mean(grad_scaled * scaled, axis=-1, keepdims=True)
    return (inner * inv_std, jnp.sum(grad_out * scaled, axis=0), jnp.sum(grad_out, axis=0))


def attention_forward(queries, key_rows, value_rows, scale):
    scores = (
        jnp.einsum("iqhd,ikhd->ihqk", queries, key_rows, preferred_element_type=jnp.float32) * scale
    )
    row_peak = jnp.max(scores, axis=-1, keepdims=True)
    log_total = row_peak + jnp.log(jnp.sum(jnp.exp(scores - row_peak), axis=-1, keepdims=True))
    weights = jnp.exp(scores - log_total).astype(jnp.bfloat16)
    attended = jnp.einsum(
        "ihqk,ikhd->iqhd", weights, value_rows, preferred_element_type=jnp.float32
    )
    return (attended, log_total)


def attention_backward(queries, key_rows, value_rows, log_total, grad_low, scale):
    scores = (
        jnp.einsum("iqhd,ikhd->ihqk", queries, key_rows, preferred_element_type=jnp.float32) * scale
    )
    probs = jnp.exp(scores - log_total)
    weights = probs.astype(jnp.bfloat16)
    grad_values = jnp.einsum(
        "ihqk,iqhd->ikhd", weights, grad_low, preferred_element_type=jnp.float32
    )
    grad_weights = jnp.einsum(
        "iqhd,ikhd->ihqk", grad_low, value_rows, preferred_element_type=jnp.float32
    )
    grad_scores = probs * (grad_weights - jnp.sum(probs * grad_weights, axis=-1, keepdims=True))
    scores_low = grad_scores.astype(jnp.bfloat16)
    grad_queries = (
        jnp.einsum("ihqk,ikhd->iqhd", scores_low, key_rows, preferred_element_type=jnp.float32)
        * scale
    )
    grad_keys = (
        jnp.einsum("ihqk,iqhd->ikhd", scores_low, queries, preferred_element_type=jnp.float32)
        * scale
    )
    return (grad_queries, grad_keys, grad_values)


def gathered_plan(
    images,
    images_held,
    routes,
    slot_index,
    first_gain,
    first_shift,
    w_qkv,
    qv_bias,
    w_out,
    out_bias,
    second_gain,
    second_shift,
    w_router,
    w_in,
    in_bias,
    w_back,
    back_bias,
    cotangent,
):
    image_count, seq_len, width = images.shape
    rows_total = image_count * seq_len
    experts_here = w_in.shape[0]
    (
        gain_first,
        shift_first,
        qkv_full,
        out_full,
        bias_out_full,
        gain_second,
        shift_second,
        router_full,
        in_full,
        back_full,
        back_bias_full,
    ) = (
        lax.all_gather(first_gain, DP, axis=0, tiled=True),
        lax.all_gather(first_shift, DP, axis=0, tiled=True),
        lax.all_gather(w_qkv, DP, axis=1, tiled=True),
        lax.all_gather(w_out, DP, axis=1, tiled=True),
        lax.all_gather(out_bias, DP, axis=0, tiled=True),
        lax.all_gather(second_gain, DP, axis=0, tiled=True),
        lax.all_gather(second_shift, DP, axis=0, tiled=True),
        lax.all_gather(w_router, DP, axis=0, tiled=True),
        lax.all_gather(w_in, DP, axis=1, tiled=True),
        lax.all_gather(w_back, DP, axis=2, tiled=True),
        lax.all_gather(back_bias, DP, axis=1, tiled=True),
    )
    gain_first = gain_first.astype(jnp.float32)
    gain_second = gain_second.astype(jnp.float32)
    inputs = images.reshape(rows_total, width).astype(jnp.float32)
    live_image = (jnp.arange(image_count, dtype=jnp.int32) < images_held[0]).astype(jnp.float32)
    live_rows = jnp.repeat(live_image, seq_len)[:, None]
    normed, scaled_first, inv_first = norm_parts(
        inputs, gain_first, shift_first.astype(jnp.float32)
    )
    normed_low = normed.astype(jnp.bfloat16)
    projected = jnp.einsum("td,cde->cte", normed_low, qkv_full, preferred_element_type=jnp.float32)
    local_width = projected.shape[2]
    head_count = local_width // HEAD_DIM
    head_shape = (image_count, seq_len, head_count, HEAD_DIM)
    bias_pair = qv_bias.astype(jnp.float32)
    queries = (projected[0] + bias_pair[0]).astype(jnp.bfloat16).reshape(head_shape)
    key_rows = projected[1].astype(jnp.bfloat16).reshape(head_shape)
    value_rows = (projected[2] + bias_pair[1]).astype(jnp.bfloat16).reshape(head_shape)
    scale = HEAD_DIM ** (-0.5)
    attended, log_total = attention_forward(queries, key_rows, value_rows, scale)
    attended_low = attended.reshape(rows_total, local_width).astype(jnp.bfloat16)
    head_part = jnp.dot(attended_low, out_full, preferred_element_type=jnp.float32)
    mixed = inputs + lax.psum(head_part, TENSOR) + bias_out_full.astype(jnp.float32)
    routed, scaled_second, inv_second = norm_parts(
        mixed, gain_second, shift_second.astype(jnp.float32)
    )
    routed_low = routed.astype(jnp.bfloat16)
    logits = jnp.dot(routed_low, router_full, preferred_element_type=jnp.float32)
    probs = jax.nn.softmax(logits, axis=-1)
    pair_routes = routes.reshape(rows_total, TOPK)
    pair_slots = slot_index.reshape(rows_total, TOPK)
    target = jnp.where(pair_slots < CAP, pair_routes * CAP + pair_slots, EXPERTS * CAP).reshape(
        rows_total * TOPK
    )
    gates = jnp.take_along_axis(probs, pair_routes, axis=1)
    pair_rows = jnp.repeat(routed_low, TOPK, axis=0)
    outgoing = (
        jnp.zeros((EXPERTS * CAP + 1, width), jnp.bfloat16)
        .at[target]
        .set(pair_rows)[: EXPERTS * CAP]
    )
    outgoing = outgoing.reshape(EXPERTS, 1, CAP, width)
    arrived = lax.all_to_all(outgoing, EXPERT, split_axis=0, concat_axis=1, tiled=True)
    sources = arrived.shape[1]
    expert_rows = arrived.reshape(experts_here, sources * CAP, width)
    hidden_pre = jnp.einsum(
        "erd,edf->erf", expert_rows, in_full, preferred_element_type=jnp.float32
    )
    hidden_pre = hidden_pre + in_bias.astype(jnp.float32)[:, None, :]
    hidden_value, gelu_pull = jax.vjp(jax.nn.gelu, hidden_pre)
    hidden_low = hidden_value.astype(jnp.bfloat16)
    expert_part = jnp.einsum(
        "erf,efd->erd", hidden_low, back_full, preferred_element_type=jnp.float32
    )
    bias_back = back_bias_full.astype(jnp.float32)[:, None, :]
    shares = lax.psum_scatter(
        expert_part.reshape(experts_here, sources, CAP, width),
        TENSOR,
        scatter_dimension=2,
        tiled=True,
    )
    share_low = (shares + bias_back[:, None]).astype(jnp.bfloat16)
    pieces = lax.all_to_all(share_low, EXPERT, split_axis=1, concat_axis=0, tiled=True)
    returned = lax.all_gather(pieces, TENSOR, axis=2, tiled=True)
    padded = jnp.concatenate(
        [returned.reshape(EXPERTS * CAP, width), jnp.zeros((1, width), jnp.bfloat16)], axis=0
    )
    picked = padded[target].astype(jnp.float32).reshape(rows_total, TOPK, width)
    expert_mix = jnp.sum(gates[:, :, None] * picked, axis=1)
    output = (live_rows * (mixed + expert_mix)).astype(jnp.bfloat16).reshape(images.shape)
    grad_rows = cotangent.reshape(rows_total, width).astype(jnp.float32) * live_rows
    grad_gates = jnp.sum(grad_rows[:, None, :] * picked, axis=-1)
    grad_picked = (
        (gates[:, :, None] * grad_rows[:, None, :])
        .astype(jnp.bfloat16)
        .reshape(rows_total * TOPK, width)
    )
    grad_outgoing = (
        jnp.zeros((EXPERTS * CAP + 1, width), jnp.bfloat16)
        .at[target]
        .set(grad_picked)[: EXPERTS * CAP]
    )
    grad_outgoing = grad_outgoing.reshape(EXPERTS, 1, CAP, width)
    grad_arrived = lax.all_to_all(grad_outgoing, EXPERT, split_axis=0, concat_axis=1, tiled=True)
    grad_arrived = grad_arrived.reshape(experts_here, sources * CAP, width)
    grad_back_bias = jnp.sum(grad_arrived.astype(jnp.float32), axis=1)
    grad_back_w = jnp.einsum(
        "erf,erd->efd", hidden_low, grad_arrived, preferred_element_type=jnp.float32
    )
    grad_hidden = jnp.einsum(
        "erd,efd->erf", grad_arrived, back_full, preferred_element_type=jnp.float32
    )
    grad_pre = gelu_pull(grad_hidden)[0]
    grad_in_bias_local = jnp.sum(grad_pre, axis=1)
    grad_pre_low = grad_pre.astype(jnp.bfloat16)
    grad_in_w = jnp.einsum(
        "erd,erf->edf", expert_rows, grad_pre_low, preferred_element_type=jnp.float32
    )
    grad_rows_part = jnp.einsum(
        "erf,edf->erd", grad_pre_low, in_full, preferred_element_type=jnp.float32
    )
    grad_shares = lax.psum_scatter(
        grad_rows_part.reshape(experts_here, sources, CAP, width),
        TENSOR,
        scatter_dimension=2,
        tiled=True,
    ).astype(jnp.bfloat16)
    grad_pieces = lax.all_to_all(grad_shares, EXPERT, split_axis=1, concat_axis=0, tiled=True)
    grad_returned = lax.all_gather(grad_pieces, TENSOR, axis=2, tiled=True)
    grad_padded = jnp.concatenate(
        [grad_returned.reshape(EXPERTS * CAP, width), jnp.zeros((1, width), jnp.bfloat16)], axis=0
    )
    grad_routed = jnp.sum(
        grad_padded[target].astype(jnp.float32).reshape(rows_total, TOPK, width), axis=1
    )
    expert_match = (
        pair_routes[:, :, None] == jnp.arange(EXPERTS, dtype=jnp.int32)[None, None, :]
    ).astype(jnp.float32)
    grad_probs = jnp.sum(expert_match * grad_gates[:, :, None], axis=1)
    grad_logits = probs * (grad_probs - jnp.sum(probs * grad_probs, axis=-1, keepdims=True))
    grad_logits_low = grad_logits.astype(jnp.bfloat16)
    grad_router = jnp.einsum(
        "td,te->de", routed_low, grad_logits_low, preferred_element_type=jnp.float32
    )
    grad_routed = grad_routed + jnp.einsum(
        "te,de->td", grad_logits_low, router_full, preferred_element_type=jnp.float32
    )
    grad_from_norm, grad_gain_second, grad_shift_second = norm_back(
        grad_routed, scaled_second, inv_second, gain_second
    )
    grad_mixed = grad_rows + grad_from_norm
    grad_bias_out = jnp.sum(grad_mixed, axis=0)
    grad_mixed_low = grad_mixed.astype(jnp.bfloat16)
    grad_out_w = jnp.einsum(
        "te,td->ed", attended_low, grad_mixed_low, preferred_element_type=jnp.float32
    )
    grad_attended = jnp.einsum(
        "td,ed->te", grad_mixed_low, out_full, preferred_element_type=jnp.float32
    )
    grad_attended = grad_attended.astype(jnp.bfloat16).reshape(head_shape)
    grad_queries, grad_keys, grad_values = attention_backward(
        queries, key_rows, value_rows, log_total, grad_attended, scale
    )
    grad_queries = grad_queries.reshape(rows_total, local_width)
    grad_keys = grad_keys.reshape(rows_total, local_width)
    grad_values = grad_values.reshape(rows_total, local_width)
    grad_pair_bias = jnp.stack([jnp.sum(grad_queries, axis=0), jnp.sum(grad_values, axis=0)])
    grad_proj_low = jnp.stack([grad_queries, grad_keys, grad_values]).astype(jnp.bfloat16)
    grad_qkv = jnp.einsum(
        "td,cte->cde", normed_low, grad_proj_low, preferred_element_type=jnp.float32
    )
    grad_normed_part = jnp.einsum(
        "cte,cde->td", grad_proj_low, qkv_full, preferred_element_type=jnp.float32
    )
    grad_normed = lax.psum(grad_normed_part, TENSOR)
    grad_from_first, grad_gain_first, grad_shift_first = norm_back(
        grad_normed, scaled_first, inv_first, gain_first
    )
    grad_images = (grad_mixed + grad_from_first).reshape(images.shape)
    expert_start = lax.axis_index(EXPERT) * experts_here
    full_in_bias = lax.dynamic_update_slice(
        jnp.zeros((EXPERTS, grad_in_bias_local.shape[1]), jnp.float32),
        grad_in_bias_local,
        (expert_start, jnp.zeros((), jnp.int32)),
    )
    summed = lax.psum(
        (
            grad_gain_first,
            grad_shift_first,
            grad_qkv,
            grad_pair_bias,
            grad_out_w,
            grad_bias_out,
            grad_gain_second,
            grad_shift_second,
            grad_router,
            full_in_bias,
        ),
        (DP, EXPERT),
    )
    shard_width = width // lax.axis_size(DP)
    shard_start = lax.axis_index(DP) * shard_width
    grad_first_gain = lax.dynamic_slice_in_dim(summed[0], shard_start, shard_width, 0)
    grad_first_shift = lax.dynamic_slice_in_dim(summed[1], shard_start, shard_width, 0)
    grad_w_qkv = lax.dynamic_slice_in_dim(summed[2], shard_start, shard_width, 1)
    grad_qv_bias = summed[3]
    grad_w_out = lax.dynamic_slice_in_dim(summed[4], shard_start, shard_width, 1)
    grad_out_bias = lax.dynamic_slice_in_dim(summed[5], shard_start, shard_width, 0)
    grad_second_gain = lax.dynamic_slice_in_dim(summed[6], shard_start, shard_width, 0)
    grad_second_shift = lax.dynamic_slice_in_dim(summed[7], shard_start, shard_width, 0)
    grad_w_router = lax.dynamic_slice_in_dim(summed[8], shard_start, shard_width, 0)
    grad_in_bias = lax.dynamic_slice_in_dim(summed[9], expert_start, experts_here, 0)
    grad_w_in, grad_w_back, grad_back_shard = (
        lax.psum_scatter(grad_in_w, DP, scatter_dimension=1, tiled=True),
        lax.psum_scatter(grad_back_w, DP, scatter_dimension=2, tiled=True),
        lax.psum_scatter(grad_back_bias, DP, scatter_dimension=1, tiled=True),
    )
    return (
        output,
        grad_images,
        grad_first_gain,
        grad_first_shift,
        grad_w_qkv,
        grad_qv_bias,
        grad_w_out,
        grad_out_bias,
        grad_second_gain,
        grad_second_shift,
        grad_w_router,
        grad_w_in,
        grad_in_bias,
        grad_w_back,
        grad_back_shard,
    )


def swap(values, axes):
    return lax.all_to_all(values, axes, split_axis=0, concat_axis=0, tiled=True)


def hop_gather(values, axes):
    count, at = lax.axis_size(axes), lax.axis_index(axes)
    hops = [values]
    for s in range(1, count):
        hops.append(lax.ppermute(values, axes, [(i, i ^ s) for i in range(count)]))
    gathered = []
    for i in range(count):
        found = hops[0]
        for s in range(1, count):
            found = jnp.where(at ^ i == s, hops[s], found)
        gathered.append(found)
    return gathered


def cross(values, s):
    count = lax.axis_size((DP, INNER))
    return lax.ppermute(values, (DP, INNER), [(i, i ^ s) for i in range(count)]) if s else values


def high_low(values):
    high = lax.reduce_precision(values, 8, 7)
    return high.astype(jnp.bfloat16), (values - high).astype(jnp.bfloat16)


def turned_dot(left, right, left_dim, right_dim):
    return lax.dot_general(
        left, right, (((left_dim,), (right_dim,)), ((), ())), preferred_element_type=jnp.float32
    )


def expert_kernel(inner, owners, at_ref, rows_ref, gate_ref, cot_ref, in_bias_ref, back_bias_ref, *refs):
    in_refs, back_refs, refs = refs[:owners], refs[owners : 2 * owners], refs[2 * owners :]
    returned_ref, grads_ref, hidden_ref, grad_pre_ref, grad_turned_ref = refs[:5]
    grad_in_bias_ref, grad_back_bias_ref, weight_ref = refs[5:]
    f32, bf16 = jnp.float32, jnp.bfloat16
    groups, cap, width = rows_ref.shape
    depth = in_refs[0].shape[1]
    for s in range(owners):
        source = at_ref[0] ^ s
        place = pl.ds(pl.multiple_of((source // inner) * depth, depth), depth)
        weight_ref[0, source % inner, place] = in_refs[s][0]
        weight_ref[1, source % inner, place] = back_refs[s][0]
    tensor, slice_width = returned_ref.shape[1:3]
    mine = back_bias_ref.shape[1]
    total = groups * cap
    at = pl.program_id(0)
    rows = rows_ref[...].reshape(total, width)
    cot_turned = cot_ref[...].reshape(total, width).T.astype(f32)
    pair = gate_ref[:, 0:1, :].astype(f32) + gate_ref[:, 1:2, :].astype(f32)
    pair = pair.reshape(groups, pair.shape[-1])
    gate = jnp.zeros((groups, cap), f32)
    for j in range(mine):
        gate = jnp.where(at == j, pair[:, j * cap : (j + 1) * cap], gate)
    gate = jnp.concatenate([gate[g : g + 1, :] for g in range(groups)], axis=1)
    grad_turned = (cot_turned * gate).astype(bf16)
    grad_turned_ref[0] = grad_turned
    grad_returned = grad_turned.T
    grad_back_bias_ref[0] = jnp.sum(grad_returned.astype(f32), axis=0, keepdims=True)
    bias_columns = back_bias_ref[...]
    bias = jnp.zeros((width, 1), f32)
    for j in range(mine):
        bias = jnp.where(at == j, bias_columns[:, j : j + 1], bias)
    part = jnp.broadcast_to(bias, (width, total))
    back = jnp.zeros((width, total), f32)
    for t in range(inner):
        w_in, w_back = weight_ref[0, t], weight_ref[1, t]
        pre = jnp.dot(rows, w_in, preferred_element_type=f32) + in_bias_ref[0, t : t + 1, :]
        square = pre * pre
        bent = jnp.tanh(GELU_SCALE * pre * (1.0 + GELU_CUBE * square))
        half = 0.5 * (1.0 + bent)
        hidden = (pre * half).astype(bf16)
        slope = half + (0.5 * GELU_SCALE) * pre * (1.0 - bent * bent) * (
            1.0 + (3.0 * GELU_CUBE) * square
        )
        hidden_ref[0, t] = hidden
        grad_pre = jnp.dot(grad_returned, w_back, preferred_element_type=f32) * slope
        grad_in_bias_ref[0, t : t + 1, :] = jnp.sum(grad_pre, axis=0, keepdims=True)
        grad_pre = grad_pre.astype(bf16)
        grad_pre_ref[0, t] = grad_pre
        part = part + turned_dot(w_back, hidden, 1, 1)
        back = back + turned_dot(w_in, grad_pre, 1, 1)
    gate_terms = jnp.sum(part * cot_turned, axis=0, keepdims=True)
    high = gate_terms.astype(bf16)
    low = (gate_terms - high.astype(f32)).astype(bf16)
    extra = grads_ref.shape[2] - slice_width
    tail = jnp.concatenate([high, low, jnp.zeros((extra - 2, total), bf16)], axis=0)
    part = part.astype(bf16)
    back = back.astype(bf16)
    for j in range(mine):

        @pl.when(at == j)
        def _():
            lanes = slice(j * cap, (j + 1) * cap)
            for g in range(groups):
                mine_lanes = slice(g * cap, (g + 1) * cap)
                for z in range(tensor):
                    features = slice(z * slice_width, (z + 1) * slice_width)
                    returned_ref[g, z, :, lanes] = part[features, mine_lanes]
                    grads_ref[g, z, :slice_width, lanes] = back[features, mine_lanes]
                    grads_ref[g, z, slice_width:, lanes] = tail[:, mine_lanes]


def run_experts(owner_at, arrived, in_pieces, back_pieces, in_bias, back_bias, inner, tensor):
    f32, bf16 = jnp.float32, jnp.bfloat16
    groups, _, width = arrived.shape
    owners = len(in_pieces)
    mine, depth, ff = in_pieces[0].shape
    total = groups * CAP
    slice_width = width // tensor
    gate_at = 2 * mine * CAP // EXTRA
    outs = [
        ((groups, tensor, slice_width, mine * CAP), bf16, lambda j: (0, 0, 0, 0), None),
        ((groups, tensor, slice_width + EXTRA, mine * CAP), bf16, lambda j: (0, 0, 0, 0), None),
        ((mine, inner, total, ff), bf16, lambda j: (j, 0, 0, 0), 1),
        ((mine, inner, total, ff), bf16, lambda j: (j, 0, 0, 0), 1),
        ((mine, width, total), bf16, lambda j: (j, 0, 0), 1),
        ((mine, inner, ff), f32, lambda j: (j, 0, 0), 1),
        ((mine, 1, width), f32, lambda j: (j, 0, 0), 1),
    ]
    return pl.pallas_call(
        functools.partial(expert_kernel, inner, owners),
        grid=(mine,),
        in_specs=[
            pl.BlockSpec(memory_space=pltpu.SMEM),
            pl.BlockSpec((groups, CAP, width), lambda j: (0, j, 0)),
            pl.BlockSpec((groups, EXTRA, mine * CAP), lambda j: (0, gate_at, 0)),
            pl.BlockSpec((groups, CAP, width), lambda j: (0, mine + j, 0)),
            pl.BlockSpec((1, inner, ff), lambda j: (j, 0, 0)),
            pl.BlockSpec((width, mine), lambda j: (0, 0)),
        ]
        + [pl.BlockSpec((1, depth, ff), lambda j: (j, 0, 0))] * (2 * owners),
        out_specs=[
            pl.BlockSpec(shape if lead is None else (lead, *shape[1:]), index)
            for shape, _, index, lead in outs
        ],
        out_shape=[jax.ShapeDtypeStruct(shape, dtype) for shape, dtype, _, _ in outs],
        scratch_shapes=[pltpu.VMEM((2, inner, width, ff), bf16)],
        compiler_params=pltpu.CompilerParams(vmem_limit_bytes=VMEM_LIMIT),
        cost_estimate=pl.CostEstimate(
            flops=8 * mine * total * width * inner * ff,
            bytes_accessed=4 * owners * mine * depth * ff + 12 * mine * total * inner * ff,
            transcendentals=mine * total * inner * ff,
        ),
    )(owner_at.reshape(1), arrived, arrived, arrived, in_bias, back_bias, *in_pieces, *back_pieces)


def weight_kernel(
    inner,
    at_ref,
    rows_ref,
    grad_pre_ref,
    grad_turned_ref,
    hidden_ref,
    in_bias_ref,
    back_bias_ref,
    *refs,
):
    f32, bf16 = jnp.float32, jnp.bfloat16
    out_refs, sums_ref, tail_ref = refs[:-2], refs[-2], refs[-1]
    groups, cap, width = rows_ref.shape
    mine = back_bias_ref.shape[0]
    ff = sums_ref.shape[-1]
    depth = width * inner // len(out_refs)
    data = width // depth
    part, at = pl.program_id(0), pl.program_id(1)
    rows = rows_ref[...].reshape(groups * cap, width)
    sums_ref[0] = turned_dot(rows, grad_pre_ref[0, 0], 0, 0).astype(bf16)
    grad_back = jnp.dot(grad_turned_ref[0], hidden_ref[0, 0], preferred_element_type=f32)
    sums_ref[1] = grad_back.astype(bf16)

    @pl.when(at == mine - 1)
    def _():
        pairs = []
        for j in range(mine):
            values = in_bias_ref[j, 0]
            high = values.astype(bf16).astype(f32)
            pairs += [high, values - high]
        for d in range(data):
            lines = list(pairs)
            for j in range(mine):
                values = back_bias_ref[j, :, d * depth : (d + 1) * depth]
                high = values.astype(bf16).astype(f32)
                gap = jnp.zeros((1, ff // 2 - depth), f32)
                lines.append(jnp.concatenate([high, gap, values - high, gap], axis=1))
            lines.append(jnp.zeros((EXTRA - len(lines), ff), f32))
            tail_ref[d] = jnp.concatenate(lines, axis=0).astype(bf16)

    for s, out_ref in enumerate(out_refs):
        owner = at_ref[0] ^ s
        d = owner // inner
        place = pl.ds(pl.multiple_of(d * depth, depth), depth)

        @pl.when(owner % inner == part)
        def _():
            for k in range(2):
                line = pl.multiple_of((k * mine + at) * depth, depth)
                out_ref[pl.ds(line, depth)] = sums_ref[k, place]

            @pl.when(at == mine - 1)
            def _():
                out_ref[2 * mine * depth :] = tail_ref[d]


def weight_grads(
    owner_at, arrived, grad_pre, grad_turned, hidden, grad_in_bias, grad_back_bias, owners
):
    mine, inner, total, ff = hidden.shape
    groups, _, width = arrived.shape
    depth = width * inner // owners
    kept = pl.BlockSpec((1, 1, total, ff), lambda t, j: (j, t, 0, 0))
    out = (2 * mine * depth + EXTRA, ff)
    return pl.pallas_call(
        functools.partial(weight_kernel, inner),
        grid=(inner, mine),
        in_specs=[
            pl.BlockSpec(memory_space=pltpu.SMEM),
            pl.BlockSpec((groups, CAP, width), lambda t, j: (0, j, 0)),
            kept,
            pl.BlockSpec((1, width, total), lambda t, j: (j, 0, 0)),
            kept,
            pl.BlockSpec((mine, 1, 1, ff), lambda t, j: (0, t, 0, 0)),
            pl.BlockSpec((mine, 1, width), lambda t, j: (0, 0, 0)),
        ],
        out_specs=[pl.BlockSpec(out, lambda t, j: (0, 0))] * owners,
        out_shape=[jax.ShapeDtypeStruct(out, jnp.bfloat16)] * owners,
        scratch_shapes=[
            pltpu.VMEM((2, width, ff), jnp.bfloat16),
            pltpu.VMEM((width // depth, EXTRA, ff), jnp.bfloat16),
        ],
        compiler_params=pltpu.CompilerParams(vmem_limit_bytes=VMEM_LIMIT),
        cost_estimate=pl.CostEstimate(
            flops=4 * mine * total * width * inner * ff,
            bytes_accessed=4 * mine * inner * (total + width) * ff,
            transcendentals=0,
        ),
    )(
        owner_at.reshape(1),
        arrived,
        grad_pre,
        grad_turned,
        hidden,
        grad_in_bias[:, :, None],
        grad_back_bias,
    )


def widen_kernel(at_ref, *refs):
    part_refs, (in_ref, back_ref) = refs[:-2], refs[-2:]
    mine, depth, ff = in_ref.shape
    rows = mine * depth
    for s, part_ref in enumerate(part_refs):

        @pl.when(pl.program_id(0) == s)
        def _():
            in_ref[...] = part_ref[:rows].astype(jnp.float32).reshape(mine, depth, ff)
            back_ref[...] = part_ref[rows : 2 * rows].astype(jnp.float32).reshape(mine, depth, ff)


def run_widen(owner_at, parts, mine, depth):
    owners, ff = len(parts), parts[0].shape[1]
    out = pl.BlockSpec((mine, depth, ff), lambda p, at: (at[0] ^ p, 0, 0))
    return pl.pallas_call(
        widen_kernel,
        grid_spec=pltpu.PrefetchScalarGridSpec(
            num_scalar_prefetch=1,
            grid=(owners,),
            in_specs=[pl.BlockSpec((2 * mine * depth, ff), lambda p, at: (0, 0))] * owners,
            out_specs=[out, out],
        ),
        out_shape=[jax.ShapeDtypeStruct((owners * mine, depth, ff), jnp.float32)] * 2,
        compiler_params=pltpu.CompilerParams(vmem_limit_bytes=VMEM_LIMIT),
    )(owner_at.reshape(1), *parts)


def norm_rows(values):
    average = jnp.mean(values, axis=-1, keepdims=True)
    centred = values - average
    spread = jnp.mean(centred * centred, axis=-1, keepdims=True)
    inv_std = lax.rsqrt(spread + EPS)
    return centred * inv_std, inv_std


def norm_rows_back(grad_out, scaled, inv_std, norm_gain):
    grad_scaled = grad_out * norm_gain
    inner = grad_scaled - jnp.mean(grad_scaled, axis=-1, keepdims=True)
    inner = inner - scaled * jnp.mean(grad_scaled * scaled, axis=-1, keepdims=True)
    return inner * inv_std


def call_kernel(kernel, grid, inputs, outputs, scratch=(), flops=0):
    smem = pl.BlockSpec(memory_space=pltpu.SMEM)
    return pl.pallas_call(
        kernel,
        grid=grid,
        in_specs=[smem if b is None else pl.BlockSpec(b, i) for _, b, i in inputs],
        out_specs=[pl.BlockSpec(b, i) for _, _, b, i in outputs],
        out_shape=[jax.ShapeDtypeStruct(shape, dtype) for shape, dtype, _, _ in outputs],
        scratch_shapes=list(scratch),
        compiler_params=pltpu.CompilerParams(vmem_limit_bytes=VMEM_LIMIT),
        cost_estimate=pl.CostEstimate(
            flops=flops,
            bytes_accessed=sum(a.size * a.dtype.itemsize for a, _, _ in inputs),
            transcendentals=0,
        ),
    )(*(a for a, _, _ in inputs))


def whole(array):
    return array, array.shape, lambda p: (0,) * array.ndim


def by_step(array, lead):
    return array, (lead, *array.shape[1:]), lambda p: (p,) + (0,) * (array.ndim - 1)


def attend_kernel(images_ref, packed_ref, vector_ref, bias_ref, attended_ref, proj_ref):
    f32, bf16 = jnp.float32, jnp.bfloat16
    local = bias_ref.shape[1]
    weight = packed_ref[:, : 3 * local]
    for h in range(images_ref.shape[0]):
        scaled, _ = norm_rows(images_ref[h].astype(f32))
        normed = (scaled * vector_ref[0:1] + vector_ref[1:2]).astype(bf16)
        proj = jnp.dot(normed, weight, preferred_element_type=f32)
        queries = (proj[:, :local] + bias_ref[0:1]).astype(bf16)
        keys = proj[:, local : 2 * local].astype(bf16)
        values = (proj[:, 2 * local :] + bias_ref[1:2]).astype(bf16)
        proj_ref[h] = jnp.concatenate([queries, keys, values], axis=1)
        parts = []
        for n in range(0, local, HEAD_DIM):
            head = slice(n, n + HEAD_DIM)
            scores = turned_dot(queries[:, head], keys[:, head], 1, 1) * HEAD_DIM**-0.5
            scores = jnp.exp(scores - jnp.max(scores, axis=-1, keepdims=True))
            weights = scores / jnp.sum(scores, axis=-1, keepdims=True)
            parts.append(
                jnp.dot(weights.astype(bf16), values[:, head], preferred_element_type=f32)
            )
        attended_ref[0, :, h * local : (h + 1) * local] = jnp.concatenate(parts, axis=1).astype(bf16)


def run_attend(images, packed, vectors, qv_bias):
    count, length, width = images.shape
    local = qv_bias.shape[1]
    return call_kernel(
        attend_kernel,
        (count // PAIR,),
        [by_step(images, PAIR), whole(packed), whole(vectors), whole(qv_bias)],
        [
            ((count // PAIR, length, PAIR * local), jnp.bfloat16, (1, length, PAIR * local), lambda p: (p, 0, 0)),
            ((count, length, 3 * local), jnp.bfloat16, (PAIR, length, 3 * local), lambda p: (p, 0, 0)),
        ],
        flops=2 * count * length * local * (3 * width + 4 * length),
    )


def slot_hits(target_row, count):
    return lax.broadcasted_iota(jnp.int32, (count, target_row.shape[1]), 0) == target_row


def route_kernel(
    router_at,
    images_ref,
    cot_ref,
    attended_ref,
    out_ref,
    packed_ref,
    vector_ref,
    routes_ref,
    target_ref,
    mixed_ref,
    probs_ref,
    sent_ref,
    sum_ref,
    gate_ref,
):
    f32, bf16 = jnp.float32, jnp.bfloat16
    slots = sum_ref.shape[1]
    tensor, local = attended_ref.shape[0], attended_ref.shape[3] // images_ref.shape[0]
    at = pl.program_id(0)

    @pl.when(at == 0)
    def _():
        sum_ref[...] = jnp.zeros_like(sum_ref)
        gate_ref[...] = jnp.zeros_like(gate_ref)

    router = packed_ref[:, router_at : router_at + EXPERTS]
    for h in range(images_ref.shape[0]):
        mixed = images_ref[h].astype(f32) + vector_ref[2:3]
        for z in range(tensor):
            part = attended_ref[z, 0, :, h * local : (h + 1) * local]
            weight = out_ref[z * local : (z + 1) * local]
            mixed = mixed + jnp.dot(part, weight, preferred_element_type=f32)
        mixed_ref[h] = mixed
        scaled, _ = norm_rows(mixed)
        routed = (scaled * vector_ref[3:4] + vector_ref[4:5]).astype(bf16)
        logits = jnp.dot(routed, router, preferred_element_type=f32)
        logits = jnp.exp(logits - jnp.max(logits, axis=-1, keepdims=True))
        probs = logits / jnp.sum(logits, axis=-1, keepdims=True)
        probs_ref[h] = probs
        experts = lax.broadcasted_iota(jnp.int32, probs.shape, 1)
        fill = jnp.zeros((slots, probs.shape[0]), f32)
        for k in range(TOPK):
            match = experts == routes_ref[h, :, k : k + 1]
            gate = jnp.sum(jnp.where(match, probs, 0.0), axis=1, keepdims=True)
            high = gate.astype(bf16)
            low = (gate - high.astype(f32)).astype(bf16)
            pair = jnp.concatenate([high, low, jnp.zeros((gate.shape[0], 6), bf16)], axis=1)
            hit = slot_hits(target_ref[h, k : k + 1], slots).astype(f32)
            fill = fill + hit
            gate_ref[...] += turned_dot(pair, hit.astype(bf16), 0, 1)
        fill = fill.astype(bf16)
        sum_ref[0] += jnp.dot(fill, routed, preferred_element_type=f32)
        sum_ref[1] += jnp.dot(fill, cot_ref[h], preferred_element_type=f32)

    @pl.when(at == pl.num_programs(0) - 1)
    def _():
        groups, lines, width = sent_ref.shape
        here = slots // groups
        for g in range(groups):
            lanes = slice(g * here, (g + 1) * here)
            sent_ref[g, :here] = sum_ref[0, lanes].astype(bf16)
            sent_ref[g, here : 2 * here] = sum_ref[1, lanes].astype(bf16)
            gates = jnp.concatenate([gate_ref[:, lanes], jnp.zeros((8, width - here), f32)], axis=1)
            gates = jnp.concatenate([gates, jnp.zeros((lines - 2 * here - 8, width), f32)], axis=0)
            sent_ref[g, 2 * here :] = gates.astype(bf16)


def run_route(
    images, cot, attended_all, out_whole, packed, vectors, routes, plane_target, groups, slots_plane
):
    f32, bf16 = jnp.float32, jnp.bfloat16
    count, length, width = images.shape
    tensor = attended_all.shape[0]
    sent = (groups, 2 * slots_plane // groups + EXTRA, width)
    return call_kernel(
        functools.partial(route_kernel, tensor * attended_all.shape[3] // PAIR),
        (count // PAIR,),
        [
            by_step(images, PAIR),
            by_step(cot, PAIR),
            (attended_all, (tensor, 1, *attended_all.shape[2:]), lambda p: (0, p, 0, 0)),
            whole(out_whole),
            whole(packed),
            whole(vectors),
            by_step(routes, PAIR),
            by_step(plane_target, PAIR),
        ],
        [
            ((count, length, width), f32, (PAIR, length, width), lambda p: (p, 0, 0)),
            ((count, length, EXPERTS), f32, (PAIR, length, EXPERTS), lambda p: (p, 0, 0)),
            (sent, bf16, sent, lambda p: (0, 0, 0)),
        ],
        [pltpu.VMEM((2, slots_plane, width), f32), pltpu.VMEM((8, slots_plane), f32)],
        flops=2 * count * length * width * (width + 2 * slots_plane),
    )


def slot_blocks(parts_ref, slots_ref, outer, inner):
    here = parts_ref.shape[2]
    for b in range(slots_ref.shape[1] // here):
        first = (b // inner) * outer * inner + b % inner
        total = parts_ref[first].astype(jnp.float32)
        for o in range(1, outer):
            total = total + parts_ref[first + o * inner].astype(jnp.float32)
        slots_ref[:, b * here : (b + 1) * here] = total


def token_hits(target_column, count):
    return lax.broadcasted_iota(jnp.int32, (target_column.shape[0], count), 1) == target_column


def take_grads_kernel(outer, inner, parts_ref, target_ref, rows_ref, gates_ref, slots_ref):
    f32, bf16 = jnp.float32, jnp.bfloat16
    slots = slots_ref.shape[1]
    local = rows_ref.shape[2] // target_ref.shape[0]

    @pl.when(pl.program_id(0) == 0)
    def _():
        slot_blocks(parts_ref, slots_ref, outer, inner)

    grads = slots_ref[:local].astype(bf16)
    gate_terms = slots_ref[local : local + 1] + slots_ref[local + 1 : local + 2]
    for h in range(target_ref.shape[0]):
        hits = [token_hits(target_ref[h, :, k : k + 1], slots) for k in range(TOPK)]
        find = jnp.logical_or(hits[0], hits[1]).astype(f32).astype(bf16)
        rows_ref[0, :, h * local : (h + 1) * local] = turned_dot(find, grads, 1, 1).astype(bf16)
        terms = [
            jnp.sum(jnp.where(hit, gate_terms, 0.0), axis=1, keepdims=True) for hit in hits
        ]
        gates_ref[h] = jnp.concatenate(terms, axis=1)


def run_take_grads(parts, target, local, outer, inner, slots):
    count, length, _ = target.shape
    return call_kernel(
        functools.partial(take_grads_kernel, outer, inner),
        (count // PAIR,),
        [whole(parts), by_step(target, PAIR)],
        [
            ((count // PAIR, length, PAIR * local), jnp.bfloat16, (1, length, PAIR * local), lambda p: (p, 0, 0)),
            ((count, length, TOPK), jnp.float32, (PAIR, length, TOPK), lambda p: (p, 0, 0)),
        ],
        [pltpu.VMEM((parts.shape[1], slots), jnp.float32)],
        flops=2 * count * length * slots * local,
    )


def take_rows_kernel(
    outer, inner, held_ref, parts_ref, target_ref, probs_ref, routes_ref, mixed_ref, out_ref, slots_ref
):
    f32, bf16 = jnp.float32, jnp.bfloat16
    slots = slots_ref.shape[1]
    pair = target_ref.shape[0]
    local = out_ref.shape[2] // pair
    at = pl.program_id(0)

    @pl.when(at == 0)
    def _():
        slot_blocks(parts_ref, slots_ref, outer, inner)

    returned = slots_ref[...].astype(bf16)
    for h in range(pair):
        probs = probs_ref[h]
        experts = lax.broadcasted_iota(jnp.int32, probs.shape, 1)
        rows = mixed_ref[h]
        for k in range(TOPK):
            match = experts == routes_ref[h, :, k : k + 1]
            gate = jnp.sum(jnp.where(match, probs, 0.0), axis=1, keepdims=True)
            find = token_hits(target_ref[h, :, k : k + 1], slots).astype(f32).astype(bf16)
            rows = rows + gate * turned_dot(find, returned, 1, 1)
        live = (at * pair + h < held_ref[0]).astype(f32)
        out_ref[0, :, h * local : (h + 1) * local] = (live * rows).astype(bf16)


def run_take_rows(held, parts, target, probs, routes, mixed_cut, outer, inner, slots):
    count, length, local = mixed_cut.shape
    return call_kernel(
        functools.partial(take_rows_kernel, outer, inner),
        (count // PAIR,),
        [
            (held, None, None),
            whole(parts),
            by_step(target, PAIR),
            by_step(probs, PAIR),
            by_step(routes, PAIR),
            by_step(mixed_cut, PAIR),
        ],
        [((count // PAIR, length, PAIR * local), jnp.bfloat16, (1, length, PAIR * local), lambda p: (p, 0, 0))],
        [pltpu.VMEM((parts.shape[1], slots), jnp.float32)],
        flops=4 * count * length * slots * local,
    )[0]


def pull_kernel(
    router_at,
    held_ref,
    images_ref,
    cot_ref,
    mixed_ref,
    probs_ref,
    routes_ref,
    gates_ref,
    rows_ref,
    attended_ref,
    proj_ref,
    packed_ref,
    vector_ref,
    grad_mixed_ref,
    normed_ref,
    matrix_ref,
    sums_ref,
    matrix_sum_ref,
):
    f32, bf16 = jnp.float32, jnp.bfloat16
    pair = images_ref.shape[0]
    tensor = rows_ref.shape[0]
    local = attended_ref.shape[2] // pair
    width = images_ref.shape[2]
    at = pl.program_id(0)

    @pl.when(at == 0)
    def _():
        sums_ref[...] = jnp.zeros_like(sums_ref)
        matrix_sum_ref[...] = jnp.zeros_like(matrix_sum_ref)

    qkv = packed_ref[:, : 3 * local]
    out_turned = packed_ref[:, 3 * local : 4 * local]
    router = packed_ref[:, router_at : router_at + EXPERTS]
    scale = HEAD_DIM**-0.5
    for h in range(pair):
        lanes = slice(h * local, (h + 1) * local)
        live = (at * pair + h < held_ref[0]).astype(f32)
        cot = cot_ref[h].astype(f32) * live
        scaled, inv_std = norm_rows(mixed_ref[h])
        routed = (scaled * vector_ref[3:4] + vector_ref[4:5]).astype(bf16)
        probs = probs_ref[h]
        experts = lax.broadcasted_iota(jnp.int32, probs.shape, 1)
        grad_probs = jnp.zeros(probs.shape, f32)
        for k in range(TOPK):
            match = experts == routes_ref[h, :, k : k + 1]
            grad_probs = grad_probs + jnp.where(match, gates_ref[h, :, k : k + 1], 0.0)
        grad_logits = probs * (grad_probs - jnp.sum(probs * grad_probs, axis=-1, keepdims=True))
        grad_logits = grad_logits.astype(bf16)
        grad_routed = jnp.concatenate([rows_ref[z, 0, :, lanes] for z in range(tensor)], axis=1)
        grad_routed = grad_routed.astype(f32) + turned_dot(grad_logits, router, 1, 1)
        grad_mixed = cot + norm_rows_back(grad_routed, scaled, inv_std, vector_ref[3:4])
        grad_mixed_ref[h] = grad_mixed
        low = grad_mixed.astype(bf16)
        grad_attended = jnp.dot(low, out_turned, preferred_element_type=f32).astype(bf16)
        proj = proj_ref[h]
        grads = [[], [], []]
        for n in range(0, local, HEAD_DIM):
            queries = proj[:, n : n + HEAD_DIM]
            keys = proj[:, local + n : local + n + HEAD_DIM]
            values = proj[:, 2 * local + n : 2 * local + n + HEAD_DIM]
            grad_head = grad_attended[:, n : n + HEAD_DIM]
            scores = turned_dot(queries, keys, 1, 1) * scale
            scores = jnp.exp(scores - jnp.max(scores, axis=-1, keepdims=True))
            weights = scores / jnp.sum(scores, axis=-1, keepdims=True)
            grads[2].append(turned_dot(weights.astype(bf16), grad_head, 0, 0))
            grad_weights = turned_dot(grad_head, values, 1, 1)
            inner = jnp.sum(weights * grad_weights, axis=-1, keepdims=True)
            grad_scores = (weights * (grad_weights - inner)).astype(bf16)
            grads[0].append(jnp.dot(grad_scores, keys, preferred_element_type=f32) * scale)
            grads[1].append(turned_dot(grad_scores, queries, 0, 0) * scale)
        grad_proj = jnp.concatenate(grads[0] + grads[1] + grads[2], axis=1)
        proj_sum = jnp.sum(grad_proj, axis=0, keepdims=True)
        grad_proj = grad_proj.astype(bf16)
        first, _ = norm_rows(images_ref[h].astype(f32))
        normed = (first * vector_ref[0:1] + vector_ref[1:2]).astype(bf16)
        grad_normed = turned_dot(grad_proj, qkv, 1, 1)
        normed_ref[h] = grad_normed.astype(bf16)
        attended = attended_ref[0, :, lanes]
        matrix = jnp.concatenate(
            [
                turned_dot(normed, grad_proj, 0, 0),
                turned_dot(low, attended, 0, 0),
                turned_dot(routed, grad_logits, 0, 0),
            ],
            axis=1,
        )
        matrix_sum_ref[...] += matrix
        column = lambda values: jnp.sum(values, axis=0, keepdims=True)
        sums_ref[2:3] += column(grad_mixed)
        sums_ref[3:4] += column(grad_routed * scaled)
        sums_ref[4:5] += column(grad_routed)
        sums_ref[5:6, : 3 * local] += proj_sum

    @pl.when(at == pl.num_programs(0) - 1)
    def _():
        matrix_ref[...] = matrix_sum_ref[...].astype(bf16)


def run_pull(held, images, cot, mixed, probs, routes, gates, rows_all, attended, proj, packed, vectors, router_at):
    f32, bf16 = jnp.float32, jnp.bfloat16
    count, length, width = images.shape
    tensor = rows_all.shape[0]
    local = proj.shape[2] // 3
    tokens = (count, length, width)
    block = (PAIR, length, width)
    step = lambda p: (p, 0, 0)
    still = lambda p: (0, 0)
    matrix = (width, 4 * local + EXPERTS)
    return call_kernel(
        functools.partial(pull_kernel, router_at),
        (count // PAIR,),
        [
            (held, None, None),
            by_step(images, PAIR),
            by_step(cot, PAIR),
            by_step(mixed, PAIR),
            by_step(probs, PAIR),
            by_step(routes, PAIR),
            by_step(gates, PAIR),
            (rows_all, (tensor, 1, *rows_all.shape[2:]), lambda p: (0, p, 0, 0)),
            by_step(attended, 1),
            by_step(proj, PAIR),
            whole(packed),
            whole(vectors),
        ],
        [
            (tokens, f32, block, step),
            (tokens, bf16, block, step),
            (matrix, bf16, matrix, still),
            ((8, width), f32, (8, width), still),
        ],
        [pltpu.VMEM(matrix, f32)],
        flops=2 * count * length * (width * 12 * local + 14 * length * local),
    )


def last_kernel(images_ref, normed_ref, mixed_ref, vector_ref, out_ref, sums_ref):
    @pl.when(pl.program_id(0) == 0)
    def _():
        sums_ref[...] = jnp.zeros_like(sums_ref)

    for h in range(images_ref.shape[0]):
        scaled, inv_std = norm_rows(images_ref[h].astype(jnp.float32))
        grad = normed_ref[h].astype(jnp.float32)
        out_ref[h] = mixed_ref[h] + norm_rows_back(grad, scaled, inv_std, vector_ref[0:1])
        sums_ref[0:1] += jnp.sum(grad * scaled, axis=0, keepdims=True)
        sums_ref[1:2] += jnp.sum(grad, axis=0, keepdims=True)


def run_last(images, grad_normed, grad_mixed, vectors):
    width = images.shape[2]
    return call_kernel(
        last_kernel,
        (images.shape[0],),
        [by_step(images, 1), by_step(grad_normed, 1), by_step(grad_mixed, 1), whole(vectors)],
        [
            (images.shape, jnp.float32, (1, *images.shape[1:]), lambda p: (p, 0, 0)),
            ((8, width), jnp.float32, (8, width), lambda p: (0, 0)),
        ],
    )


def moved_plan(
    images,
    images_held,
    routes,
    slot_index,
    first_gain,
    first_shift,
    w_qkv,
    qv_bias,
    w_out,
    out_bias,
    second_gain,
    second_shift,
    w_router,
    w_in,
    in_bias,
    w_back,
    back_bias,
    cotangent,
):
    f32, bf16 = jnp.float32, jnp.bfloat16
    image_count, seq_len, width = images.shape
    experts_here, shard_width, ff_here = w_in.shape
    data, sources = lax.axis_size(DP), lax.axis_size(EXPERT)
    outer, inner = lax.axis_size(OUTER), lax.axis_size(INNER)
    tensor = outer * inner
    tensor_axes = (OUTER, INNER)
    everywhere = (DP, EXPERT, OUTER, INNER)
    groups = data * sources
    owners = data * inner
    mine = experts_here // owners
    slots = EXPERTS * CAP
    dp_at = lax.axis_index(DP)
    inner_at = lax.axis_index(INNER)
    tensor_at = lax.axis_index(tensor_axes)
    owner_at = dp_at * inner + inner_at
    local_width = w_out.shape[0]
    slice_width = width // tensor
    router_at = 4 * local_width

    packed = jnp.concatenate(
        [
            w_qkv.transpose(1, 0, 2).reshape(shard_width, 3 * local_width),
            w_out.T,
            w_router,
            back_bias.T,
            jnp.stack([first_gain, first_shift, out_bias, second_gain, second_shift], axis=1),
        ],
        axis=1,
    )
    packed = swap(jnp.broadcast_to(packed[None], (data, *packed.shape)), DP).reshape(width, -1)
    out_rows = jnp.concatenate(hop_gather(w_out, tensor_axes), axis=0)
    in_bias_all = jnp.stack(hop_gather(in_bias, INNER))

    def piece(shard, s):
        return cross(lax.dynamic_slice_in_dim(shard, (owner_at ^ s) * mine, mine, 0), s)

    in_pieces = [piece(w_in, s) for s in range(owners)]
    back_pieces = [piece(w_back.transpose(0, 2, 1), s) for s in range(owners)]
    far = owners // 2
    packed, out_rows, in_bias_all, in_pieces[far] = lax.optimization_barrier(
        (packed, out_rows, in_bias_all, in_pieces[far])
    )
    vectors = packed[:, router_at + EXPERTS + experts_here :].T.astype(f32)
    out_whole = jnp.concatenate(hop_gather(out_rows, DP), axis=1)
    in_bias_mine = lax.dynamic_slice_in_dim(in_bias_all, owner_at * mine, mine, 1)
    in_bias_mine = in_bias_mine.transpose(1, 0, 2).astype(f32)

    home, within = routes // experts_here, routes % experts_here
    owner, nth = within // mine, within % mine
    kept = slot_index < CAP
    group_place = (owner // inner) * sources + home
    target = ((group_place * inner + owner % inner) * mine + nth) * CAP + slot_index
    target = jnp.where(kept, target, slots)
    plane_target = (group_place * mine + nth) * CAP + slot_index
    plane_target = jnp.where(jnp.logical_and(kept, owner % inner == inner_at), plane_target, -1)
    plane_target = plane_target.transpose(0, 2, 1)

    attended, proj = run_attend(images, packed, vectors, qv_bias.astype(f32))

    attended, out_whole = lax.optimization_barrier((attended, out_whole))
    attended_all = lax.all_gather(attended, tensor_axes)
    attended_all, in_pieces[far + 1 :], back_pieces[: far + 1] = lax.optimization_barrier(
        (attended_all, in_pieces[far + 1 :], back_pieces[: far + 1])
    )
    mixed, probs, sent = run_route(
        images,
        cotangent,
        attended_all,
        out_whole,
        packed,
        vectors,
        routes,
        plane_target,
        groups,
        slots // inner,
    )
    sent, back_pieces = lax.optimization_barrier((sent, back_pieces))
    arrived = swap(sent, (DP, EXPERT))
    back_bias_mine = lax.dynamic_slice_in_dim(packed, router_at + EXPERTS + owner_at * mine, mine, 1)
    back_bias_mine = jnp.where(lax.axis_index(OUTER) == 0, back_bias_mine.astype(f32), 0.0)
    (
        returned_out,
        grads_out,
        hidden_low,
        grad_pre_low,
        grad_turned,
        grad_in_bias_mine,
        grad_back_bias_mine,
    ) = run_experts(
        owner_at, arrived, in_pieces, back_pieces, in_bias_mine, back_bias_mine, inner, tensor
    )

    def bring(parts):
        return swap(parts.reshape(groups * tensor, *parts.shape[2:]), everywhere)

    grad_parts = bring(grads_out)
    weight_parts = weight_grads(
        owner_at,
        arrived,
        grad_pre_low,
        grad_turned,
        hidden_low,
        grad_in_bias_mine,
        grad_back_bias_mine,
        owners,
    )
    weight_parts = [cross(part, s) for s, part in enumerate(weight_parts)]
    grad_parts, weight_parts[: far + 1] = lax.optimization_barrier(
        (grad_parts, weight_parts[: far + 1])
    )
    rows_cut, grad_gates = run_take_grads(grad_parts, target, slice_width, outer, inner, slots)
    rows_cut, returned_out = lax.optimization_barrier((rows_cut, returned_out))
    rows_all = lax.all_gather(rows_cut, tensor_axes)
    returned = bring(returned_out)
    rows_all, returned, weight_parts = lax.optimization_barrier((rows_all, returned, weight_parts))
    grad_mixed, normed_part, matrix, sums = run_pull(
        images_held,
        images,
        cotangent,
        mixed,
        probs,
        routes,
        grad_gates,
        rows_all,
        attended,
        proj,
        packed,
        vectors,
        router_at,
    )
    grad_normed = lax.psum(normed_part, tensor_axes)
    grad_normed, returned, weight_parts = lax.optimization_barrier(
        (grad_normed, returned, weight_parts)
    )
    grad_images, first_sums = run_last(images, grad_normed, grad_mixed, vectors)
    mixed_cut = lax.dynamic_slice_in_dim(mixed, tensor_at * slice_width, slice_width, 2)
    output_cut = run_take_rows(
        images_held, returned, target, probs, routes, mixed_cut, outer, inner, slots
    )
    output = lax.all_gather(output_cut, tensor_axes)
    output = output.reshape(tensor, image_count // PAIR, seq_len, PAIR, slice_width)
    output = output.transpose(1, 3, 2, 0, 4).reshape(images.shape)

    pair_sums = [sums[5, :local_width], sums[5, 2 * local_width : 3 * local_width]]
    pair_sums = jnp.tile(jnp.stack(pair_sums), (1, data))
    vector_grads = jnp.concatenate([first_sums[:2], sums[2:5], pair_sums], axis=0)
    high, low = high_low(vector_grads)
    small = jnp.concatenate([matrix, high.T, low.T], axis=1)
    small = swap(small.reshape(groups, shard_width // sources, -1), (DP, EXPERT))
    small = jnp.sum(small.astype(f32), axis=0)
    small = jnp.concatenate(hop_gather(small, EXPERT), axis=0)
    grad_w_qkv = small[:, : 3 * local_width].reshape(shard_width, 3, local_width).transpose(1, 0, 2)
    grad_w_out = small[:, 3 * local_width : router_at].T
    grad_w_router = small[:, router_at : router_at + EXPERTS]
    vector_grads = small[:, router_at + EXPERTS :].T
    vector_grads = vector_grads[:7] + vector_grads[7:]
    grad_w_in, grad_w_back = run_widen(owner_at, weight_parts, mine, shard_width)
    grad_w_back = grad_w_back.transpose(0, 2, 1)
    grad_in_bias = jnp.zeros((experts_here, ff_here), f32)
    grad_back_shard = jnp.zeros((experts_here, shard_width), f32)
    for s, part in enumerate(weight_parts):
        start = (owner_at ^ s) * mine
        lines = part[2 * mine * shard_width :].astype(f32)
        line = jnp.sum(lines[: 2 * mine].reshape(mine, 2, ff_here), axis=1)
        grad_in_bias = lax.dynamic_update_slice_in_dim(grad_in_bias, line, start, 0)
        line = lines[2 * mine : 3 * mine]
        line = line[:, :shard_width] + line[:, ff_here // 2 : ff_here // 2 + shard_width]
        grad_back_shard = lax.dynamic_update_slice_in_dim(grad_back_shard, line, start, 0)
    return (
        output,
        grad_images,
        vector_grads[0],
        vector_grads[1],
        grad_w_qkv,
        vector_grads[5:7],
        grad_w_out,
        vector_grads[2],
        vector_grads[3],
        vector_grads[4],
        grad_w_router,
        grad_w_in,
        grad_in_bias,
        grad_w_back,
        grad_back_shard,
    )


def specs(tensor):
    rows = P((DP, EXPERT), None, None)
    vector, square = P(DP), P(tensor, DP)
    qkv, pair, router = P(None, DP, tensor), P(None, tensor), P(DP, None)
    inward, outward = P(EXPERT, DP, tensor), P(EXPERT, tensor, DP)
    params = (vector, vector, qkv, pair, square, vector, vector, vector, router)
    experts = (inward, P(EXPERT, tensor), outward, P(EXPERT, DP))
    taken = (rows, P((DP, EXPERT)), rows, rows, *params, *experts, rows)
    given = (rows, rows, *params, *experts)
    return taken, given


def solution(mesh):
    data, expert, tensor = (mesh.shape[name] for name in (DP, EXPERT, TENSOR))
    inner = FF_PAIR if tensor % FF_PAIR == 0 else 1
    owners = data * inner
    if (EXPERTS // expert) % owners or any(n & (n - 1) for n in (data, expert, tensor)):
        taken, given = specs(TENSOR)
        return jax.shard_map(
            gathered_plan, mesh=mesh, in_specs=taken, out_specs=given, check_vma=False
        )
    devices = mesh.devices.reshape(data, expert, tensor // inner, inner)
    split_mesh = Mesh(devices, (DP, EXPERT, OUTER, INNER))
    taken, given = specs((OUTER, INNER))
    return jax.shard_map(
        moved_plan, mesh=split_mesh, in_specs=taken, out_specs=given, check_vma=False
    )
```

```python
import functools
import math

import jax
import jax.numpy as jnp
from jax import lax
from jax.experimental import pallas as pl
from jax.experimental.pallas import tpu as pltpu
from jax.sharding import Mesh
from jax.sharding import PartitionSpec as P

HEAD_DIM = 64
EXPERTS = 32
TOPK = 2
CAP = 64
FF_PAIR = 2
PAIR = 2
EXTRA = 16
VMEM_LIMIT = 56 * 1024 * 1024
GELU_SCALE = (2.0 / math.pi) ** 0.5
GELU_CUBE = 0.044715

DP = "dp"
EXPERT = "expert"
TENSOR = "tensor"
OUTER = "outer"
INNER = "inner"


EPS = 1e-06


def norm_parts(values, norm_gain, norm_shift):
    average = jnp.mean(values, axis=-1, keepdims=True)
    centred = values - average
    spread = jnp.mean(centred * centred, axis=-1, keepdims=True)
    inv_std = lax.rsqrt(spread + EPS)
    scaled = centred * inv_std
    return (scaled * norm_gain + norm_shift, scaled, inv_std)


def norm_back(grad_out, scaled, inv_std, norm_gain):
    grad_scaled = grad_out * norm_gain
    inner = grad_scaled - jnp.mean(grad_scaled, axis=-1, keepdims=True)
    inner = inner - scaled * jnp.mean(grad_scaled * scaled, axis=-1, keepdims=True)
    return (inner * inv_std, jnp.sum(grad_out * scaled, axis=0), jnp.sum(grad_out, axis=0))


def attention_forward(queries, key_rows, value_rows, scale):
    scores = (
        jnp.einsum("iqhd,ikhd->ihqk", queries, key_rows, preferred_element_type=jnp.float32) * scale
    )
    row_peak = jnp.max(scores, axis=-1, keepdims=True)
    log_total = row_peak + jnp.log(jnp.sum(jnp.exp(scores - row_peak), axis=-1, keepdims=True))
    weights = jnp.exp(scores - log_total).astype(jnp.bfloat16)
    attended = jnp.einsum(
        "ihqk,ikhd->iqhd", weights, value_rows, preferred_element_type=jnp.float32
    )
    return (attended, log_total)


def attention_backward(queries, key_rows, value_rows, log_total, grad_low, scale):
    scores = (
        jnp.einsum("iqhd,ikhd->ihqk", queries, key_rows, preferred_element_type=jnp.float32) * scale
    )
    probs = jnp.exp(scores - log_total)
    weights = probs.astype(jnp.bfloat16)
    grad_values = jnp.einsum(
        "ihqk,iqhd->ikhd", weights, grad_low, preferred_element_type=jnp.float32
    )
    grad_weights = jnp.einsum(
        "iqhd,ikhd->ihqk", grad_low, value_rows, preferred_element_type=jnp.float32
    )
    grad_scores = probs * (grad_weights - jnp.sum(probs * grad_weights, axis=-1, keepdims=True))
    scores_low = grad_scores.astype(jnp.bfloat16)
    grad_queries = (
        jnp.einsum("ihqk,ikhd->iqhd", scores_low, key_rows, preferred_element_type=jnp.float32)
        * scale
    )
    grad_keys = (
        jnp.einsum("ihqk,iqhd->ikhd", scores_low, queries, preferred_element_type=jnp.float32)
        * scale
    )
    return (grad_queries, grad_keys, grad_values)


def gathered_plan(
    images,
    images_held,
    routes,
    slot_index,
    first_gain,
    first_shift,
    w_qkv,
    qv_bias,
    w_out,
    out_bias,
    second_gain,
    second_shift,
    w_router,
    w_in,
    in_bias,
    w_back,
    back_bias,
    cotangent,
):
    image_count, seq_len, width = images.shape
    rows_total = image_count * seq_len
    experts_here = w_in.shape[0]
    (
        gain_first,
        shift_first,
        qkv_full,
        out_full,
        bias_out_full,
        gain_second,
        shift_second,
        router_full,
        in_full,
        back_full,
        back_bias_full,
    ) = (
        lax.all_gather(first_gain, DP, axis=0, tiled=True),
        lax.all_gather(first_shift, DP, axis=0, tiled=True),
        lax.all_gather(w_qkv, DP, axis=1, tiled=True),
        lax.all_gather(w_out, DP, axis=1, tiled=True),
        lax.all_gather(out_bias, DP, axis=0, tiled=True),
        lax.all_gather(second_gain, DP, axis=0, tiled=True),
        lax.all_gather(second_shift, DP, axis=0, tiled=True),
        lax.all_gather(w_router, DP, axis=0, tiled=True),
        lax.all_gather(w_in, DP, axis=1, tiled=True),
        lax.all_gather(w_back, DP, axis=2, tiled=True),
        lax.all_gather(back_bias, DP, axis=1, tiled=True),
    )
    gain_first = gain_first.astype(jnp.float32)
    gain_second = gain_second.astype(jnp.float32)
    inputs = images.reshape(rows_total, width).astype(jnp.float32)
    live_image = (jnp.arange(image_count, dtype=jnp.int32) < images_held[0]).astype(jnp.float32)
    live_rows = jnp.repeat(live_image, seq_len)[:, None]
    normed, scaled_first, inv_first = norm_parts(
        inputs, gain_first, shift_first.astype(jnp.float32)
    )
    normed_low = normed.astype(jnp.bfloat16)
    projected = jnp.einsum("td,cde->cte", normed_low, qkv_full, preferred_element_type=jnp.float32)
    local_width = projected.shape[2]
    head_count = local_width // HEAD_DIM
    head_shape = (image_count, seq_len, head_count, HEAD_DIM)
    bias_pair = qv_bias.astype(jnp.float32)
    queries = (projected[0] + bias_pair[0]).astype(jnp.bfloat16).reshape(head_shape)
    key_rows = projected[1].astype(jnp.bfloat16).reshape(head_shape)
    value_rows = (projected[2] + bias_pair[1]).astype(jnp.bfloat16).reshape(head_shape)
    scale = HEAD_DIM ** (-0.5)
    attended, log_total = attention_forward(queries, key_rows, value_rows, scale)
    attended_low = attended.reshape(rows_total, local_width).astype(jnp.bfloat16)
    head_part = jnp.dot(attended_low, out_full, preferred_element_type=jnp.float32)
    mixed = inputs + lax.psum(head_part, TENSOR) + bias_out_full.astype(jnp.float32)
    routed, scaled_second, inv_second = norm_parts(
        mixed, gain_second, shift_second.astype(jnp.float32)
    )
    routed_low = routed.astype(jnp.bfloat16)
    logits = jnp.dot(routed_low, router_full, preferred_element_type=jnp.float32)
    probs = jax.nn.softmax(logits, axis=-1)
    pair_routes = routes.reshape(rows_total, TOPK)
    pair_slots = slot_index.reshape(rows_total, TOPK)
    target = jnp.where(pair_slots < CAP, pair_routes * CAP + pair_slots, EXPERTS * CAP).reshape(
        rows_total * TOPK
    )
    gates = jnp.take_along_axis(probs, pair_routes, axis=1)
    pair_rows = jnp.repeat(routed_low, TOPK, axis=0)
    outgoing = (
        jnp.zeros((EXPERTS * CAP + 1, width), jnp.bfloat16)
        .at[target]
        .set(pair_rows)[: EXPERTS * CAP]
    )
    outgoing = outgoing.reshape(EXPERTS, 1, CAP, width)
    arrived = lax.all_to_all(outgoing, EXPERT, split_axis=0, concat_axis=1, tiled=True)
    sources = arrived.shape[1]
    expert_rows = arrived.reshape(experts_here, sources * CAP, width)
    hidden_pre = jnp.einsum(
        "erd,edf->erf", expert_rows, in_full, preferred_element_type=jnp.float32
    )
    hidden_pre = hidden_pre + in_bias.astype(jnp.float32)[:, None, :]
    hidden_value, gelu_pull = jax.vjp(jax.nn.gelu, hidden_pre)
    hidden_low = hidden_value.astype(jnp.bfloat16)
    expert_part = jnp.einsum(
        "erf,efd->erd", hidden_low, back_full, preferred_element_type=jnp.float32
    )
    bias_back = back_bias_full.astype(jnp.float32)[:, None, :]
    shares = lax.psum_scatter(
        expert_part.reshape(experts_here, sources, CAP, width),
        TENSOR,
        scatter_dimension=2,
        tiled=True,
    )
    share_low = (shares + bias_back[:, None]).astype(jnp.bfloat16)
    pieces = lax.all_to_all(share_low, EXPERT, split_axis=1, concat_axis=0, tiled=True)
    returned = lax.all_gather(pieces, TENSOR, axis=2, tiled=True)
    padded = jnp.concatenate(
        [returned.reshape(EXPERTS * CAP, width), jnp.zeros((1, width), jnp.bfloat16)], axis=0
    )
    picked = padded[target].astype(jnp.float32).reshape(rows_total, TOPK, width)
    expert_mix = jnp.sum(gates[:, :, None] * picked, axis=1)
    output = (live_rows * (mixed + expert_mix)).astype(jnp.bfloat16).reshape(images.shape)
    grad_rows = cotangent.reshape(rows_total, width).astype(jnp.float32) * live_rows
    grad_gates = jnp.sum(grad_rows[:, None, :] * picked, axis=-1)
    grad_picked = (
        (gates[:, :, None] * grad_rows[:, None, :])
        .astype(jnp.bfloat16)
        .reshape(rows_total * TOPK, width)
    )
    grad_outgoing = (
        jnp.zeros((EXPERTS * CAP + 1, width), jnp.bfloat16)
        .at[target]
        .set(grad_picked)[: EXPERTS * CAP]
    )
    grad_outgoing = grad_outgoing.reshape(EXPERTS, 1, CAP, width)
    grad_arrived = lax.all_to_all(grad_outgoing, EXPERT, split_axis=0, concat_axis=1, tiled=True)
    grad_arrived = grad_arrived.reshape(experts_here, sources * CAP, width)
    grad_back_bias = jnp.sum(grad_arrived.astype(jnp.float32), axis=1)
    grad_back_w = jnp.einsum(
        "erf,erd->efd", hidden_low, grad_arrived, preferred_element_type=jnp.float32
    )
    grad_hidden = jnp.einsum(
        "erd,efd->erf", grad_arrived, back_full, preferred_element_type=jnp.float32
    )
    grad_pre = gelu_pull(grad_hidden)[0]
    grad_in_bias_local = jnp.sum(grad_pre, axis=1)
    grad_pre_low = grad_pre.astype(jnp.bfloat16)
    grad_in_w = jnp.einsum(
        "erd,erf->edf", expert_rows, grad_pre_low, preferred_element_type=jnp.float32
    )
    grad_rows_part = jnp.einsum(
        "erf,edf->erd", grad_pre_low, in_full, preferred_element_type=jnp.float32
    )
    grad_shares = lax.psum_scatter(
        grad_rows_part.reshape(experts_here, sources, CAP, width),
        TENSOR,
        scatter_dimension=2,
        tiled=True,
    ).astype(jnp.bfloat16)
    grad_pieces = lax.all_to_all(grad_shares, EXPERT, split_axis=1, concat_axis=0, tiled=True)
    grad_returned = lax.all_gather(grad_pieces, TENSOR, axis=2, tiled=True)
    grad_padded = jnp.concatenate(
        [grad_returned.reshape(EXPERTS * CAP, width), jnp.zeros((1, width), jnp.bfloat16)], axis=0
    )
    grad_routed = jnp.sum(
        grad_padded[target].astype(jnp.float32).reshape(rows_total, TOPK, width), axis=1
    )
    expert_match = (
        pair_routes[:, :, None] == jnp.arange(EXPERTS, dtype=jnp.int32)[None, None, :]
    ).astype(jnp.float32)
    grad_probs = jnp.sum(expert_match * grad_gates[:, :, None], axis=1)
    grad_logits = probs * (grad_probs - jnp.sum(probs * grad_probs, axis=-1, keepdims=True))
    grad_logits_low = grad_logits.astype(jnp.bfloat16)
    grad_router = jnp.einsum(
        "td,te->de", routed_low, grad_logits_low, preferred_element_type=jnp.float32
    )
    grad_routed = grad_routed + jnp.einsum(
        "te,de->td", grad_logits_low, router_full, preferred_element_type=jnp.float32
    )
    grad_from_norm, grad_gain_second, grad_shift_second = norm_back(
        grad_routed, scaled_second, inv_second, gain_second
    )
    grad_mixed = grad_rows + grad_from_norm
    grad_bias_out = jnp.sum(grad_mixed, axis=0)
    grad_mixed_low = grad_mixed.astype(jnp.bfloat16)
    grad_out_w = jnp.einsum(
        "te,td->ed", attended_low, grad_mixed_low, preferred_element_type=jnp.float32
    )
    grad_attended = jnp.einsum(
        "td,ed->te", grad_mixed_low, out_full, preferred_element_type=jnp.float32
    )
    grad_attended = grad_attended.astype(jnp.bfloat16).reshape(head_shape)
    grad_queries, grad_keys, grad_values = attention_backward(
        queries, key_rows, value_rows, log_total, grad_attended, scale
    )
    grad_queries = grad_queries.reshape(rows_total, local_width)
    grad_keys = grad_keys.reshape(rows_total, local_width)
    grad_values = grad_values.reshape(rows_total, local_width)
    grad_pair_bias = jnp.stack([jnp.sum(grad_queries, axis=0), jnp.sum(grad_values, axis=0)])
    grad_proj_low = jnp.stack([grad_queries, grad_keys, grad_values]).astype(jnp.bfloat16)
    grad_qkv = jnp.einsum(
        "td,cte->cde", normed_low, grad_proj_low, preferred_element_type=jnp.float32
    )
    grad_normed_part = jnp.einsum(
        "cte,cde->td", grad_proj_low, qkv_full, preferred_element_type=jnp.float32
    )
    grad_normed = lax.psum(grad_normed_part, TENSOR)
    grad_from_first, grad_gain_first, grad_shift_first = norm_back(
        grad_normed, scaled_first, inv_first, gain_first
    )
    grad_images = (grad_mixed + grad_from_first).reshape(images.shape)
    expert_start = lax.axis_index(EXPERT) * experts_here
    full_in_bias = lax.dynamic_update_slice(
        jnp.zeros((EXPERTS, grad_in_bias_local.shape[1]), jnp.float32),
        grad_in_bias_local,
        (expert_start, jnp.zeros((), jnp.int32)),
    )
    summed = lax.psum(
        (
            grad_gain_first,
            grad_shift_first,
            grad_qkv,
            grad_pair_bias,
            grad_out_w,
            grad_bias_out,
            grad_gain_second,
            grad_shift_second,
            grad_router,
            full_in_bias,
        ),
        (DP, EXPERT),
    )
    shard_width = width // lax.axis_size(DP)
    shard_start = lax.axis_index(DP) * shard_width
    grad_first_gain = lax.dynamic_slice_in_dim(summed[0], shard_start, shard_width, 0)
    grad_first_shift = lax.dynamic_slice_in_dim(summed[1], shard_start, shard_width, 0)
    grad_w_qkv = lax.dynamic_slice_in_dim(summed[2], shard_start, shard_width, 1)
    grad_qv_bias = summed[3]
    grad_w_out = lax.dynamic_slice_in_dim(summed[4], shard_start, shard_width, 1)
    grad_out_bias = lax.dynamic_slice_in_dim(summed[5], shard_start, shard_width, 0)
    grad_second_gain = lax.dynamic_slice_in_dim(summed[6], shard_start, shard_width, 0)
    grad_second_shift = lax.dynamic_slice_in_dim(summed[7], shard_start, shard_width, 0)
    grad_w_router = lax.dynamic_slice_in_dim(summed[8], shard_start, shard_width, 0)
    grad_in_bias = lax.dynamic_slice_in_dim(summed[9], expert_start, experts_here, 0)
    grad_w_in, grad_w_back, grad_back_shard = (
        lax.psum_scatter(grad_in_w, DP, scatter_dimension=1, tiled=True),
        lax.psum_scatter(grad_back_w, DP, scatter_dimension=2, tiled=True),
        lax.psum_scatter(grad_back_bias, DP, scatter_dimension=1, tiled=True),
    )
    return (
        output,
        grad_images,
        grad_first_gain,
        grad_first_shift,
        grad_w_qkv,
        grad_qv_bias,
        grad_w_out,
        grad_out_bias,
        grad_second_gain,
        grad_second_shift,
        grad_w_router,
        grad_w_in,
        grad_in_bias,
        grad_w_back,
        grad_back_shard,
    )


def swap(values, axes):
    return lax.all_to_all(values, axes, split_axis=0, concat_axis=0, tiled=True)


def hop_gather(values, axes):
    count, at = lax.axis_size(axes), lax.axis_index(axes)
    hops = [values]
    for s in range(1, count):
        hops.append(lax.ppermute(values, axes, [(i, i ^ s) for i in range(count)]))
    gathered = []
    for i in range(count):
        found = hops[0]
        for s in range(1, count):
            found = jnp.where(at ^ i == s, hops[s], found)
        gathered.append(found)
    return gathered


def cross(values, s):
    count = lax.axis_size((DP, INNER))
    return lax.ppermute(values, (DP, INNER), [(i, i ^ s) for i in range(count)]) if s else values


def high_low(values):
    high = lax.reduce_precision(values, 8, 7)
    return high.astype(jnp.bfloat16), (values - high).astype(jnp.bfloat16)


def turned_dot(left, right, left_dim, right_dim):
    return lax.dot_general(
        left, right, (((left_dim,), (right_dim,)), ((), ())), preferred_element_type=jnp.float32
    )


def expert_kernel(inner, owners, at_ref, rows_ref, gate_ref, cot_ref, in_bias_ref, back_bias_ref, *refs):
    piece_refs, refs = refs[:owners], refs[owners:]
    returned_ref, grads_ref, hidden_ref, grad_pre_ref, grad_turned_ref = refs[:5]
    grad_in_bias_ref, grad_back_bias_ref, weight_ref = refs[5:]
    f32, bf16 = jnp.float32, jnp.bfloat16
    groups, cap, width = rows_ref.shape
    depth = piece_refs[0].shape[2]
    for s in range(owners):
        source = at_ref[0] ^ s
        place = pl.ds(pl.multiple_of((source // inner) * depth, depth), depth)
        for k in range(2):
            weight_ref[k, source % inner, place] = piece_refs[s][k, 0]
    tensor, slice_width = returned_ref.shape[1:3]
    mine = back_bias_ref.shape[1]
    total = groups * cap
    at = pl.program_id(0)
    rows = rows_ref[...].reshape(total, width)
    cot_turned = cot_ref[...].reshape(total, width).T.astype(f32)
    pair = gate_ref[:, 0:1, :].astype(f32) + gate_ref[:, 1:2, :].astype(f32)
    pair = pair.reshape(groups, pair.shape[-1])
    gate = jnp.zeros((groups, cap), f32)
    for j in range(mine):
        gate = jnp.where(at == j, pair[:, j * cap : (j + 1) * cap], gate)
    gate = jnp.concatenate([gate[g : g + 1, :] for g in range(groups)], axis=1)
    grad_turned = (cot_turned * gate).astype(bf16)
    grad_turned_ref[0] = grad_turned
    grad_returned = grad_turned.T
    grad_back_bias_ref[0] = jnp.sum(grad_returned.astype(f32), axis=0, keepdims=True)
    bias_columns = back_bias_ref[...]
    bias = jnp.zeros((width, 1), f32)
    for j in range(mine):
        bias = jnp.where(at == j, bias_columns[:, j : j + 1], bias)
    part = jnp.broadcast_to(bias, (width, total))
    back = jnp.zeros((width, total), f32)
    for t in range(inner):
        w_in, w_back = weight_ref[0, t], weight_ref[1, t]
        pre = jnp.dot(rows, w_in, preferred_element_type=f32) + in_bias_ref[0, t : t + 1, :]
        square = pre * pre
        bent = jnp.tanh(GELU_SCALE * pre * (1.0 + GELU_CUBE * square))
        half = 0.5 * (1.0 + bent)
        hidden = (pre * half).astype(bf16)
        slope = half + (0.5 * GELU_SCALE) * pre * (1.0 - bent * bent) * (
            1.0 + (3.0 * GELU_CUBE) * square
        )
        hidden_ref[0, t] = hidden
        grad_pre = jnp.dot(grad_returned, w_back, preferred_element_type=f32) * slope
        grad_in_bias_ref[0, t : t + 1, :] = jnp.sum(grad_pre, axis=0, keepdims=True)
        grad_pre = grad_pre.astype(bf16)
        grad_pre_ref[0, t] = grad_pre
        part = part + turned_dot(w_back, hidden, 1, 1)
        back = back + turned_dot(w_in, grad_pre, 1, 1)
    gate_terms = jnp.sum(part * cot_turned, axis=0, keepdims=True)
    high = gate_terms.astype(bf16)
    low = (gate_terms - high.astype(f32)).astype(bf16)
    extra = grads_ref.shape[2] - slice_width
    tail = jnp.concatenate([high, low, jnp.zeros((extra - 2, total), bf16)], axis=0)
    part = part.astype(bf16)
    back = back.astype(bf16)
    for j in range(mine):

        @pl.when(at == j)
        def _():
            lanes = slice(j * cap, (j + 1) * cap)
            for g in range(groups):
                mine_lanes = slice(g * cap, (g + 1) * cap)
                for z in range(tensor):
                    features = slice(z * slice_width, (z + 1) * slice_width)
                    returned_ref[g, z, :, lanes] = part[features, mine_lanes]
                    grads_ref[g, z, :slice_width, lanes] = back[features, mine_lanes]
                    grads_ref[g, z, slice_width:, lanes] = tail[:, mine_lanes]


def run_experts(owner_at, arrived, pieces, in_bias, back_bias, inner, tensor):
    f32, bf16 = jnp.float32, jnp.bfloat16
    groups, _, width = arrived.shape
    owners = len(pieces)
    _, mine, depth, ff = pieces[0].shape
    total = groups * CAP
    slice_width = width // tensor
    gate_at = 2 * mine * CAP // EXTRA
    outs = [
        ((groups, tensor, slice_width, mine * CAP), bf16, lambda j: (0, 0, 0, 0), None),
        ((groups, tensor, slice_width + EXTRA, mine * CAP), bf16, lambda j: (0, 0, 0, 0), None),
        ((mine, inner, total, ff), bf16, lambda j: (j, 0, 0, 0), 1),
        ((mine, inner, total, ff), bf16, lambda j: (j, 0, 0, 0), 1),
        ((mine, width, total), bf16, lambda j: (j, 0, 0), 1),
        ((mine, inner, ff), f32, lambda j: (j, 0, 0), 1),
        ((mine, 1, width), f32, lambda j: (j, 0, 0), 1),
    ]
    return pl.pallas_call(
        functools.partial(expert_kernel, inner, owners),
        grid=(mine,),
        in_specs=[
            pl.BlockSpec(memory_space=pltpu.SMEM),
            pl.BlockSpec((groups, CAP, width), lambda j: (0, j, 0)),
            pl.BlockSpec((groups, EXTRA, mine * CAP), lambda j: (0, gate_at, 0)),
            pl.BlockSpec((groups, CAP, width), lambda j: (0, mine + j, 0)),
            pl.BlockSpec((1, inner, ff), lambda j: (j, 0, 0)),
            pl.BlockSpec((width, mine), lambda j: (0, 0)),
        ]
        + [pl.BlockSpec((2, 1, depth, ff), lambda j: (0, j, 0, 0))] * owners,
        out_specs=[
            pl.BlockSpec(shape if lead is None else (lead, *shape[1:]), index)
            for shape, _, index, lead in outs
        ],
        out_shape=[jax.ShapeDtypeStruct(shape, dtype) for shape, dtype, _, _ in outs],
        scratch_shapes=[pltpu.VMEM((2, inner, width, ff), bf16)],
        compiler_params=pltpu.CompilerParams(vmem_limit_bytes=VMEM_LIMIT),
        cost_estimate=pl.CostEstimate(
            flops=8 * mine * total * width * inner * ff,
            bytes_accessed=4 * owners * mine * depth * ff + 12 * mine * total * inner * ff,
            transcendentals=mine * total * inner * ff,
        ),
    )(owner_at.reshape(1), arrived, arrived, arrived, in_bias, back_bias, *pieces)


def weight_kernel(
    inner,
    at_ref,
    rows_ref,
    grad_pre_ref,
    grad_turned_ref,
    hidden_ref,
    in_bias_ref,
    back_bias_ref,
    *refs,
):
    f32, bf16 = jnp.float32, jnp.bfloat16
    out_refs, sums_ref, tail_ref = refs[:-2], refs[-2], refs[-1]
    groups, cap, width = rows_ref.shape
    mine = back_bias_ref.shape[0]
    ff = sums_ref.shape[-1]
    depth = width * inner // len(out_refs)
    data = width // depth
    part, at = pl.program_id(0), pl.program_id(1)
    rows = rows_ref[...].reshape(groups * cap, width)
    sums_ref[0] = turned_dot(rows, grad_pre_ref[0, 0], 0, 0).astype(bf16)
    grad_back = jnp.dot(grad_turned_ref[0], hidden_ref[0, 0], preferred_element_type=f32)
    sums_ref[1] = grad_back.astype(bf16)

    @pl.when(at == mine - 1)
    def _():
        pairs = []
        for j in range(mine):
            values = in_bias_ref[j, 0]
            high = values.astype(bf16).astype(f32)
            pairs += [high, values - high]
        for d in range(data):
            lines = list(pairs)
            for j in range(mine):
                values = back_bias_ref[j, :, d * depth : (d + 1) * depth]
                high = values.astype(bf16).astype(f32)
                gap = jnp.zeros((1, ff // 2 - depth), f32)
                lines.append(jnp.concatenate([high, gap, values - high, gap], axis=1))
            lines.append(jnp.zeros((EXTRA - len(lines), ff), f32))
            tail_ref[d] = jnp.concatenate(lines, axis=0).astype(bf16)

    for s, out_ref in enumerate(out_refs):
        owner = at_ref[0] ^ s
        d = owner // inner
        place = pl.ds(pl.multiple_of(d * depth, depth), depth)

        @pl.when(owner % inner == part)
        def _():
            for k in range(2):
                line = pl.multiple_of((k * mine + at) * depth, depth)
                out_ref[pl.ds(line, depth)] = sums_ref[k, place]

            @pl.when(at == mine - 1)
            def _():
                out_ref[2 * mine * depth :] = tail_ref[d]


def weight_grads(
    owner_at, arrived, grad_pre, grad_turned, hidden, grad_in_bias, grad_back_bias, owners
):
    mine, inner, total, ff = hidden.shape
    groups, _, width = arrived.shape
    depth = width * inner // owners
    kept = pl.BlockSpec((1, 1, total, ff), lambda t, j: (j, t, 0, 0))
    out = (2 * mine * depth + EXTRA, ff)
    return pl.pallas_call(
        functools.partial(weight_kernel, inner),
        grid=(inner, mine),
        in_specs=[
            pl.BlockSpec(memory_space=pltpu.SMEM),
            pl.BlockSpec((groups, CAP, width), lambda t, j: (0, j, 0)),
            kept,
            pl.BlockSpec((1, width, total), lambda t, j: (j, 0, 0)),
            kept,
            pl.BlockSpec((mine, 1, 1, ff), lambda t, j: (0, t, 0, 0)),
            pl.BlockSpec((mine, 1, width), lambda t, j: (0, 0, 0)),
        ],
        out_specs=[pl.BlockSpec(out, lambda t, j: (0, 0))] * owners,
        out_shape=[jax.ShapeDtypeStruct(out, jnp.bfloat16)] * owners,
        scratch_shapes=[
            pltpu.VMEM((2, width, ff), jnp.bfloat16),
            pltpu.VMEM((width // depth, EXTRA, ff), jnp.bfloat16),
        ],
        compiler_params=pltpu.CompilerParams(vmem_limit_bytes=VMEM_LIMIT),
        cost_estimate=pl.CostEstimate(
            flops=4 * mine * total * width * inner * ff,
            bytes_accessed=4 * mine * inner * (total + width) * ff,
            transcendentals=0,
        ),
    )(
        owner_at.reshape(1),
        arrived,
        grad_pre,
        grad_turned,
        hidden,
        grad_in_bias[:, :, None],
        grad_back_bias,
    )


def widen_kernel(at_ref, *refs):
    part_refs, (in_ref, back_ref) = refs[:-2], refs[-2:]
    mine, depth, ff = in_ref.shape
    rows = mine * depth
    for s, part_ref in enumerate(part_refs):

        @pl.when(pl.program_id(0) == s)
        def _():
            in_ref[...] = part_ref[:rows].astype(jnp.float32).reshape(mine, depth, ff)
            back_ref[...] = part_ref[rows : 2 * rows].astype(jnp.float32).reshape(mine, depth, ff)


def run_widen(owner_at, parts, mine, depth):
    owners, ff = len(parts), parts[0].shape[1]
    out = pl.BlockSpec((mine, depth, ff), lambda p, at: (at[0] ^ p, 0, 0))
    return pl.pallas_call(
        widen_kernel,
        grid_spec=pltpu.PrefetchScalarGridSpec(
            num_scalar_prefetch=1,
            grid=(owners,),
            in_specs=[pl.BlockSpec((2 * mine * depth, ff), lambda p, at: (0, 0))] * owners,
            out_specs=[out, out],
        ),
        out_shape=[jax.ShapeDtypeStruct((owners * mine, depth, ff), jnp.float32)] * 2,
        compiler_params=pltpu.CompilerParams(vmem_limit_bytes=VMEM_LIMIT),
    )(owner_at.reshape(1), *parts)


def norm_rows(values):
    average = jnp.mean(values, axis=-1, keepdims=True)
    centred = values - average
    spread = jnp.mean(centred * centred, axis=-1, keepdims=True)
    inv_std = lax.rsqrt(spread + EPS)
    return centred * inv_std, inv_std


def norm_rows_back(grad_out, scaled, inv_std, norm_gain):
    grad_scaled = grad_out * norm_gain
    inner = grad_scaled - jnp.mean(grad_scaled, axis=-1, keepdims=True)
    inner = inner - scaled * jnp.mean(grad_scaled * scaled, axis=-1, keepdims=True)
    return inner * inv_std


def call_kernel(kernel, grid, inputs, outputs, scratch=(), flops=0):
    smem = pl.BlockSpec(memory_space=pltpu.SMEM)
    return pl.pallas_call(
        kernel,
        grid=grid,
        in_specs=[smem if b is None else pl.BlockSpec(b, i) for _, b, i in inputs],
        out_specs=[pl.BlockSpec(b, i) for _, _, b, i in outputs],
        out_shape=[jax.ShapeDtypeStruct(shape, dtype) for shape, dtype, _, _ in outputs],
        scratch_shapes=list(scratch),
        compiler_params=pltpu.CompilerParams(vmem_limit_bytes=VMEM_LIMIT),
        cost_estimate=pl.CostEstimate(
            flops=flops,
            bytes_accessed=sum(a.size * a.dtype.itemsize for a, _, _ in inputs),
            transcendentals=0,
        ),
    )(*(a for a, _, _ in inputs))


def whole(array):
    return array, array.shape, lambda p: (0,) * array.ndim


def by_step(array, lead):
    return array, (lead, *array.shape[1:]), lambda p: (p,) + (0,) * (array.ndim - 1)


def attend_kernel(images_ref, packed_ref, vector_ref, bias_ref, attended_ref, proj_ref):
    f32, bf16 = jnp.float32, jnp.bfloat16
    local = bias_ref.shape[1]
    weight = packed_ref[:, : 3 * local]
    for h in range(images_ref.shape[0]):
        scaled, _ = norm_rows(images_ref[h].astype(f32))
        normed = (scaled * vector_ref[0:1] + vector_ref[1:2]).astype(bf16)
        proj = jnp.dot(normed, weight, preferred_element_type=f32)
        queries = (proj[:, :local] + bias_ref[0:1]).astype(bf16)
        keys = proj[:, local : 2 * local].astype(bf16)
        values = (proj[:, 2 * local :] + bias_ref[1:2]).astype(bf16)
        proj_ref[h] = jnp.concatenate([queries, keys, values], axis=1)
        parts = []
        for n in range(0, local, HEAD_DIM):
            head = slice(n, n + HEAD_DIM)
            scores = turned_dot(queries[:, head], keys[:, head], 1, 1) * HEAD_DIM**-0.5
            scores = jnp.exp(scores - jnp.max(scores, axis=-1, keepdims=True))
            weights = scores / jnp.sum(scores, axis=-1, keepdims=True)
            parts.append(
                jnp.dot(weights.astype(bf16), values[:, head], preferred_element_type=f32)
            )
        attended_ref[0, :, h * local : (h + 1) * local] = jnp.concatenate(parts, axis=1).astype(bf16)


def run_attend(images, packed, vectors, qv_bias):
    count, length, width = images.shape
    local = qv_bias.shape[1]
    return call_kernel(
        attend_kernel,
        (count // PAIR,),
        [by_step(images, PAIR), whole(packed), whole(vectors), whole(qv_bias)],
        [
            ((count // PAIR, length, PAIR * local), jnp.bfloat16, (1, length, PAIR * local), lambda p: (p, 0, 0)),
            ((count, length, 3 * local), jnp.bfloat16, (PAIR, length, 3 * local), lambda p: (p, 0, 0)),
        ],
        flops=2 * count * length * local * (3 * width + 4 * length),
    )


def slot_hits(target_row, count):
    return lax.broadcasted_iota(jnp.int32, (count, target_row.shape[1]), 0) == target_row


def route_kernel(
    router_at,
    images_ref,
    cot_ref,
    attended_ref,
    out_ref,
    packed_ref,
    vector_ref,
    routes_ref,
    target_ref,
    mixed_ref,
    probs_ref,
    sent_ref,
    sum_ref,
    gate_ref,
):
    f32, bf16 = jnp.float32, jnp.bfloat16
    slots = sum_ref.shape[1]
    tensor, local = attended_ref.shape[0], attended_ref.shape[3] // images_ref.shape[0]
    at = pl.program_id(0)

    @pl.when(at == 0)
    def _():
        sum_ref[...] = jnp.zeros_like(sum_ref)
        gate_ref[...] = jnp.zeros_like(gate_ref)

    router = packed_ref[:, router_at : router_at + EXPERTS]
    for h in range(images_ref.shape[0]):
        mixed = images_ref[h].astype(f32) + vector_ref[2:3]
        for z in range(tensor):
            part = attended_ref[z, 0, :, h * local : (h + 1) * local]
            weight = out_ref[z * local : (z + 1) * local]
            mixed = mixed + jnp.dot(part, weight, preferred_element_type=f32)
        mixed_ref[h] = mixed
        scaled, _ = norm_rows(mixed)
        routed = (scaled * vector_ref[3:4] + vector_ref[4:5]).astype(bf16)
        logits = jnp.dot(routed, router, preferred_element_type=f32)
        logits = jnp.exp(logits - jnp.max(logits, axis=-1, keepdims=True))
        probs = logits / jnp.sum(logits, axis=-1, keepdims=True)
        probs_ref[h] = probs
        experts = lax.broadcasted_iota(jnp.int32, probs.shape, 1)
        fill = jnp.zeros((slots, probs.shape[0]), f32)
        for k in range(TOPK):
            match = experts == routes_ref[h, :, k : k + 1]
            gate = jnp.sum(jnp.where(match, probs, 0.0), axis=1, keepdims=True)
            high = gate.astype(bf16)
            low = (gate - high.astype(f32)).astype(bf16)
            pair = jnp.concatenate([high, low, jnp.zeros((gate.shape[0], 6), bf16)], axis=1)
            hit = slot_hits(target_ref[h, k : k + 1], slots).astype(f32)
            fill = fill + hit
            gate_ref[...] += turned_dot(pair, hit.astype(bf16), 0, 1)
        fill = fill.astype(bf16)
        sum_ref[0] += jnp.dot(fill, routed, preferred_element_type=f32)
        sum_ref[1] += jnp.dot(fill, cot_ref[h], preferred_element_type=f32)

    @pl.when(at == pl.num_programs(0) - 1)
    def _():
        groups, lines, width = sent_ref.shape
        here = slots // groups
        for g in range(groups):
            lanes = slice(g * here, (g + 1) * here)
            sent_ref[g, :here] = sum_ref[0, lanes].astype(bf16)
            sent_ref[g, here : 2 * here] = sum_ref[1, lanes].astype(bf16)
            gates = jnp.concatenate([gate_ref[:, lanes], jnp.zeros((8, width - here), f32)], axis=1)
            gates = jnp.concatenate([gates, jnp.zeros((lines - 2 * here - 8, width), f32)], axis=0)
            sent_ref[g, 2 * here :] = gates.astype(bf16)


def run_route(
    images, cot, attended_all, out_whole, packed, vectors, routes, plane_target, groups, slots_plane
):
    f32, bf16 = jnp.float32, jnp.bfloat16
    count, length, width = images.shape
    tensor = attended_all.shape[0]
    sent = (groups, 2 * slots_plane // groups + EXTRA, width)
    return call_kernel(
        functools.partial(route_kernel, tensor * attended_all.shape[3] // PAIR),
        (count // PAIR,),
        [
            by_step(images, PAIR),
            by_step(cot, PAIR),
            (attended_all, (tensor, 1, *attended_all.shape[2:]), lambda p: (0, p, 0, 0)),
            whole(out_whole),
            whole(packed),
            whole(vectors),
            by_step(routes, PAIR),
            by_step(plane_target, PAIR),
        ],
        [
            ((count, length, width), f32, (PAIR, length, width), lambda p: (p, 0, 0)),
            ((count, length, EXPERTS), f32, (PAIR, length, EXPERTS), lambda p: (p, 0, 0)),
            (sent, bf16, sent, lambda p: (0, 0, 0)),
        ],
        [pltpu.VMEM((2, slots_plane, width), f32), pltpu.VMEM((8, slots_plane), f32)],
        flops=2 * count * length * width * (width + 2 * slots_plane),
    )


def slot_blocks(parts_ref, slots_ref, outer, inner):
    here = parts_ref.shape[2]
    for b in range(slots_ref.shape[1] // here):
        first = (b // inner) * outer * inner + b % inner
        total = parts_ref[first].astype(jnp.float32)
        for o in range(1, outer):
            total = total + parts_ref[first + o * inner].astype(jnp.float32)
        slots_ref[:, b * here : (b + 1) * here] = total


def token_hits(target_column, count):
    return lax.broadcasted_iota(jnp.int32, (target_column.shape[0], count), 1) == target_column


def take_grads_kernel(outer, inner, parts_ref, target_ref, rows_ref, gates_ref, slots_ref):
    f32, bf16 = jnp.float32, jnp.bfloat16
    slots = slots_ref.shape[1]
    local = rows_ref.shape[2] // target_ref.shape[0]

    @pl.when(pl.program_id(0) == 0)
    def _():
        slot_blocks(parts_ref, slots_ref, outer, inner)

    grads = slots_ref[:local].astype(bf16)
    gate_terms = slots_ref[local : local + 1] + slots_ref[local + 1 : local + 2]
    for h in range(target_ref.shape[0]):
        hits = [token_hits(target_ref[h, :, k : k + 1], slots) for k in range(TOPK)]
        find = jnp.logical_or(hits[0], hits[1]).astype(f32).astype(bf16)
        rows_ref[0, :, h * local : (h + 1) * local] = turned_dot(find, grads, 1, 1).astype(bf16)
        terms = [
            jnp.sum(jnp.where(hit, gate_terms, 0.0), axis=1, keepdims=True) for hit in hits
        ]
        gates_ref[h] = jnp.concatenate(terms, axis=1)


def run_take_grads(parts, target, local, outer, inner, slots):
    count, length, _ = target.shape
    return call_kernel(
        functools.partial(take_grads_kernel, outer, inner),
        (count // PAIR,),
        [whole(parts), by_step(target, PAIR)],
        [
            ((count // PAIR, length, PAIR * local), jnp.bfloat16, (1, length, PAIR * local), lambda p: (p, 0, 0)),
            ((count, length, TOPK), jnp.float32, (PAIR, length, TOPK), lambda p: (p, 0, 0)),
        ],
        [pltpu.VMEM((parts.shape[1], slots), jnp.float32)],
        flops=2 * count * length * slots * local,
    )


def take_rows_kernel(
    outer, inner, held_ref, parts_ref, target_ref, probs_ref, routes_ref, mixed_ref, out_ref, slots_ref
):
    f32, bf16 = jnp.float32, jnp.bfloat16
    slots = slots_ref.shape[1]
    pair = target_ref.shape[0]
    local = out_ref.shape[2] // pair
    at = pl.program_id(0)

    @pl.when(at == 0)
    def _():
        slot_blocks(parts_ref, slots_ref, outer, inner)

    returned = slots_ref[...].astype(bf16)
    for h in range(pair):
        probs = probs_ref[h]
        experts = lax.broadcasted_iota(jnp.int32, probs.shape, 1)
        rows = mixed_ref[h]
        for k in range(TOPK):
            match = experts == routes_ref[h, :, k : k + 1]
            gate = jnp.sum(jnp.where(match, probs, 0.0), axis=1, keepdims=True)
            find = token_hits(target_ref[h, :, k : k + 1], slots).astype(f32).astype(bf16)
            rows = rows + gate * turned_dot(find, returned, 1, 1)
        live = (at * pair + h < held_ref[0]).astype(f32)
        out_ref[0, :, h * local : (h + 1) * local] = (live * rows).astype(bf16)


def run_take_rows(held, parts, target, probs, routes, mixed_cut, outer, inner, slots):
    count, length, local = mixed_cut.shape
    return call_kernel(
        functools.partial(take_rows_kernel, outer, inner),
        (count // PAIR,),
        [
            (held, None, None),
            whole(parts),
            by_step(target, PAIR),
            by_step(probs, PAIR),
            by_step(routes, PAIR),
            by_step(mixed_cut, PAIR),
        ],
        [((count // PAIR, length, PAIR * local), jnp.bfloat16, (1, length, PAIR * local), lambda p: (p, 0, 0))],
        [pltpu.VMEM((parts.shape[1], slots), jnp.float32)],
        flops=4 * count * length * slots * local,
    )[0]


def pull_kernel(
    router_at,
    held_ref,
    images_ref,
    cot_ref,
    mixed_ref,
    probs_ref,
    routes_ref,
    gates_ref,
    rows_ref,
    attended_ref,
    proj_ref,
    packed_ref,
    vector_ref,
    grad_mixed_ref,
    normed_ref,
    matrix_ref,
    sums_ref,
    matrix_sum_ref,
):
    f32, bf16 = jnp.float32, jnp.bfloat16
    pair = images_ref.shape[0]
    tensor = rows_ref.shape[0]
    local = attended_ref.shape[2] // pair
    width = images_ref.shape[2]
    at = pl.program_id(0)

    @pl.when(at == 0)
    def _():
        sums_ref[...] = jnp.zeros_like(sums_ref)
        matrix_sum_ref[...] = jnp.zeros_like(matrix_sum_ref)

    qkv = packed_ref[:, : 3 * local]
    out_turned = packed_ref[:, 3 * local : 4 * local]
    router = packed_ref[:, router_at : router_at + EXPERTS]
    scale = HEAD_DIM**-0.5
    for h in range(pair):
        lanes = slice(h * local, (h + 1) * local)
        live = (at * pair + h < held_ref[0]).astype(f32)
        cot = cot_ref[h].astype(f32) * live
        scaled, inv_std = norm_rows(mixed_ref[h])
        routed = (scaled * vector_ref[3:4] + vector_ref[4:5]).astype(bf16)
        probs = probs_ref[h]
        experts = lax.broadcasted_iota(jnp.int32, probs.shape, 1)
        grad_probs = jnp.zeros(probs.shape, f32)
        for k in range(TOPK):
            match = experts == routes_ref[h, :, k : k + 1]
            grad_probs = grad_probs + jnp.where(match, gates_ref[h, :, k : k + 1], 0.0)
        grad_logits = probs * (grad_probs - jnp.sum(probs * grad_probs, axis=-1, keepdims=True))
        grad_logits = grad_logits.astype(bf16)
        grad_routed = jnp.concatenate([rows_ref[z, 0, :, lanes] for z in range(tensor)], axis=1)
        grad_routed = grad_routed.astype(f32) + turned_dot(grad_logits, router, 1, 1)
        grad_mixed = cot + norm_rows_back(grad_routed, scaled, inv_std, vector_ref[3:4])
        grad_mixed_ref[h] = grad_mixed
        low = grad_mixed.astype(bf16)
        grad_attended = jnp.dot(low, out_turned, preferred_element_type=f32).astype(bf16)
        proj = proj_ref[h]
        grads = [[], [], []]
        for n in range(0, local, HEAD_DIM):
            queries = proj[:, n : n + HEAD_DIM]
            keys = proj[:, local + n : local + n + HEAD_DIM]
            values = proj[:, 2 * local + n : 2 * local + n + HEAD_DIM]
            grad_head = grad_attended[:, n : n + HEAD_DIM]
            scores = turned_dot(queries, keys, 1, 1) * scale
            scores = jnp.exp(scores - jnp.max(scores, axis=-1, keepdims=True))
            weights = scores / jnp.sum(scores, axis=-1, keepdims=True)
            grads[2].append(turned_dot(weights.astype(bf16), grad_head, 0, 0))
            grad_weights = turned_dot(grad_head, values, 1, 1)
            inner = jnp.sum(weights * grad_weights, axis=-1, keepdims=True)
            grad_scores = (weights * (grad_weights - inner)).astype(bf16)
            grads[0].append(jnp.dot(grad_scores, keys, preferred_element_type=f32) * scale)
            grads[1].append(turned_dot(grad_scores, queries, 0, 0) * scale)
        grad_proj = jnp.concatenate(grads[0] + grads[1] + grads[2], axis=1)
        proj_sum = jnp.sum(grad_proj, axis=0, keepdims=True)
        grad_proj = grad_proj.astype(bf16)
        first, _ = norm_rows(images_ref[h].astype(f32))
        normed = (first * vector_ref[0:1] + vector_ref[1:2]).astype(bf16)
        grad_normed = turned_dot(grad_proj, qkv, 1, 1)
        normed_ref[h] = grad_normed.astype(bf16)
        attended = attended_ref[0, :, lanes]
        matrix = jnp.concatenate(
            [
                turned_dot(normed, grad_proj, 0, 0),
                turned_dot(low, attended, 0, 0),
                turned_dot(routed, grad_logits, 0, 0),
            ],
            axis=1,
        )
        matrix_sum_ref[...] += matrix
        column = lambda values: jnp.sum(values, axis=0, keepdims=True)
        sums_ref[2:3] += column(grad_mixed)
        sums_ref[3:4] += column(grad_routed * scaled)
        sums_ref[4:5] += column(grad_routed)
        sums_ref[5:6, : 3 * local] += proj_sum

    @pl.when(at == pl.num_programs(0) - 1)
    def _():
        matrix_ref[...] = matrix_sum_ref[...].astype(bf16)


def run_pull(held, images, cot, mixed, probs, routes, gates, rows_all, attended, proj, packed, vectors, router_at):
    f32, bf16 = jnp.float32, jnp.bfloat16
    count, length, width = images.shape
    tensor = rows_all.shape[0]
    local = proj.shape[2] // 3
    tokens = (count, length, width)
    block = (PAIR, length, width)
    step = lambda p: (p, 0, 0)
    still = lambda p: (0, 0)
    matrix = (width, 4 * local + EXPERTS)
    return call_kernel(
        functools.partial(pull_kernel, router_at),
        (count // PAIR,),
        [
            (held, None, None),
            by_step(images, PAIR),
            by_step(cot, PAIR),
            by_step(mixed, PAIR),
            by_step(probs, PAIR),
            by_step(routes, PAIR),
            by_step(gates, PAIR),
            (rows_all, (tensor, 1, *rows_all.shape[2:]), lambda p: (0, p, 0, 0)),
            by_step(attended, 1),
            by_step(proj, PAIR),
            whole(packed),
            whole(vectors),
        ],
        [
            (tokens, f32, block, step),
            (tokens, bf16, block, step),
            (matrix, bf16, matrix, still),
            ((8, width), f32, (8, width), still),
        ],
        [pltpu.VMEM(matrix, f32)],
        flops=2 * count * length * (width * 12 * local + 14 * length * local),
    )


def last_kernel(images_ref, normed_ref, mixed_ref, vector_ref, out_ref, sums_ref):
    @pl.when(pl.program_id(0) == 0)
    def _():
        sums_ref[...] = jnp.zeros_like(sums_ref)

    for h in range(images_ref.shape[0]):
        scaled, inv_std = norm_rows(images_ref[h].astype(jnp.float32))
        grad = normed_ref[h].astype(jnp.float32)
        out_ref[h] = mixed_ref[h] + norm_rows_back(grad, scaled, inv_std, vector_ref[0:1])
        sums_ref[0:1] += jnp.sum(grad * scaled, axis=0, keepdims=True)
        sums_ref[1:2] += jnp.sum(grad, axis=0, keepdims=True)


def run_last(images, grad_normed, grad_mixed, vectors):
    width = images.shape[2]
    return call_kernel(
        last_kernel,
        (images.shape[0],),
        [by_step(images, 1), by_step(grad_normed, 1), by_step(grad_mixed, 1), whole(vectors)],
        [
            (images.shape, jnp.float32, (1, *images.shape[1:]), lambda p: (p, 0, 0)),
            ((8, width), jnp.float32, (8, width), lambda p: (0, 0)),
        ],
    )


def moved_plan(
    images,
    images_held,
    routes,
    slot_index,
    first_gain,
    first_shift,
    w_qkv,
    qv_bias,
    w_out,
    out_bias,
    second_gain,
    second_shift,
    w_router,
    w_in,
    in_bias,
    w_back,
    back_bias,
    cotangent,
):
    f32, bf16 = jnp.float32, jnp.bfloat16
    image_count, seq_len, width = images.shape
    experts_here, shard_width, ff_here = w_in.shape
    data, sources = lax.axis_size(DP), lax.axis_size(EXPERT)
    outer, inner = lax.axis_size(OUTER), lax.axis_size(INNER)
    tensor = outer * inner
    tensor_axes = (OUTER, INNER)
    everywhere = (DP, EXPERT, OUTER, INNER)
    groups = data * sources
    owners = data * inner
    mine = experts_here // owners
    slots = EXPERTS * CAP
    dp_at = lax.axis_index(DP)
    inner_at = lax.axis_index(INNER)
    tensor_at = lax.axis_index(tensor_axes)
    owner_at = dp_at * inner + inner_at
    local_width = w_out.shape[0]
    slice_width = width // tensor
    router_at = 4 * local_width

    packed = jnp.concatenate(
        [
            w_qkv.transpose(1, 0, 2).reshape(shard_width, 3 * local_width),
            w_out.T,
            w_router,
            back_bias.T,
            jnp.stack([first_gain, first_shift, out_bias, second_gain, second_shift], axis=1),
        ],
        axis=1,
    )
    packed = swap(jnp.broadcast_to(packed[None], (data, *packed.shape)), DP).reshape(width, -1)
    out_rows = jnp.concatenate(hop_gather(w_out, tensor_axes), axis=0)
    in_bias_all = jnp.stack(hop_gather(in_bias, INNER))

    shards = (w_in, w_back.transpose(0, 2, 1))
    pieces = []
    for s in range(owners):
        start = (owner_at ^ s) * mine
        piece = [lax.dynamic_slice_in_dim(shard, start, mine, 0) for shard in shards]
        pieces.append(cross(jnp.stack(piece), s))
    packed, out_rows, in_bias_all = lax.optimization_barrier((packed, out_rows, in_bias_all))
    vectors = packed[:, router_at + EXPERTS + experts_here :].T.astype(f32)
    out_whole = jnp.concatenate(hop_gather(out_rows, DP), axis=1)
    in_bias_mine = lax.dynamic_slice_in_dim(in_bias_all, owner_at * mine, mine, 1)
    in_bias_mine = in_bias_mine.transpose(1, 0, 2).astype(f32)

    home, within = routes // experts_here, routes % experts_here
    owner, nth = within // mine, within % mine
    kept = slot_index < CAP
    group_place = (owner // inner) * sources + home
    target = ((group_place * inner + owner % inner) * mine + nth) * CAP + slot_index
    target = jnp.where(kept, target, slots)
    plane_target = (group_place * mine + nth) * CAP + slot_index
    plane_target = jnp.where(jnp.logical_and(kept, owner % inner == inner_at), plane_target, -1)
    plane_target = plane_target.transpose(0, 2, 1)

    attended, proj = run_attend(images, packed, vectors, qv_bias.astype(f32))

    attended, out_whole = lax.optimization_barrier((attended, out_whole))
    attended_all = lax.all_gather(attended, tensor_axes)
    attended_all, pieces[::inner] = lax.optimization_barrier((attended_all, pieces[::inner]))
    mixed, probs, sent = run_route(
        images,
        cotangent,
        attended_all,
        out_whole,
        packed,
        vectors,
        routes,
        plane_target,
        groups,
        slots // inner,
    )
    sent, pieces = lax.optimization_barrier((sent, pieces))
    arrived = swap(sent, (DP, EXPERT))
    back_bias_mine = lax.dynamic_slice_in_dim(packed, router_at + EXPERTS + owner_at * mine, mine, 1)
    back_bias_mine = jnp.where(lax.axis_index(OUTER) == 0, back_bias_mine.astype(f32), 0.0)
    (
        returned_out,
        grads_out,
        hidden_low,
        grad_pre_low,
        grad_turned,
        grad_in_bias_mine,
        grad_back_bias_mine,
    ) = run_experts(
        owner_at, arrived, pieces, in_bias_mine, back_bias_mine, inner, tensor
    )

    def bring(parts):
        return swap(parts.reshape(groups * tensor, *parts.shape[2:]), everywhere)

    grad_parts = bring(grads_out)
    weight_parts = weight_grads(
        owner_at,
        arrived,
        grad_pre_low,
        grad_turned,
        hidden_low,
        grad_in_bias_mine,
        grad_back_bias_mine,
        owners,
    )
    weight_parts = [cross(part, s) for s, part in enumerate(weight_parts)]
    far = owners // 2
    grad_parts, weight_parts[: far + 1 : inner] = lax.optimization_barrier(
        (grad_parts, weight_parts[: far + 1 : inner])
    )
    rows_cut, grad_gates = run_take_grads(grad_parts, target, slice_width, outer, inner, slots)
    rows_cut, returned_out = lax.optimization_barrier((rows_cut, returned_out))
    rows_all = lax.all_gather(rows_cut, tensor_axes)
    returned = bring(returned_out)
    rows_all, returned, weight_parts[:far], weight_parts[far::inner] = lax.optimization_barrier(
        (rows_all, returned, weight_parts[:far], weight_parts[far::inner])
    )
    grad_mixed, normed_part, matrix, sums = run_pull(
        images_held,
        images,
        cotangent,
        mixed,
        probs,
        routes,
        grad_gates,
        rows_all,
        attended,
        proj,
        packed,
        vectors,
        router_at,
    )
    grad_normed = lax.psum(normed_part, tensor_axes)
    grad_images, first_sums = run_last(images, grad_normed, grad_mixed, vectors)
    first_sums, returned, weight_parts = lax.optimization_barrier(
        (first_sums, returned, weight_parts)
    )
    mixed_cut = lax.dynamic_slice_in_dim(mixed, tensor_at * slice_width, slice_width, 2)
    output_cut = run_take_rows(
        images_held, returned, target, probs, routes, mixed_cut, outer, inner, slots
    )
    output = lax.all_gather(output_cut, tensor_axes)
    output = output.reshape(tensor, image_count // PAIR, seq_len, PAIR, slice_width)
    output = output.transpose(1, 3, 2, 0, 4).reshape(images.shape)

    pair_sums = [sums[5, :local_width], sums[5, 2 * local_width : 3 * local_width]]
    pair_sums = jnp.tile(jnp.stack(pair_sums), (1, data))
    vector_grads = jnp.concatenate([first_sums[:2], sums[2:5], pair_sums], axis=0)
    high, low = high_low(vector_grads)
    small = jnp.concatenate([matrix, high.T, low.T], axis=1)
    small = swap(small.reshape(groups, shard_width // sources, -1), (DP, EXPERT))
    small = jnp.sum(small.astype(f32), axis=0)
    small = jnp.concatenate(hop_gather(small, EXPERT), axis=0)
    grad_w_qkv = small[:, : 3 * local_width].reshape(shard_width, 3, local_width).transpose(1, 0, 2)
    grad_w_out = small[:, 3 * local_width : router_at].T
    grad_w_router = small[:, router_at : router_at + EXPERTS]
    vector_grads = small[:, router_at + EXPERTS :].T
    vector_grads = vector_grads[:7] + vector_grads[7:]
    grad_w_in, grad_w_back = run_widen(owner_at, weight_parts, mine, shard_width)
    grad_w_back = grad_w_back.transpose(0, 2, 1)
    grad_in_bias = jnp.zeros((experts_here, ff_here), f32)
    grad_back_shard = jnp.zeros((experts_here, shard_width), f32)
    for s, part in enumerate(weight_parts):
        start = (owner_at ^ s) * mine
        lines = part[2 * mine * shard_width :].astype(f32)
        line = jnp.sum(lines[: 2 * mine].reshape(mine, 2, ff_here), axis=1)
        grad_in_bias = lax.dynamic_update_slice_in_dim(grad_in_bias, line, start, 0)
        line = lines[2 * mine : 3 * mine]
        line = line[:, :shard_width] + line[:, ff_here // 2 : ff_here // 2 + shard_width]
        grad_back_shard = lax.dynamic_update_slice_in_dim(grad_back_shard, line, start, 0)
    return (
        output,
        grad_images,
        vector_grads[0],
        vector_grads[1],
        grad_w_qkv,
        vector_grads[5:7],
        grad_w_out,
        vector_grads[2],
        vector_grads[3],
        vector_grads[4],
        grad_w_router,
        grad_w_in,
        grad_in_bias,
        grad_w_back,
        grad_back_shard,
    )


def specs(tensor):
    rows = P((DP, EXPERT), None, None)
    vector, square = P(DP), P(tensor, DP)
    qkv, pair, router = P(None, DP, tensor), P(None, tensor), P(DP, None)
    inward, outward = P(EXPERT, DP, tensor), P(EXPERT, tensor, DP)
    params = (vector, vector, qkv, pair, square, vector, vector, vector, router)
    experts = (inward, P(EXPERT, tensor), outward, P(EXPERT, DP))
    taken = (rows, P((DP, EXPERT)), rows, rows, *params, *experts, rows)
    given = (rows, rows, *params, *experts)
    return taken, given


def solution(mesh):
    data, expert, tensor = (mesh.shape[name] for name in (DP, EXPERT, TENSOR))
    inner = FF_PAIR if tensor % FF_PAIR == 0 else 1
    owners = data * inner
    if (EXPERTS // expert) % owners or any(n & (n - 1) for n in (data, expert, tensor)):
        taken, given = specs(TENSOR)
        return jax.shard_map(
            gathered_plan, mesh=mesh, in_specs=taken, out_specs=given, check_vma=False
        )
    devices = mesh.devices.reshape(data, expert, tensor // inner, inner)
    split_mesh = Mesh(devices, (DP, EXPERT, OUTER, INNER))
    taken, given = specs((OUTER, INNER))
    return jax.shard_map(
        moved_plan, mesh=split_mesh, in_specs=taken, out_specs=given, check_vma=False
    )
```

```python
import functools
import math

import jax
import jax.numpy as jnp
from jax import lax
from jax.experimental import pallas as pl
from jax.experimental.pallas import tpu as pltpu
from jax.sharding import Mesh
from jax.sharding import PartitionSpec as P

HEAD_DIM = 64
EXPERTS = 32
TOPK = 2
CAP = 64
FF_PAIR = 1
PAIR = 2
EXTRA = 16
VMEM_LIMIT = 56 * 1024 * 1024
GELU_SCALE = (2.0 / math.pi) ** 0.5
GELU_CUBE = 0.044715

DP = "dp"
EXPERT = "expert"
TENSOR = "tensor"
OUTER = "outer"
INNER = "inner"


EPS = 1e-06


def norm_parts(values, norm_gain, norm_shift):
    average = jnp.mean(values, axis=-1, keepdims=True)
    centred = values - average
    spread = jnp.mean(centred * centred, axis=-1, keepdims=True)
    inv_std = lax.rsqrt(spread + EPS)
    scaled = centred * inv_std
    return (scaled * norm_gain + norm_shift, scaled, inv_std)


def norm_back(grad_out, scaled, inv_std, norm_gain):
    grad_scaled = grad_out * norm_gain
    inner = grad_scaled - jnp.mean(grad_scaled, axis=-1, keepdims=True)
    inner = inner - scaled * jnp.mean(grad_scaled * scaled, axis=-1, keepdims=True)
    return (inner * inv_std, jnp.sum(grad_out * scaled, axis=0), jnp.sum(grad_out, axis=0))


def attention_forward(queries, key_rows, value_rows, scale):
    scores = (
        jnp.einsum("iqhd,ikhd->ihqk", queries, key_rows, preferred_element_type=jnp.float32) * scale
    )
    row_peak = jnp.max(scores, axis=-1, keepdims=True)
    log_total = row_peak + jnp.log(jnp.sum(jnp.exp(scores - row_peak), axis=-1, keepdims=True))
    weights = jnp.exp(scores - log_total).astype(jnp.bfloat16)
    attended = jnp.einsum(
        "ihqk,ikhd->iqhd", weights, value_rows, preferred_element_type=jnp.float32
    )
    return (attended, log_total)


def attention_backward(queries, key_rows, value_rows, log_total, grad_low, scale):
    scores = (
        jnp.einsum("iqhd,ikhd->ihqk", queries, key_rows, preferred_element_type=jnp.float32) * scale
    )
    probs = jnp.exp(scores - log_total)
    weights = probs.astype(jnp.bfloat16)
    grad_values = jnp.einsum(
        "ihqk,iqhd->ikhd", weights, grad_low, preferred_element_type=jnp.float32
    )
    grad_weights = jnp.einsum(
        "iqhd,ikhd->ihqk", grad_low, value_rows, preferred_element_type=jnp.float32
    )
    grad_scores = probs * (grad_weights - jnp.sum(probs * grad_weights, axis=-1, keepdims=True))
    scores_low = grad_scores.astype(jnp.bfloat16)
    grad_queries = (
        jnp.einsum("ihqk,ikhd->iqhd", scores_low, key_rows, preferred_element_type=jnp.float32)
        * scale
    )
    grad_keys = (
        jnp.einsum("ihqk,iqhd->ikhd", scores_low, queries, preferred_element_type=jnp.float32)
        * scale
    )
    return (grad_queries, grad_keys, grad_values)


def gathered_plan(
    images,
    images_held,
    routes,
    slot_index,
    first_gain,
    first_shift,
    w_qkv,
    qv_bias,
    w_out,
    out_bias,
    second_gain,
    second_shift,
    w_router,
    w_in,
    in_bias,
    w_back,
    back_bias,
    cotangent,
):
    image_count, seq_len, width = images.shape
    rows_total = image_count * seq_len
    experts_here = w_in.shape[0]
    (
        gain_first,
        shift_first,
        qkv_full,
        out_full,
        bias_out_full,
        gain_second,
        shift_second,
        router_full,
        in_full,
        back_full,
        back_bias_full,
    ) = (
        lax.all_gather(first_gain, DP, axis=0, tiled=True),
        lax.all_gather(first_shift, DP, axis=0, tiled=True),
        lax.all_gather(w_qkv, DP, axis=1, tiled=True),
        lax.all_gather(w_out, DP, axis=1, tiled=True),
        lax.all_gather(out_bias, DP, axis=0, tiled=True),
        lax.all_gather(second_gain, DP, axis=0, tiled=True),
        lax.all_gather(second_shift, DP, axis=0, tiled=True),
        lax.all_gather(w_router, DP, axis=0, tiled=True),
        lax.all_gather(w_in, DP, axis=1, tiled=True),
        lax.all_gather(w_back, DP, axis=2, tiled=True),
        lax.all_gather(back_bias, DP, axis=1, tiled=True),
    )
    gain_first = gain_first.astype(jnp.float32)
    gain_second = gain_second.astype(jnp.float32)
    inputs = images.reshape(rows_total, width).astype(jnp.float32)
    live_image = (jnp.arange(image_count, dtype=jnp.int32) < images_held[0]).astype(jnp.float32)
    live_rows = jnp.repeat(live_image, seq_len)[:, None]
    normed, scaled_first, inv_first = norm_parts(
        inputs, gain_first, shift_first.astype(jnp.float32)
    )
    normed_low = normed.astype(jnp.bfloat16)
    projected = jnp.einsum("td,cde->cte", normed_low, qkv_full, preferred_element_type=jnp.float32)
    local_width = projected.shape[2]
    head_count = local_width // HEAD_DIM
    head_shape = (image_count, seq_len, head_count, HEAD_DIM)
    bias_pair = qv_bias.astype(jnp.float32)
    queries = (projected[0] + bias_pair[0]).astype(jnp.bfloat16).reshape(head_shape)
    key_rows = projected[1].astype(jnp.bfloat16).reshape(head_shape)
    value_rows = (projected[2] + bias_pair[1]).astype(jnp.bfloat16).reshape(head_shape)
    scale = HEAD_DIM ** (-0.5)
    attended, log_total = attention_forward(queries, key_rows, value_rows, scale)
    attended_low = attended.reshape(rows_total, local_width).astype(jnp.bfloat16)
    head_part = jnp.dot(attended_low, out_full, preferred_element_type=jnp.float32)
    mixed = inputs + lax.psum(head_part, TENSOR) + bias_out_full.astype(jnp.float32)
    routed, scaled_second, inv_second = norm_parts(
        mixed, gain_second, shift_second.astype(jnp.float32)
    )
    routed_low = routed.astype(jnp.bfloat16)
    logits = jnp.dot(routed_low, router_full, preferred_element_type=jnp.float32)
    probs = jax.nn.softmax(logits, axis=-1)
    pair_routes = routes.reshape(rows_total, TOPK)
    pair_slots = slot_index.reshape(rows_total, TOPK)
    target = jnp.where(pair_slots < CAP, pair_routes * CAP + pair_slots, EXPERTS * CAP).reshape(
        rows_total * TOPK
    )
    gates = jnp.take_along_axis(probs, pair_routes, axis=1)
    pair_rows = jnp.repeat(routed_low, TOPK, axis=0)
    outgoing = (
        jnp.zeros((EXPERTS * CAP + 1, width), jnp.bfloat16)
        .at[target]
        .set(pair_rows)[: EXPERTS * CAP]
    )
    outgoing = outgoing.reshape(EXPERTS, 1, CAP, width)
    arrived = lax.all_to_all(outgoing, EXPERT, split_axis=0, concat_axis=1, tiled=True)
    sources = arrived.shape[1]
    expert_rows = arrived.reshape(experts_here, sources * CAP, width)
    hidden_pre = jnp.einsum(
        "erd,edf->erf", expert_rows, in_full, preferred_element_type=jnp.float32
    )
    hidden_pre = hidden_pre + in_bias.astype(jnp.float32)[:, None, :]
    hidden_value, gelu_pull = jax.vjp(jax.nn.gelu, hidden_pre)
    hidden_low = hidden_value.astype(jnp.bfloat16)
    expert_part = jnp.einsum(
        "erf,efd->erd", hidden_low, back_full, preferred_element_type=jnp.float32
    )
    bias_back = back_bias_full.astype(jnp.float32)[:, None, :]
    shares = lax.psum_scatter(
        expert_part.reshape(experts_here, sources, CAP, width),
        TENSOR,
        scatter_dimension=2,
        tiled=True,
    )
    share_low = (shares + bias_back[:, None]).astype(jnp.bfloat16)
    pieces = lax.all_to_all(share_low, EXPERT, split_axis=1, concat_axis=0, tiled=True)
    returned = lax.all_gather(pieces, TENSOR, axis=2, tiled=True)
    padded = jnp.concatenate(
        [returned.reshape(EXPERTS * CAP, width), jnp.zeros((1, width), jnp.bfloat16)], axis=0
    )
    picked = padded[target].astype(jnp.float32).reshape(rows_total, TOPK, width)
    expert_mix = jnp.sum(gates[:, :, None] * picked, axis=1)
    output = (live_rows * (mixed + expert_mix)).astype(jnp.bfloat16).reshape(images.shape)
    grad_rows = cotangent.reshape(rows_total, width).astype(jnp.float32) * live_rows
    grad_gates = jnp.sum(grad_rows[:, None, :] * picked, axis=-1)
    grad_picked = (
        (gates[:, :, None] * grad_rows[:, None, :])
        .astype(jnp.bfloat16)
        .reshape(rows_total * TOPK, width)
    )
    grad_outgoing = (
        jnp.zeros((EXPERTS * CAP + 1, width), jnp.bfloat16)
        .at[target]
        .set(grad_picked)[: EXPERTS * CAP]
    )
    grad_outgoing = grad_outgoing.reshape(EXPERTS, 1, CAP, width)
    grad_arrived = lax.all_to_all(grad_outgoing, EXPERT, split_axis=0, concat_axis=1, tiled=True)
    grad_arrived = grad_arrived.reshape(experts_here, sources * CAP, width)
    grad_back_bias = jnp.sum(grad_arrived.astype(jnp.float32), axis=1)
    grad_back_w = jnp.einsum(
        "erf,erd->efd", hidden_low, grad_arrived, preferred_element_type=jnp.float32
    )
    grad_hidden = jnp.einsum(
        "erd,efd->erf", grad_arrived, back_full, preferred_element_type=jnp.float32
    )
    grad_pre = gelu_pull(grad_hidden)[0]
    grad_in_bias_local = jnp.sum(grad_pre, axis=1)
    grad_pre_low = grad_pre.astype(jnp.bfloat16)
    grad_in_w = jnp.einsum(
        "erd,erf->edf", expert_rows, grad_pre_low, preferred_element_type=jnp.float32
    )
    grad_rows_part = jnp.einsum(
        "erf,edf->erd", grad_pre_low, in_full, preferred_element_type=jnp.float32
    )
    grad_shares = lax.psum_scatter(
        grad_rows_part.reshape(experts_here, sources, CAP, width),
        TENSOR,
        scatter_dimension=2,
        tiled=True,
    ).astype(jnp.bfloat16)
    grad_pieces = lax.all_to_all(grad_shares, EXPERT, split_axis=1, concat_axis=0, tiled=True)
    grad_returned = lax.all_gather(grad_pieces, TENSOR, axis=2, tiled=True)
    grad_padded = jnp.concatenate(
        [grad_returned.reshape(EXPERTS * CAP, width), jnp.zeros((1, width), jnp.bfloat16)], axis=0
    )
    grad_routed = jnp.sum(
        grad_padded[target].astype(jnp.float32).reshape(rows_total, TOPK, width), axis=1
    )
    expert_match = (
        pair_routes[:, :, None] == jnp.arange(EXPERTS, dtype=jnp.int32)[None, None, :]
    ).astype(jnp.float32)
    grad_probs = jnp.sum(expert_match * grad_gates[:, :, None], axis=1)
    grad_logits = probs * (grad_probs - jnp.sum(probs * grad_probs, axis=-1, keepdims=True))
    grad_logits_low = grad_logits.astype(jnp.bfloat16)
    grad_router = jnp.einsum(
        "td,te->de", routed_low, grad_logits_low, preferred_element_type=jnp.float32
    )
    grad_routed = grad_routed + jnp.einsum(
        "te,de->td", grad_logits_low, router_full, preferred_element_type=jnp.float32
    )
    grad_from_norm, grad_gain_second, grad_shift_second = norm_back(
        grad_routed, scaled_second, inv_second, gain_second
    )
    grad_mixed = grad_rows + grad_from_norm
    grad_bias_out = jnp.sum(grad_mixed, axis=0)
    grad_mixed_low = grad_mixed.astype(jnp.bfloat16)
    grad_out_w = jnp.einsum(
        "te,td->ed", attended_low, grad_mixed_low, preferred_element_type=jnp.float32
    )
    grad_attended = jnp.einsum(
        "td,ed->te", grad_mixed_low, out_full, preferred_element_type=jnp.float32
    )
    grad_attended = grad_attended.astype(jnp.bfloat16).reshape(head_shape)
    grad_queries, grad_keys, grad_values = attention_backward(
        queries, key_rows, value_rows, log_total, grad_attended, scale
    )
    grad_queries = grad_queries.reshape(rows_total, local_width)
    grad_keys = grad_keys.reshape(rows_total, local_width)
    grad_values = grad_values.reshape(rows_total, local_width)
    grad_pair_bias = jnp.stack([jnp.sum(grad_queries, axis=0), jnp.sum(grad_values, axis=0)])
    grad_proj_low = jnp.stack([grad_queries, grad_keys, grad_values]).astype(jnp.bfloat16)
    grad_qkv = jnp.einsum(
        "td,cte->cde", normed_low, grad_proj_low, preferred_element_type=jnp.float32
    )
    grad_normed_part = jnp.einsum(
        "cte,cde->td", grad_proj_low, qkv_full, preferred_element_type=jnp.float32
    )
    grad_normed = lax.psum(grad_normed_part, TENSOR)
    grad_from_first, grad_gain_first, grad_shift_first = norm_back(
        grad_normed, scaled_first, inv_first, gain_first
    )
    grad_images = (grad_mixed + grad_from_first).reshape(images.shape)
    expert_start = lax.axis_index(EXPERT) * experts_here
    full_in_bias = lax.dynamic_update_slice(
        jnp.zeros((EXPERTS, grad_in_bias_local.shape[1]), jnp.float32),
        grad_in_bias_local,
        (expert_start, jnp.zeros((), jnp.int32)),
    )
    summed = lax.psum(
        (
            grad_gain_first,
            grad_shift_first,
            grad_qkv,
            grad_pair_bias,
            grad_out_w,
            grad_bias_out,
            grad_gain_second,
            grad_shift_second,
            grad_router,
            full_in_bias,
        ),
        (DP, EXPERT),
    )
    shard_width = width // lax.axis_size(DP)
    shard_start = lax.axis_index(DP) * shard_width
    grad_first_gain = lax.dynamic_slice_in_dim(summed[0], shard_start, shard_width, 0)
    grad_first_shift = lax.dynamic_slice_in_dim(summed[1], shard_start, shard_width, 0)
    grad_w_qkv = lax.dynamic_slice_in_dim(summed[2], shard_start, shard_width, 1)
    grad_qv_bias = summed[3]
    grad_w_out = lax.dynamic_slice_in_dim(summed[4], shard_start, shard_width, 1)
    grad_out_bias = lax.dynamic_slice_in_dim(summed[5], shard_start, shard_width, 0)
    grad_second_gain = lax.dynamic_slice_in_dim(summed[6], shard_start, shard_width, 0)
    grad_second_shift = lax.dynamic_slice_in_dim(summed[7], shard_start, shard_width, 0)
    grad_w_router = lax.dynamic_slice_in_dim(summed[8], shard_start, shard_width, 0)
    grad_in_bias = lax.dynamic_slice_in_dim(summed[9], expert_start, experts_here, 0)
    grad_w_in, grad_w_back, grad_back_shard = (
        lax.psum_scatter(grad_in_w, DP, scatter_dimension=1, tiled=True),
        lax.psum_scatter(grad_back_w, DP, scatter_dimension=2, tiled=True),
        lax.psum_scatter(grad_back_bias, DP, scatter_dimension=1, tiled=True),
    )
    return (
        output,
        grad_images,
        grad_first_gain,
        grad_first_shift,
        grad_w_qkv,
        grad_qv_bias,
        grad_w_out,
        grad_out_bias,
        grad_second_gain,
        grad_second_shift,
        grad_w_router,
        grad_w_in,
        grad_in_bias,
        grad_w_back,
        grad_back_shard,
    )


def swap(values, axes):
    return lax.all_to_all(values, axes, split_axis=0, concat_axis=0, tiled=True)


def hop_gather(values, axes):
    count, at = lax.axis_size(axes), lax.axis_index(axes)
    hops = [values]
    for s in range(1, count):
        hops.append(lax.ppermute(values, axes, [(i, i ^ s) for i in range(count)]))
    gathered = []
    for i in range(count):
        found = hops[0]
        for s in range(1, count):
            found = jnp.where(at ^ i == s, hops[s], found)
        gathered.append(found)
    return gathered


def cross(values, s):
    count = lax.axis_size((DP, INNER))
    return lax.ppermute(values, (DP, INNER), [(i, i ^ s) for i in range(count)]) if s else values


def high_low(values):
    high = lax.reduce_precision(values, 8, 7)
    return high.astype(jnp.bfloat16), (values - high).astype(jnp.bfloat16)


def turned_dot(left, right, left_dim, right_dim):
    return lax.dot_general(
        left, right, (((left_dim,), (right_dim,)), ((), ())), preferred_element_type=jnp.float32
    )


def expert_kernel(inner, owners, at_ref, rows_ref, gate_ref, cot_ref, in_bias_ref, back_bias_ref, *refs):
    in_refs, back_refs, refs = refs[:owners], refs[owners : 2 * owners], refs[2 * owners :]
    returned_ref, grads_ref, hidden_ref, grad_pre_ref, grad_turned_ref = refs[:5]
    grad_in_bias_ref, grad_back_bias_ref, weight_ref = refs[5:]
    f32, bf16 = jnp.float32, jnp.bfloat16
    groups, cap, width = rows_ref.shape
    depth = in_refs[0].shape[1]
    for s in range(owners):
        source = at_ref[0] ^ s
        place = pl.ds(pl.multiple_of((source // inner) * depth, depth), depth)
        weight_ref[0, source % inner, place] = in_refs[s][0]
        weight_ref[1, source % inner, place] = back_refs[s][0]
    tensor, slice_width = returned_ref.shape[1:3]
    mine = back_bias_ref.shape[1]
    total = groups * cap
    at = pl.program_id(0)
    rows = rows_ref[...].reshape(total, width)
    cot_turned = cot_ref[...].reshape(total, width).T.astype(f32)
    pair = gate_ref[:, 0:1, :].astype(f32) + gate_ref[:, 1:2, :].astype(f32)
    pair = pair.reshape(groups, pair.shape[-1])
    gate = jnp.zeros((groups, cap), f32)
    for j in range(mine):
        gate = jnp.where(at == j, pair[:, j * cap : (j + 1) * cap], gate)
    gate = jnp.concatenate([gate[g : g + 1, :] for g in range(groups)], axis=1)
    grad_turned = (cot_turned * gate).astype(bf16)
    grad_turned_ref[0] = grad_turned
    grad_returned = grad_turned.T
    grad_back_bias_ref[0] = jnp.sum(grad_returned.astype(f32), axis=0, keepdims=True)
    bias_columns = back_bias_ref[...]
    bias = jnp.zeros((width, 1), f32)
    for j in range(mine):
        bias = jnp.where(at == j, bias_columns[:, j : j + 1], bias)
    part = jnp.broadcast_to(bias, (width, total))
    back = jnp.zeros((width, total), f32)
    for t in range(inner):
        w_in, w_back = weight_ref[0, t], weight_ref[1, t]
        pre = jnp.dot(rows, w_in, preferred_element_type=f32) + in_bias_ref[0, t : t + 1, :]
        square = pre * pre
        bent = jnp.tanh(GELU_SCALE * pre * (1.0 + GELU_CUBE * square))
        half = 0.5 * (1.0 + bent)
        hidden = (pre * half).astype(bf16)
        slope = half + (0.5 * GELU_SCALE) * pre * (1.0 - bent * bent) * (
            1.0 + (3.0 * GELU_CUBE) * square
        )
        hidden_ref[0, t] = hidden
        grad_pre = jnp.dot(grad_returned, w_back, preferred_element_type=f32) * slope
        grad_in_bias_ref[0, t : t + 1, :] = jnp.sum(grad_pre, axis=0, keepdims=True)
        grad_pre = grad_pre.astype(bf16)
        grad_pre_ref[0, t] = grad_pre
        part = part + turned_dot(w_back, hidden, 1, 1)
        back = back + turned_dot(w_in, grad_pre, 1, 1)
    gate_terms = jnp.sum(part * cot_turned, axis=0, keepdims=True)
    high = gate_terms.astype(bf16)
    low = (gate_terms - high.astype(f32)).astype(bf16)
    extra = grads_ref.shape[2] - slice_width
    tail = jnp.concatenate([high, low, jnp.zeros((extra - 2, total), bf16)], axis=0)
    part = part.astype(bf16)
    back = back.astype(bf16)
    for j in range(mine):

        @pl.when(at == j)
        def _():
            lanes = slice(j * cap, (j + 1) * cap)
            for g in range(groups):
                mine_lanes = slice(g * cap, (g + 1) * cap)
                for z in range(tensor):
                    features = slice(z * slice_width, (z + 1) * slice_width)
                    returned_ref[g, z, :, lanes] = part[features, mine_lanes]
                    grads_ref[g, z, :slice_width, lanes] = back[features, mine_lanes]
                    grads_ref[g, z, slice_width:, lanes] = tail[:, mine_lanes]


def run_experts(owner_at, arrived, in_pieces, back_pieces, in_bias, back_bias, inner, tensor):
    f32, bf16 = jnp.float32, jnp.bfloat16
    groups, _, width = arrived.shape
    owners = len(in_pieces)
    mine, depth, ff = in_pieces[0].shape
    total = groups * CAP
    slice_width = width // tensor
    gate_at = 2 * mine * CAP // EXTRA
    outs = [
        ((groups, tensor, slice_width, mine * CAP), bf16, lambda j: (0, 0, 0, 0), None),
        ((groups, tensor, slice_width + EXTRA, mine * CAP), bf16, lambda j: (0, 0, 0, 0), None),
        ((mine, inner, total, ff), bf16, lambda j: (j, 0, 0, 0), 1),
        ((mine, inner, total, ff), bf16, lambda j: (j, 0, 0, 0), 1),
        ((mine, width, total), bf16, lambda j: (j, 0, 0), 1),
        ((mine, inner, ff), f32, lambda j: (j, 0, 0), 1),
        ((mine, 1, width), f32, lambda j: (j, 0, 0), 1),
    ]
    return pl.pallas_call(
        functools.partial(expert_kernel, inner, owners),
        grid=(mine,),
        in_specs=[
            pl.BlockSpec(memory_space=pltpu.SMEM),
            pl.BlockSpec((groups, CAP, width), lambda j: (0, j, 0)),
            pl.BlockSpec((groups, EXTRA, mine * CAP), lambda j: (0, gate_at, 0)),
            pl.BlockSpec((groups, CAP, width), lambda j: (0, mine + j, 0)),
            pl.BlockSpec((1, inner, ff), lambda j: (j, 0, 0)),
            pl.BlockSpec((width, mine), lambda j: (0, 0)),
        ]
        + [pl.BlockSpec((1, depth, ff), lambda j: (j, 0, 0))] * (2 * owners),
        out_specs=[
            pl.BlockSpec(shape if lead is None else (lead, *shape[1:]), index)
            for shape, _, index, lead in outs
        ],
        out_shape=[jax.ShapeDtypeStruct(shape, dtype) for shape, dtype, _, _ in outs],
        scratch_shapes=[pltpu.VMEM((2, inner, width, ff), bf16)],
        compiler_params=pltpu.CompilerParams(vmem_limit_bytes=VMEM_LIMIT),
        cost_estimate=pl.CostEstimate(
            flops=8 * mine * total * width * inner * ff,
            bytes_accessed=4 * owners * mine * depth * ff + 12 * mine * total * inner * ff,
            transcendentals=mine * total * inner * ff,
        ),
    )(owner_at.reshape(1), arrived, arrived, arrived, in_bias, back_bias, *in_pieces, *back_pieces)


def weight_kernel(
    inner,
    at_ref,
    rows_ref,
    grad_pre_ref,
    grad_turned_ref,
    hidden_ref,
    in_bias_ref,
    back_bias_ref,
    *refs,
):
    f32, bf16 = jnp.float32, jnp.bfloat16
    out_refs, sums_ref, tail_ref = refs[:-2], refs[-2], refs[-1]
    groups, cap, width = rows_ref.shape
    mine = back_bias_ref.shape[0]
    ff = sums_ref.shape[-1]
    depth = width * inner // len(out_refs)
    data = width // depth
    part, at = pl.program_id(0), pl.program_id(1)
    rows = rows_ref[...].reshape(groups * cap, width)
    sums_ref[0] = turned_dot(rows, grad_pre_ref[0, 0], 0, 0).astype(bf16)
    grad_back = jnp.dot(grad_turned_ref[0], hidden_ref[0, 0], preferred_element_type=f32)
    sums_ref[1] = grad_back.astype(bf16)

    @pl.when(at == mine - 1)
    def _():
        pairs = []
        for j in range(mine):
            values = in_bias_ref[j, 0]
            high = values.astype(bf16).astype(f32)
            pairs += [high, values - high]
        for d in range(data):
            lines = list(pairs)
            for j in range(mine):
                values = back_bias_ref[j, :, d * depth : (d + 1) * depth]
                high = values.astype(bf16).astype(f32)
                gap = jnp.zeros((1, ff // 2 - depth), f32)
                lines.append(jnp.concatenate([high, gap, values - high, gap], axis=1))
            lines.append(jnp.zeros((EXTRA - len(lines), ff), f32))
            tail_ref[d] = jnp.concatenate(lines, axis=0).astype(bf16)

    for s, out_ref in enumerate(out_refs):
        owner = at_ref[0] ^ s
        d = owner // inner
        place = pl.ds(pl.multiple_of(d * depth, depth), depth)

        @pl.when(owner % inner == part)
        def _():
            for k in range(2):
                line = pl.multiple_of((k * mine + at) * depth, depth)
                out_ref[pl.ds(line, depth)] = sums_ref[k, place]

            @pl.when(at == mine - 1)
            def _():
                out_ref[2 * mine * depth :] = tail_ref[d]


def weight_grads(
    owner_at, arrived, grad_pre, grad_turned, hidden, grad_in_bias, grad_back_bias, owners
):
    mine, inner, total, ff = hidden.shape
    groups, _, width = arrived.shape
    depth = width * inner // owners
    kept = pl.BlockSpec((1, 1, total, ff), lambda t, j: (j, t, 0, 0))
    out = (2 * mine * depth + EXTRA, ff)
    return pl.pallas_call(
        functools.partial(weight_kernel, inner),
        grid=(inner, mine),
        in_specs=[
            pl.BlockSpec(memory_space=pltpu.SMEM),
            pl.BlockSpec((groups, CAP, width), lambda t, j: (0, j, 0)),
            kept,
            pl.BlockSpec((1, width, total), lambda t, j: (j, 0, 0)),
            kept,
            pl.BlockSpec((mine, 1, 1, ff), lambda t, j: (0, t, 0, 0)),
            pl.BlockSpec((mine, 1, width), lambda t, j: (0, 0, 0)),
        ],
        out_specs=[pl.BlockSpec(out, lambda t, j: (0, 0))] * owners,
        out_shape=[jax.ShapeDtypeStruct(out, jnp.bfloat16)] * owners,
        scratch_shapes=[
            pltpu.VMEM((2, width, ff), jnp.bfloat16),
            pltpu.VMEM((width // depth, EXTRA, ff), jnp.bfloat16),
        ],
        compiler_params=pltpu.CompilerParams(vmem_limit_bytes=VMEM_LIMIT),
        cost_estimate=pl.CostEstimate(
            flops=4 * mine * total * width * inner * ff,
            bytes_accessed=4 * mine * inner * (total + width) * ff,
            transcendentals=0,
        ),
    )(
        owner_at.reshape(1),
        arrived,
        grad_pre,
        grad_turned,
        hidden,
        grad_in_bias[:, :, None],
        grad_back_bias,
    )


def widen_kernel(at_ref, *refs):
    part_refs, (in_ref, back_ref) = refs[:-2], refs[-2:]
    mine, depth, ff = in_ref.shape
    rows = mine * depth
    for s, part_ref in enumerate(part_refs):

        @pl.when(pl.program_id(0) == s)
        def _():
            in_ref[...] = part_ref[:rows].astype(jnp.float32).reshape(mine, depth, ff)
            back_ref[...] = part_ref[rows : 2 * rows].astype(jnp.float32).reshape(mine, depth, ff)


def run_widen(owner_at, parts, mine, depth):
    owners, ff = len(parts), parts[0].shape[1]
    out = pl.BlockSpec((mine, depth, ff), lambda p, at: (at[0] ^ p, 0, 0))
    return pl.pallas_call(
        widen_kernel,
        grid_spec=pltpu.PrefetchScalarGridSpec(
            num_scalar_prefetch=1,
            grid=(owners,),
            in_specs=[pl.BlockSpec((2 * mine * depth, ff), lambda p, at: (0, 0))] * owners,
            out_specs=[out, out],
        ),
        out_shape=[jax.ShapeDtypeStruct((owners * mine, depth, ff), jnp.float32)] * 2,
        compiler_params=pltpu.CompilerParams(vmem_limit_bytes=VMEM_LIMIT),
    )(owner_at.reshape(1), *parts)


def norm_rows(values):
    average = jnp.mean(values, axis=-1, keepdims=True)
    centred = values - average
    spread = jnp.mean(centred * centred, axis=-1, keepdims=True)
    inv_std = lax.rsqrt(spread + EPS)
    return centred * inv_std, inv_std


def norm_rows_back(grad_out, scaled, inv_std, norm_gain):
    grad_scaled = grad_out * norm_gain
    inner = grad_scaled - jnp.mean(grad_scaled, axis=-1, keepdims=True)
    inner = inner - scaled * jnp.mean(grad_scaled * scaled, axis=-1, keepdims=True)
    return inner * inv_std


def call_kernel(kernel, grid, inputs, outputs, scratch=(), flops=0):
    smem = pl.BlockSpec(memory_space=pltpu.SMEM)
    return pl.pallas_call(
        kernel,
        grid=grid,
        in_specs=[smem if b is None else pl.BlockSpec(b, i) for _, b, i in inputs],
        out_specs=[pl.BlockSpec(b, i) for _, _, b, i in outputs],
        out_shape=[jax.ShapeDtypeStruct(shape, dtype) for shape, dtype, _, _ in outputs],
        scratch_shapes=list(scratch),
        compiler_params=pltpu.CompilerParams(vmem_limit_bytes=VMEM_LIMIT),
        cost_estimate=pl.CostEstimate(
            flops=flops,
            bytes_accessed=sum(a.size * a.dtype.itemsize for a, _, _ in inputs),
            transcendentals=0,
        ),
    )(*(a for a, _, _ in inputs))


def whole(array):
    return array, array.shape, lambda p: (0,) * array.ndim


def by_step(array, lead):
    return array, (lead, *array.shape[1:]), lambda p: (p,) + (0,) * (array.ndim - 1)


def attend_kernel(images_ref, packed_ref, vector_ref, bias_ref, attended_ref, proj_ref):
    f32, bf16 = jnp.float32, jnp.bfloat16
    local = bias_ref.shape[1]
    weight = packed_ref[:, : 3 * local]
    for h in range(images_ref.shape[0]):
        scaled, _ = norm_rows(images_ref[h].astype(f32))
        normed = (scaled * vector_ref[0:1] + vector_ref[1:2]).astype(bf16)
        proj = jnp.dot(normed, weight, preferred_element_type=f32)
        queries = (proj[:, :local] + bias_ref[0:1]).astype(bf16)
        keys = proj[:, local : 2 * local].astype(bf16)
        values = (proj[:, 2 * local :] + bias_ref[1:2]).astype(bf16)
        proj_ref[h] = jnp.concatenate([queries, keys, values], axis=1)
        parts = []
        for n in range(0, local, HEAD_DIM):
            head = slice(n, n + HEAD_DIM)
            scores = turned_dot(queries[:, head], keys[:, head], 1, 1) * HEAD_DIM**-0.5
            scores = jnp.exp(scores - jnp.max(scores, axis=-1, keepdims=True))
            weights = scores / jnp.sum(scores, axis=-1, keepdims=True)
            parts.append(
                jnp.dot(weights.astype(bf16), values[:, head], preferred_element_type=f32)
            )
        attended_ref[0, :, h * local : (h + 1) * local] = jnp.concatenate(parts, axis=1).astype(bf16)


def run_attend(images, packed, vectors, qv_bias):
    count, length, width = images.shape
    local = qv_bias.shape[1]
    return call_kernel(
        attend_kernel,
        (count // PAIR,),
        [by_step(images, PAIR), whole(packed), whole(vectors), whole(qv_bias)],
        [
            ((count // PAIR, length, PAIR * local), jnp.bfloat16, (1, length, PAIR * local), lambda p: (p, 0, 0)),
            ((count, length, 3 * local), jnp.bfloat16, (PAIR, length, 3 * local), lambda p: (p, 0, 0)),
        ],
        flops=2 * count * length * local * (3 * width + 4 * length),
    )


def slot_hits(target_row, count):
    return lax.broadcasted_iota(jnp.int32, (count, target_row.shape[1]), 0) == target_row


def route_kernel(
    router_at,
    images_ref,
    cot_ref,
    attended_ref,
    out_ref,
    packed_ref,
    vector_ref,
    routes_ref,
    target_ref,
    mixed_ref,
    probs_ref,
    sent_ref,
    sum_ref,
    gate_ref,
):
    f32, bf16 = jnp.float32, jnp.bfloat16
    slots = sum_ref.shape[1]
    tensor, local = attended_ref.shape[0], attended_ref.shape[3] // images_ref.shape[0]
    at = pl.program_id(0)

    @pl.when(at == 0)
    def _():
        sum_ref[...] = jnp.zeros_like(sum_ref)
        gate_ref[...] = jnp.zeros_like(gate_ref)

    router = packed_ref[:, router_at : router_at + EXPERTS]
    for h in range(images_ref.shape[0]):
        mixed = images_ref[h].astype(f32) + vector_ref[2:3]
        for z in range(tensor):
            part = attended_ref[z, 0, :, h * local : (h + 1) * local]
            weight = out_ref[z * local : (z + 1) * local]
            mixed = mixed + jnp.dot(part, weight, preferred_element_type=f32)
        mixed_ref[h] = mixed
        scaled, _ = norm_rows(mixed)
        routed = (scaled * vector_ref[3:4] + vector_ref[4:5]).astype(bf16)
        logits = jnp.dot(routed, router, preferred_element_type=f32)
        logits = jnp.exp(logits - jnp.max(logits, axis=-1, keepdims=True))
        probs = logits / jnp.sum(logits, axis=-1, keepdims=True)
        probs_ref[h] = probs
        experts = lax.broadcasted_iota(jnp.int32, probs.shape, 1)
        fill = jnp.zeros((slots, probs.shape[0]), f32)
        for k in range(TOPK):
            match = experts == routes_ref[h, :, k : k + 1]
            gate = jnp.sum(jnp.where(match, probs, 0.0), axis=1, keepdims=True)
            high = gate.astype(bf16)
            low = (gate - high.astype(f32)).astype(bf16)
            pair = jnp.concatenate([high, low, jnp.zeros((gate.shape[0], 6), bf16)], axis=1)
            hit = slot_hits(target_ref[h, k : k + 1], slots).astype(f32)
            fill = fill + hit
            gate_ref[...] += turned_dot(pair, hit.astype(bf16), 0, 1)
        fill = fill.astype(bf16)
        sum_ref[0] += jnp.dot(fill, routed, preferred_element_type=f32)
        sum_ref[1] += jnp.dot(fill, cot_ref[h], preferred_element_type=f32)

    @pl.when(at == pl.num_programs(0) - 1)
    def _():
        groups, lines, width = sent_ref.shape
        here = slots // groups
        for g in range(groups):
            lanes = slice(g * here, (g + 1) * here)
            sent_ref[g, :here] = sum_ref[0, lanes].astype(bf16)
            sent_ref[g, here : 2 * here] = sum_ref[1, lanes].astype(bf16)
            gates = jnp.concatenate([gate_ref[:, lanes], jnp.zeros((8, width - here), f32)], axis=1)
            gates = jnp.concatenate([gates, jnp.zeros((lines - 2 * here - 8, width), f32)], axis=0)
            sent_ref[g, 2 * here :] = gates.astype(bf16)


def run_route(
    images, cot, attended_all, out_whole, packed, vectors, routes, plane_target, groups, slots_plane
):
    f32, bf16 = jnp.float32, jnp.bfloat16
    count, length, width = images.shape
    tensor = attended_all.shape[0]
    sent = (groups, 2 * slots_plane // groups + EXTRA, width)
    return call_kernel(
        functools.partial(route_kernel, tensor * attended_all.shape[3] // PAIR),
        (count // PAIR,),
        [
            by_step(images, PAIR),
            by_step(cot, PAIR),
            (attended_all, (tensor, 1, *attended_all.shape[2:]), lambda p: (0, p, 0, 0)),
            whole(out_whole),
            whole(packed),
            whole(vectors),
            by_step(routes, PAIR),
            by_step(plane_target, PAIR),
        ],
        [
            ((count, length, width), f32, (PAIR, length, width), lambda p: (p, 0, 0)),
            ((count, length, EXPERTS), f32, (PAIR, length, EXPERTS), lambda p: (p, 0, 0)),
            (sent, bf16, sent, lambda p: (0, 0, 0)),
        ],
        [pltpu.VMEM((2, slots_plane, width), f32), pltpu.VMEM((8, slots_plane), f32)],
        flops=2 * count * length * width * (width + 2 * slots_plane),
    )


def slot_blocks(parts_ref, slots_ref, outer, inner):
    here = parts_ref.shape[2]
    for b in range(slots_ref.shape[1] // here):
        first = (b // inner) * outer * inner + b % inner
        total = parts_ref[first].astype(jnp.float32)
        for o in range(1, outer):
            total = total + parts_ref[first + o * inner].astype(jnp.float32)
        slots_ref[:, b * here : (b + 1) * here] = total


def token_hits(target_column, count):
    return lax.broadcasted_iota(jnp.int32, (target_column.shape[0], count), 1) == target_column


def take_grads_kernel(outer, inner, parts_ref, target_ref, rows_ref, gates_ref, slots_ref):
    f32, bf16 = jnp.float32, jnp.bfloat16
    slots = slots_ref.shape[1]
    local = rows_ref.shape[2] // target_ref.shape[0]

    @pl.when(pl.program_id(0) == 0)
    def _():
        slot_blocks(parts_ref, slots_ref, outer, inner)

    grads = slots_ref[:local].astype(bf16)
    gate_terms = slots_ref[local : local + 1] + slots_ref[local + 1 : local + 2]
    for h in range(target_ref.shape[0]):
        hits = [token_hits(target_ref[h, :, k : k + 1], slots) for k in range(TOPK)]
        find = jnp.logical_or(hits[0], hits[1]).astype(f32).astype(bf16)
        rows_ref[0, :, h * local : (h + 1) * local] = turned_dot(find, grads, 1, 1).astype(bf16)
        terms = [
            jnp.sum(jnp.where(hit, gate_terms, 0.0), axis=1, keepdims=True) for hit in hits
        ]
        gates_ref[h] = jnp.concatenate(terms, axis=1)


def run_take_grads(parts, target, local, outer, inner, slots):
    count, length, _ = target.shape
    return call_kernel(
        functools.partial(take_grads_kernel, outer, inner),
        (count // PAIR,),
        [whole(parts), by_step(target, PAIR)],
        [
            ((count // PAIR, length, PAIR * local), jnp.bfloat16, (1, length, PAIR * local), lambda p: (p, 0, 0)),
            ((count, length, TOPK), jnp.float32, (PAIR, length, TOPK), lambda p: (p, 0, 0)),
        ],
        [pltpu.VMEM((parts.shape[1], slots), jnp.float32)],
        flops=2 * count * length * slots * local,
    )


def take_rows_kernel(
    outer, inner, held_ref, parts_ref, target_ref, probs_ref, routes_ref, mixed_ref, out_ref, slots_ref
):
    f32, bf16 = jnp.float32, jnp.bfloat16
    slots = slots_ref.shape[1]
    pair = target_ref.shape[0]
    local = out_ref.shape[2] // pair
    at = pl.program_id(0)

    @pl.when(at == 0)
    def _():
        slot_blocks(parts_ref, slots_ref, outer, inner)

    returned = slots_ref[...].astype(bf16)
    for h in range(pair):
        probs = probs_ref[h]
        experts = lax.broadcasted_iota(jnp.int32, probs.shape, 1)
        rows = mixed_ref[h]
        for k in range(TOPK):
            match = experts == routes_ref[h, :, k : k + 1]
            gate = jnp.sum(jnp.where(match, probs, 0.0), axis=1, keepdims=True)
            find = token_hits(target_ref[h, :, k : k + 1], slots).astype(f32).astype(bf16)
            rows = rows + gate * turned_dot(find, returned, 1, 1)
        live = (at * pair + h < held_ref[0]).astype(f32)
        out_ref[0, :, h * local : (h + 1) * local] = (live * rows).astype(bf16)


def run_take_rows(held, parts, target, probs, routes, mixed_cut, outer, inner, slots):
    count, length, local = mixed_cut.shape
    return call_kernel(
        functools.partial(take_rows_kernel, outer, inner),
        (count // PAIR,),
        [
            (held, None, None),
            whole(parts),
            by_step(target, PAIR),
            by_step(probs, PAIR),
            by_step(routes, PAIR),
            by_step(mixed_cut, PAIR),
        ],
        [((count // PAIR, length, PAIR * local), jnp.bfloat16, (1, length, PAIR * local), lambda p: (p, 0, 0))],
        [pltpu.VMEM((parts.shape[1], slots), jnp.float32)],
        flops=4 * count * length * slots * local,
    )[0]


def pull_kernel(
    router_at,
    held_ref,
    images_ref,
    cot_ref,
    mixed_ref,
    probs_ref,
    routes_ref,
    gates_ref,
    rows_ref,
    attended_ref,
    proj_ref,
    packed_ref,
    vector_ref,
    grad_mixed_ref,
    normed_ref,
    matrix_ref,
    sums_ref,
    matrix_sum_ref,
):
    f32, bf16 = jnp.float32, jnp.bfloat16
    pair = images_ref.shape[0]
    tensor = rows_ref.shape[0]
    local = attended_ref.shape[2] // pair
    width = images_ref.shape[2]
    at = pl.program_id(0)

    @pl.when(at == 0)
    def _():
        sums_ref[...] = jnp.zeros_like(sums_ref)
        matrix_sum_ref[...] = jnp.zeros_like(matrix_sum_ref)

    qkv = packed_ref[:, : 3 * local]
    out_turned = packed_ref[:, 3 * local : 4 * local]
    router = packed_ref[:, router_at : router_at + EXPERTS]
    scale = HEAD_DIM**-0.5
    for h in range(pair):
        lanes = slice(h * local, (h + 1) * local)
        live = (at * pair + h < held_ref[0]).astype(f32)
        cot = cot_ref[h].astype(f32) * live
        scaled, inv_std = norm_rows(mixed_ref[h])
        routed = (scaled * vector_ref[3:4] + vector_ref[4:5]).astype(bf16)
        probs = probs_ref[h]
        experts = lax.broadcasted_iota(jnp.int32, probs.shape, 1)
        grad_probs = jnp.zeros(probs.shape, f32)
        for k in range(TOPK):
            match = experts == routes_ref[h, :, k : k + 1]
            grad_probs = grad_probs + jnp.where(match, gates_ref[h, :, k : k + 1], 0.0)
        grad_logits = probs * (grad_probs - jnp.sum(probs * grad_probs, axis=-1, keepdims=True))
        grad_logits = grad_logits.astype(bf16)
        grad_routed = jnp.concatenate([rows_ref[z, 0, :, lanes] for z in range(tensor)], axis=1)
        grad_routed = grad_routed.astype(f32) + turned_dot(grad_logits, router, 1, 1)
        grad_mixed = cot + norm_rows_back(grad_routed, scaled, inv_std, vector_ref[3:4])
        grad_mixed_ref[h] = grad_mixed
        low = grad_mixed.astype(bf16)
        grad_attended = jnp.dot(low, out_turned, preferred_element_type=f32).astype(bf16)
        proj = proj_ref[h]
        grads = [[], [], []]
        for n in range(0, local, HEAD_DIM):
            queries = proj[:, n : n + HEAD_DIM]
            keys = proj[:, local + n : local + n + HEAD_DIM]
            values = proj[:, 2 * local + n : 2 * local + n + HEAD_DIM]
            grad_head = grad_attended[:, n : n + HEAD_DIM]
            scores = turned_dot(queries, keys, 1, 1) * scale
            scores = jnp.exp(scores - jnp.max(scores, axis=-1, keepdims=True))
            weights = scores / jnp.sum(scores, axis=-1, keepdims=True)
            grads[2].append(turned_dot(weights.astype(bf16), grad_head, 0, 0))
            grad_weights = turned_dot(grad_head, values, 1, 1)
            inner = jnp.sum(weights * grad_weights, axis=-1, keepdims=True)
            grad_scores = (weights * (grad_weights - inner)).astype(bf16)
            grads[0].append(jnp.dot(grad_scores, keys, preferred_element_type=f32) * scale)
            grads[1].append(turned_dot(grad_scores, queries, 0, 0) * scale)
        grad_proj = jnp.concatenate(grads[0] + grads[1] + grads[2], axis=1)
        proj_sum = jnp.sum(grad_proj, axis=0, keepdims=True)
        grad_proj = grad_proj.astype(bf16)
        first, _ = norm_rows(images_ref[h].astype(f32))
        normed = (first * vector_ref[0:1] + vector_ref[1:2]).astype(bf16)
        grad_normed = turned_dot(grad_proj, qkv, 1, 1)
        normed_ref[h] = grad_normed.astype(bf16)
        attended = attended_ref[0, :, lanes]
        matrix = jnp.concatenate(
            [
                turned_dot(normed, grad_proj, 0, 0),
                turned_dot(low, attended, 0, 0),
                turned_dot(routed, grad_logits, 0, 0),
            ],
            axis=1,
        )
        matrix_sum_ref[...] += matrix
        column = lambda values: jnp.sum(values, axis=0, keepdims=True)
        sums_ref[2:3] += column(grad_mixed)
        sums_ref[3:4] += column(grad_routed * scaled)
        sums_ref[4:5] += column(grad_routed)
        sums_ref[5:6, : 3 * local] += proj_sum

    @pl.when(at == pl.num_programs(0) - 1)
    def _():
        matrix_ref[...] = matrix_sum_ref[...].astype(bf16)


def run_pull(held, images, cot, mixed, probs, routes, gates, rows_all, attended, proj, packed, vectors, router_at):
    f32, bf16 = jnp.float32, jnp.bfloat16
    count, length, width = images.shape
    tensor = rows_all.shape[0]
    local = proj.shape[2] // 3
    tokens = (count, length, width)
    block = (PAIR, length, width)
    step = lambda p: (p, 0, 0)
    still = lambda p: (0, 0)
    matrix = (width, 4 * local + EXPERTS)
    return call_kernel(
        functools.partial(pull_kernel, router_at),
        (count // PAIR,),
        [
            (held, None, None),
            by_step(images, PAIR),
            by_step(cot, PAIR),
            by_step(mixed, PAIR),
            by_step(probs, PAIR),
            by_step(routes, PAIR),
            by_step(gates, PAIR),
            (rows_all, (tensor, 1, *rows_all.shape[2:]), lambda p: (0, p, 0, 0)),
            by_step(attended, 1),
            by_step(proj, PAIR),
            whole(packed),
            whole(vectors),
        ],
        [
            (tokens, f32, block, step),
            (tokens, bf16, block, step),
            (matrix, bf16, matrix, still),
            ((8, width), f32, (8, width), still),
        ],
        [pltpu.VMEM(matrix, f32)],
        flops=2 * count * length * (width * 12 * local + 14 * length * local),
    )


def last_kernel(images_ref, normed_ref, mixed_ref, vector_ref, out_ref, sums_ref):
    @pl.when(pl.program_id(0) == 0)
    def _():
        sums_ref[...] = jnp.zeros_like(sums_ref)

    for h in range(images_ref.shape[0]):
        scaled, inv_std = norm_rows(images_ref[h].astype(jnp.float32))
        grad = normed_ref[h].astype(jnp.float32)
        out_ref[h] = mixed_ref[h] + norm_rows_back(grad, scaled, inv_std, vector_ref[0:1])
        sums_ref[0:1] += jnp.sum(grad * scaled, axis=0, keepdims=True)
        sums_ref[1:2] += jnp.sum(grad, axis=0, keepdims=True)


def run_last(images, grad_normed, grad_mixed, vectors):
    width = images.shape[2]
    return call_kernel(
        last_kernel,
        (images.shape[0],),
        [by_step(images, 1), by_step(grad_normed, 1), by_step(grad_mixed, 1), whole(vectors)],
        [
            (images.shape, jnp.float32, (1, *images.shape[1:]), lambda p: (p, 0, 0)),
            ((8, width), jnp.float32, (8, width), lambda p: (0, 0)),
        ],
    )


def moved_plan(
    images,
    images_held,
    routes,
    slot_index,
    first_gain,
    first_shift,
    w_qkv,
    qv_bias,
    w_out,
    out_bias,
    second_gain,
    second_shift,
    w_router,
    w_in,
    in_bias,
    w_back,
    back_bias,
    cotangent,
):
    f32, bf16 = jnp.float32, jnp.bfloat16
    image_count, seq_len, width = images.shape
    experts_here, shard_width, ff_here = w_in.shape
    data, sources = lax.axis_size(DP), lax.axis_size(EXPERT)
    outer, inner = lax.axis_size(OUTER), lax.axis_size(INNER)
    tensor = outer * inner
    tensor_axes = (OUTER, INNER)
    everywhere = (DP, EXPERT, OUTER, INNER)
    groups = data * sources
    owners = data * inner
    mine = experts_here // owners
    slots = EXPERTS * CAP
    dp_at = lax.axis_index(DP)
    inner_at = lax.axis_index(INNER)
    tensor_at = lax.axis_index(tensor_axes)
    owner_at = dp_at * inner + inner_at
    local_width = w_out.shape[0]
    slice_width = width // tensor
    router_at = 4 * local_width

    packed = jnp.concatenate(
        [
            w_qkv.transpose(1, 0, 2).reshape(shard_width, 3 * local_width),
            w_out.T,
            w_router,
            back_bias.T,
            jnp.stack([first_gain, first_shift, out_bias, second_gain, second_shift], axis=1),
        ],
        axis=1,
    )
    packed = swap(jnp.broadcast_to(packed[None], (data, *packed.shape)), DP).reshape(width, -1)
    out_rows = jnp.concatenate(hop_gather(w_out, tensor_axes), axis=0)
    in_bias_all = jnp.stack(hop_gather(in_bias, INNER))

    def piece(shard, s):
        return cross(lax.dynamic_slice_in_dim(shard, (owner_at ^ s) * mine, mine, 0), s)

    in_pieces = [piece(w_in, s) for s in range(owners)]
    back_pieces = [piece(w_back.transpose(0, 2, 1), s) for s in range(owners)]
    far = owners // 2
    packed, out_rows, in_bias_all, in_pieces[far] = lax.optimization_barrier(
        (packed, out_rows, in_bias_all, in_pieces[far])
    )
    vectors = packed[:, router_at + EXPERTS + experts_here :].T.astype(f32)
    out_whole = jnp.concatenate(hop_gather(out_rows, DP), axis=1)
    in_bias_mine = lax.dynamic_slice_in_dim(in_bias_all, owner_at * mine, mine, 1)
    in_bias_mine = in_bias_mine.transpose(1, 0, 2).astype(f32)

    home, within = routes // experts_here, routes % experts_here
    owner, nth = within // mine, within % mine
    kept = slot_index < CAP
    group_place = (owner // inner) * sources + home
    target = ((group_place * inner + owner % inner) * mine + nth) * CAP + slot_index
    target = jnp.where(kept, target, slots)
    plane_target = (group_place * mine + nth) * CAP + slot_index
    plane_target = jnp.where(jnp.logical_and(kept, owner % inner == inner_at), plane_target, -1)
    plane_target = plane_target.transpose(0, 2, 1)

    attended, proj = run_attend(images, packed, vectors, qv_bias.astype(f32))

    attended_all = lax.all_gather(attended, tensor_axes)
    attended_all, in_pieces = lax.optimization_barrier((attended_all, in_pieces))
    mixed, probs, sent = run_route(
        images,
        cotangent,
        attended_all,
        out_whole,
        packed,
        vectors,
        routes,
        plane_target,
        groups,
        slots // inner,
    )
    sent, back_pieces = lax.optimization_barrier((sent, back_pieces))
    arrived = swap(sent, (DP, EXPERT))
    back_bias_mine = lax.dynamic_slice_in_dim(packed, router_at + EXPERTS + owner_at * mine, mine, 1)
    back_bias_mine = jnp.where(lax.axis_index(OUTER) == 0, back_bias_mine.astype(f32), 0.0)
    (
        returned_out,
        grads_out,
        hidden_low,
        grad_pre_low,
        grad_turned,
        grad_in_bias_mine,
        grad_back_bias_mine,
    ) = run_experts(
        owner_at, arrived, in_pieces, back_pieces, in_bias_mine, back_bias_mine, inner, tensor
    )

    def bring(parts):
        return swap(parts.reshape(groups * tensor, *parts.shape[2:]), everywhere)

    grad_parts = bring(grads_out)
    weight_parts = weight_grads(
        owner_at,
        arrived,
        grad_pre_low,
        grad_turned,
        hidden_low,
        grad_in_bias_mine,
        grad_back_bias_mine,
        owners,
    )
    weight_parts = list(weight_parts)
    weight_parts[: far + 1] = [cross(part, s) for s, part in enumerate(weight_parts[: far + 1])]
    grad_parts, weight_parts[: far + 1] = lax.optimization_barrier(
        (grad_parts, weight_parts[: far + 1])
    )
    rows_cut, grad_gates = run_take_grads(grad_parts, target, slice_width, outer, inner, slots)
    rows_cut, returned_out = lax.optimization_barrier((rows_cut, returned_out))
    rows_all = lax.all_gather(rows_cut, tensor_axes)
    returned = bring(returned_out)
    rows_all, returned, weight_parts[far + 1 :] = lax.optimization_barrier(
        (rows_all, returned, weight_parts[far + 1 :])
    )
    grad_mixed, normed_part, matrix, sums = run_pull(
        images_held,
        images,
        cotangent,
        mixed,
        probs,
        routes,
        grad_gates,
        rows_all,
        attended,
        proj,
        packed,
        vectors,
        router_at,
    )
    grad_normed = lax.psum(normed_part, tensor_axes)
    last_parts = [cross(part, far + 1 + s) for s, part in enumerate(weight_parts[far + 1 :])]
    grad_normed, weight_parts[far + 1 :] = lax.optimization_barrier((grad_normed, last_parts))
    grad_images, first_sums = run_last(images, grad_normed, grad_mixed, vectors)
    first_sums, returned = lax.optimization_barrier((first_sums, returned))
    mixed_cut = lax.dynamic_slice_in_dim(mixed, tensor_at * slice_width, slice_width, 2)
    output_cut = run_take_rows(
        images_held, returned, target, probs, routes, mixed_cut, outer, inner, slots
    )
    output = lax.all_gather(output_cut, tensor_axes)
    output = output.reshape(tensor, image_count // PAIR, seq_len, PAIR, slice_width)
    output = output.transpose(1, 3, 2, 0, 4).reshape(images.shape)

    pair_sums = [sums[5, :local_width], sums[5, 2 * local_width : 3 * local_width]]
    pair_sums = jnp.tile(jnp.stack(pair_sums), (1, data))
    vector_grads = jnp.concatenate([first_sums[:2], sums[2:5], pair_sums], axis=0)
    high, low = high_low(vector_grads)
    small = jnp.concatenate([matrix, high.T, low.T], axis=1)
    small = swap(small.reshape(groups, shard_width // sources, -1), (DP, EXPERT))
    small, weight_parts = lax.optimization_barrier((small, weight_parts))
    small = jnp.sum(small.astype(f32), axis=0)
    small = jnp.concatenate(hop_gather(small, EXPERT), axis=0)
    grad_w_qkv = small[:, : 3 * local_width].reshape(shard_width, 3, local_width).transpose(1, 0, 2)
    grad_w_out = small[:, 3 * local_width : router_at].T
    grad_w_router = small[:, router_at : router_at + EXPERTS]
    vector_grads = small[:, router_at + EXPERTS :].T
    vector_grads = vector_grads[:7] + vector_grads[7:]
    grad_w_in, grad_w_back = run_widen(owner_at, weight_parts, mine, shard_width)
    grad_w_back = grad_w_back.transpose(0, 2, 1)
    grad_in_bias = jnp.zeros((experts_here, ff_here), f32)
    grad_back_shard = jnp.zeros((experts_here, shard_width), f32)
    for s, part in enumerate(weight_parts):
        start = (owner_at ^ s) * mine
        lines = part[2 * mine * shard_width :].astype(f32)
        line = jnp.sum(lines[: 2 * mine].reshape(mine, 2, ff_here), axis=1)
        grad_in_bias = lax.dynamic_update_slice_in_dim(grad_in_bias, line, start, 0)
        line = lines[2 * mine : 3 * mine]
        line = line[:, :shard_width] + line[:, ff_here // 2 : ff_here // 2 + shard_width]
        grad_back_shard = lax.dynamic_update_slice_in_dim(grad_back_shard, line, start, 0)
    return (
        output,
        grad_images,
        vector_grads[0],
        vector_grads[1],
        grad_w_qkv,
        vector_grads[5:7],
        grad_w_out,
        vector_grads[2],
        vector_grads[3],
        vector_grads[4],
        grad_w_router,
        grad_w_in,
        grad_in_bias,
        grad_w_back,
        grad_back_shard,
    )


def specs(tensor):
    rows = P((DP, EXPERT), None, None)
    vector, square = P(DP), P(tensor, DP)
    qkv, pair, router = P(None, DP, tensor), P(None, tensor), P(DP, None)
    inward, outward = P(EXPERT, DP, tensor), P(EXPERT, tensor, DP)
    params = (vector, vector, qkv, pair, square, vector, vector, vector, router)
    experts = (inward, P(EXPERT, tensor), outward, P(EXPERT, DP))
    taken = (rows, P((DP, EXPERT)), rows, rows, *params, *experts, rows)
    given = (rows, rows, *params, *experts)
    return taken, given


def solution(mesh):
    data, expert, tensor = (mesh.shape[name] for name in (DP, EXPERT, TENSOR))
    inner = FF_PAIR if tensor % FF_PAIR == 0 else 1
    owners = data * inner
    if (EXPERTS // expert) % owners or any(n & (n - 1) for n in (data, expert, tensor)):
        taken, given = specs(TENSOR)
        return jax.shard_map(
            gathered_plan, mesh=mesh, in_specs=taken, out_specs=given, check_vma=False
        )
    devices = mesh.devices.reshape(data, expert, tensor // inner, inner)
    split_mesh = Mesh(devices, (DP, EXPERT, OUTER, INNER))
    taken, given = specs((OUTER, INNER))
    return jax.shard_map(
        moved_plan, mesh=split_mesh, in_specs=taken, out_specs=given, check_vma=False
    )
```

```python
import functools
import math

import jax
import jax.numpy as jnp
from jax import lax
from jax.experimental import pallas as pl
from jax.experimental.pallas import tpu as pltpu
from jax.sharding import Mesh
from jax.sharding import PartitionSpec as P

HEAD_DIM = 64
EXPERTS = 32
TOPK = 2
CAP = 64
FF_PAIR = 1
PAIR = 2
EXTRA = 16
VMEM_LIMIT = 56 * 1024 * 1024
GELU_SCALE = (2.0 / math.pi) ** 0.5
GELU_CUBE = 0.044715

DP = "dp"
EXPERT = "expert"
TENSOR = "tensor"
OUTER = "outer"
INNER = "inner"


EPS = 1e-06


def norm_parts(values, norm_gain, norm_shift):
    average = jnp.mean(values, axis=-1, keepdims=True)
    centred = values - average
    spread = jnp.mean(centred * centred, axis=-1, keepdims=True)
    inv_std = lax.rsqrt(spread + EPS)
    scaled = centred * inv_std
    return (scaled * norm_gain + norm_shift, scaled, inv_std)


def norm_back(grad_out, scaled, inv_std, norm_gain):
    grad_scaled = grad_out * norm_gain
    inner = grad_scaled - jnp.mean(grad_scaled, axis=-1, keepdims=True)
    inner = inner - scaled * jnp.mean(grad_scaled * scaled, axis=-1, keepdims=True)
    return (inner * inv_std, jnp.sum(grad_out * scaled, axis=0), jnp.sum(grad_out, axis=0))


def attention_forward(queries, key_rows, value_rows, scale):
    scores = (
        jnp.einsum("iqhd,ikhd->ihqk", queries, key_rows, preferred_element_type=jnp.float32) * scale
    )
    row_peak = jnp.max(scores, axis=-1, keepdims=True)
    log_total = row_peak + jnp.log(jnp.sum(jnp.exp(scores - row_peak), axis=-1, keepdims=True))
    weights = jnp.exp(scores - log_total).astype(jnp.bfloat16)
    attended = jnp.einsum(
        "ihqk,ikhd->iqhd", weights, value_rows, preferred_element_type=jnp.float32
    )
    return (attended, log_total)


def attention_backward(queries, key_rows, value_rows, log_total, grad_low, scale):
    scores = (
        jnp.einsum("iqhd,ikhd->ihqk", queries, key_rows, preferred_element_type=jnp.float32) * scale
    )
    probs = jnp.exp(scores - log_total)
    weights = probs.astype(jnp.bfloat16)
    grad_values = jnp.einsum(
        "ihqk,iqhd->ikhd", weights, grad_low, preferred_element_type=jnp.float32
    )
    grad_weights = jnp.einsum(
        "iqhd,ikhd->ihqk", grad_low, value_rows, preferred_element_type=jnp.float32
    )
    grad_scores = probs * (grad_weights - jnp.sum(probs * grad_weights, axis=-1, keepdims=True))
    scores_low = grad_scores.astype(jnp.bfloat16)
    grad_queries = (
        jnp.einsum("ihqk,ikhd->iqhd", scores_low, key_rows, preferred_element_type=jnp.float32)
        * scale
    )
    grad_keys = (
        jnp.einsum("ihqk,iqhd->ikhd", scores_low, queries, preferred_element_type=jnp.float32)
        * scale
    )
    return (grad_queries, grad_keys, grad_values)


def gathered_plan(
    images,
    images_held,
    routes,
    slot_index,
    first_gain,
    first_shift,
    w_qkv,
    qv_bias,
    w_out,
    out_bias,
    second_gain,
    second_shift,
    w_router,
    w_in,
    in_bias,
    w_back,
    back_bias,
    cotangent,
):
    image_count, seq_len, width = images.shape
    rows_total = image_count * seq_len
    experts_here = w_in.shape[0]
    (
        gain_first,
        shift_first,
        qkv_full,
        out_full,
        bias_out_full,
        gain_second,
        shift_second,
        router_full,
        in_full,
        back_full,
        back_bias_full,
    ) = (
        lax.all_gather(first_gain, DP, axis=0, tiled=True),
        lax.all_gather(first_shift, DP, axis=0, tiled=True),
        lax.all_gather(w_qkv, DP, axis=1, tiled=True),
        lax.all_gather(w_out, DP, axis=1, tiled=True),
        lax.all_gather(out_bias, DP, axis=0, tiled=True),
        lax.all_gather(second_gain, DP, axis=0, tiled=True),
        lax.all_gather(second_shift, DP, axis=0, tiled=True),
        lax.all_gather(w_router, DP, axis=0, tiled=True),
        lax.all_gather(w_in, DP, axis=1, tiled=True),
        lax.all_gather(w_back, DP, axis=2, tiled=True),
        lax.all_gather(back_bias, DP, axis=1, tiled=True),
    )
    gain_first = gain_first.astype(jnp.float32)
    gain_second = gain_second.astype(jnp.float32)
    inputs = images.reshape(rows_total, width).astype(jnp.float32)
    live_image = (jnp.arange(image_count, dtype=jnp.int32) < images_held[0]).astype(jnp.float32)
    live_rows = jnp.repeat(live_image, seq_len)[:, None]
    normed, scaled_first, inv_first = norm_parts(
        inputs, gain_first, shift_first.astype(jnp.float32)
    )
    normed_low = normed.astype(jnp.bfloat16)
    projected = jnp.einsum("td,cde->cte", normed_low, qkv_full, preferred_element_type=jnp.float32)
    local_width = projected.shape[2]
    head_count = local_width // HEAD_DIM
    head_shape = (image_count, seq_len, head_count, HEAD_DIM)
    bias_pair = qv_bias.astype(jnp.float32)
    queries = (projected[0] + bias_pair[0]).astype(jnp.bfloat16).reshape(head_shape)
    key_rows = projected[1].astype(jnp.bfloat16).reshape(head_shape)
    value_rows = (projected[2] + bias_pair[1]).astype(jnp.bfloat16).reshape(head_shape)
    scale = HEAD_DIM ** (-0.5)
    attended, log_total = attention_forward(queries, key_rows, value_rows, scale)
    attended_low = attended.reshape(rows_total, local_width).astype(jnp.bfloat16)
    head_part = jnp.dot(attended_low, out_full, preferred_element_type=jnp.float32)
    mixed = inputs + lax.psum(head_part, TENSOR) + bias_out_full.astype(jnp.float32)
    routed, scaled_second, inv_second = norm_parts(
        mixed, gain_second, shift_second.astype(jnp.float32)
    )
    routed_low = routed.astype(jnp.bfloat16)
    logits = jnp.dot(routed_low, router_full, preferred_element_type=jnp.float32)
    probs = jax.nn.softmax(logits, axis=-1)
    pair_routes = routes.reshape(rows_total, TOPK)
    pair_slots = slot_index.reshape(rows_total, TOPK)
    target = jnp.where(pair_slots < CAP, pair_routes * CAP + pair_slots, EXPERTS * CAP).reshape(
        rows_total * TOPK
    )
    gates = jnp.take_along_axis(probs, pair_routes, axis=1)
    pair_rows = jnp.repeat(routed_low, TOPK, axis=0)
    outgoing = (
        jnp.zeros((EXPERTS * CAP + 1, width), jnp.bfloat16)
        .at[target]
        .set(pair_rows)[: EXPERTS * CAP]
    )
    outgoing = outgoing.reshape(EXPERTS, 1, CAP, width)
    arrived = lax.all_to_all(outgoing, EXPERT, split_axis=0, concat_axis=1, tiled=True)
    sources = arrived.shape[1]
    expert_rows = arrived.reshape(experts_here, sources * CAP, width)
    hidden_pre = jnp.einsum(
        "erd,edf->erf", expert_rows, in_full, preferred_element_type=jnp.float32
    )
    hidden_pre = hidden_pre + in_bias.astype(jnp.float32)[:, None, :]
    hidden_value, gelu_pull = jax.vjp(jax.nn.gelu, hidden_pre)
    hidden_low = hidden_value.astype(jnp.bfloat16)
    expert_part = jnp.einsum(
        "erf,efd->erd", hidden_low, back_full, preferred_element_type=jnp.float32
    )
    bias_back = back_bias_full.astype(jnp.float32)[:, None, :]
    shares = lax.psum_scatter(
        expert_part.reshape(experts_here, sources, CAP, width),
        TENSOR,
        scatter_dimension=2,
        tiled=True,
    )
    share_low = (shares + bias_back[:, None]).astype(jnp.bfloat16)
    pieces = lax.all_to_all(share_low, EXPERT, split_axis=1, concat_axis=0, tiled=True)
    returned = lax.all_gather(pieces, TENSOR, axis=2, tiled=True)
    padded = jnp.concatenate(
        [returned.reshape(EXPERTS * CAP, width), jnp.zeros((1, width), jnp.bfloat16)], axis=0
    )
    picked = padded[target].astype(jnp.float32).reshape(rows_total, TOPK, width)
    expert_mix = jnp.sum(gates[:, :, None] * picked, axis=1)
    output = (live_rows * (mixed + expert_mix)).astype(jnp.bfloat16).reshape(images.shape)
    grad_rows = cotangent.reshape(rows_total, width).astype(jnp.float32) * live_rows
    grad_gates = jnp.sum(grad_rows[:, None, :] * picked, axis=-1)
    grad_picked = (
        (gates[:, :, None] * grad_rows[:, None, :])
        .astype(jnp.bfloat16)
        .reshape(rows_total * TOPK, width)
    )
    grad_outgoing = (
        jnp.zeros((EXPERTS * CAP + 1, width), jnp.bfloat16)
        .at[target]
        .set(grad_picked)[: EXPERTS * CAP]
    )
    grad_outgoing = grad_outgoing.reshape(EXPERTS, 1, CAP, width)
    grad_arrived = lax.all_to_all(grad_outgoing, EXPERT, split_axis=0, concat_axis=1, tiled=True)
    grad_arrived = grad_arrived.reshape(experts_here, sources * CAP, width)
    grad_back_bias = jnp.sum(grad_arrived.astype(jnp.float32), axis=1)
    grad_back_w = jnp.einsum(
        "erf,erd->efd", hidden_low, grad_arrived, preferred_element_type=jnp.float32
    )
    grad_hidden = jnp.einsum(
        "erd,efd->erf", grad_arrived, back_full, preferred_element_type=jnp.float32
    )
    grad_pre = gelu_pull(grad_hidden)[0]
    grad_in_bias_local = jnp.sum(grad_pre, axis=1)
    grad_pre_low = grad_pre.astype(jnp.bfloat16)
    grad_in_w = jnp.einsum(
        "erd,erf->edf", expert_rows, grad_pre_low, preferred_element_type=jnp.float32
    )
    grad_rows_part = jnp.einsum(
        "erf,edf->erd", grad_pre_low, in_full, preferred_element_type=jnp.float32
    )
    grad_shares = lax.psum_scatter(
        grad_rows_part.reshape(experts_here, sources, CAP, width),
        TENSOR,
        scatter_dimension=2,
        tiled=True,
    ).astype(jnp.bfloat16)
    grad_pieces = lax.all_to_all(grad_shares, EXPERT, split_axis=1, concat_axis=0, tiled=True)
    grad_returned = lax.all_gather(grad_pieces, TENSOR, axis=2, tiled=True)
    grad_padded = jnp.concatenate(
        [grad_returned.reshape(EXPERTS * CAP, width), jnp.zeros((1, width), jnp.bfloat16)], axis=0
    )
    grad_routed = jnp.sum(
        grad_padded[target].astype(jnp.float32).reshape(rows_total, TOPK, width), axis=1
    )
    expert_match = (
        pair_routes[:, :, None] == jnp.arange(EXPERTS, dtype=jnp.int32)[None, None, :]
    ).astype(jnp.float32)
    grad_probs = jnp.sum(expert_match * grad_gates[:, :, None], axis=1)
    grad_logits = probs * (grad_probs - jnp.sum(probs * grad_probs, axis=-1, keepdims=True))
    grad_logits_low = grad_logits.astype(jnp.bfloat16)
    grad_router = jnp.einsum(
        "td,te->de", routed_low, grad_logits_low, preferred_element_type=jnp.float32
    )
    grad_routed = grad_routed + jnp.einsum(
        "te,de->td", grad_logits_low, router_full, preferred_element_type=jnp.float32
    )
    grad_from_norm, grad_gain_second, grad_shift_second = norm_back(
        grad_routed, scaled_second, inv_second, gain_second
    )
    grad_mixed = grad_rows + grad_from_norm
    grad_bias_out = jnp.sum(grad_mixed, axis=0)
    grad_mixed_low = grad_mixed.astype(jnp.bfloat16)
    grad_out_w = jnp.einsum(
        "te,td->ed", attended_low, grad_mixed_low, preferred_element_type=jnp.float32
    )
    grad_attended = jnp.einsum(
        "td,ed->te", grad_mixed_low, out_full, preferred_element_type=jnp.float32
    )
    grad_attended = grad_attended.astype(jnp.bfloat16).reshape(head_shape)
    grad_queries, grad_keys, grad_values = attention_backward(
        queries, key_rows, value_rows, log_total, grad_attended, scale
    )
    grad_queries = grad_queries.reshape(rows_total, local_width)
    grad_keys = grad_keys.reshape(rows_total, local_width)
    grad_values = grad_values.reshape(rows_total, local_width)
    grad_pair_bias = jnp.stack([jnp.sum(grad_queries, axis=0), jnp.sum(grad_values, axis=0)])
    grad_proj_low = jnp.stack([grad_queries, grad_keys, grad_values]).astype(jnp.bfloat16)
    grad_qkv = jnp.einsum(
        "td,cte->cde", normed_low, grad_proj_low, preferred_element_type=jnp.float32
    )
    grad_normed_part = jnp.einsum(
        "cte,cde->td", grad_proj_low, qkv_full, preferred_element_type=jnp.float32
    )
    grad_normed = lax.psum(grad_normed_part, TENSOR)
    grad_from_first, grad_gain_first, grad_shift_first = norm_back(
        grad_normed, scaled_first, inv_first, gain_first
    )
    grad_images = (grad_mixed + grad_from_first).reshape(images.shape)
    expert_start = lax.axis_index(EXPERT) * experts_here
    full_in_bias = lax.dynamic_update_slice(
        jnp.zeros((EXPERTS, grad_in_bias_local.shape[1]), jnp.float32),
        grad_in_bias_local,
        (expert_start, jnp.zeros((), jnp.int32)),
    )
    summed = lax.psum(
        (
            grad_gain_first,
            grad_shift_first,
            grad_qkv,
            grad_pair_bias,
            grad_out_w,
            grad_bias_out,
            grad_gain_second,
            grad_shift_second,
            grad_router,
            full_in_bias,
        ),
        (DP, EXPERT),
    )
    shard_width = width // lax.axis_size(DP)
    shard_start = lax.axis_index(DP) * shard_width
    grad_first_gain = lax.dynamic_slice_in_dim(summed[0], shard_start, shard_width, 0)
    grad_first_shift = lax.dynamic_slice_in_dim(summed[1], shard_start, shard_width, 0)
    grad_w_qkv = lax.dynamic_slice_in_dim(summed[2], shard_start, shard_width, 1)
    grad_qv_bias = summed[3]
    grad_w_out = lax.dynamic_slice_in_dim(summed[4], shard_start, shard_width, 1)
    grad_out_bias = lax.dynamic_slice_in_dim(summed[5], shard_start, shard_width, 0)
    grad_second_gain = lax.dynamic_slice_in_dim(summed[6], shard_start, shard_width, 0)
    grad_second_shift = lax.dynamic_slice_in_dim(summed[7], shard_start, shard_width, 0)
    grad_w_router = lax.dynamic_slice_in_dim(summed[8], shard_start, shard_width, 0)
    grad_in_bias = lax.dynamic_slice_in_dim(summed[9], expert_start, experts_here, 0)
    grad_w_in, grad_w_back, grad_back_shard = (
        lax.psum_scatter(grad_in_w, DP, scatter_dimension=1, tiled=True),
        lax.psum_scatter(grad_back_w, DP, scatter_dimension=2, tiled=True),
        lax.psum_scatter(grad_back_bias, DP, scatter_dimension=1, tiled=True),
    )
    return (
        output,
        grad_images,
        grad_first_gain,
        grad_first_shift,
        grad_w_qkv,
        grad_qv_bias,
        grad_w_out,
        grad_out_bias,
        grad_second_gain,
        grad_second_shift,
        grad_w_router,
        grad_w_in,
        grad_in_bias,
        grad_w_back,
        grad_back_shard,
    )


def swap(values, axes):
    return lax.all_to_all(values, axes, split_axis=0, concat_axis=0, tiled=True)


def hop_gather(values, axes):
    count, at = lax.axis_size(axes), lax.axis_index(axes)
    hops = [values]
    for s in range(1, count):
        hops.append(lax.ppermute(values, axes, [(i, i ^ s) for i in range(count)]))
    gathered = []
    for i in range(count):
        found = hops[0]
        for s in range(1, count):
            found = jnp.where(at ^ i == s, hops[s], found)
        gathered.append(found)
    return gathered


def cross(values, s):
    count = lax.axis_size((DP, INNER))
    return lax.ppermute(values, (DP, INNER), [(i, i ^ s) for i in range(count)]) if s else values


def high_low(values):
    high = lax.reduce_precision(values, 8, 7)
    return high.astype(jnp.bfloat16), (values - high).astype(jnp.bfloat16)


def turned_dot(left, right, left_dim, right_dim):
    return lax.dot_general(
        left, right, (((left_dim,), (right_dim,)), ((), ())), preferred_element_type=jnp.float32
    )


def expert_kernel(inner, owners, at_ref, rows_ref, gate_ref, cot_ref, in_bias_ref, back_bias_ref, *refs):
    in_refs, back_refs, refs = refs[:owners], refs[owners : 2 * owners], refs[2 * owners :]
    returned_ref, grads_ref, hidden_ref, grad_pre_ref, grad_turned_ref = refs[:5]
    grad_in_bias_ref, grad_back_bias_ref, weight_ref = refs[5:]
    f32, bf16 = jnp.float32, jnp.bfloat16
    groups, cap, width = rows_ref.shape
    depth = in_refs[0].shape[1]
    for s in range(owners):
        source = at_ref[0] ^ s
        place = pl.ds(pl.multiple_of((source // inner) * depth, depth), depth)
        weight_ref[0, source % inner, place] = in_refs[s][0]
        weight_ref[1, source % inner, place] = back_refs[s][0]
    tensor, slice_width = returned_ref.shape[1:3]
    mine = back_bias_ref.shape[1]
    total = groups * cap
    at = pl.program_id(0)
    rows = rows_ref[...].reshape(total, width)
    cot_turned = cot_ref[...].reshape(total, width).T.astype(f32)
    pair = gate_ref[:, 0:1, :].astype(f32) + gate_ref[:, 1:2, :].astype(f32)
    pair = pair.reshape(groups, pair.shape[-1])
    gate = jnp.zeros((groups, cap), f32)
    for j in range(mine):
        gate = jnp.where(at == j, pair[:, j * cap : (j + 1) * cap], gate)
    gate = jnp.concatenate([gate[g : g + 1, :] for g in range(groups)], axis=1)
    grad_turned = (cot_turned * gate).astype(bf16)
    grad_turned_ref[0] = grad_turned
    grad_returned = grad_turned.T
    grad_back_bias_ref[0] = jnp.sum(grad_returned.astype(f32), axis=0, keepdims=True)
    bias_columns = back_bias_ref[...]
    bias = jnp.zeros((width, 1), f32)
    for j in range(mine):
        bias = jnp.where(at == j, bias_columns[:, j : j + 1], bias)
    part = jnp.broadcast_to(bias, (width, total))
    back = jnp.zeros((width, total), f32)
    for t in range(inner):
        w_in, w_back = weight_ref[0, t], weight_ref[1, t]
        pre = jnp.dot(rows, w_in, preferred_element_type=f32) + in_bias_ref[0, t : t + 1, :]
        square = pre * pre
        bent = jnp.tanh(GELU_SCALE * pre * (1.0 + GELU_CUBE * square))
        half = 0.5 * (1.0 + bent)
        hidden = (pre * half).astype(bf16)
        slope = half + (0.5 * GELU_SCALE) * pre * (1.0 - bent * bent) * (
            1.0 + (3.0 * GELU_CUBE) * square
        )
        hidden_ref[0, t] = hidden
        grad_pre = jnp.dot(grad_returned, w_back, preferred_element_type=f32) * slope
        grad_in_bias_ref[0, t : t + 1, :] = jnp.sum(grad_pre, axis=0, keepdims=True)
        grad_pre = grad_pre.astype(bf16)
        grad_pre_ref[0, t] = grad_pre
        part = part + turned_dot(w_back, hidden, 1, 1)
        back = back + turned_dot(w_in, grad_pre, 1, 1)
    gate_terms = jnp.sum(part * cot_turned, axis=0, keepdims=True)
    high = gate_terms.astype(bf16)
    low = (gate_terms - high.astype(f32)).astype(bf16)
    extra = grads_ref.shape[2] - slice_width
    tail = jnp.concatenate([high, low, jnp.zeros((extra - 2, total), bf16)], axis=0)
    part = part.astype(bf16)
    back = back.astype(bf16)
    for j in range(mine):

        @pl.when(at == j)
        def _():
            lanes = slice(j * cap, (j + 1) * cap)
            for g in range(groups):
                mine_lanes = slice(g * cap, (g + 1) * cap)
                for z in range(tensor):
                    features = slice(z * slice_width, (z + 1) * slice_width)
                    returned_ref[g, z, :, lanes] = part[features, mine_lanes]
                    grads_ref[g, z, :slice_width, lanes] = back[features, mine_lanes]
                    grads_ref[g, z, slice_width:, lanes] = tail[:, mine_lanes]


def run_experts(owner_at, arrived, in_pieces, back_pieces, in_bias, back_bias, inner, tensor):
    f32, bf16 = jnp.float32, jnp.bfloat16
    groups, _, width = arrived.shape
    owners = len(in_pieces)
    mine, depth, ff = in_pieces[0].shape
    total = groups * CAP
    slice_width = width // tensor
    gate_at = 2 * mine * CAP // EXTRA
    outs = [
        ((groups, tensor, slice_width, mine * CAP), bf16, lambda j: (0, 0, 0, 0), None),
        ((groups, tensor, slice_width + EXTRA, mine * CAP), bf16, lambda j: (0, 0, 0, 0), None),
        ((mine, inner, total, ff), bf16, lambda j: (j, 0, 0, 0), 1),
        ((mine, inner, total, ff), bf16, lambda j: (j, 0, 0, 0), 1),
        ((mine, width, total), bf16, lambda j: (j, 0, 0), 1),
        ((mine, inner, ff), f32, lambda j: (j, 0, 0), 1),
        ((mine, 1, width), f32, lambda j: (j, 0, 0), 1),
    ]
    return pl.pallas_call(
        functools.partial(expert_kernel, inner, owners),
        grid=(mine,),
        in_specs=[
            pl.BlockSpec(memory_space=pltpu.SMEM),
            pl.BlockSpec((groups, CAP, width), lambda j: (0, j, 0)),
            pl.BlockSpec((groups, EXTRA, mine * CAP), lambda j: (0, gate_at, 0)),
            pl.BlockSpec((groups, CAP, width), lambda j: (0, mine + j, 0)),
            pl.BlockSpec((1, inner, ff), lambda j: (j, 0, 0)),
            pl.BlockSpec((width, mine), lambda j: (0, 0)),
        ]
        + [pl.BlockSpec((1, depth, ff), lambda j: (j, 0, 0))] * (2 * owners),
        out_specs=[
            pl.BlockSpec(shape if lead is None else (lead, *shape[1:]), index)
            for shape, _, index, lead in outs
        ],
        out_shape=[jax.ShapeDtypeStruct(shape, dtype) for shape, dtype, _, _ in outs],
        scratch_shapes=[pltpu.VMEM((2, inner, width, ff), bf16)],
        compiler_params=pltpu.CompilerParams(vmem_limit_bytes=VMEM_LIMIT),
        cost_estimate=pl.CostEstimate(
            flops=8 * mine * total * width * inner * ff,
            bytes_accessed=4 * owners * mine * depth * ff + 12 * mine * total * inner * ff,
            transcendentals=mine * total * inner * ff,
        ),
    )(owner_at.reshape(1), arrived, arrived, arrived, in_bias, back_bias, *in_pieces, *back_pieces)


def weight_kernel(
    inner,
    at_ref,
    rows_ref,
    grad_pre_ref,
    grad_turned_ref,
    hidden_ref,
    in_bias_ref,
    back_bias_ref,
    *refs,
):
    f32, bf16 = jnp.float32, jnp.bfloat16
    out_refs, sums_ref, tail_ref = refs[:-2], refs[-2], refs[-1]
    groups, cap, width = rows_ref.shape
    mine = back_bias_ref.shape[0]
    ff = sums_ref.shape[-1]
    depth = width * inner // len(out_refs)
    data = width // depth
    part, at = pl.program_id(0), pl.program_id(1)
    rows = rows_ref[...].reshape(groups * cap, width)
    sums_ref[0] = turned_dot(rows, grad_pre_ref[0, 0], 0, 0).astype(bf16)
    grad_back = jnp.dot(grad_turned_ref[0], hidden_ref[0, 0], preferred_element_type=f32)
    sums_ref[1] = grad_back.astype(bf16)

    @pl.when(at == mine - 1)
    def _():
        pairs = []
        for j in range(mine):
            values = in_bias_ref[j, 0]
            high = values.astype(bf16).astype(f32)
            pairs += [high, values - high]
        for d in range(data):
            lines = list(pairs)
            for j in range(mine):
                values = back_bias_ref[j, :, d * depth : (d + 1) * depth]
                high = values.astype(bf16).astype(f32)
                gap = jnp.zeros((1, ff // 2 - depth), f32)
                lines.append(jnp.concatenate([high, gap, values - high, gap], axis=1))
            lines.append(jnp.zeros((EXTRA - len(lines), ff), f32))
            tail_ref[d] = jnp.concatenate(lines, axis=0).astype(bf16)

    for s, out_ref in enumerate(out_refs):
        owner = at_ref[0] ^ s
        d = owner // inner
        place = pl.ds(pl.multiple_of(d * depth, depth), depth)

        @pl.when(owner % inner == part)
        def _():
            for k in range(2):
                line = pl.multiple_of((k * mine + at) * depth, depth)
                out_ref[pl.ds(line, depth)] = sums_ref[k, place]

            @pl.when(at == mine - 1)
            def _():
                out_ref[2 * mine * depth :] = tail_ref[d]


def weight_grads(
    owner_at, arrived, grad_pre, grad_turned, hidden, grad_in_bias, grad_back_bias, owners
):
    mine, inner, total, ff = hidden.shape
    groups, _, width = arrived.shape
    depth = width * inner // owners
    kept = pl.BlockSpec((1, 1, total, ff), lambda t, j: (j, t, 0, 0))
    out = (2 * mine * depth + EXTRA, ff)
    return pl.pallas_call(
        functools.partial(weight_kernel, inner),
        grid=(inner, mine),
        in_specs=[
            pl.BlockSpec(memory_space=pltpu.SMEM),
            pl.BlockSpec((groups, CAP, width), lambda t, j: (0, j, 0)),
            kept,
            pl.BlockSpec((1, width, total), lambda t, j: (j, 0, 0)),
            kept,
            pl.BlockSpec((mine, 1, 1, ff), lambda t, j: (0, t, 0, 0)),
            pl.BlockSpec((mine, 1, width), lambda t, j: (0, 0, 0)),
        ],
        out_specs=[pl.BlockSpec(out, lambda t, j: (0, 0))] * owners,
        out_shape=[jax.ShapeDtypeStruct(out, jnp.bfloat16)] * owners,
        scratch_shapes=[
            pltpu.VMEM((2, width, ff), jnp.bfloat16),
            pltpu.VMEM((width // depth, EXTRA, ff), jnp.bfloat16),
        ],
        compiler_params=pltpu.CompilerParams(vmem_limit_bytes=VMEM_LIMIT),
        cost_estimate=pl.CostEstimate(
            flops=4 * mine * total * width * inner * ff,
            bytes_accessed=4 * mine * inner * (total + width) * ff,
            transcendentals=0,
        ),
    )(
        owner_at.reshape(1),
        arrived,
        grad_pre,
        grad_turned,
        hidden,
        grad_in_bias[:, :, None],
        grad_back_bias,
    )


def widen_kernel(at_ref, *refs):
    part_refs, (in_ref, back_ref) = refs[:-2], refs[-2:]
    mine, depth, ff = in_ref.shape
    rows = mine * depth
    for s, part_ref in enumerate(part_refs):

        @pl.when(pl.program_id(0) == s)
        def _():
            in_ref[...] = part_ref[:rows].astype(jnp.float32).reshape(mine, depth, ff)
            back_ref[...] = part_ref[rows : 2 * rows].astype(jnp.float32).reshape(mine, depth, ff)


def run_widen(owner_at, parts, owners, mine, depth):
    count, ff = len(parts), parts[0].shape[1]
    out = pl.BlockSpec((mine, depth, ff), lambda p, at: (at[0] ^ p, 0, 0))
    return pl.pallas_call(
        widen_kernel,
        grid_spec=pltpu.PrefetchScalarGridSpec(
            num_scalar_prefetch=1,
            grid=(count,),
            in_specs=[pl.BlockSpec((2 * mine * depth, ff), lambda p, at: (0, 0))] * count,
            out_specs=[out, out],
        ),
        out_shape=[jax.ShapeDtypeStruct((owners * mine, depth, ff), jnp.float32)] * 2,
        compiler_params=pltpu.CompilerParams(vmem_limit_bytes=VMEM_LIMIT),
    )(owner_at.reshape(1), *parts)


def norm_rows(values):
    average = jnp.mean(values, axis=-1, keepdims=True)
    centred = values - average
    spread = jnp.mean(centred * centred, axis=-1, keepdims=True)
    inv_std = lax.rsqrt(spread + EPS)
    return centred * inv_std, inv_std


def norm_rows_back(grad_out, scaled, inv_std, norm_gain):
    grad_scaled = grad_out * norm_gain
    inner = grad_scaled - jnp.mean(grad_scaled, axis=-1, keepdims=True)
    inner = inner - scaled * jnp.mean(grad_scaled * scaled, axis=-1, keepdims=True)
    return inner * inv_std


def call_kernel(kernel, grid, inputs, outputs, scratch=(), flops=0):
    smem = pl.BlockSpec(memory_space=pltpu.SMEM)
    return pl.pallas_call(
        kernel,
        grid=grid,
        in_specs=[smem if b is None else pl.BlockSpec(b, i) for _, b, i in inputs],
        out_specs=[pl.BlockSpec(b, i) for _, _, b, i in outputs],
        out_shape=[jax.ShapeDtypeStruct(shape, dtype) for shape, dtype, _, _ in outputs],
        scratch_shapes=list(scratch),
        compiler_params=pltpu.CompilerParams(vmem_limit_bytes=VMEM_LIMIT),
        cost_estimate=pl.CostEstimate(
            flops=flops,
            bytes_accessed=sum(a.size * a.dtype.itemsize for a, _, _ in inputs),
            transcendentals=0,
        ),
    )(*(a for a, _, _ in inputs))


def whole(array):
    return array, array.shape, lambda p: (0,) * array.ndim


def by_step(array, lead):
    return array, (lead, *array.shape[1:]), lambda p: (p,) + (0,) * (array.ndim - 1)


def attend_kernel(images_ref, packed_ref, vector_ref, bias_ref, attended_ref, proj_ref):
    f32, bf16 = jnp.float32, jnp.bfloat16
    local = bias_ref.shape[1]
    weight = packed_ref[:, : 3 * local]
    for h in range(images_ref.shape[0]):
        scaled, _ = norm_rows(images_ref[h].astype(f32))
        normed = (scaled * vector_ref[0:1] + vector_ref[1:2]).astype(bf16)
        proj = jnp.dot(normed, weight, preferred_element_type=f32)
        queries = (proj[:, :local] + bias_ref[0:1]).astype(bf16)
        keys = proj[:, local : 2 * local].astype(bf16)
        values = (proj[:, 2 * local :] + bias_ref[1:2]).astype(bf16)
        proj_ref[h] = jnp.concatenate([queries, keys, values], axis=1)
        parts = []
        for n in range(0, local, HEAD_DIM):
            head = slice(n, n + HEAD_DIM)
            scores = turned_dot(queries[:, head], keys[:, head], 1, 1) * HEAD_DIM**-0.5
            scores = jnp.exp(scores - jnp.max(scores, axis=-1, keepdims=True))
            weights = scores / jnp.sum(scores, axis=-1, keepdims=True)
            parts.append(
                jnp.dot(weights.astype(bf16), values[:, head], preferred_element_type=f32)
            )
        attended_ref[0, :, h * local : (h + 1) * local] = jnp.concatenate(parts, axis=1).astype(bf16)


def run_attend(images, packed, vectors, qv_bias):
    count, length, width = images.shape
    local = qv_bias.shape[1]
    return call_kernel(
        attend_kernel,
        (count // PAIR,),
        [by_step(images, PAIR), whole(packed), whole(vectors), whole(qv_bias)],
        [
            ((count // PAIR, length, PAIR * local), jnp.bfloat16, (1, length, PAIR * local), lambda p: (p, 0, 0)),
            ((count, length, 3 * local), jnp.bfloat16, (PAIR, length, 3 * local), lambda p: (p, 0, 0)),
        ],
        flops=2 * count * length * local * (3 * width + 4 * length),
    )


def slot_hits(target_row, count):
    return lax.broadcasted_iota(jnp.int32, (count, target_row.shape[1]), 0) == target_row


def route_kernel(
    router_at,
    images_ref,
    cot_ref,
    attended_ref,
    out_ref,
    packed_ref,
    vector_ref,
    routes_ref,
    target_ref,
    mixed_ref,
    probs_ref,
    sent_ref,
    sum_ref,
    gate_ref,
):
    f32, bf16 = jnp.float32, jnp.bfloat16
    slots = sum_ref.shape[1]
    tensor, local = attended_ref.shape[0], attended_ref.shape[3] // images_ref.shape[0]
    at = pl.program_id(0)

    @pl.when(at == 0)
    def _():
        sum_ref[...] = jnp.zeros_like(sum_ref)
        gate_ref[...] = jnp.zeros_like(gate_ref)

    router = packed_ref[:, router_at : router_at + EXPERTS]
    for h in range(images_ref.shape[0]):
        mixed = images_ref[h].astype(f32) + vector_ref[2:3]
        for z in range(tensor):
            part = attended_ref[z, 0, :, h * local : (h + 1) * local]
            weight = out_ref[z * local : (z + 1) * local]
            mixed = mixed + jnp.dot(part, weight, preferred_element_type=f32)
        mixed_ref[h] = mixed
        scaled, _ = norm_rows(mixed)
        routed = (scaled * vector_ref[3:4] + vector_ref[4:5]).astype(bf16)
        logits = jnp.dot(routed, router, preferred_element_type=f32)
        logits = jnp.exp(logits - jnp.max(logits, axis=-1, keepdims=True))
        probs = logits / jnp.sum(logits, axis=-1, keepdims=True)
        probs_ref[h] = probs
        experts = lax.broadcasted_iota(jnp.int32, probs.shape, 1)
        fill = jnp.zeros((slots, probs.shape[0]), f32)
        for k in range(TOPK):
            match = experts == routes_ref[h, :, k : k + 1]
            gate = jnp.sum(jnp.where(match, probs, 0.0), axis=1, keepdims=True)
            high = gate.astype(bf16)
            low = (gate - high.astype(f32)).astype(bf16)
            pair = jnp.concatenate([high, low, jnp.zeros((gate.shape[0], 6), bf16)], axis=1)
            hit = slot_hits(target_ref[h, k : k + 1], slots).astype(f32)
            fill = fill + hit
            gate_ref[...] += turned_dot(pair, hit.astype(bf16), 0, 1)
        fill = fill.astype(bf16)
        sum_ref[0] += jnp.dot(fill, routed, preferred_element_type=f32)
        sum_ref[1] += jnp.dot(fill, cot_ref[h], preferred_element_type=f32)

    @pl.when(at == pl.num_programs(0) - 1)
    def _():
        groups, lines, width = sent_ref.shape
        here = slots // groups
        for g in range(groups):
            lanes = slice(g * here, (g + 1) * here)
            sent_ref[g, :here] = sum_ref[0, lanes].astype(bf16)
            sent_ref[g, here : 2 * here] = sum_ref[1, lanes].astype(bf16)
            gates = jnp.concatenate([gate_ref[:, lanes], jnp.zeros((8, width - here), f32)], axis=1)
            gates = jnp.concatenate([gates, jnp.zeros((lines - 2 * here - 8, width), f32)], axis=0)
            sent_ref[g, 2 * here :] = gates.astype(bf16)


def run_route(
    images, cot, attended_all, out_whole, packed, vectors, routes, plane_target, groups, slots_plane
):
    f32, bf16 = jnp.float32, jnp.bfloat16
    count, length, width = images.shape
    tensor = attended_all.shape[0]
    sent = (groups, 2 * slots_plane // groups + EXTRA, width)
    return call_kernel(
        functools.partial(route_kernel, tensor * attended_all.shape[3] // PAIR),
        (count // PAIR,),
        [
            by_step(images, PAIR),
            by_step(cot, PAIR),
            (attended_all, (tensor, 1, *attended_all.shape[2:]), lambda p: (0, p, 0, 0)),
            whole(out_whole),
            whole(packed),
            whole(vectors),
            by_step(routes, PAIR),
            by_step(plane_target, PAIR),
        ],
        [
            ((count, length, width), f32, (PAIR, length, width), lambda p: (p, 0, 0)),
            ((count, length, EXPERTS), f32, (PAIR, length, EXPERTS), lambda p: (p, 0, 0)),
            (sent, bf16, sent, lambda p: (0, 0, 0)),
        ],
        [pltpu.VMEM((2, slots_plane, width), f32), pltpu.VMEM((8, slots_plane), f32)],
        flops=2 * count * length * width * (width + 2 * slots_plane),
    )


def slot_blocks(parts_ref, slots_ref, outer, inner):
    here = parts_ref.shape[2]
    for b in range(slots_ref.shape[1] // here):
        first = (b // inner) * outer * inner + b % inner
        total = parts_ref[first].astype(jnp.float32)
        for o in range(1, outer):
            total = total + parts_ref[first + o * inner].astype(jnp.float32)
        slots_ref[:, b * here : (b + 1) * here] = total


def token_hits(target_column, count):
    return lax.broadcasted_iota(jnp.int32, (target_column.shape[0], count), 1) == target_column


def take_grads_kernel(outer, inner, parts_ref, target_ref, rows_ref, gates_ref, slots_ref):
    f32, bf16 = jnp.float32, jnp.bfloat16
    slots = slots_ref.shape[1]
    local = rows_ref.shape[2] // target_ref.shape[0]

    @pl.when(pl.program_id(0) == 0)
    def _():
        slot_blocks(parts_ref, slots_ref, outer, inner)

    grads = slots_ref[:local].astype(bf16)
    gate_terms = slots_ref[local : local + 1] + slots_ref[local + 1 : local + 2]
    for h in range(target_ref.shape[0]):
        hits = [token_hits(target_ref[h, :, k : k + 1], slots) for k in range(TOPK)]
        find = jnp.logical_or(hits[0], hits[1]).astype(f32).astype(bf16)
        rows_ref[0, :, h * local : (h + 1) * local] = turned_dot(find, grads, 1, 1).astype(bf16)
        terms = [
            jnp.sum(jnp.where(hit, gate_terms, 0.0), axis=1, keepdims=True) for hit in hits
        ]
        gates_ref[h] = jnp.concatenate(terms, axis=1)


def run_take_grads(parts, target, local, outer, inner, slots):
    count, length, _ = target.shape
    return call_kernel(
        functools.partial(take_grads_kernel, outer, inner),
        (count // PAIR,),
        [whole(parts), by_step(target, PAIR)],
        [
            ((count // PAIR, length, PAIR * local), jnp.bfloat16, (1, length, PAIR * local), lambda p: (p, 0, 0)),
            ((count, length, TOPK), jnp.float32, (PAIR, length, TOPK), lambda p: (p, 0, 0)),
        ],
        [pltpu.VMEM((parts.shape[1], slots), jnp.float32)],
        flops=2 * count * length * slots * local,
    )


def take_rows_kernel(
    outer, inner, held_ref, parts_ref, target_ref, probs_ref, routes_ref, mixed_ref, out_ref, slots_ref
):
    f32, bf16 = jnp.float32, jnp.bfloat16
    slots = slots_ref.shape[1]
    pair = target_ref.shape[0]
    local = out_ref.shape[2] // pair
    at = pl.program_id(0)

    @pl.when(at == 0)
    def _():
        slot_blocks(parts_ref, slots_ref, outer, inner)

    returned = slots_ref[...].astype(bf16)
    for h in range(pair):
        probs = probs_ref[h]
        experts = lax.broadcasted_iota(jnp.int32, probs.shape, 1)
        rows = mixed_ref[h]
        for k in range(TOPK):
            match = experts == routes_ref[h, :, k : k + 1]
            gate = jnp.sum(jnp.where(match, probs, 0.0), axis=1, keepdims=True)
            find = token_hits(target_ref[h, :, k : k + 1], slots).astype(f32).astype(bf16)
            rows = rows + gate * turned_dot(find, returned, 1, 1)
        live = (at * pair + h < held_ref[0]).astype(f32)
        out_ref[0, :, h * local : (h + 1) * local] = (live * rows).astype(bf16)


def run_take_rows(held, parts, target, probs, routes, mixed_cut, outer, inner, slots):
    count, length, local = mixed_cut.shape
    return call_kernel(
        functools.partial(take_rows_kernel, outer, inner),
        (count // PAIR,),
        [
            (held, None, None),
            whole(parts),
            by_step(target, PAIR),
            by_step(probs, PAIR),
            by_step(routes, PAIR),
            by_step(mixed_cut, PAIR),
        ],
        [((count // PAIR, length, PAIR * local), jnp.bfloat16, (1, length, PAIR * local), lambda p: (p, 0, 0))],
        [pltpu.VMEM((parts.shape[1], slots), jnp.float32)],
        flops=4 * count * length * slots * local,
    )[0]


def pull_kernel(
    router_at,
    held_ref,
    images_ref,
    cot_ref,
    mixed_ref,
    probs_ref,
    routes_ref,
    gates_ref,
    rows_ref,
    attended_ref,
    proj_ref,
    packed_ref,
    vector_ref,
    grad_mixed_ref,
    normed_ref,
    matrix_ref,
    sums_ref,
    matrix_sum_ref,
):
    f32, bf16 = jnp.float32, jnp.bfloat16
    pair = images_ref.shape[0]
    tensor = rows_ref.shape[0]
    local = attended_ref.shape[2] // pair
    width = images_ref.shape[2]
    at = pl.program_id(0)

    @pl.when(at == 0)
    def _():
        sums_ref[...] = jnp.zeros_like(sums_ref)
        matrix_sum_ref[...] = jnp.zeros_like(matrix_sum_ref)

    qkv = packed_ref[:, : 3 * local]
    out_turned = packed_ref[:, 3 * local : 4 * local]
    router = packed_ref[:, router_at : router_at + EXPERTS]
    scale = HEAD_DIM**-0.5
    for h in range(pair):
        lanes = slice(h * local, (h + 1) * local)
        live = (at * pair + h < held_ref[0]).astype(f32)
        cot = cot_ref[h].astype(f32) * live
        scaled, inv_std = norm_rows(mixed_ref[h])
        routed = (scaled * vector_ref[3:4] + vector_ref[4:5]).astype(bf16)
        probs = probs_ref[h]
        experts = lax.broadcasted_iota(jnp.int32, probs.shape, 1)
        grad_probs = jnp.zeros(probs.shape, f32)
        for k in range(TOPK):
            match = experts == routes_ref[h, :, k : k + 1]
            grad_probs = grad_probs + jnp.where(match, gates_ref[h, :, k : k + 1], 0.0)
        grad_logits = probs * (grad_probs - jnp.sum(probs * grad_probs, axis=-1, keepdims=True))
        grad_logits = grad_logits.astype(bf16)
        grad_routed = jnp.concatenate([rows_ref[z, 0, :, lanes] for z in range(tensor)], axis=1)
        grad_routed = grad_routed.astype(f32) + turned_dot(grad_logits, router, 1, 1)
        grad_mixed = cot + norm_rows_back(grad_routed, scaled, inv_std, vector_ref[3:4])
        grad_mixed_ref[h] = grad_mixed
        low = grad_mixed.astype(bf16)
        grad_attended = jnp.dot(low, out_turned, preferred_element_type=f32).astype(bf16)
        proj = proj_ref[h]
        grads = [[], [], []]
        for n in range(0, local, HEAD_DIM):
            queries = proj[:, n : n + HEAD_DIM]
            keys = proj[:, local + n : local + n + HEAD_DIM]
            values = proj[:, 2 * local + n : 2 * local + n + HEAD_DIM]
            grad_head = grad_attended[:, n : n + HEAD_DIM]
            scores = turned_dot(queries, keys, 1, 1) * scale
            scores = jnp.exp(scores - jnp.max(scores, axis=-1, keepdims=True))
            weights = scores / jnp.sum(scores, axis=-1, keepdims=True)
            grads[2].append(turned_dot(weights.astype(bf16), grad_head, 0, 0))
            grad_weights = turned_dot(grad_head, values, 1, 1)
            inner = jnp.sum(weights * grad_weights, axis=-1, keepdims=True)
            grad_scores = (weights * (grad_weights - inner)).astype(bf16)
            grads[0].append(jnp.dot(grad_scores, keys, preferred_element_type=f32) * scale)
            grads[1].append(turned_dot(grad_scores, queries, 0, 0) * scale)
        grad_proj = jnp.concatenate(grads[0] + grads[1] + grads[2], axis=1)
        proj_sum = jnp.sum(grad_proj, axis=0, keepdims=True)
        grad_proj = grad_proj.astype(bf16)
        first, _ = norm_rows(images_ref[h].astype(f32))
        normed = (first * vector_ref[0:1] + vector_ref[1:2]).astype(bf16)
        grad_normed = turned_dot(grad_proj, qkv, 1, 1)
        normed_ref[h] = grad_normed.astype(bf16)
        attended = attended_ref[0, :, lanes]
        matrix = jnp.concatenate(
            [
                turned_dot(normed, grad_proj, 0, 0),
                turned_dot(low, attended, 0, 0),
                turned_dot(routed, grad_logits, 0, 0),
            ],
            axis=1,
        )
        matrix_sum_ref[...] += matrix
        column = lambda values: jnp.sum(values, axis=0, keepdims=True)
        sums_ref[2:3] += column(grad_mixed)
        sums_ref[3:4] += column(grad_routed * scaled)
        sums_ref[4:5] += column(grad_routed)
        sums_ref[5:6, : 3 * local] += proj_sum

    @pl.when(at == pl.num_programs(0) - 1)
    def _():
        matrix_ref[...] = matrix_sum_ref[...].astype(bf16)


def run_pull(held, images, cot, mixed, probs, routes, gates, rows_all, attended, proj, packed, vectors, router_at):
    f32, bf16 = jnp.float32, jnp.bfloat16
    count, length, width = images.shape
    tensor = rows_all.shape[0]
    local = proj.shape[2] // 3
    tokens = (count, length, width)
    block = (PAIR, length, width)
    step = lambda p: (p, 0, 0)
    still = lambda p: (0, 0)
    matrix = (width, 4 * local + EXPERTS)
    return call_kernel(
        functools.partial(pull_kernel, router_at),
        (count // PAIR,),
        [
            (held, None, None),
            by_step(images, PAIR),
            by_step(cot, PAIR),
            by_step(mixed, PAIR),
            by_step(probs, PAIR),
            by_step(routes, PAIR),
            by_step(gates, PAIR),
            (rows_all, (tensor, 1, *rows_all.shape[2:]), lambda p: (0, p, 0, 0)),
            by_step(attended, 1),
            by_step(proj, PAIR),
            whole(packed),
            whole(vectors),
        ],
        [
            (tokens, f32, block, step),
            (tokens, bf16, block, step),
            (matrix, bf16, matrix, still),
            ((8, width), f32, (8, width), still),
        ],
        [pltpu.VMEM(matrix, f32)],
        flops=2 * count * length * (width * 12 * local + 14 * length * local),
    )


def last_kernel(images_ref, normed_ref, mixed_ref, vector_ref, out_ref, sums_ref):
    @pl.when(pl.program_id(0) == 0)
    def _():
        sums_ref[...] = jnp.zeros_like(sums_ref)

    for h in range(images_ref.shape[0]):
        scaled, inv_std = norm_rows(images_ref[h].astype(jnp.float32))
        grad = normed_ref[h].astype(jnp.float32)
        out_ref[h] = mixed_ref[h] + norm_rows_back(grad, scaled, inv_std, vector_ref[0:1])
        sums_ref[0:1] += jnp.sum(grad * scaled, axis=0, keepdims=True)
        sums_ref[1:2] += jnp.sum(grad, axis=0, keepdims=True)


def run_last(images, grad_normed, grad_mixed, vectors):
    width = images.shape[2]
    return call_kernel(
        last_kernel,
        (images.shape[0],),
        [by_step(images, 1), by_step(grad_normed, 1), by_step(grad_mixed, 1), whole(vectors)],
        [
            (images.shape, jnp.float32, (1, *images.shape[1:]), lambda p: (p, 0, 0)),
            ((8, width), jnp.float32, (8, width), lambda p: (0, 0)),
        ],
    )


def moved_plan(
    images,
    images_held,
    routes,
    slot_index,
    first_gain,
    first_shift,
    w_qkv,
    qv_bias,
    w_out,
    out_bias,
    second_gain,
    second_shift,
    w_router,
    w_in,
    in_bias,
    w_back,
    back_bias,
    cotangent,
):
    f32, bf16 = jnp.float32, jnp.bfloat16
    image_count, seq_len, width = images.shape
    experts_here, shard_width, ff_here = w_in.shape
    data, sources = lax.axis_size(DP), lax.axis_size(EXPERT)
    outer, inner = lax.axis_size(OUTER), lax.axis_size(INNER)
    tensor = outer * inner
    tensor_axes = (OUTER, INNER)
    everywhere = (DP, EXPERT, OUTER, INNER)
    groups = data * sources
    owners = data * inner
    mine = experts_here // owners
    slots = EXPERTS * CAP
    dp_at = lax.axis_index(DP)
    inner_at = lax.axis_index(INNER)
    tensor_at = lax.axis_index(tensor_axes)
    owner_at = dp_at * inner + inner_at
    local_width = w_out.shape[0]
    slice_width = width // tensor
    router_at = 4 * local_width

    packed = jnp.concatenate(
        [
            w_qkv.transpose(1, 0, 2).reshape(shard_width, 3 * local_width),
            w_out.T,
            w_router,
            back_bias.T,
            jnp.stack([first_gain, first_shift, out_bias, second_gain, second_shift], axis=1),
        ],
        axis=1,
    )
    packed = swap(jnp.broadcast_to(packed[None], (data, *packed.shape)), DP).reshape(width, -1)
    out_rows = jnp.concatenate(hop_gather(w_out, tensor_axes), axis=0)
    in_bias_all = jnp.stack(hop_gather(in_bias, INNER))

    def piece(shard, s):
        return cross(lax.dynamic_slice_in_dim(shard, (owner_at ^ s) * mine, mine, 0), s)

    in_pieces = [piece(w_in, s) for s in range(owners)]
    back_pieces = [piece(w_back.transpose(0, 2, 1), s) for s in range(owners)]
    far = owners // 2
    packed, out_rows, in_bias_all, in_pieces[far] = lax.optimization_barrier(
        (packed, out_rows, in_bias_all, in_pieces[far])
    )
    vectors = packed[:, router_at + EXPERTS + experts_here :].T.astype(f32)
    out_whole = jnp.concatenate(hop_gather(out_rows, DP), axis=1)
    in_bias_mine = lax.dynamic_slice_in_dim(in_bias_all, owner_at * mine, mine, 1)
    in_bias_mine = in_bias_mine.transpose(1, 0, 2).astype(f32)

    home, within = routes // experts_here, routes % experts_here
    owner, nth = within // mine, within % mine
    kept = slot_index < CAP
    group_place = (owner // inner) * sources + home
    target = ((group_place * inner + owner % inner) * mine + nth) * CAP + slot_index
    target = jnp.where(kept, target, slots)
    plane_target = (group_place * mine + nth) * CAP + slot_index
    plane_target = jnp.where(jnp.logical_and(kept, owner % inner == inner_at), plane_target, -1)
    plane_target = plane_target.transpose(0, 2, 1)

    attended, proj = run_attend(images, packed, vectors, qv_bias.astype(f32))

    attended_all = lax.all_gather(attended, tensor_axes)
    attended_all, in_pieces = lax.optimization_barrier((attended_all, in_pieces))
    mixed, probs, sent = run_route(
        images,
        cotangent,
        attended_all,
        out_whole,
        packed,
        vectors,
        routes,
        plane_target,
        groups,
        slots // inner,
    )
    sent, back_pieces = lax.optimization_barrier((sent, back_pieces))
    arrived = swap(sent, (DP, EXPERT))
    back_bias_mine = lax.dynamic_slice_in_dim(packed, router_at + EXPERTS + owner_at * mine, mine, 1)
    back_bias_mine = jnp.where(lax.axis_index(OUTER) == 0, back_bias_mine.astype(f32), 0.0)
    (
        returned_out,
        grads_out,
        hidden_low,
        grad_pre_low,
        grad_turned,
        grad_in_bias_mine,
        grad_back_bias_mine,
    ) = run_experts(
        owner_at, arrived, in_pieces, back_pieces, in_bias_mine, back_bias_mine, inner, tensor
    )

    def bring(parts):
        return swap(parts.reshape(groups * tensor, *parts.shape[2:]), everywhere)

    grad_parts = bring(grads_out)
    weight_parts = weight_grads(
        owner_at,
        arrived,
        grad_pre_low,
        grad_turned,
        hidden_low,
        grad_in_bias_mine,
        grad_back_bias_mine,
        owners,
    )
    weight_parts = list(weight_parts)
    weight_parts[: far + 1] = [cross(part, s) for s, part in enumerate(weight_parts[: far + 1])]
    grad_parts, weight_parts[: far + 1] = lax.optimization_barrier(
        (grad_parts, weight_parts[: far + 1])
    )
    rows_cut, grad_gates = run_take_grads(grad_parts, target, slice_width, outer, inner, slots)
    rows_cut, returned_out = lax.optimization_barrier((rows_cut, returned_out))
    rows_all = lax.all_gather(rows_cut, tensor_axes)
    returned = bring(returned_out)
    wide = run_widen(owner_at, weight_parts[: far + 1], owners, mine, shard_width)
    rows_all, wide, weight_parts[far + 1 :] = lax.optimization_barrier(
        (rows_all, wide, weight_parts[far + 1 :])
    )
    grad_mixed, normed_part, matrix, sums = run_pull(
        images_held,
        images,
        cotangent,
        mixed,
        probs,
        routes,
        grad_gates,
        rows_all,
        attended,
        proj,
        packed,
        vectors,
        router_at,
    )
    grad_normed = lax.psum(normed_part, tensor_axes)
    last_parts = [cross(part, far + 1 + s) for s, part in enumerate(weight_parts[far + 1 :])]
    grad_normed, weight_parts[far + 1 :] = lax.optimization_barrier((grad_normed, last_parts))
    normed_part, returned = lax.optimization_barrier((normed_part, returned))
    mixed_cut = lax.dynamic_slice_in_dim(mixed, tensor_at * slice_width, slice_width, 2)
    output_cut = run_take_rows(
        images_held, returned, target, probs, routes, mixed_cut, outer, inner, slots
    )
    grad_normed, output_cut = lax.optimization_barrier((grad_normed, output_cut))
    grad_images, first_sums = run_last(images, grad_normed, grad_mixed, vectors)
    output = lax.all_gather(output_cut, tensor_axes)
    output = output.reshape(tensor, image_count // PAIR, seq_len, PAIR, slice_width)
    output = output.transpose(1, 3, 2, 0, 4).reshape(images.shape)

    pair_sums = [sums[5, :local_width], sums[5, 2 * local_width : 3 * local_width]]
    pair_sums = jnp.tile(jnp.stack(pair_sums), (1, data))
    vector_grads = jnp.concatenate([first_sums[:2], sums[2:5], pair_sums], axis=0)
    high, low = high_low(vector_grads)
    small = jnp.concatenate([matrix, high.T, low.T], axis=1)
    small = swap(small.reshape(groups, shard_width // sources, -1), (DP, EXPERT))
    small, weight_parts[far + 1 :] = lax.optimization_barrier((small, weight_parts[far + 1 :]))
    small = jnp.sum(small.astype(f32), axis=0)
    small = jnp.concatenate(hop_gather(small, EXPERT), axis=0)
    grad_w_qkv = small[:, : 3 * local_width].reshape(shard_width, 3, local_width).transpose(1, 0, 2)
    grad_w_out = small[:, 3 * local_width : router_at].T
    grad_w_router = small[:, router_at : router_at + EXPERTS]
    vector_grads = small[:, router_at + EXPERTS :].T
    vector_grads = vector_grads[:7] + vector_grads[7:]
    grad_w_in, grad_w_back = wide
    for s in range(far + 1, owners):
        two = weight_parts[s][: 2 * mine * shard_width].astype(f32)
        two = two.reshape(2, mine, shard_width, ff_here)
        start = (owner_at ^ s) * mine
        grad_w_in = lax.dynamic_update_slice_in_dim(grad_w_in, two[0], start, 0)
        grad_w_back = lax.dynamic_update_slice_in_dim(grad_w_back, two[1], start, 0)
    grad_w_back = grad_w_back.transpose(0, 2, 1)
    grad_in_bias = jnp.zeros((experts_here, ff_here), f32)
    grad_back_shard = jnp.zeros((experts_here, shard_width), f32)
    for s, part in enumerate(weight_parts):
        start = (owner_at ^ s) * mine
        lines = part[2 * mine * shard_width :].astype(f32)
        line = jnp.sum(lines[: 2 * mine].reshape(mine, 2, ff_here), axis=1)
        grad_in_bias = lax.dynamic_update_slice_in_dim(grad_in_bias, line, start, 0)
        line = lines[2 * mine : 3 * mine]
        line = line[:, :shard_width] + line[:, ff_here // 2 : ff_here // 2 + shard_width]
        grad_back_shard = lax.dynamic_update_slice_in_dim(grad_back_shard, line, start, 0)
    return (
        output,
        grad_images,
        vector_grads[0],
        vector_grads[1],
        grad_w_qkv,
        vector_grads[5:7],
        grad_w_out,
        vector_grads[2],
        vector_grads[3],
        vector_grads[4],
        grad_w_router,
        grad_w_in,
        grad_in_bias,
        grad_w_back,
        grad_back_shard,
    )


def specs(tensor):
    rows = P((DP, EXPERT), None, None)
    vector, square = P(DP), P(tensor, DP)
    qkv, pair, router = P(None, DP, tensor), P(None, tensor), P(DP, None)
    inward, outward = P(EXPERT, DP, tensor), P(EXPERT, tensor, DP)
    params = (vector, vector, qkv, pair, square, vector, vector, vector, router)
    experts = (inward, P(EXPERT, tensor), outward, P(EXPERT, DP))
    taken = (rows, P((DP, EXPERT)), rows, rows, *params, *experts, rows)
    given = (rows, rows, *params, *experts)
    return taken, given


def solution(mesh):
    data, expert, tensor = (mesh.shape[name] for name in (DP, EXPERT, TENSOR))
    inner = FF_PAIR if tensor % FF_PAIR == 0 else 1
    owners = data * inner
    if (EXPERTS // expert) % owners or any(n & (n - 1) for n in (data, expert, tensor)):
        taken, given = specs(TENSOR)
        return jax.shard_map(
            gathered_plan, mesh=mesh, in_specs=taken, out_specs=given, check_vma=False
        )
    devices = mesh.devices.reshape(data, expert, tensor // inner, inner)
    split_mesh = Mesh(devices, (DP, EXPERT, OUTER, INNER))
    taken, given = specs((OUTER, INNER))
    return jax.shard_map(
        moved_plan, mesh=split_mesh, in_specs=taken, out_specs=given, check_vma=False
    )
```

```python
import functools
import math

import jax
import jax.numpy as jnp
from jax import lax
from jax.experimental import pallas as pl
from jax.experimental.pallas import tpu as pltpu
from jax.sharding import Mesh
from jax.sharding import PartitionSpec as P

HEAD_DIM = 64
EXPERTS = 32
TOPK = 2
CAP = 64
FF_PAIR = 1
PAIR = 2
EXTRA = 16
VMEM_LIMIT = 56 * 1024 * 1024
GELU_SCALE = (2.0 / math.pi) ** 0.5
GELU_CUBE = 0.044715

DP = "dp"
EXPERT = "expert"
TENSOR = "tensor"
OUTER = "outer"
INNER = "inner"


EPS = 1e-06


def norm_parts(values, norm_gain, norm_shift):
    average = jnp.mean(values, axis=-1, keepdims=True)
    centred = values - average
    spread = jnp.mean(centred * centred, axis=-1, keepdims=True)
    inv_std = lax.rsqrt(spread + EPS)
    scaled = centred * inv_std
    return (scaled * norm_gain + norm_shift, scaled, inv_std)


def norm_back(grad_out, scaled, inv_std, norm_gain):
    grad_scaled = grad_out * norm_gain
    inner = grad_scaled - jnp.mean(grad_scaled, axis=-1, keepdims=True)
    inner = inner - scaled * jnp.mean(grad_scaled * scaled, axis=-1, keepdims=True)
    return (inner * inv_std, jnp.sum(grad_out * scaled, axis=0), jnp.sum(grad_out, axis=0))


def attention_forward(queries, key_rows, value_rows, scale):
    scores = (
        jnp.einsum("iqhd,ikhd->ihqk", queries, key_rows, preferred_element_type=jnp.float32) * scale
    )
    row_peak = jnp.max(scores, axis=-1, keepdims=True)
    log_total = row_peak + jnp.log(jnp.sum(jnp.exp(scores - row_peak), axis=-1, keepdims=True))
    weights = jnp.exp(scores - log_total).astype(jnp.bfloat16)
    attended = jnp.einsum(
        "ihqk,ikhd->iqhd", weights, value_rows, preferred_element_type=jnp.float32
    )
    return (attended, log_total)


def attention_backward(queries, key_rows, value_rows, log_total, grad_low, scale):
    scores = (
        jnp.einsum("iqhd,ikhd->ihqk", queries, key_rows, preferred_element_type=jnp.float32) * scale
    )
    probs = jnp.exp(scores - log_total)
    weights = probs.astype(jnp.bfloat16)
    grad_values = jnp.einsum(
        "ihqk,iqhd->ikhd", weights, grad_low, preferred_element_type=jnp.float32
    )
    grad_weights = jnp.einsum(
        "iqhd,ikhd->ihqk", grad_low, value_rows, preferred_element_type=jnp.float32
    )
    grad_scores = probs * (grad_weights - jnp.sum(probs * grad_weights, axis=-1, keepdims=True))
    scores_low = grad_scores.astype(jnp.bfloat16)
    grad_queries = (
        jnp.einsum("ihqk,ikhd->iqhd", scores_low, key_rows, preferred_element_type=jnp.float32)
        * scale
    )
    grad_keys = (
        jnp.einsum("ihqk,iqhd->ikhd", scores_low, queries, preferred_element_type=jnp.float32)
        * scale
    )
    return (grad_queries, grad_keys, grad_values)


def gathered_plan(
    images,
    images_held,
    routes,
    slot_index,
    first_gain,
    first_shift,
    w_qkv,
    qv_bias,
    w_out,
    out_bias,
    second_gain,
    second_shift,
    w_router,
    w_in,
    in_bias,
    w_back,
    back_bias,
    cotangent,
):
    image_count, seq_len, width = images.shape
    rows_total = image_count * seq_len
    experts_here = w_in.shape[0]
    (
        gain_first,
        shift_first,
        qkv_full,
        out_full,
        bias_out_full,
        gain_second,
        shift_second,
        router_full,
        in_full,
        back_full,
        back_bias_full,
    ) = (
        lax.all_gather(first_gain, DP, axis=0, tiled=True),
        lax.all_gather(first_shift, DP, axis=0, tiled=True),
        lax.all_gather(w_qkv, DP, axis=1, tiled=True),
        lax.all_gather(w_out, DP, axis=1, tiled=True),
        lax.all_gather(out_bias, DP, axis=0, tiled=True),
        lax.all_gather(second_gain, DP, axis=0, tiled=True),
        lax.all_gather(second_shift, DP, axis=0, tiled=True),
        lax.all_gather(w_router, DP, axis=0, tiled=True),
        lax.all_gather(w_in, DP, axis=1, tiled=True),
        lax.all_gather(w_back, DP, axis=2, tiled=True),
        lax.all_gather(back_bias, DP, axis=1, tiled=True),
    )
    gain_first = gain_first.astype(jnp.float32)
    gain_second = gain_second.astype(jnp.float32)
    inputs = images.reshape(rows_total, width).astype(jnp.float32)
    live_image = (jnp.arange(image_count, dtype=jnp.int32) < images_held[0]).astype(jnp.float32)
    live_rows = jnp.repeat(live_image, seq_len)[:, None]
    normed, scaled_first, inv_first = norm_parts(
        inputs, gain_first, shift_first.astype(jnp.float32)
    )
    normed_low = normed.astype(jnp.bfloat16)
    projected = jnp.einsum("td,cde->cte", normed_low, qkv_full, preferred_element_type=jnp.float32)
    local_width = projected.shape[2]
    head_count = local_width // HEAD_DIM
    head_shape = (image_count, seq_len, head_count, HEAD_DIM)
    bias_pair = qv_bias.astype(jnp.float32)
    queries = (projected[0] + bias_pair[0]).astype(jnp.bfloat16).reshape(head_shape)
    key_rows = projected[1].astype(jnp.bfloat16).reshape(head_shape)
    value_rows = (projected[2] + bias_pair[1]).astype(jnp.bfloat16).reshape(head_shape)
    scale = HEAD_DIM ** (-0.5)
    attended, log_total = attention_forward(queries, key_rows, value_rows, scale)
    attended_low = attended.reshape(rows_total, local_width).astype(jnp.bfloat16)
    head_part = jnp.dot(attended_low, out_full, preferred_element_type=jnp.float32)
    mixed = inputs + lax.psum(head_part, TENSOR) + bias_out_full.astype(jnp.float32)
    routed, scaled_second, inv_second = norm_parts(
        mixed, gain_second, shift_second.astype(jnp.float32)
    )
    routed_low = routed.astype(jnp.bfloat16)
    logits = jnp.dot(routed_low, router_full, preferred_element_type=jnp.float32)
    probs = jax.nn.softmax(logits, axis=-1)
    pair_routes = routes.reshape(rows_total, TOPK)
    pair_slots = slot_index.reshape(rows_total, TOPK)
    target = jnp.where(pair_slots < CAP, pair_routes * CAP + pair_slots, EXPERTS * CAP).reshape(
        rows_total * TOPK
    )
    gates = jnp.take_along_axis(probs, pair_routes, axis=1)
    pair_rows = jnp.repeat(routed_low, TOPK, axis=0)
    outgoing = (
        jnp.zeros((EXPERTS * CAP + 1, width), jnp.bfloat16)
        .at[target]
        .set(pair_rows)[: EXPERTS * CAP]
    )
    outgoing = outgoing.reshape(EXPERTS, 1, CAP, width)
    arrived = lax.all_to_all(outgoing, EXPERT, split_axis=0, concat_axis=1, tiled=True)
    sources = arrived.shape[1]
    expert_rows = arrived.reshape(experts_here, sources * CAP, width)
    hidden_pre = jnp.einsum(
        "erd,edf->erf", expert_rows, in_full, preferred_element_type=jnp.float32
    )
    hidden_pre = hidden_pre + in_bias.astype(jnp.float32)[:, None, :]
    hidden_value, gelu_pull = jax.vjp(jax.nn.gelu, hidden_pre)
    hidden_low = hidden_value.astype(jnp.bfloat16)
    expert_part = jnp.einsum(
        "erf,efd->erd", hidden_low, back_full, preferred_element_type=jnp.float32
    )
    bias_back = back_bias_full.astype(jnp.float32)[:, None, :]
    shares = lax.psum_scatter(
        expert_part.reshape(experts_here, sources, CAP, width),
        TENSOR,
        scatter_dimension=2,
        tiled=True,
    )
    share_low = (shares + bias_back[:, None]).astype(jnp.bfloat16)
    pieces = lax.all_to_all(share_low, EXPERT, split_axis=1, concat_axis=0, tiled=True)
    returned = lax.all_gather(pieces, TENSOR, axis=2, tiled=True)
    padded = jnp.concatenate(
        [returned.reshape(EXPERTS * CAP, width), jnp.zeros((1, width), jnp.bfloat16)], axis=0
    )
    picked = padded[target].astype(jnp.float32).reshape(rows_total, TOPK, width)
    expert_mix = jnp.sum(gates[:, :, None] * picked, axis=1)
    output = (live_rows * (mixed + expert_mix)).astype(jnp.bfloat16).reshape(images.shape)
    grad_rows = cotangent.reshape(rows_total, width).astype(jnp.float32) * live_rows
    grad_gates = jnp.sum(grad_rows[:, None, :] * picked, axis=-1)
    grad_picked = (
        (gates[:, :, None] * grad_rows[:, None, :])
        .astype(jnp.bfloat16)
        .reshape(rows_total * TOPK, width)
    )
    grad_outgoing = (
        jnp.zeros((EXPERTS * CAP + 1, width), jnp.bfloat16)
        .at[target]
        .set(grad_picked)[: EXPERTS * CAP]
    )
    grad_outgoing = grad_outgoing.reshape(EXPERTS, 1, CAP, width)
    grad_arrived = lax.all_to_all(grad_outgoing, EXPERT, split_axis=0, concat_axis=1, tiled=True)
    grad_arrived = grad_arrived.reshape(experts_here, sources * CAP, width)
    grad_back_bias = jnp.sum(grad_arrived.astype(jnp.float32), axis=1)
    grad_back_w = jnp.einsum(
        "erf,erd->efd", hidden_low, grad_arrived, preferred_element_type=jnp.float32
    )
    grad_hidden = jnp.einsum(
        "erd,efd->erf", grad_arrived, back_full, preferred_element_type=jnp.float32
    )
    grad_pre = gelu_pull(grad_hidden)[0]
    grad_in_bias_local = jnp.sum(grad_pre, axis=1)
    grad_pre_low = grad_pre.astype(jnp.bfloat16)
    grad_in_w = jnp.einsum(
        "erd,erf->edf", expert_rows, grad_pre_low, preferred_element_type=jnp.float32
    )
    grad_rows_part = jnp.einsum(
        "erf,edf->erd", grad_pre_low, in_full, preferred_element_type=jnp.float32
    )
    grad_shares = lax.psum_scatter(
        grad_rows_part.reshape(experts_here, sources, CAP, width),
        TENSOR,
        scatter_dimension=2,
        tiled=True,
    ).astype(jnp.bfloat16)
    grad_pieces = lax.all_to_all(grad_shares, EXPERT, split_axis=1, concat_axis=0, tiled=True)
    grad_returned = lax.all_gather(grad_pieces, TENSOR, axis=2, tiled=True)
    grad_padded = jnp.concatenate(
        [grad_returned.reshape(EXPERTS * CAP, width), jnp.zeros((1, width), jnp.bfloat16)], axis=0
    )
    grad_routed = jnp.sum(
        grad_padded[target].astype(jnp.float32).reshape(rows_total, TOPK, width), axis=1
    )
    expert_match = (
        pair_routes[:, :, None] == jnp.arange(EXPERTS, dtype=jnp.int32)[None, None, :]
    ).astype(jnp.float32)
    grad_probs = jnp.sum(expert_match * grad_gates[:, :, None], axis=1)
    grad_logits = probs * (grad_probs - jnp.sum(probs * grad_probs, axis=-1, keepdims=True))
    grad_logits_low = grad_logits.astype(jnp.bfloat16)
    grad_router = jnp.einsum(
        "td,te->de", routed_low, grad_logits_low, preferred_element_type=jnp.float32
    )
    grad_routed = grad_routed + jnp.einsum(
        "te,de->td", grad_logits_low, router_full, preferred_element_type=jnp.float32
    )
    grad_from_norm, grad_gain_second, grad_shift_second = norm_back(
        grad_routed, scaled_second, inv_second, gain_second
    )
    grad_mixed = grad_rows + grad_from_norm
    grad_bias_out = jnp.sum(grad_mixed, axis=0)
    grad_mixed_low = grad_mixed.astype(jnp.bfloat16)
    grad_out_w = jnp.einsum(
        "te,td->ed", attended_low, grad_mixed_low, preferred_element_type=jnp.float32
    )
    grad_attended = jnp.einsum(
        "td,ed->te", grad_mixed_low, out_full, preferred_element_type=jnp.float32
    )
    grad_attended = grad_attended.astype(jnp.bfloat16).reshape(head_shape)
    grad_queries, grad_keys, grad_values = attention_backward(
        queries, key_rows, value_rows, log_total, grad_attended, scale
    )
    grad_queries = grad_queries.reshape(rows_total, local_width)
    grad_keys = grad_keys.reshape(rows_total, local_width)
    grad_values = grad_values.reshape(rows_total, local_width)
    grad_pair_bias = jnp.stack([jnp.sum(grad_queries, axis=0), jnp.sum(grad_values, axis=0)])
    grad_proj_low = jnp.stack([grad_queries, grad_keys, grad_values]).astype(jnp.bfloat16)
    grad_qkv = jnp.einsum(
        "td,cte->cde", normed_low, grad_proj_low, preferred_element_type=jnp.float32
    )
    grad_normed_part = jnp.einsum(
        "cte,cde->td", grad_proj_low, qkv_full, preferred_element_type=jnp.float32
    )
    grad_normed = lax.psum(grad_normed_part, TENSOR)
    grad_from_first, grad_gain_first, grad_shift_first = norm_back(
        grad_normed, scaled_first, inv_first, gain_first
    )
    grad_images = (grad_mixed + grad_from_first).reshape(images.shape)
    expert_start = lax.axis_index(EXPERT) * experts_here
    full_in_bias = lax.dynamic_update_slice(
        jnp.zeros((EXPERTS, grad_in_bias_local.shape[1]), jnp.float32),
        grad_in_bias_local,
        (expert_start, jnp.zeros((), jnp.int32)),
    )
    summed = lax.psum(
        (
            grad_gain_first,
            grad_shift_first,
            grad_qkv,
            grad_pair_bias,
            grad_out_w,
            grad_bias_out,
            grad_gain_second,
            grad_shift_second,
            grad_router,
            full_in_bias,
        ),
        (DP, EXPERT),
    )
    shard_width = width // lax.axis_size(DP)
    shard_start = lax.axis_index(DP) * shard_width
    grad_first_gain = lax.dynamic_slice_in_dim(summed[0], shard_start, shard_width, 0)
    grad_first_shift = lax.dynamic_slice_in_dim(summed[1], shard_start, shard_width, 0)
    grad_w_qkv = lax.dynamic_slice_in_dim(summed[2], shard_start, shard_width, 1)
    grad_qv_bias = summed[3]
    grad_w_out = lax.dynamic_slice_in_dim(summed[4], shard_start, shard_width, 1)
    grad_out_bias = lax.dynamic_slice_in_dim(summed[5], shard_start, shard_width, 0)
    grad_second_gain = lax.dynamic_slice_in_dim(summed[6], shard_start, shard_width, 0)
    grad_second_shift = lax.dynamic_slice_in_dim(summed[7], shard_start, shard_width, 0)
    grad_w_router = lax.dynamic_slice_in_dim(summed[8], shard_start, shard_width, 0)
    grad_in_bias = lax.dynamic_slice_in_dim(summed[9], expert_start, experts_here, 0)
    grad_w_in, grad_w_back, grad_back_shard = (
        lax.psum_scatter(grad_in_w, DP, scatter_dimension=1, tiled=True),
        lax.psum_scatter(grad_back_w, DP, scatter_dimension=2, tiled=True),
        lax.psum_scatter(grad_back_bias, DP, scatter_dimension=1, tiled=True),
    )
    return (
        output,
        grad_images,
        grad_first_gain,
        grad_first_shift,
        grad_w_qkv,
        grad_qv_bias,
        grad_w_out,
        grad_out_bias,
        grad_second_gain,
        grad_second_shift,
        grad_w_router,
        grad_w_in,
        grad_in_bias,
        grad_w_back,
        grad_back_shard,
    )


def swap(values, axes):
    return lax.all_to_all(values, axes, split_axis=0, concat_axis=0, tiled=True)


def hop_gather(values, axes):
    count, at = lax.axis_size(axes), lax.axis_index(axes)
    hops = [values]
    for s in range(1, count):
        hops.append(lax.ppermute(values, axes, [(i, i ^ s) for i in range(count)]))
    gathered = []
    for i in range(count):
        found = hops[0]
        for s in range(1, count):
            found = jnp.where(at ^ i == s, hops[s], found)
        gathered.append(found)
    return gathered


def cross(values, s):
    count = lax.axis_size((DP, INNER))
    return lax.ppermute(values, (DP, INNER), [(i, i ^ s) for i in range(count)]) if s else values


def high_low(values):
    high = lax.reduce_precision(values, 8, 7)
    return high.astype(jnp.bfloat16), (values - high).astype(jnp.bfloat16)


def turned_dot(left, right, left_dim, right_dim):
    return lax.dot_general(
        left, right, (((left_dim,), (right_dim,)), ((), ())), preferred_element_type=jnp.float32
    )


def expert_kernel(inner, owners, at_ref, rows_ref, gate_ref, cot_ref, in_bias_ref, back_bias_ref, *refs):
    in_refs, back_refs, refs = refs[:owners], refs[owners : 2 * owners], refs[2 * owners :]
    returned_ref, grads_ref, hidden_ref, grad_pre_ref, grad_turned_ref = refs[:5]
    grad_in_bias_ref, grad_back_bias_ref, weight_ref = refs[5:]
    f32, bf16 = jnp.float32, jnp.bfloat16
    groups, cap, width = rows_ref.shape
    depth = in_refs[0].shape[1]
    for s in range(owners):
        source = at_ref[0] ^ s
        place = pl.ds(pl.multiple_of((source // inner) * depth, depth), depth)
        weight_ref[0, source % inner, place] = in_refs[s][0]
        weight_ref[1, source % inner, place] = back_refs[s][0]
    tensor, slice_width = returned_ref.shape[1:3]
    mine = back_bias_ref.shape[1]
    total = groups * cap
    at = pl.program_id(0)
    rows = rows_ref[...].reshape(total, width)
    cot_turned = cot_ref[...].reshape(total, width).T.astype(f32)
    pair = gate_ref[:, 0:1, :].astype(f32) + gate_ref[:, 1:2, :].astype(f32)
    pair = pair.reshape(groups, pair.shape[-1])
    gate = jnp.zeros((groups, cap), f32)
    for j in range(mine):
        gate = jnp.where(at == j, pair[:, j * cap : (j + 1) * cap], gate)
    gate = jnp.concatenate([gate[g : g + 1, :] for g in range(groups)], axis=1)
    grad_turned = (cot_turned * gate).astype(bf16)
    grad_turned_ref[0] = grad_turned
    grad_returned = grad_turned.T
    grad_back_bias_ref[0] = jnp.sum(grad_returned.astype(f32), axis=0, keepdims=True)
    bias_columns = back_bias_ref[...]
    bias = jnp.zeros((width, 1), f32)
    for j in range(mine):
        bias = jnp.where(at == j, bias_columns[:, j : j + 1], bias)
    part = jnp.broadcast_to(bias, (width, total))
    back = jnp.zeros((width, total), f32)
    for t in range(inner):
        w_in, w_back = weight_ref[0, t], weight_ref[1, t]
        pre = jnp.dot(rows, w_in, preferred_element_type=f32) + in_bias_ref[0, t : t + 1, :]
        square = pre * pre
        bent = jnp.tanh(GELU_SCALE * pre * (1.0 + GELU_CUBE * square))
        half = 0.5 * (1.0 + bent)
        hidden = (pre * half).astype(bf16)
        slope = half + (0.5 * GELU_SCALE) * pre * (1.0 - bent * bent) * (
            1.0 + (3.0 * GELU_CUBE) * square
        )
        hidden_ref[0, t] = hidden
        grad_pre = jnp.dot(grad_returned, w_back, preferred_element_type=f32) * slope
        grad_in_bias_ref[0, t : t + 1, :] = jnp.sum(grad_pre, axis=0, keepdims=True)
        grad_pre = grad_pre.astype(bf16)
        grad_pre_ref[0, t] = grad_pre
        part = part + turned_dot(w_back, hidden, 1, 1)
        back = back + turned_dot(w_in, grad_pre, 1, 1)
    gate_terms = jnp.sum(part * cot_turned, axis=0, keepdims=True)
    high = gate_terms.astype(bf16)
    low = (gate_terms - high.astype(f32)).astype(bf16)
    extra = grads_ref.shape[2] - slice_width
    tail = jnp.concatenate([high, low, jnp.zeros((extra - 2, total), bf16)], axis=0)
    part = part.astype(bf16)
    back = back.astype(bf16)
    for j in range(mine):

        @pl.when(at == j)
        def _():
            lanes = slice(j * cap, (j + 1) * cap)
            for g in range(groups):
                mine_lanes = slice(g * cap, (g + 1) * cap)
                for z in range(tensor):
                    features = slice(z * slice_width, (z + 1) * slice_width)
                    returned_ref[g, z, :, lanes] = part[features, mine_lanes]
                    grads_ref[g, z, :slice_width, lanes] = back[features, mine_lanes]
                    grads_ref[g, z, slice_width:, lanes] = tail[:, mine_lanes]


def run_experts(owner_at, arrived, in_pieces, back_pieces, in_bias, back_bias, inner, tensor):
    f32, bf16 = jnp.float32, jnp.bfloat16
    groups, _, width = arrived.shape
    owners = len(in_pieces)
    mine, depth, ff = in_pieces[0].shape
    total = groups * CAP
    slice_width = width // tensor
    gate_at = 2 * mine * CAP // EXTRA
    outs = [
        ((groups, tensor, slice_width, mine * CAP), bf16, lambda j: (0, 0, 0, 0), None),
        ((groups, tensor, slice_width + EXTRA, mine * CAP), bf16, lambda j: (0, 0, 0, 0), None),
        ((mine, inner, total, ff), bf16, lambda j: (j, 0, 0, 0), 1),
        ((mine, inner, total, ff), bf16, lambda j: (j, 0, 0, 0), 1),
        ((mine, width, total), bf16, lambda j: (j, 0, 0), 1),
        ((mine, inner, ff), f32, lambda j: (j, 0, 0), 1),
        ((mine, 1, width), f32, lambda j: (j, 0, 0), 1),
    ]
    return pl.pallas_call(
        functools.partial(expert_kernel, inner, owners),
        grid=(mine,),
        in_specs=[
            pl.BlockSpec(memory_space=pltpu.SMEM),
            pl.BlockSpec((groups, CAP, width), lambda j: (0, j, 0)),
            pl.BlockSpec((groups, EXTRA, mine * CAP), lambda j: (0, gate_at, 0)),
            pl.BlockSpec((groups, CAP, width), lambda j: (0, mine + j, 0)),
            pl.BlockSpec((1, inner, ff), lambda j: (j, 0, 0)),
            pl.BlockSpec((width, mine), lambda j: (0, 0)),
        ]
        + [pl.BlockSpec((1, depth, ff), lambda j: (j, 0, 0))] * (2 * owners),
        out_specs=[
            pl.BlockSpec(shape if lead is None else (lead, *shape[1:]), index)
            for shape, _, index, lead in outs
        ],
        out_shape=[jax.ShapeDtypeStruct(shape, dtype) for shape, dtype, _, _ in outs],
        scratch_shapes=[pltpu.VMEM((2, inner, width, ff), bf16)],
        compiler_params=pltpu.CompilerParams(vmem_limit_bytes=VMEM_LIMIT),
        cost_estimate=pl.CostEstimate(
            flops=8 * mine * total * width * inner * ff,
            bytes_accessed=4 * owners * mine * depth * ff + 12 * mine * total * inner * ff,
            transcendentals=mine * total * inner * ff,
        ),
    )(owner_at.reshape(1), arrived, arrived, arrived, in_bias, back_bias, *in_pieces, *back_pieces)


def weight_kernel(
    inner,
    at_ref,
    rows_ref,
    grad_pre_ref,
    grad_turned_ref,
    hidden_ref,
    in_bias_ref,
    back_bias_ref,
    *refs,
):
    f32, bf16 = jnp.float32, jnp.bfloat16
    out_refs, sums_ref, tail_ref = refs[:-2], refs[-2], refs[-1]
    groups, cap, width = rows_ref.shape
    mine = back_bias_ref.shape[0]
    ff = sums_ref.shape[-1]
    depth = width * inner // len(out_refs)
    data = width // depth
    part, at = pl.program_id(0), pl.program_id(1)
    rows = rows_ref[...].reshape(groups * cap, width)
    sums_ref[0] = turned_dot(rows, grad_pre_ref[0, 0], 0, 0).astype(bf16)
    grad_back = jnp.dot(grad_turned_ref[0], hidden_ref[0, 0], preferred_element_type=f32)
    sums_ref[1] = grad_back.astype(bf16)

    @pl.when(at == mine - 1)
    def _():
        pairs = []
        for j in range(mine):
            values = in_bias_ref[j, 0]
            high = values.astype(bf16).astype(f32)
            pairs += [high, values - high]
        for d in range(data):
            lines = list(pairs)
            for j in range(mine):
                values = back_bias_ref[j, :, d * depth : (d + 1) * depth]
                high = values.astype(bf16).astype(f32)
                gap = jnp.zeros((1, ff // 2 - depth), f32)
                lines.append(jnp.concatenate([high, gap, values - high, gap], axis=1))
            lines.append(jnp.zeros((EXTRA - len(lines), ff), f32))
            tail_ref[d] = jnp.concatenate(lines, axis=0).astype(bf16)

    for s, out_ref in enumerate(out_refs):
        owner = at_ref[0] ^ s
        d = owner // inner
        place = pl.ds(pl.multiple_of(d * depth, depth), depth)

        @pl.when(owner % inner == part)
        def _():
            for k in range(2):
                line = pl.multiple_of((k * mine + at) * depth, depth)
                out_ref[pl.ds(line, depth)] = sums_ref[k, place]

            @pl.when(at == mine - 1)
            def _():
                out_ref[2 * mine * depth :] = tail_ref[d]


def weight_grads(
    owner_at, arrived, grad_pre, grad_turned, hidden, grad_in_bias, grad_back_bias, owners
):
    mine, inner, total, ff = hidden.shape
    groups, _, width = arrived.shape
    depth = width * inner // owners
    kept = pl.BlockSpec((1, 1, total, ff), lambda t, j: (j, t, 0, 0))
    out = (2 * mine * depth + EXTRA, ff)
    return pl.pallas_call(
        functools.partial(weight_kernel, inner),
        grid=(inner, mine),
        in_specs=[
            pl.BlockSpec(memory_space=pltpu.SMEM),
            pl.BlockSpec((groups, CAP, width), lambda t, j: (0, j, 0)),
            kept,
            pl.BlockSpec((1, width, total), lambda t, j: (j, 0, 0)),
            kept,
            pl.BlockSpec((mine, 1, 1, ff), lambda t, j: (0, t, 0, 0)),
            pl.BlockSpec((mine, 1, width), lambda t, j: (0, 0, 0)),
        ],
        out_specs=[pl.BlockSpec(out, lambda t, j: (0, 0))] * owners,
        out_shape=[jax.ShapeDtypeStruct(out, jnp.bfloat16)] * owners,
        scratch_shapes=[
            pltpu.VMEM((2, width, ff), jnp.bfloat16),
            pltpu.VMEM((width // depth, EXTRA, ff), jnp.bfloat16),
        ],
        compiler_params=pltpu.CompilerParams(vmem_limit_bytes=VMEM_LIMIT),
        cost_estimate=pl.CostEstimate(
            flops=4 * mine * total * width * inner * ff,
            bytes_accessed=4 * mine * inner * (total + width) * ff,
            transcendentals=0,
        ),
    )(
        owner_at.reshape(1),
        arrived,
        grad_pre,
        grad_turned,
        hidden,
        grad_in_bias[:, :, None],
        grad_back_bias,
    )


def widen_kernel(at_ref, *refs):
    part_refs, (in_ref, back_ref) = refs[:-2], refs[-2:]
    mine, depth, ff = in_ref.shape
    rows = mine * depth
    for s, part_ref in enumerate(part_refs):

        @pl.when(pl.program_id(0) == s)
        def _():
            in_ref[...] = part_ref[:rows].astype(jnp.float32).reshape(mine, depth, ff)
            back_ref[...] = part_ref[rows : 2 * rows].astype(jnp.float32).reshape(mine, depth, ff)


def run_widen(owner_at, parts, owners, mine, depth):
    count, ff = len(parts), parts[0].shape[1]
    out = pl.BlockSpec((mine, depth, ff), lambda p, at: (at[0] ^ p, 0, 0))
    return pl.pallas_call(
        widen_kernel,
        grid_spec=pltpu.PrefetchScalarGridSpec(
            num_scalar_prefetch=1,
            grid=(count,),
            in_specs=[pl.BlockSpec((2 * mine * depth, ff), lambda p, at: (0, 0))] * count,
            out_specs=[out, out],
        ),
        out_shape=[jax.ShapeDtypeStruct((owners * mine, depth, ff), jnp.float32)] * 2,
        compiler_params=pltpu.CompilerParams(vmem_limit_bytes=VMEM_LIMIT),
    )(owner_at.reshape(1), *parts)


def norm_rows(values):
    average = jnp.mean(values, axis=-1, keepdims=True)
    centred = values - average
    spread = jnp.mean(centred * centred, axis=-1, keepdims=True)
    inv_std = lax.rsqrt(spread + EPS)
    return centred * inv_std, inv_std


def norm_rows_back(grad_out, scaled, inv_std, norm_gain):
    grad_scaled = grad_out * norm_gain
    inner = grad_scaled - jnp.mean(grad_scaled, axis=-1, keepdims=True)
    inner = inner - scaled * jnp.mean(grad_scaled * scaled, axis=-1, keepdims=True)
    return inner * inv_std


def call_kernel(kernel, grid, inputs, outputs, scratch=(), flops=0):
    smem = pl.BlockSpec(memory_space=pltpu.SMEM)
    return pl.pallas_call(
        kernel,
        grid=grid,
        in_specs=[smem if b is None else pl.BlockSpec(b, i) for _, b, i in inputs],
        out_specs=[pl.BlockSpec(b, i) for _, _, b, i in outputs],
        out_shape=[jax.ShapeDtypeStruct(shape, dtype) for shape, dtype, _, _ in outputs],
        scratch_shapes=list(scratch),
        compiler_params=pltpu.CompilerParams(vmem_limit_bytes=VMEM_LIMIT),
        cost_estimate=pl.CostEstimate(
            flops=flops,
            bytes_accessed=sum(a.size * a.dtype.itemsize for a, _, _ in inputs),
            transcendentals=0,
        ),
    )(*(a for a, _, _ in inputs))


def whole(array):
    return array, array.shape, lambda p: (0,) * array.ndim


def by_step(array, lead):
    return array, (lead, *array.shape[1:]), lambda p: (p,) + (0,) * (array.ndim - 1)


def attend_kernel(images_ref, packed_ref, vector_ref, bias_ref, attended_ref, proj_ref):
    f32, bf16 = jnp.float32, jnp.bfloat16
    local = bias_ref.shape[1]
    weight = packed_ref[:, : 3 * local]
    for h in range(images_ref.shape[0]):
        scaled, _ = norm_rows(images_ref[h].astype(f32))
        normed = (scaled * vector_ref[0:1] + vector_ref[1:2]).astype(bf16)
        proj = jnp.dot(normed, weight, preferred_element_type=f32)
        queries = (proj[:, :local] + bias_ref[0:1]).astype(bf16)
        keys = proj[:, local : 2 * local].astype(bf16)
        values = (proj[:, 2 * local :] + bias_ref[1:2]).astype(bf16)
        proj_ref[h] = jnp.concatenate([queries, keys, values], axis=1)
        parts = []
        for n in range(0, local, HEAD_DIM):
            head = slice(n, n + HEAD_DIM)
            scores = turned_dot(queries[:, head], keys[:, head], 1, 1) * HEAD_DIM**-0.5
            scores = jnp.exp(scores - jnp.max(scores, axis=-1, keepdims=True))
            weights = scores / jnp.sum(scores, axis=-1, keepdims=True)
            parts.append(
                jnp.dot(weights.astype(bf16), values[:, head], preferred_element_type=f32)
            )
        attended_ref[0, :, h * local : (h + 1) * local] = jnp.concatenate(parts, axis=1).astype(bf16)


def run_attend(images, packed, vectors, qv_bias):
    count, length, width = images.shape
    local = qv_bias.shape[1]
    return call_kernel(
        attend_kernel,
        (count // PAIR,),
        [by_step(images, PAIR), whole(packed), whole(vectors), whole(qv_bias)],
        [
            ((count // PAIR, length, PAIR * local), jnp.bfloat16, (1, length, PAIR * local), lambda p: (p, 0, 0)),
            ((count, length, 3 * local), jnp.bfloat16, (PAIR, length, 3 * local), lambda p: (p, 0, 0)),
        ],
        flops=2 * count * length * local * (3 * width + 4 * length),
    )


def slot_hits(target_row, count):
    return lax.broadcasted_iota(jnp.int32, (count, target_row.shape[1]), 0) == target_row


def route_kernel(
    router_at,
    images_ref,
    cot_ref,
    attended_ref,
    out_ref,
    packed_ref,
    vector_ref,
    routes_ref,
    target_ref,
    mixed_ref,
    probs_ref,
    sent_ref,
    sum_ref,
    gate_ref,
):
    f32, bf16 = jnp.float32, jnp.bfloat16
    slots = sum_ref.shape[1]
    tensor, local = attended_ref.shape[0], attended_ref.shape[3] // images_ref.shape[0]
    at = pl.program_id(0)

    @pl.when(at == 0)
    def _():
        sum_ref[...] = jnp.zeros_like(sum_ref)
        gate_ref[...] = jnp.zeros_like(gate_ref)

    router = packed_ref[:, router_at : router_at + EXPERTS]
    for h in range(images_ref.shape[0]):
        mixed = images_ref[h].astype(f32) + vector_ref[2:3]
        for z in range(tensor):
            part = attended_ref[z, 0, :, h * local : (h + 1) * local]
            weight = out_ref[z * local : (z + 1) * local]
            mixed = mixed + jnp.dot(part, weight, preferred_element_type=f32)
        mixed_ref[h] = mixed
        scaled, _ = norm_rows(mixed)
        routed = (scaled * vector_ref[3:4] + vector_ref[4:5]).astype(bf16)
        logits = jnp.dot(routed, router, preferred_element_type=f32)
        logits = jnp.exp(logits - jnp.max(logits, axis=-1, keepdims=True))
        probs = logits / jnp.sum(logits, axis=-1, keepdims=True)
        probs_ref[h] = probs
        experts = lax.broadcasted_iota(jnp.int32, probs.shape, 1)
        fill = jnp.zeros((slots, probs.shape[0]), f32)
        for k in range(TOPK):
            match = experts == routes_ref[h, :, k : k + 1]
            gate = jnp.sum(jnp.where(match, probs, 0.0), axis=1, keepdims=True)
            high = gate.astype(bf16)
            low = (gate - high.astype(f32)).astype(bf16)
            pair = jnp.concatenate([high, low, jnp.zeros((gate.shape[0], 6), bf16)], axis=1)
            hit = slot_hits(target_ref[h, k : k + 1], slots).astype(f32)
            fill = fill + hit
            gate_ref[...] += turned_dot(pair, hit.astype(bf16), 0, 1)
        fill = fill.astype(bf16)
        sum_ref[0] += jnp.dot(fill, routed, preferred_element_type=f32)
        sum_ref[1] += jnp.dot(fill, cot_ref[h], preferred_element_type=f32)

    @pl.when(at == pl.num_programs(0) - 1)
    def _():
        groups, lines, width = sent_ref.shape
        here = slots // groups
        for g in range(groups):
            lanes = slice(g * here, (g + 1) * here)
            sent_ref[g, :here] = sum_ref[0, lanes].astype(bf16)
            sent_ref[g, here : 2 * here] = sum_ref[1, lanes].astype(bf16)
            gates = jnp.concatenate([gate_ref[:, lanes], jnp.zeros((8, width - here), f32)], axis=1)
            gates = jnp.concatenate([gates, jnp.zeros((lines - 2 * here - 8, width), f32)], axis=0)
            sent_ref[g, 2 * here :] = gates.astype(bf16)


def run_route(
    images, cot, attended_all, out_whole, packed, vectors, routes, plane_target, groups, slots_plane
):
    f32, bf16 = jnp.float32, jnp.bfloat16
    count, length, width = images.shape
    tensor = attended_all.shape[0]
    sent = (groups, 2 * slots_plane // groups + EXTRA, width)
    return call_kernel(
        functools.partial(route_kernel, tensor * attended_all.shape[3] // PAIR),
        (count // PAIR,),
        [
            by_step(images, PAIR),
            by_step(cot, PAIR),
            (attended_all, (tensor, 1, *attended_all.shape[2:]), lambda p: (0, p, 0, 0)),
            whole(out_whole),
            whole(packed),
            whole(vectors),
            by_step(routes, PAIR),
            by_step(plane_target, PAIR),
        ],
        [
            ((count, length, width), f32, (PAIR, length, width), lambda p: (p, 0, 0)),
            ((count, length, EXPERTS), f32, (PAIR, length, EXPERTS), lambda p: (p, 0, 0)),
            (sent, bf16, sent, lambda p: (0, 0, 0)),
        ],
        [pltpu.VMEM((2, slots_plane, width), f32), pltpu.VMEM((8, slots_plane), f32)],
        flops=2 * count * length * width * (width + 2 * slots_plane),
    )


def slot_blocks(parts_ref, slots_ref, outer, inner):
    here = parts_ref.shape[2]
    for b in range(slots_ref.shape[1] // here):
        first = (b // inner) * outer * inner + b % inner
        total = parts_ref[first].astype(jnp.float32)
        for o in range(1, outer):
            total = total + parts_ref[first + o * inner].astype(jnp.float32)
        slots_ref[:, b * here : (b + 1) * here] = total


def token_hits(target_column, count):
    return lax.broadcasted_iota(jnp.int32, (target_column.shape[0], count), 1) == target_column


def take_grads_kernel(outer, inner, parts_ref, target_ref, rows_ref, gates_ref, slots_ref):
    f32, bf16 = jnp.float32, jnp.bfloat16
    slots = slots_ref.shape[1]
    local = rows_ref.shape[2] // target_ref.shape[0]

    @pl.when(pl.program_id(0) == 0)
    def _():
        slot_blocks(parts_ref, slots_ref, outer, inner)

    grads = slots_ref[:local].astype(bf16)
    gate_terms = slots_ref[local : local + 1] + slots_ref[local + 1 : local + 2]
    for h in range(target_ref.shape[0]):
        hits = [token_hits(target_ref[h, :, k : k + 1], slots) for k in range(TOPK)]
        find = jnp.logical_or(hits[0], hits[1]).astype(f32).astype(bf16)
        rows_ref[0, :, h * local : (h + 1) * local] = turned_dot(find, grads, 1, 1).astype(bf16)
        terms = [
            jnp.sum(jnp.where(hit, gate_terms, 0.0), axis=1, keepdims=True) for hit in hits
        ]
        gates_ref[h] = jnp.concatenate(terms, axis=1)


def run_take_grads(parts, target, local, outer, inner, slots):
    count, length, _ = target.shape
    return call_kernel(
        functools.partial(take_grads_kernel, outer, inner),
        (count // PAIR,),
        [whole(parts), by_step(target, PAIR)],
        [
            ((count // PAIR, length, PAIR * local), jnp.bfloat16, (1, length, PAIR * local), lambda p: (p, 0, 0)),
            ((count, length, TOPK), jnp.float32, (PAIR, length, TOPK), lambda p: (p, 0, 0)),
        ],
        [pltpu.VMEM((parts.shape[1], slots), jnp.float32)],
        flops=2 * count * length * slots * local,
    )


def take_rows_kernel(
    outer, inner, held_ref, parts_ref, target_ref, probs_ref, routes_ref, mixed_ref, out_ref, slots_ref
):
    f32, bf16 = jnp.float32, jnp.bfloat16
    slots = slots_ref.shape[1]
    pair = target_ref.shape[0]
    local = out_ref.shape[2] // pair
    at = pl.program_id(0)

    @pl.when(at == 0)
    def _():
        slot_blocks(parts_ref, slots_ref, outer, inner)

    returned = slots_ref[...].astype(bf16)
    for h in range(pair):
        probs = probs_ref[h]
        experts = lax.broadcasted_iota(jnp.int32, probs.shape, 1)
        rows = mixed_ref[h]
        for k in range(TOPK):
            match = experts == routes_ref[h, :, k : k + 1]
            gate = jnp.sum(jnp.where(match, probs, 0.0), axis=1, keepdims=True)
            find = token_hits(target_ref[h, :, k : k + 1], slots).astype(f32).astype(bf16)
            rows = rows + gate * turned_dot(find, returned, 1, 1)
        live = (at * pair + h < held_ref[0]).astype(f32)
        out_ref[0, :, h * local : (h + 1) * local] = (live * rows).astype(bf16)


def run_take_rows(held, parts, target, probs, routes, mixed_cut, outer, inner, slots):
    count, length, local = mixed_cut.shape
    return call_kernel(
        functools.partial(take_rows_kernel, outer, inner),
        (count // PAIR,),
        [
            (held, None, None),
            whole(parts),
            by_step(target, PAIR),
            by_step(probs, PAIR),
            by_step(routes, PAIR),
            by_step(mixed_cut, PAIR),
        ],
        [((count // PAIR, length, PAIR * local), jnp.bfloat16, (1, length, PAIR * local), lambda p: (p, 0, 0))],
        [pltpu.VMEM((parts.shape[1], slots), jnp.float32)],
        flops=4 * count * length * slots * local,
    )[0]


def pull_kernel(
    router_at,
    held_ref,
    images_ref,
    cot_ref,
    mixed_ref,
    probs_ref,
    routes_ref,
    gates_ref,
    rows_ref,
    attended_ref,
    proj_ref,
    packed_ref,
    vector_ref,
    grad_mixed_ref,
    normed_ref,
    matrix_ref,
    sums_ref,
    matrix_sum_ref,
):
    f32, bf16 = jnp.float32, jnp.bfloat16
    pair = images_ref.shape[0]
    tensor = rows_ref.shape[0]
    local = attended_ref.shape[2] // pair
    width = images_ref.shape[2]
    at = pl.program_id(0)

    @pl.when(at == 0)
    def _():
        sums_ref[...] = jnp.zeros_like(sums_ref)
        matrix_sum_ref[...] = jnp.zeros_like(matrix_sum_ref)

    qkv = packed_ref[:, : 3 * local]
    out_turned = packed_ref[:, 3 * local : 4 * local]
    router = packed_ref[:, router_at : router_at + EXPERTS]
    scale = HEAD_DIM**-0.5
    for h in range(pair):
        lanes = slice(h * local, (h + 1) * local)
        live = (at * pair + h < held_ref[0]).astype(f32)
        cot = cot_ref[h].astype(f32) * live
        scaled, inv_std = norm_rows(mixed_ref[h])
        routed = (scaled * vector_ref[3:4] + vector_ref[4:5]).astype(bf16)
        probs = probs_ref[h]
        experts = lax.broadcasted_iota(jnp.int32, probs.shape, 1)
        grad_probs = jnp.zeros(probs.shape, f32)
        for k in range(TOPK):
            match = experts == routes_ref[h, :, k : k + 1]
            grad_probs = grad_probs + jnp.where(match, gates_ref[h, :, k : k + 1], 0.0)
        grad_logits = probs * (grad_probs - jnp.sum(probs * grad_probs, axis=-1, keepdims=True))
        grad_logits = grad_logits.astype(bf16)
        grad_routed = jnp.concatenate([rows_ref[z, 0, :, lanes] for z in range(tensor)], axis=1)
        grad_routed = grad_routed.astype(f32) + turned_dot(grad_logits, router, 1, 1)
        grad_mixed = cot + norm_rows_back(grad_routed, scaled, inv_std, vector_ref[3:4])
        grad_mixed_ref[h] = grad_mixed
        low = grad_mixed.astype(bf16)
        grad_attended = jnp.dot(low, out_turned, preferred_element_type=f32).astype(bf16)
        proj = proj_ref[h]
        grads = [[], [], []]
        for n in range(0, local, HEAD_DIM):
            queries = proj[:, n : n + HEAD_DIM]
            keys = proj[:, local + n : local + n + HEAD_DIM]
            values = proj[:, 2 * local + n : 2 * local + n + HEAD_DIM]
            grad_head = grad_attended[:, n : n + HEAD_DIM]
            scores = turned_dot(queries, keys, 1, 1) * scale
            scores = jnp.exp(scores - jnp.max(scores, axis=-1, keepdims=True))
            weights = scores / jnp.sum(scores, axis=-1, keepdims=True)
            grads[2].append(turned_dot(weights.astype(bf16), grad_head, 0, 0))
            grad_weights = turned_dot(grad_head, values, 1, 1)
            inner = jnp.sum(weights * grad_weights, axis=-1, keepdims=True)
            grad_scores = (weights * (grad_weights - inner)).astype(bf16)
            grads[0].append(jnp.dot(grad_scores, keys, preferred_element_type=f32) * scale)
            grads[1].append(turned_dot(grad_scores, queries, 0, 0) * scale)
        grad_proj = jnp.concatenate(grads[0] + grads[1] + grads[2], axis=1)
        proj_sum = jnp.sum(grad_proj, axis=0, keepdims=True)
        grad_proj = grad_proj.astype(bf16)
        first, _ = norm_rows(images_ref[h].astype(f32))
        normed = (first * vector_ref[0:1] + vector_ref[1:2]).astype(bf16)
        grad_normed = turned_dot(grad_proj, qkv, 1, 1)
        normed_ref[h] = grad_normed.astype(bf16)
        attended = attended_ref[0, :, lanes]
        matrix = jnp.concatenate(
            [
                turned_dot(normed, grad_proj, 0, 0),
                turned_dot(low, attended, 0, 0),
                turned_dot(routed, grad_logits, 0, 0),
            ],
            axis=1,
        )
        matrix_sum_ref[...] += matrix
        column = lambda values: jnp.sum(values, axis=0, keepdims=True)
        sums_ref[2:3] += column(grad_mixed)
        sums_ref[3:4] += column(grad_routed * scaled)
        sums_ref[4:5] += column(grad_routed)
        sums_ref[5:6, : 3 * local] += proj_sum

    @pl.when(at == pl.num_programs(0) - 1)
    def _():
        matrix_ref[...] = matrix_sum_ref[...].astype(bf16)


def run_pull(held, images, cot, mixed, probs, routes, gates, rows_all, attended, proj, packed, vectors, router_at):
    f32, bf16 = jnp.float32, jnp.bfloat16
    count, length, width = images.shape
    tensor = rows_all.shape[0]
    local = proj.shape[2] // 3
    tokens = (count, length, width)
    block = (PAIR, length, width)
    step = lambda p: (p, 0, 0)
    still = lambda p: (0, 0)
    matrix = (width, 4 * local + EXPERTS)
    return call_kernel(
        functools.partial(pull_kernel, router_at),
        (count // PAIR,),
        [
            (held, None, None),
            by_step(images, PAIR),
            by_step(cot, PAIR),
            by_step(mixed, PAIR),
            by_step(probs, PAIR),
            by_step(routes, PAIR),
            by_step(gates, PAIR),
            (rows_all, (tensor, 1, *rows_all.shape[2:]), lambda p: (0, p, 0, 0)),
            by_step(attended, 1),
            by_step(proj, PAIR),
            whole(packed),
            whole(vectors),
        ],
        [
            (tokens, f32, block, step),
            (tokens, bf16, block, step),
            (matrix, bf16, matrix, still),
            ((8, width), f32, (8, width), still),
        ],
        [pltpu.VMEM(matrix, f32)],
        flops=2 * count * length * (width * 12 * local + 14 * length * local),
    )


def last_kernel(images_ref, normed_ref, mixed_ref, vector_ref, out_ref, sums_ref):
    @pl.when(pl.program_id(0) == 0)
    def _():
        sums_ref[...] = jnp.zeros_like(sums_ref)

    for h in range(images_ref.shape[0]):
        scaled, inv_std = norm_rows(images_ref[h].astype(jnp.float32))
        grad = normed_ref[h].astype(jnp.float32)
        out_ref[h] = mixed_ref[h] + norm_rows_back(grad, scaled, inv_std, vector_ref[0:1])
        sums_ref[0:1] += jnp.sum(grad * scaled, axis=0, keepdims=True)
        sums_ref[1:2] += jnp.sum(grad, axis=0, keepdims=True)


def run_last(images, grad_normed, grad_mixed, vectors):
    width = images.shape[2]
    return call_kernel(
        last_kernel,
        (images.shape[0],),
        [by_step(images, 1), by_step(grad_normed, 1), by_step(grad_mixed, 1), whole(vectors)],
        [
            (images.shape, jnp.float32, (1, *images.shape[1:]), lambda p: (p, 0, 0)),
            ((8, width), jnp.float32, (8, width), lambda p: (0, 0)),
        ],
    )


def moved_plan(
    images,
    images_held,
    routes,
    slot_index,
    first_gain,
    first_shift,
    w_qkv,
    qv_bias,
    w_out,
    out_bias,
    second_gain,
    second_shift,
    w_router,
    w_in,
    in_bias,
    w_back,
    back_bias,
    cotangent,
):
    f32, bf16 = jnp.float32, jnp.bfloat16
    image_count, seq_len, width = images.shape
    experts_here, shard_width, ff_here = w_in.shape
    data, sources = lax.axis_size(DP), lax.axis_size(EXPERT)
    outer, inner = lax.axis_size(OUTER), lax.axis_size(INNER)
    tensor = outer * inner
    tensor_axes = (OUTER, INNER)
    everywhere = (DP, EXPERT, OUTER, INNER)
    groups = data * sources
    owners = data * inner
    mine = experts_here // owners
    slots = EXPERTS * CAP
    dp_at = lax.axis_index(DP)
    inner_at = lax.axis_index(INNER)
    tensor_at = lax.axis_index(tensor_axes)
    owner_at = dp_at * inner + inner_at
    local_width = w_out.shape[0]
    slice_width = width // tensor
    router_at = 4 * local_width

    packed = jnp.concatenate(
        [
            w_qkv.transpose(1, 0, 2).reshape(shard_width, 3 * local_width),
            w_out.T,
            w_router,
            back_bias.T,
            jnp.stack([first_gain, first_shift, out_bias, second_gain, second_shift], axis=1),
        ],
        axis=1,
    )
    packed = swap(jnp.broadcast_to(packed[None], (data, *packed.shape)), DP).reshape(width, -1)
    out_rows = jnp.concatenate(hop_gather(w_out, tensor_axes), axis=0)
    in_bias_all = jnp.stack(hop_gather(in_bias, INNER))

    def piece(shard, s):
        return cross(lax.dynamic_slice_in_dim(shard, (owner_at ^ s) * mine, mine, 0), s)

    in_pieces = [piece(w_in, s) for s in range(owners)]
    back_pieces = [piece(w_back.transpose(0, 2, 1), s) for s in range(owners)]
    far = owners // 2
    packed, out_rows, in_bias_all, in_pieces[far:] = lax.optimization_barrier(
        (packed, out_rows, in_bias_all, in_pieces[far:])
    )
    vectors = packed[:, router_at + EXPERTS + experts_here :].T.astype(f32)
    out_whole = jnp.concatenate(hop_gather(out_rows, DP), axis=1)
    in_bias_mine = lax.dynamic_slice_in_dim(in_bias_all, owner_at * mine, mine, 1)
    in_bias_mine = in_bias_mine.transpose(1, 0, 2).astype(f32)

    home, within = routes // experts_here, routes % experts_here
    owner, nth = within // mine, within % mine
    kept = slot_index < CAP
    group_place = (owner // inner) * sources + home
    target = ((group_place * inner + owner % inner) * mine + nth) * CAP + slot_index
    target = jnp.where(kept, target, slots)
    plane_target = (group_place * mine + nth) * CAP + slot_index
    plane_target = jnp.where(jnp.logical_and(kept, owner % inner == inner_at), plane_target, -1)
    plane_target = plane_target.transpose(0, 2, 1)

    attended, proj = run_attend(images, packed, vectors, qv_bias.astype(f32))

    attended_all = lax.all_gather(attended, tensor_axes)
    attended_all, in_pieces = lax.optimization_barrier((attended_all, in_pieces))
    mixed, probs, sent = run_route(
        images,
        cotangent,
        attended_all,
        out_whole,
        packed,
        vectors,
        routes,
        plane_target,
        groups,
        slots // inner,
    )
    sent, back_pieces = lax.optimization_barrier((sent, back_pieces))
    arrived = swap(sent, (DP, EXPERT))
    back_bias_mine = lax.dynamic_slice_in_dim(packed, router_at + EXPERTS + owner_at * mine, mine, 1)
    back_bias_mine = jnp.where(lax.axis_index(OUTER) == 0, back_bias_mine.astype(f32), 0.0)
    (
        returned_out,
        grads_out,
        hidden_low,
        grad_pre_low,
        grad_turned,
        grad_in_bias_mine,
        grad_back_bias_mine,
    ) = run_experts(
        owner_at, arrived, in_pieces, back_pieces, in_bias_mine, back_bias_mine, inner, tensor
    )

    def bring(parts):
        return swap(parts.reshape(groups * tensor, *parts.shape[2:]), everywhere)

    grad_parts = bring(grads_out)
    weight_parts = weight_grads(
        owner_at,
        arrived,
        grad_pre_low,
        grad_turned,
        hidden_low,
        grad_in_bias_mine,
        grad_back_bias_mine,
        owners,
    )
    weight_parts = list(weight_parts)
    grad_parts, weight_parts[far:] = lax.optimization_barrier((grad_parts, weight_parts[far:]))
    weight_parts[: far + 1] = [cross(part, s) for s, part in enumerate(weight_parts[: far + 1])]
    rows_cut, grad_gates = run_take_grads(grad_parts, target, slice_width, outer, inner, slots)
    rows_cut, returned_out = lax.optimization_barrier((rows_cut, returned_out))
    rows_all = lax.all_gather(rows_cut, tensor_axes)
    returned = bring(returned_out)
    wide = run_widen(owner_at, weight_parts[: far + 1], owners, mine, shard_width)
    rows_all, wide, weight_parts[far + 1 :] = lax.optimization_barrier(
        (rows_all, wide, weight_parts[far + 1 :])
    )
    grad_mixed, normed_part, matrix, sums = run_pull(
        images_held,
        images,
        cotangent,
        mixed,
        probs,
        routes,
        grad_gates,
        rows_all,
        attended,
        proj,
        packed,
        vectors,
        router_at,
    )
    grad_normed = lax.psum(normed_part, tensor_axes)
    last_parts = [cross(part, far + 1 + s) for s, part in enumerate(weight_parts[far + 1 :])]
    weight_parts[far + 1 :] = last_parts
    grad_w_in, grad_w_back = wide
    for s in range(far + 1, owners):
        two = weight_parts[s][: 2 * mine * shard_width].astype(f32)
        two = two.reshape(2, mine, shard_width, ff_here)
        start = (owner_at ^ s) * mine
        grad_w_in = lax.dynamic_update_slice_in_dim(grad_w_in, two[0], start, 0)
        grad_w_back = lax.dynamic_update_slice_in_dim(grad_w_back, two[1], start, 0)
    normed_part, returned = lax.optimization_barrier((normed_part, returned))
    mixed_cut = lax.dynamic_slice_in_dim(mixed, tensor_at * slice_width, slice_width, 2)
    output_cut = run_take_rows(
        images_held, returned, target, probs, routes, mixed_cut, outer, inner, slots
    )
    grad_normed, output_cut, grad_w_in, grad_w_back = lax.optimization_barrier(
        (grad_normed, output_cut, grad_w_in, grad_w_back)
    )
    grad_images, first_sums = run_last(images, grad_normed, grad_mixed, vectors)
    output = lax.all_gather(output_cut, tensor_axes)
    output = output.reshape(tensor, image_count // PAIR, seq_len, PAIR, slice_width)
    output = output.transpose(1, 3, 2, 0, 4).reshape(images.shape)

    pair_sums = [sums[5, :local_width], sums[5, 2 * local_width : 3 * local_width]]
    pair_sums = jnp.tile(jnp.stack(pair_sums), (1, data))
    vector_grads = jnp.concatenate([first_sums[:2], sums[2:5], pair_sums], axis=0)
    high, low = high_low(vector_grads)
    small = jnp.concatenate([matrix, high.T, low.T], axis=1)
    small = swap(small.reshape(groups, shard_width // sources, -1), (DP, EXPERT))
    small = jnp.sum(small.astype(f32), axis=0)
    small = jnp.concatenate(hop_gather(small, EXPERT), axis=0)
    grad_w_qkv = small[:, : 3 * local_width].reshape(shard_width, 3, local_width).transpose(1, 0, 2)
    grad_w_out = small[:, 3 * local_width : router_at].T
    grad_w_router = small[:, router_at : router_at + EXPERTS]
    vector_grads = small[:, router_at + EXPERTS :].T
    vector_grads = vector_grads[:7] + vector_grads[7:]
    grad_w_back = grad_w_back.transpose(0, 2, 1)
    grad_in_bias = jnp.zeros((experts_here, ff_here), f32)
    grad_back_shard = jnp.zeros((experts_here, shard_width), f32)
    for s, part in enumerate(weight_parts):
        start = (owner_at ^ s) * mine
        lines = part[2 * mine * shard_width :].astype(f32)
        line = jnp.sum(lines[: 2 * mine].reshape(mine, 2, ff_here), axis=1)
        grad_in_bias = lax.dynamic_update_slice_in_dim(grad_in_bias, line, start, 0)
        line = lines[2 * mine : 3 * mine]
        line = line[:, :shard_width] + line[:, ff_here // 2 : ff_here // 2 + shard_width]
        grad_back_shard = lax.dynamic_update_slice_in_dim(grad_back_shard, line, start, 0)
    return (
        output,
        grad_images,
        vector_grads[0],
        vector_grads[1],
        grad_w_qkv,
        vector_grads[5:7],
        grad_w_out,
        vector_grads[2],
        vector_grads[3],
        vector_grads[4],
        grad_w_router,
        grad_w_in,
        grad_in_bias,
        grad_w_back,
        grad_back_shard,
    )


def specs(tensor):
    rows = P((DP, EXPERT), None, None)
    vector, square = P(DP), P(tensor, DP)
    qkv, pair, router = P(None, DP, tensor), P(None, tensor), P(DP, None)
    inward, outward = P(EXPERT, DP, tensor), P(EXPERT, tensor, DP)
    params = (vector, vector, qkv, pair, square, vector, vector, vector, router)
    experts = (inward, P(EXPERT, tensor), outward, P(EXPERT, DP))
    taken = (rows, P((DP, EXPERT)), rows, rows, *params, *experts, rows)
    given = (rows, rows, *params, *experts)
    return taken, given


def solution(mesh):
    data, expert, tensor = (mesh.shape[name] for name in (DP, EXPERT, TENSOR))
    inner = FF_PAIR if tensor % FF_PAIR == 0 else 1
    owners = data * inner
    if (EXPERTS // expert) % owners or any(n & (n - 1) for n in (data, expert, tensor)):
        taken, given = specs(TENSOR)
        return jax.shard_map(
            gathered_plan, mesh=mesh, in_specs=taken, out_specs=given, check_vma=False
        )
    devices = mesh.devices.reshape(data, expert, tensor // inner, inner)
    split_mesh = Mesh(devices, (DP, EXPERT, OUTER, INNER))
    taken, given = specs((OUTER, INNER))
    return jax.shard_map(
        moved_plan, mesh=split_mesh, in_specs=taken, out_specs=given, check_vma=False
    )
```

```python
import functools
import math

import jax
import jax.numpy as jnp
from jax import lax
from jax.experimental import pallas as pl
from jax.experimental.pallas import tpu as pltpu
from jax.sharding import Mesh
from jax.sharding import PartitionSpec as P

HEAD_DIM = 64
EXPERTS = 32
TOPK = 2
CAP = 64
FF_PAIR = 1
PAIR = 2
EXTRA = 16
VMEM_LIMIT = 56 * 1024 * 1024
GELU_SCALE = (2.0 / math.pi) ** 0.5
GELU_CUBE = 0.044715

DP = "dp"
EXPERT = "expert"
TENSOR = "tensor"
OUTER = "outer"
INNER = "inner"


EPS = 1e-06


def norm_parts(values, norm_gain, norm_shift):
    average = jnp.mean(values, axis=-1, keepdims=True)
    centred = values - average
    spread = jnp.mean(centred * centred, axis=-1, keepdims=True)
    inv_std = lax.rsqrt(spread + EPS)
    scaled = centred * inv_std
    return (scaled * norm_gain + norm_shift, scaled, inv_std)


def norm_back(grad_out, scaled, inv_std, norm_gain):
    grad_scaled = grad_out * norm_gain
    inner = grad_scaled - jnp.mean(grad_scaled, axis=-1, keepdims=True)
    inner = inner - scaled * jnp.mean(grad_scaled * scaled, axis=-1, keepdims=True)
    return (inner * inv_std, jnp.sum(grad_out * scaled, axis=0), jnp.sum(grad_out, axis=0))


def attention_forward(queries, key_rows, value_rows, scale):
    scores = (
        jnp.einsum("iqhd,ikhd->ihqk", queries, key_rows, preferred_element_type=jnp.float32) * scale
    )
    row_peak = jnp.max(scores, axis=-1, keepdims=True)
    log_total = row_peak + jnp.log(jnp.sum(jnp.exp(scores - row_peak), axis=-1, keepdims=True))
    weights = jnp.exp(scores - log_total).astype(jnp.bfloat16)
    attended = jnp.einsum(
        "ihqk,ikhd->iqhd", weights, value_rows, preferred_element_type=jnp.float32
    )
    return (attended, log_total)


def attention_backward(queries, key_rows, value_rows, log_total, grad_low, scale):
    scores = (
        jnp.einsum("iqhd,ikhd->ihqk", queries, key_rows, preferred_element_type=jnp.float32) * scale
    )
    probs = jnp.exp(scores - log_total)
    weights = probs.astype(jnp.bfloat16)
    grad_values = jnp.einsum(
        "ihqk,iqhd->ikhd", weights, grad_low, preferred_element_type=jnp.float32
    )
    grad_weights = jnp.einsum(
        "iqhd,ikhd->ihqk", grad_low, value_rows, preferred_element_type=jnp.float32
    )
    grad_scores = probs * (grad_weights - jnp.sum(probs * grad_weights, axis=-1, keepdims=True))
    scores_low = grad_scores.astype(jnp.bfloat16)
    grad_queries = (
        jnp.einsum("ihqk,ikhd->iqhd", scores_low, key_rows, preferred_element_type=jnp.float32)
        * scale
    )
    grad_keys = (
        jnp.einsum("ihqk,iqhd->ikhd", scores_low, queries, preferred_element_type=jnp.float32)
        * scale
    )
    return (grad_queries, grad_keys, grad_values)


def gathered_plan(
    images,
    images_held,
    routes,
    slot_index,
    first_gain,
    first_shift,
    w_qkv,
    qv_bias,
    w_out,
    out_bias,
    second_gain,
    second_shift,
    w_router,
    w_in,
    in_bias,
    w_back,
    back_bias,
    cotangent,
):
    image_count, seq_len, width = images.shape
    rows_total = image_count * seq_len
    experts_here = w_in.shape[0]
    (
        gain_first,
        shift_first,
        qkv_full,
        out_full,
        bias_out_full,
        gain_second,
        shift_second,
        router_full,
        in_full,
        back_full,
        back_bias_full,
    ) = (
        lax.all_gather(first_gain, DP, axis=0, tiled=True),
        lax.all_gather(first_shift, DP, axis=0, tiled=True),
        lax.all_gather(w_qkv, DP, axis=1, tiled=True),
        lax.all_gather(w_out, DP, axis=1, tiled=True),
        lax.all_gather(out_bias, DP, axis=0, tiled=True),
        lax.all_gather(second_gain, DP, axis=0, tiled=True),
        lax.all_gather(second_shift, DP, axis=0, tiled=True),
        lax.all_gather(w_router, DP, axis=0, tiled=True),
        lax.all_gather(w_in, DP, axis=1, tiled=True),
        lax.all_gather(w_back, DP, axis=2, tiled=True),
        lax.all_gather(back_bias, DP, axis=1, tiled=True),
    )
    gain_first = gain_first.astype(jnp.float32)
    gain_second = gain_second.astype(jnp.float32)
    inputs = images.reshape(rows_total, width).astype(jnp.float32)
    live_image = (jnp.arange(image_count, dtype=jnp.int32) < images_held[0]).astype(jnp.float32)
    live_rows = jnp.repeat(live_image, seq_len)[:, None]
    normed, scaled_first, inv_first = norm_parts(
        inputs, gain_first, shift_first.astype(jnp.float32)
    )
    normed_low = normed.astype(jnp.bfloat16)
    projected = jnp.einsum("td,cde->cte", normed_low, qkv_full, preferred_element_type=jnp.float32)
    local_width = projected.shape[2]
    head_count = local_width // HEAD_DIM
    head_shape = (image_count, seq_len, head_count, HEAD_DIM)
    bias_pair = qv_bias.astype(jnp.float32)
    queries = (projected[0] + bias_pair[0]).astype(jnp.bfloat16).reshape(head_shape)
    key_rows = projected[1].astype(jnp.bfloat16).reshape(head_shape)
    value_rows = (projected[2] + bias_pair[1]).astype(jnp.bfloat16).reshape(head_shape)
    scale = HEAD_DIM ** (-0.5)
    attended, log_total = attention_forward(queries, key_rows, value_rows, scale)
    attended_low = attended.reshape(rows_total, local_width).astype(jnp.bfloat16)
    head_part = jnp.dot(attended_low, out_full, preferred_element_type=jnp.float32)
    mixed = inputs + lax.psum(head_part, TENSOR) + bias_out_full.astype(jnp.float32)
    routed, scaled_second, inv_second = norm_parts(
        mixed, gain_second, shift_second.astype(jnp.float32)
    )
    routed_low = routed.astype(jnp.bfloat16)
    logits = jnp.dot(routed_low, router_full, preferred_element_type=jnp.float32)
    probs = jax.nn.softmax(logits, axis=-1)
    pair_routes = routes.reshape(rows_total, TOPK)
    pair_slots = slot_index.reshape(rows_total, TOPK)
    target = jnp.where(pair_slots < CAP, pair_routes * CAP + pair_slots, EXPERTS * CAP).reshape(
        rows_total * TOPK
    )
    gates = jnp.take_along_axis(probs, pair_routes, axis=1)
    pair_rows = jnp.repeat(routed_low, TOPK, axis=0)
    outgoing = (
        jnp.zeros((EXPERTS * CAP + 1, width), jnp.bfloat16)
        .at[target]
        .set(pair_rows)[: EXPERTS * CAP]
    )
    outgoing = outgoing.reshape(EXPERTS, 1, CAP, width)
    arrived = lax.all_to_all(outgoing, EXPERT, split_axis=0, concat_axis=1, tiled=True)
    sources = arrived.shape[1]
    expert_rows = arrived.reshape(experts_here, sources * CAP, width)
    hidden_pre = jnp.einsum(
        "erd,edf->erf", expert_rows, in_full, preferred_element_type=jnp.float32
    )
    hidden_pre = hidden_pre + in_bias.astype(jnp.float32)[:, None, :]
    hidden_value, gelu_pull = jax.vjp(jax.nn.gelu, hidden_pre)
    hidden_low = hidden_value.astype(jnp.bfloat16)
    expert_part = jnp.einsum(
        "erf,efd->erd", hidden_low, back_full, preferred_element_type=jnp.float32
    )
    bias_back = back_bias_full.astype(jnp.float32)[:, None, :]
    shares = lax.psum_scatter(
        expert_part.reshape(experts_here, sources, CAP, width),
        TENSOR,
        scatter_dimension=2,
        tiled=True,
    )
    share_low = (shares + bias_back[:, None]).astype(jnp.bfloat16)
    pieces = lax.all_to_all(share_low, EXPERT, split_axis=1, concat_axis=0, tiled=True)
    returned = lax.all_gather(pieces, TENSOR, axis=2, tiled=True)
    padded = jnp.concatenate(
        [returned.reshape(EXPERTS * CAP, width), jnp.zeros((1, width), jnp.bfloat16)], axis=0
    )
    picked = padded[target].astype(jnp.float32).reshape(rows_total, TOPK, width)
    expert_mix = jnp.sum(gates[:, :, None] * picked, axis=1)
    output = (live_rows * (mixed + expert_mix)).astype(jnp.bfloat16).reshape(images.shape)
    grad_rows = cotangent.reshape(rows_total, width).astype(jnp.float32) * live_rows
    grad_gates = jnp.sum(grad_rows[:, None, :] * picked, axis=-1)
    grad_picked = (
        (gates[:, :, None] * grad_rows[:, None, :])
        .astype(jnp.bfloat16)
        .reshape(rows_total * TOPK, width)
    )
    grad_outgoing = (
        jnp.zeros((EXPERTS * CAP + 1, width), jnp.bfloat16)
        .at[target]
        .set(grad_picked)[: EXPERTS * CAP]
    )
    grad_outgoing = grad_outgoing.reshape(EXPERTS, 1, CAP, width)
    grad_arrived = lax.all_to_all(grad_outgoing, EXPERT, split_axis=0, concat_axis=1, tiled=True)
    grad_arrived = grad_arrived.reshape(experts_here, sources * CAP, width)
    grad_back_bias = jnp.sum(grad_arrived.astype(jnp.float32), axis=1)
    grad_back_w = jnp.einsum(
        "erf,erd->efd", hidden_low, grad_arrived, preferred_element_type=jnp.float32
    )
    grad_hidden = jnp.einsum(
        "erd,efd->erf", grad_arrived, back_full, preferred_element_type=jnp.float32
    )
    grad_pre = gelu_pull(grad_hidden)[0]
    grad_in_bias_local = jnp.sum(grad_pre, axis=1)
    grad_pre_low = grad_pre.astype(jnp.bfloat16)
    grad_in_w = jnp.einsum(
        "erd,erf->edf", expert_rows, grad_pre_low, preferred_element_type=jnp.float32
    )
    grad_rows_part = jnp.einsum(
        "erf,edf->erd", grad_pre_low, in_full, preferred_element_type=jnp.float32
    )
    grad_shares = lax.psum_scatter(
        grad_rows_part.reshape(experts_here, sources, CAP, width),
        TENSOR,
        scatter_dimension=2,
        tiled=True,
    ).astype(jnp.bfloat16)
    grad_pieces = lax.all_to_all(grad_shares, EXPERT, split_axis=1, concat_axis=0, tiled=True)
    grad_returned = lax.all_gather(grad_pieces, TENSOR, axis=2, tiled=True)
    grad_padded = jnp.concatenate(
        [grad_returned.reshape(EXPERTS * CAP, width), jnp.zeros((1, width), jnp.bfloat16)], axis=0
    )
    grad_routed = jnp.sum(
        grad_padded[target].astype(jnp.float32).reshape(rows_total, TOPK, width), axis=1
    )
    expert_match = (
        pair_routes[:, :, None] == jnp.arange(EXPERTS, dtype=jnp.int32)[None, None, :]
    ).astype(jnp.float32)
    grad_probs = jnp.sum(expert_match * grad_gates[:, :, None], axis=1)
    grad_logits = probs * (grad_probs - jnp.sum(probs * grad_probs, axis=-1, keepdims=True))
    grad_logits_low = grad_logits.astype(jnp.bfloat16)
    grad_router = jnp.einsum(
        "td,te->de", routed_low, grad_logits_low, preferred_element_type=jnp.float32
    )
    grad_routed = grad_routed + jnp.einsum(
        "te,de->td", grad_logits_low, router_full, preferred_element_type=jnp.float32
    )
    grad_from_norm, grad_gain_second, grad_shift_second = norm_back(
        grad_routed, scaled_second, inv_second, gain_second
    )
    grad_mixed = grad_rows + grad_from_norm
    grad_bias_out = jnp.sum(grad_mixed, axis=0)
    grad_mixed_low = grad_mixed.astype(jnp.bfloat16)
    grad_out_w = jnp.einsum(
        "te,td->ed", attended_low, grad_mixed_low, preferred_element_type=jnp.float32
    )
    grad_attended = jnp.einsum(
        "td,ed->te", grad_mixed_low, out_full, preferred_element_type=jnp.float32
    )
    grad_attended = grad_attended.astype(jnp.bfloat16).reshape(head_shape)
    grad_queries, grad_keys, grad_values = attention_backward(
        queries, key_rows, value_rows, log_total, grad_attended, scale
    )
    grad_queries = grad_queries.reshape(rows_total, local_width)
    grad_keys = grad_keys.reshape(rows_total, local_width)
    grad_values = grad_values.reshape(rows_total, local_width)
    grad_pair_bias = jnp.stack([jnp.sum(grad_queries, axis=0), jnp.sum(grad_values, axis=0)])
    grad_proj_low = jnp.stack([grad_queries, grad_keys, grad_values]).astype(jnp.bfloat16)
    grad_qkv = jnp.einsum(
        "td,cte->cde", normed_low, grad_proj_low, preferred_element_type=jnp.float32
    )
    grad_normed_part = jnp.einsum(
        "cte,cde->td", grad_proj_low, qkv_full, preferred_element_type=jnp.float32
    )
    grad_normed = lax.psum(grad_normed_part, TENSOR)
    grad_from_first, grad_gain_first, grad_shift_first = norm_back(
        grad_normed, scaled_first, inv_first, gain_first
    )
    grad_images = (grad_mixed + grad_from_first).reshape(images.shape)
    expert_start = lax.axis_index(EXPERT) * experts_here
    full_in_bias = lax.dynamic_update_slice(
        jnp.zeros((EXPERTS, grad_in_bias_local.shape[1]), jnp.float32),
        grad_in_bias_local,
        (expert_start, jnp.zeros((), jnp.int32)),
    )
    summed = lax.psum(
        (
            grad_gain_first,
            grad_shift_first,
            grad_qkv,
            grad_pair_bias,
            grad_out_w,
            grad_bias_out,
            grad_gain_second,
            grad_shift_second,
            grad_router,
            full_in_bias,
        ),
        (DP, EXPERT),
    )
    shard_width = width // lax.axis_size(DP)
    shard_start = lax.axis_index(DP) * shard_width
    grad_first_gain = lax.dynamic_slice_in_dim(summed[0], shard_start, shard_width, 0)
    grad_first_shift = lax.dynamic_slice_in_dim(summed[1], shard_start, shard_width, 0)
    grad_w_qkv = lax.dynamic_slice_in_dim(summed[2], shard_start, shard_width, 1)
    grad_qv_bias = summed[3]
    grad_w_out = lax.dynamic_slice_in_dim(summed[4], shard_start, shard_width, 1)
    grad_out_bias = lax.dynamic_slice_in_dim(summed[5], shard_start, shard_width, 0)
    grad_second_gain = lax.dynamic_slice_in_dim(summed[6], shard_start, shard_width, 0)
    grad_second_shift = lax.dynamic_slice_in_dim(summed[7], shard_start, shard_width, 0)
    grad_w_router = lax.dynamic_slice_in_dim(summed[8], shard_start, shard_width, 0)
    grad_in_bias = lax.dynamic_slice_in_dim(summed[9], expert_start, experts_here, 0)
    grad_w_in, grad_w_back, grad_back_shard = (
        lax.psum_scatter(grad_in_w, DP, scatter_dimension=1, tiled=True),
        lax.psum_scatter(grad_back_w, DP, scatter_dimension=2, tiled=True),
        lax.psum_scatter(grad_back_bias, DP, scatter_dimension=1, tiled=True),
    )
    return (
        output,
        grad_images,
        grad_first_gain,
        grad_first_shift,
        grad_w_qkv,
        grad_qv_bias,
        grad_w_out,
        grad_out_bias,
        grad_second_gain,
        grad_second_shift,
        grad_w_router,
        grad_w_in,
        grad_in_bias,
        grad_w_back,
        grad_back_shard,
    )


def swap(values, axes):
    return lax.all_to_all(values, axes, split_axis=0, concat_axis=0, tiled=True)


def hop_gather(values, axes):
    count, at = lax.axis_size(axes), lax.axis_index(axes)
    hops = [values]
    for s in range(1, count):
        hops.append(lax.ppermute(values, axes, [(i, i ^ s) for i in range(count)]))
    gathered = []
    for i in range(count):
        found = hops[0]
        for s in range(1, count):
            found = jnp.where(at ^ i == s, hops[s], found)
        gathered.append(found)
    return gathered


def cross(values, s):
    count = lax.axis_size((DP, INNER))
    return lax.ppermute(values, (DP, INNER), [(i, i ^ s) for i in range(count)]) if s else values


def high_low(values):
    high = lax.reduce_precision(values, 8, 7)
    return high.astype(jnp.bfloat16), (values - high).astype(jnp.bfloat16)


def turned_dot(left, right, left_dim, right_dim):
    return lax.dot_general(
        left, right, (((left_dim,), (right_dim,)), ((), ())), preferred_element_type=jnp.float32
    )


def expert_kernel(inner, owners, at_ref, rows_ref, gate_ref, cot_ref, in_bias_ref, back_bias_ref, *refs):
    in_refs, back_refs, refs = refs[:owners], refs[owners : 2 * owners], refs[2 * owners :]
    returned_ref, grads_ref, hidden_ref, grad_pre_ref, grad_turned_ref = refs[:5]
    grad_in_bias_ref, grad_back_bias_ref, weight_ref = refs[5:]
    f32, bf16 = jnp.float32, jnp.bfloat16
    groups, cap, width = rows_ref.shape
    depth = in_refs[0].shape[1]
    for s in range(owners):
        source = at_ref[0] ^ s
        place = pl.ds(pl.multiple_of((source // inner) * depth, depth), depth)
        weight_ref[0, source % inner, place] = in_refs[s][0]
        weight_ref[1, source % inner, place] = back_refs[s][0]
    tensor, slice_width = returned_ref.shape[1:3]
    mine = back_bias_ref.shape[1]
    total = groups * cap
    at = pl.program_id(0)
    rows = rows_ref[...].reshape(total, width)
    cot_turned = cot_ref[...].reshape(total, width).T.astype(f32)
    pair = gate_ref[:, 0:1, :].astype(f32) + gate_ref[:, 1:2, :].astype(f32)
    pair = pair.reshape(groups, pair.shape[-1])
    gate = jnp.zeros((groups, cap), f32)
    for j in range(mine):
        gate = jnp.where(at == j, pair[:, j * cap : (j + 1) * cap], gate)
    gate = jnp.concatenate([gate[g : g + 1, :] for g in range(groups)], axis=1)
    grad_turned = (cot_turned * gate).astype(bf16)
    grad_turned_ref[0] = grad_turned
    grad_returned = grad_turned.T
    grad_back_bias_ref[0] = jnp.sum(grad_returned.astype(f32), axis=0, keepdims=True)
    bias_columns = back_bias_ref[...]
    bias = jnp.zeros((width, 1), f32)
    for j in range(mine):
        bias = jnp.where(at == j, bias_columns[:, j : j + 1], bias)
    part = jnp.broadcast_to(bias, (width, total))
    back = jnp.zeros((width, total), f32)
    for t in range(inner):
        w_in, w_back = weight_ref[0, t], weight_ref[1, t]
        pre = jnp.dot(rows, w_in, preferred_element_type=f32) + in_bias_ref[0, t : t + 1, :]
        square = pre * pre
        bent = jnp.tanh(GELU_SCALE * pre * (1.0 + GELU_CUBE * square))
        half = 0.5 * (1.0 + bent)
        hidden = (pre * half).astype(bf16)
        slope = half + (0.5 * GELU_SCALE) * pre * (1.0 - bent * bent) * (
            1.0 + (3.0 * GELU_CUBE) * square
        )
        hidden_ref[0, t] = hidden
        grad_pre = jnp.dot(grad_returned, w_back, preferred_element_type=f32) * slope
        grad_in_bias_ref[0, t : t + 1, :] = jnp.sum(grad_pre, axis=0, keepdims=True)
        grad_pre = grad_pre.astype(bf16)
        grad_pre_ref[0, t] = grad_pre
        part = part + turned_dot(w_back, hidden, 1, 1)
        back = back + turned_dot(w_in, grad_pre, 1, 1)
    gate_terms = jnp.sum(part * cot_turned, axis=0, keepdims=True)
    high = gate_terms.astype(bf16)
    low = (gate_terms - high.astype(f32)).astype(bf16)
    extra = grads_ref.shape[2] - slice_width
    tail = jnp.concatenate([high, low, jnp.zeros((extra - 2, total), bf16)], axis=0)
    part = part.astype(bf16)
    back = back.astype(bf16)
    for j in range(mine):

        @pl.when(at == j)
        def _():
            lanes = slice(j * cap, (j + 1) * cap)
            for g in range(groups):
                mine_lanes = slice(g * cap, (g + 1) * cap)
                for z in range(tensor):
                    features = slice(z * slice_width, (z + 1) * slice_width)
                    returned_ref[g, z, :, lanes] = part[features, mine_lanes]
                    grads_ref[g, z, :slice_width, lanes] = back[features, mine_lanes]
                    grads_ref[g, z, slice_width:, lanes] = tail[:, mine_lanes]


def run_experts(owner_at, arrived, in_pieces, back_pieces, in_bias, back_bias, inner, tensor):
    f32, bf16 = jnp.float32, jnp.bfloat16
    groups, _, width = arrived.shape
    owners = len(in_pieces)
    mine, depth, ff = in_pieces[0].shape
    total = groups * CAP
    slice_width = width // tensor
    gate_at = 2 * mine * CAP // EXTRA
    outs = [
        ((groups, tensor, slice_width, mine * CAP), bf16, lambda j: (0, 0, 0, 0), None),
        ((groups, tensor, slice_width + EXTRA, mine * CAP), bf16, lambda j: (0, 0, 0, 0), None),
        ((mine, inner, total, ff), bf16, lambda j: (j, 0, 0, 0), 1),
        ((mine, inner, total, ff), bf16, lambda j: (j, 0, 0, 0), 1),
        ((mine, width, total), bf16, lambda j: (j, 0, 0), 1),
        ((mine, inner, ff), f32, lambda j: (j, 0, 0), 1),
        ((mine, 1, width), f32, lambda j: (j, 0, 0), 1),
    ]
    return pl.pallas_call(
        functools.partial(expert_kernel, inner, owners),
        grid=(mine,),
        in_specs=[
            pl.BlockSpec(memory_space=pltpu.SMEM),
            pl.BlockSpec((groups, CAP, width), lambda j: (0, j, 0)),
            pl.BlockSpec((groups, EXTRA, mine * CAP), lambda j: (0, gate_at, 0)),
            pl.BlockSpec((groups, CAP, width), lambda j: (0, mine + j, 0)),
            pl.BlockSpec((1, inner, ff), lambda j: (j, 0, 0)),
            pl.BlockSpec((width, mine), lambda j: (0, 0)),
        ]
        + [pl.BlockSpec((1, depth, ff), lambda j: (j, 0, 0))] * (2 * owners),
        out_specs=[
            pl.BlockSpec(shape if lead is None else (lead, *shape[1:]), index)
            for shape, _, index, lead in outs
        ],
        out_shape=[jax.ShapeDtypeStruct(shape, dtype) for shape, dtype, _, _ in outs],
        scratch_shapes=[pltpu.VMEM((2, inner, width, ff), bf16)],
        compiler_params=pltpu.CompilerParams(vmem_limit_bytes=VMEM_LIMIT),
        cost_estimate=pl.CostEstimate(
            flops=8 * mine * total * width * inner * ff,
            bytes_accessed=4 * owners * mine * depth * ff + 12 * mine * total * inner * ff,
            transcendentals=mine * total * inner * ff,
        ),
    )(owner_at.reshape(1), arrived, arrived, arrived, in_bias, back_bias, *in_pieces, *back_pieces)


def weight_kernel(
    inner,
    at_ref,
    rows_ref,
    grad_pre_ref,
    grad_turned_ref,
    hidden_ref,
    in_bias_ref,
    back_bias_ref,
    *refs,
):
    f32, bf16 = jnp.float32, jnp.bfloat16
    out_refs, sums_ref, tail_ref = refs[:-2], refs[-2], refs[-1]
    groups, cap, width = rows_ref.shape
    mine = back_bias_ref.shape[0]
    ff = sums_ref.shape[-1]
    depth = width * inner // len(out_refs)
    data = width // depth
    part, at = pl.program_id(0), pl.program_id(1)
    rows = rows_ref[...].reshape(groups * cap, width)
    sums_ref[0] = turned_dot(rows, grad_pre_ref[0, 0], 0, 0).astype(bf16)
    grad_back = jnp.dot(grad_turned_ref[0], hidden_ref[0, 0], preferred_element_type=f32)
    sums_ref[1] = grad_back.astype(bf16)

    @pl.when(at == mine - 1)
    def _():
        pairs = []
        for j in range(mine):
            values = in_bias_ref[j, 0]
            high = values.astype(bf16).astype(f32)
            pairs += [high, values - high]
        for d in range(data):
            lines = list(pairs)
            for j in range(mine):
                values = back_bias_ref[j, :, d * depth : (d + 1) * depth]
                high = values.astype(bf16).astype(f32)
                gap = jnp.zeros((1, ff // 2 - depth), f32)
                lines.append(jnp.concatenate([high, gap, values - high, gap], axis=1))
            lines.append(jnp.zeros((EXTRA - len(lines), ff), f32))
            tail_ref[d] = jnp.concatenate(lines, axis=0).astype(bf16)

    for s, out_ref in enumerate(out_refs):
        owner = at_ref[0] ^ s
        d = owner // inner
        place = pl.ds(pl.multiple_of(d * depth, depth), depth)

        @pl.when(owner % inner == part)
        def _():
            for k in range(2):
                line = pl.multiple_of((k * mine + at) * depth, depth)
                out_ref[pl.ds(line, depth)] = sums_ref[k, place]

            @pl.when(at == mine - 1)
            def _():
                out_ref[2 * mine * depth :] = tail_ref[d]


def weight_grads(
    owner_at, arrived, grad_pre, grad_turned, hidden, grad_in_bias, grad_back_bias, owners
):
    mine, inner, total, ff = hidden.shape
    groups, _, width = arrived.shape
    depth = width * inner // owners
    kept = pl.BlockSpec((1, 1, total, ff), lambda t, j: (j, t, 0, 0))
    out = (2 * mine * depth + EXTRA, ff)
    return pl.pallas_call(
        functools.partial(weight_kernel, inner),
        grid=(inner, mine),
        in_specs=[
            pl.BlockSpec(memory_space=pltpu.SMEM),
            pl.BlockSpec((groups, CAP, width), lambda t, j: (0, j, 0)),
            kept,
            pl.BlockSpec((1, width, total), lambda t, j: (j, 0, 0)),
            kept,
            pl.BlockSpec((mine, 1, 1, ff), lambda t, j: (0, t, 0, 0)),
            pl.BlockSpec((mine, 1, width), lambda t, j: (0, 0, 0)),
        ],
        out_specs=[pl.BlockSpec(out, lambda t, j: (0, 0))] * owners,
        out_shape=[jax.ShapeDtypeStruct(out, jnp.bfloat16)] * owners,
        scratch_shapes=[
            pltpu.VMEM((2, width, ff), jnp.bfloat16),
            pltpu.VMEM((width // depth, EXTRA, ff), jnp.bfloat16),
        ],
        compiler_params=pltpu.CompilerParams(vmem_limit_bytes=VMEM_LIMIT),
        cost_estimate=pl.CostEstimate(
            flops=4 * mine * total * width * inner * ff,
            bytes_accessed=4 * mine * inner * (total + width) * ff,
            transcendentals=0,
        ),
    )(
        owner_at.reshape(1),
        arrived,
        grad_pre,
        grad_turned,
        hidden,
        grad_in_bias[:, :, None],
        grad_back_bias,
    )


def widen_kernel(at_ref, *refs):
    part_refs, (in_ref, back_ref) = refs[:-2], refs[-2:]
    mine, depth, ff = in_ref.shape
    rows = mine * depth
    for s, part_ref in enumerate(part_refs):

        @pl.when(pl.program_id(0) == s)
        def _():
            in_ref[...] = part_ref[:rows].astype(jnp.float32).reshape(mine, depth, ff)
            back_ref[...] = part_ref[rows : 2 * rows].astype(jnp.float32).reshape(mine, depth, ff)


def run_widen(owner_at, parts, owners, mine, depth):
    count, ff = len(parts), parts[0].shape[1]
    out = pl.BlockSpec((mine, depth, ff), lambda p, at: (at[0] ^ p, 0, 0))
    return pl.pallas_call(
        widen_kernel,
        grid_spec=pltpu.PrefetchScalarGridSpec(
            num_scalar_prefetch=1,
            grid=(count,),
            in_specs=[pl.BlockSpec((2 * mine * depth, ff), lambda p, at: (0, 0))] * count,
            out_specs=[out, out],
        ),
        out_shape=[jax.ShapeDtypeStruct((owners * mine, depth, ff), jnp.float32)] * 2,
        compiler_params=pltpu.CompilerParams(vmem_limit_bytes=VMEM_LIMIT),
    )(owner_at.reshape(1), *parts)


def norm_rows(values):
    average = jnp.mean(values, axis=-1, keepdims=True)
    centred = values - average
    spread = jnp.mean(centred * centred, axis=-1, keepdims=True)
    inv_std = lax.rsqrt(spread + EPS)
    return centred * inv_std, inv_std


def norm_rows_back(grad_out, scaled, inv_std, norm_gain):
    grad_scaled = grad_out * norm_gain
    inner = grad_scaled - jnp.mean(grad_scaled, axis=-1, keepdims=True)
    inner = inner - scaled * jnp.mean(grad_scaled * scaled, axis=-1, keepdims=True)
    return inner * inv_std


def call_kernel(kernel, grid, inputs, outputs, scratch=(), flops=0):
    smem = pl.BlockSpec(memory_space=pltpu.SMEM)
    return pl.pallas_call(
        kernel,
        grid=grid,
        in_specs=[smem if b is None else pl.BlockSpec(b, i) for _, b, i in inputs],
        out_specs=[pl.BlockSpec(b, i) for _, _, b, i in outputs],
        out_shape=[jax.ShapeDtypeStruct(shape, dtype) for shape, dtype, _, _ in outputs],
        scratch_shapes=list(scratch),
        compiler_params=pltpu.CompilerParams(vmem_limit_bytes=VMEM_LIMIT),
        cost_estimate=pl.CostEstimate(
            flops=flops,
            bytes_accessed=sum(a.size * a.dtype.itemsize for a, _, _ in inputs),
            transcendentals=0,
        ),
    )(*(a for a, _, _ in inputs))


def whole(array):
    return array, array.shape, lambda p: (0,) * array.ndim


def by_step(array, lead):
    return array, (lead, *array.shape[1:]), lambda p: (p,) + (0,) * (array.ndim - 1)


def attend_kernel(images_ref, packed_ref, vector_ref, bias_ref, attended_ref, proj_ref):
    f32, bf16 = jnp.float32, jnp.bfloat16
    local = bias_ref.shape[1]
    weight = packed_ref[:, : 3 * local]
    for h in range(images_ref.shape[0]):
        scaled, _ = norm_rows(images_ref[h].astype(f32))
        normed = (scaled * vector_ref[0:1] + vector_ref[1:2]).astype(bf16)
        proj = jnp.dot(normed, weight, preferred_element_type=f32)
        queries = (proj[:, :local] + bias_ref[0:1]).astype(bf16)
        keys = proj[:, local : 2 * local].astype(bf16)
        values = (proj[:, 2 * local :] + bias_ref[1:2]).astype(bf16)
        proj_ref[h] = jnp.concatenate([queries, keys, values], axis=1)
        parts = []
        for n in range(0, local, HEAD_DIM):
            head = slice(n, n + HEAD_DIM)
            scores = turned_dot(queries[:, head], keys[:, head], 1, 1) * HEAD_DIM**-0.5
            scores = jnp.exp(scores - jnp.max(scores, axis=-1, keepdims=True))
            weights = scores / jnp.sum(scores, axis=-1, keepdims=True)
            parts.append(
                jnp.dot(weights.astype(bf16), values[:, head], preferred_element_type=f32)
            )
        attended_ref[0, :, h * local : (h + 1) * local] = jnp.concatenate(parts, axis=1).astype(bf16)


def run_attend(images, packed, vectors, qv_bias):
    count, length, width = images.shape
    local = qv_bias.shape[1]
    return call_kernel(
        attend_kernel,
        (count // PAIR,),
        [by_step(images, PAIR), whole(packed), whole(vectors), whole(qv_bias)],
        [
            ((count // PAIR, length, PAIR * local), jnp.bfloat16, (1, length, PAIR * local), lambda p: (p, 0, 0)),
            ((count, length, 3 * local), jnp.bfloat16, (PAIR, length, 3 * local), lambda p: (p, 0, 0)),
        ],
        flops=2 * count * length * local * (3 * width + 4 * length),
    )


def slot_hits(target_row, count):
    return lax.broadcasted_iota(jnp.int32, (count, target_row.shape[1]), 0) == target_row


def route_kernel(
    router_at,
    images_ref,
    cot_ref,
    attended_ref,
    out_ref,
    packed_ref,
    vector_ref,
    routes_ref,
    target_ref,
    mixed_ref,
    probs_ref,
    sent_ref,
    sum_ref,
    gate_ref,
):
    f32, bf16 = jnp.float32, jnp.bfloat16
    slots = sum_ref.shape[1]
    tensor, local = attended_ref.shape[0], attended_ref.shape[3] // images_ref.shape[0]
    at = pl.program_id(0)

    @pl.when(at == 0)
    def _():
        sum_ref[...] = jnp.zeros_like(sum_ref)
        gate_ref[...] = jnp.zeros_like(gate_ref)

    router = packed_ref[:, router_at : router_at + EXPERTS]
    for h in range(images_ref.shape[0]):
        mixed = images_ref[h].astype(f32) + vector_ref[2:3]
        for z in range(tensor):
            part = attended_ref[z, 0, :, h * local : (h + 1) * local]
            weight = out_ref[z * local : (z + 1) * local]
            mixed = mixed + jnp.dot(part, weight, preferred_element_type=f32)
        mixed_ref[h] = mixed
        scaled, _ = norm_rows(mixed)
        routed = (scaled * vector_ref[3:4] + vector_ref[4:5]).astype(bf16)
        logits = jnp.dot(routed, router, preferred_element_type=f32)
        logits = jnp.exp(logits - jnp.max(logits, axis=-1, keepdims=True))
        probs = logits / jnp.sum(logits, axis=-1, keepdims=True)
        probs_ref[h] = probs
        experts = lax.broadcasted_iota(jnp.int32, probs.shape, 1)
        fill = jnp.zeros((slots, probs.shape[0]), f32)
        for k in range(TOPK):
            match = experts == routes_ref[h, :, k : k + 1]
            gate = jnp.sum(jnp.where(match, probs, 0.0), axis=1, keepdims=True)
            high = gate.astype(bf16)
            low = (gate - high.astype(f32)).astype(bf16)
            pair = jnp.concatenate([high, low, jnp.zeros((gate.shape[0], 6), bf16)], axis=1)
            hit = slot_hits(target_ref[h, k : k + 1], slots).astype(f32)
            fill = fill + hit
            gate_ref[...] += turned_dot(pair, hit.astype(bf16), 0, 1)
        fill = fill.astype(bf16)
        sum_ref[0] += jnp.dot(fill, routed, preferred_element_type=f32)
        sum_ref[1] += jnp.dot(fill, cot_ref[h], preferred_element_type=f32)

    @pl.when(at == pl.num_programs(0) - 1)
    def _():
        groups, lines, width = sent_ref.shape
        here = slots // groups
        for g in range(groups):
            lanes = slice(g * here, (g + 1) * here)
            sent_ref[g, :here] = sum_ref[0, lanes].astype(bf16)
            sent_ref[g, here : 2 * here] = sum_ref[1, lanes].astype(bf16)
            gates = jnp.concatenate([gate_ref[:, lanes], jnp.zeros((8, width - here), f32)], axis=1)
            gates = jnp.concatenate([gates, jnp.zeros((lines - 2 * here - 8, width), f32)], axis=0)
            sent_ref[g, 2 * here :] = gates.astype(bf16)


def run_route(
    images, cot, attended_all, out_whole, packed, vectors, routes, plane_target, groups, slots_plane
):
    f32, bf16 = jnp.float32, jnp.bfloat16
    count, length, width = images.shape
    tensor = attended_all.shape[0]
    sent = (groups, 2 * slots_plane // groups + EXTRA, width)
    return call_kernel(
        functools.partial(route_kernel, tensor * attended_all.shape[3] // PAIR),
        (count // PAIR,),
        [
            by_step(images, PAIR),
            by_step(cot, PAIR),
            (attended_all, (tensor, 1, *attended_all.shape[2:]), lambda p: (0, p, 0, 0)),
            whole(out_whole),
            whole(packed),
            whole(vectors),
            by_step(routes, PAIR),
            by_step(plane_target, PAIR),
        ],
        [
            ((count, length, width), f32, (PAIR, length, width), lambda p: (p, 0, 0)),
            ((count, length, EXPERTS), f32, (PAIR, length, EXPERTS), lambda p: (p, 0, 0)),
            (sent, bf16, sent, lambda p: (0, 0, 0)),
        ],
        [pltpu.VMEM((2, slots_plane, width), f32), pltpu.VMEM((8, slots_plane), f32)],
        flops=2 * count * length * width * (width + 2 * slots_plane),
    )


def slot_blocks(parts_ref, slots_ref, outer, inner):
    here = parts_ref.shape[2]
    for b in range(slots_ref.shape[1] // here):
        first = (b // inner) * outer * inner + b % inner
        total = parts_ref[first].astype(jnp.float32)
        for o in range(1, outer):
            total = total + parts_ref[first + o * inner].astype(jnp.float32)
        slots_ref[:, b * here : (b + 1) * here] = total


def token_hits(target_column, count):
    return lax.broadcasted_iota(jnp.int32, (target_column.shape[0], count), 1) == target_column


def take_grads_kernel(outer, inner, parts_ref, target_ref, rows_ref, gates_ref, slots_ref):
    f32, bf16 = jnp.float32, jnp.bfloat16
    slots = slots_ref.shape[1]
    local = rows_ref.shape[2] // target_ref.shape[0]

    @pl.when(pl.program_id(0) == 0)
    def _():
        slot_blocks(parts_ref, slots_ref, outer, inner)

    grads = slots_ref[:local].astype(bf16)
    gate_terms = slots_ref[local : local + 1] + slots_ref[local + 1 : local + 2]
    for h in range(target_ref.shape[0]):
        hits = [token_hits(target_ref[h, :, k : k + 1], slots) for k in range(TOPK)]
        find = jnp.logical_or(hits[0], hits[1]).astype(f32).astype(bf16)
        rows_ref[0, :, h * local : (h + 1) * local] = turned_dot(find, grads, 1, 1).astype(bf16)
        terms = [
            jnp.sum(jnp.where(hit, gate_terms, 0.0), axis=1, keepdims=True) for hit in hits
        ]
        gates_ref[h] = jnp.concatenate(terms, axis=1)


def run_take_grads(parts, target, local, outer, inner, slots):
    count, length, _ = target.shape
    return call_kernel(
        functools.partial(take_grads_kernel, outer, inner),
        (count // PAIR,),
        [whole(parts), by_step(target, PAIR)],
        [
            ((count // PAIR, length, PAIR * local), jnp.bfloat16, (1, length, PAIR * local), lambda p: (p, 0, 0)),
            ((count, length, TOPK), jnp.float32, (PAIR, length, TOPK), lambda p: (p, 0, 0)),
        ],
        [pltpu.VMEM((parts.shape[1], slots), jnp.float32)],
        flops=2 * count * length * slots * local,
    )


def take_rows_kernel(
    outer, inner, held_ref, parts_ref, target_ref, probs_ref, routes_ref, mixed_ref, out_ref, slots_ref
):
    f32, bf16 = jnp.float32, jnp.bfloat16
    slots = slots_ref.shape[1]
    pair = target_ref.shape[0]
    local = out_ref.shape[2] // pair
    at = pl.program_id(0)

    @pl.when(at == 0)
    def _():
        slot_blocks(parts_ref, slots_ref, outer, inner)

    returned = slots_ref[...].astype(bf16)
    for h in range(pair):
        probs = probs_ref[h]
        experts = lax.broadcasted_iota(jnp.int32, probs.shape, 1)
        rows = mixed_ref[h]
        for k in range(TOPK):
            match = experts == routes_ref[h, :, k : k + 1]
            gate = jnp.sum(jnp.where(match, probs, 0.0), axis=1, keepdims=True)
            find = token_hits(target_ref[h, :, k : k + 1], slots).astype(f32).astype(bf16)
            rows = rows + gate * turned_dot(find, returned, 1, 1)
        live = (at * pair + h < held_ref[0]).astype(f32)
        out_ref[0, :, h * local : (h + 1) * local] = (live * rows).astype(bf16)


def run_take_rows(held, parts, target, probs, routes, mixed_cut, outer, inner, slots):
    count, length, local = mixed_cut.shape
    return call_kernel(
        functools.partial(take_rows_kernel, outer, inner),
        (count // PAIR,),
        [
            (held, None, None),
            whole(parts),
            by_step(target, PAIR),
            by_step(probs, PAIR),
            by_step(routes, PAIR),
            by_step(mixed_cut, PAIR),
        ],
        [((count // PAIR, length, PAIR * local), jnp.bfloat16, (1, length, PAIR * local), lambda p: (p, 0, 0))],
        [pltpu.VMEM((parts.shape[1], slots), jnp.float32)],
        flops=4 * count * length * slots * local,
    )[0]


def pull_kernel(
    router_at,
    held_ref,
    images_ref,
    cot_ref,
    mixed_ref,
    probs_ref,
    routes_ref,
    gates_ref,
    rows_ref,
    attended_ref,
    proj_ref,
    packed_ref,
    vector_ref,
    grad_mixed_ref,
    normed_ref,
    matrix_ref,
    sums_ref,
    matrix_sum_ref,
):
    f32, bf16 = jnp.float32, jnp.bfloat16
    pair = images_ref.shape[0]
    tensor = rows_ref.shape[0]
    local = attended_ref.shape[2] // pair
    width = images_ref.shape[2]
    at = pl.program_id(0)

    @pl.when(at == 0)
    def _():
        sums_ref[...] = jnp.zeros_like(sums_ref)
        matrix_sum_ref[...] = jnp.zeros_like(matrix_sum_ref)

    qkv = packed_ref[:, : 3 * local]
    out_turned = packed_ref[:, 3 * local : 4 * local]
    router = packed_ref[:, router_at : router_at + EXPERTS]
    scale = HEAD_DIM**-0.5
    for h in range(pair):
        lanes = slice(h * local, (h + 1) * local)
        live = (at * pair + h < held_ref[0]).astype(f32)
        cot = cot_ref[h].astype(f32) * live
        scaled, inv_std = norm_rows(mixed_ref[h])
        routed = (scaled * vector_ref[3:4] + vector_ref[4:5]).astype(bf16)
        probs = probs_ref[h]
        experts = lax.broadcasted_iota(jnp.int32, probs.shape, 1)
        grad_probs = jnp.zeros(probs.shape, f32)
        for k in range(TOPK):
            match = experts == routes_ref[h, :, k : k + 1]
            grad_probs = grad_probs + jnp.where(match, gates_ref[h, :, k : k + 1], 0.0)
        grad_logits = probs * (grad_probs - jnp.sum(probs * grad_probs, axis=-1, keepdims=True))
        grad_logits = grad_logits.astype(bf16)
        grad_routed = jnp.concatenate([rows_ref[z, 0, :, lanes] for z in range(tensor)], axis=1)
        grad_routed = grad_routed.astype(f32) + turned_dot(grad_logits, router, 1, 1)
        grad_mixed = cot + norm_rows_back(grad_routed, scaled, inv_std, vector_ref[3:4])
        grad_mixed_ref[h] = grad_mixed
        low = grad_mixed.astype(bf16)
        grad_attended = jnp.dot(low, out_turned, preferred_element_type=f32).astype(bf16)
        proj = proj_ref[h]
        grads = [[], [], []]
        for n in range(0, local, HEAD_DIM):
            queries = proj[:, n : n + HEAD_DIM]
            keys = proj[:, local + n : local + n + HEAD_DIM]
            values = proj[:, 2 * local + n : 2 * local + n + HEAD_DIM]
            grad_head = grad_attended[:, n : n + HEAD_DIM]
            scores = turned_dot(queries, keys, 1, 1) * scale
            scores = jnp.exp(scores - jnp.max(scores, axis=-1, keepdims=True))
            weights = scores / jnp.sum(scores, axis=-1, keepdims=True)
            grads[2].append(turned_dot(weights.astype(bf16), grad_head, 0, 0))
            grad_weights = turned_dot(grad_head, values, 1, 1)
            inner = jnp.sum(weights * grad_weights, axis=-1, keepdims=True)
            grad_scores = (weights * (grad_weights - inner)).astype(bf16)
            grads[0].append(jnp.dot(grad_scores, keys, preferred_element_type=f32) * scale)
            grads[1].append(turned_dot(grad_scores, queries, 0, 0) * scale)
        grad_proj = jnp.concatenate(grads[0] + grads[1] + grads[2], axis=1)
        proj_sum = jnp.sum(grad_proj, axis=0, keepdims=True)
        grad_proj = grad_proj.astype(bf16)
        first, _ = norm_rows(images_ref[h].astype(f32))
        normed = (first * vector_ref[0:1] + vector_ref[1:2]).astype(bf16)
        grad_normed = turned_dot(grad_proj, qkv, 1, 1)
        normed_ref[h] = grad_normed.astype(bf16)
        attended = attended_ref[0, :, lanes]
        matrix = jnp.concatenate(
            [
                turned_dot(normed, grad_proj, 0, 0),
                turned_dot(low, attended, 0, 0),
                turned_dot(routed, grad_logits, 0, 0),
            ],
            axis=1,
        )
        matrix_sum_ref[...] += matrix
        column = lambda values: jnp.sum(values, axis=0, keepdims=True)
        sums_ref[2:3] += column(grad_mixed)
        sums_ref[3:4] += column(grad_routed * scaled)
        sums_ref[4:5] += column(grad_routed)
        sums_ref[5:6, : 3 * local] += proj_sum

    @pl.when(at == pl.num_programs(0) - 1)
    def _():
        matrix_ref[...] = matrix_sum_ref[...].astype(bf16)


def run_pull(held, images, cot, mixed, probs, routes, gates, rows_all, attended, proj, packed, vectors, router_at):
    f32, bf16 = jnp.float32, jnp.bfloat16
    count, length, width = images.shape
    tensor = rows_all.shape[0]
    local = proj.shape[2] // 3
    tokens = (count, length, width)
    block = (PAIR, length, width)
    step = lambda p: (p, 0, 0)
    still = lambda p: (0, 0)
    matrix = (width, 4 * local + EXPERTS)
    return call_kernel(
        functools.partial(pull_kernel, router_at),
        (count // PAIR,),
        [
            (held, None, None),
            by_step(images, PAIR),
            by_step(cot, PAIR),
            by_step(mixed, PAIR),
            by_step(probs, PAIR),
            by_step(routes, PAIR),
            by_step(gates, PAIR),
            (rows_all, (tensor, 1, *rows_all.shape[2:]), lambda p: (0, p, 0, 0)),
            by_step(attended, 1),
            by_step(proj, PAIR),
            whole(packed),
            whole(vectors),
        ],
        [
            (tokens, f32, block, step),
            (tokens, bf16, block, step),
            (matrix, bf16, matrix, still),
            ((8, width), f32, (8, width), still),
        ],
        [pltpu.VMEM(matrix, f32)],
        flops=2 * count * length * (width * 12 * local + 14 * length * local),
    )


def last_kernel(images_ref, normed_ref, mixed_ref, vector_ref, out_ref, sums_ref):
    @pl.when(pl.program_id(0) == 0)
    def _():
        sums_ref[...] = jnp.zeros_like(sums_ref)

    for h in range(images_ref.shape[0]):
        scaled, inv_std = norm_rows(images_ref[h].astype(jnp.float32))
        grad = normed_ref[h].astype(jnp.float32)
        out_ref[h] = mixed_ref[h] + norm_rows_back(grad, scaled, inv_std, vector_ref[0:1])
        sums_ref[0:1] += jnp.sum(grad * scaled, axis=0, keepdims=True)
        sums_ref[1:2] += jnp.sum(grad, axis=0, keepdims=True)


def run_last(images, grad_normed, grad_mixed, vectors):
    width = images.shape[2]
    return call_kernel(
        last_kernel,
        (images.shape[0],),
        [by_step(images, 1), by_step(grad_normed, 1), by_step(grad_mixed, 1), whole(vectors)],
        [
            (images.shape, jnp.float32, (1, *images.shape[1:]), lambda p: (p, 0, 0)),
            ((8, width), jnp.float32, (8, width), lambda p: (0, 0)),
        ],
    )


def moved_plan(
    images,
    images_held,
    routes,
    slot_index,
    first_gain,
    first_shift,
    w_qkv,
    qv_bias,
    w_out,
    out_bias,
    second_gain,
    second_shift,
    w_router,
    w_in,
    in_bias,
    w_back,
    back_bias,
    cotangent,
):
    f32, bf16 = jnp.float32, jnp.bfloat16
    image_count, seq_len, width = images.shape
    experts_here, shard_width, ff_here = w_in.shape
    data, sources = lax.axis_size(DP), lax.axis_size(EXPERT)
    outer, inner = lax.axis_size(OUTER), lax.axis_size(INNER)
    tensor = outer * inner
    tensor_axes = (OUTER, INNER)
    everywhere = (DP, EXPERT, OUTER, INNER)
    groups = data * sources
    owners = data * inner
    mine = experts_here // owners
    slots = EXPERTS * CAP
    dp_at = lax.axis_index(DP)
    inner_at = lax.axis_index(INNER)
    tensor_at = lax.axis_index(tensor_axes)
    owner_at = dp_at * inner + inner_at
    local_width = w_out.shape[0]
    slice_width = width // tensor
    router_at = 4 * local_width

    packed = jnp.concatenate(
        [
            w_qkv.transpose(1, 0, 2).reshape(shard_width, 3 * local_width),
            w_out.T,
            w_router,
            back_bias.T,
            jnp.stack([first_gain, first_shift, out_bias, second_gain, second_shift], axis=1),
        ],
        axis=1,
    )
    packed = swap(jnp.broadcast_to(packed[None], (data, *packed.shape)), DP).reshape(width, -1)
    out_rows = jnp.concatenate(hop_gather(w_out, tensor_axes), axis=0)
    in_bias_all = jnp.stack(hop_gather(in_bias, INNER))

    def piece(shard, s):
        return cross(lax.dynamic_slice_in_dim(shard, (owner_at ^ s) * mine, mine, 0), s)

    in_pieces = [piece(w_in, s) for s in range(owners)]
    back_pieces = [piece(w_back.transpose(0, 2, 1), s) for s in range(owners)]
    far = owners // 2
    packed, out_rows, in_bias_all, in_pieces[far] = lax.optimization_barrier(
        (packed, out_rows, in_bias_all, in_pieces[far])
    )
    vectors = packed[:, router_at + EXPERTS + experts_here :].T.astype(f32)
    out_whole = jnp.concatenate(hop_gather(out_rows, DP), axis=1)
    in_bias_mine = lax.dynamic_slice_in_dim(in_bias_all, owner_at * mine, mine, 1)
    in_bias_mine = in_bias_mine.transpose(1, 0, 2).astype(f32)

    home, within = routes // experts_here, routes % experts_here
    owner, nth = within // mine, within % mine
    kept = slot_index < CAP
    group_place = (owner // inner) * sources + home
    target = ((group_place * inner + owner % inner) * mine + nth) * CAP + slot_index
    target = jnp.where(kept, target, slots)
    plane_target = (group_place * mine + nth) * CAP + slot_index
    plane_target = jnp.where(jnp.logical_and(kept, owner % inner == inner_at), plane_target, -1)
    plane_target = plane_target.transpose(0, 2, 1)

    attended, proj = run_attend(images, packed, vectors, qv_bias.astype(f32))

    attended_all = lax.all_gather(attended, tensor_axes)
    attended_all, in_pieces = lax.optimization_barrier((attended_all, in_pieces))
    mixed, probs, sent = run_route(
        images,
        cotangent,
        attended_all,
        out_whole,
        packed,
        vectors,
        routes,
        plane_target,
        groups,
        slots // inner,
    )
    sent, back_pieces = lax.optimization_barrier((sent, back_pieces))
    arrived = swap(sent, (DP, EXPERT))
    back_bias_mine = lax.dynamic_slice_in_dim(packed, router_at + EXPERTS + owner_at * mine, mine, 1)
    back_bias_mine = jnp.where(lax.axis_index(OUTER) == 0, back_bias_mine.astype(f32), 0.0)
    (
        returned_out,
        grads_out,
        hidden_low,
        grad_pre_low,
        grad_turned,
        grad_in_bias_mine,
        grad_back_bias_mine,
    ) = run_experts(
        owner_at, arrived, in_pieces, back_pieces, in_bias_mine, back_bias_mine, inner, tensor
    )

    def bring(parts):
        return swap(parts.reshape(groups * tensor, *parts.shape[2:]), everywhere)

    grad_parts = bring(grads_out)
    weight_parts = weight_grads(
        owner_at,
        arrived,
        grad_pre_low,
        grad_turned,
        hidden_low,
        grad_in_bias_mine,
        grad_back_bias_mine,
        owners,
    )
    weight_parts = list(weight_parts)
    grad_parts, weight_parts[far:] = lax.optimization_barrier((grad_parts, weight_parts[far:]))
    weight_parts[: far + 1] = [cross(part, s) for s, part in enumerate(weight_parts[: far + 1])]
    rows_cut, grad_gates = run_take_grads(grad_parts, target, slice_width, outer, inner, slots)
    rows_cut, returned_out = lax.optimization_barrier((rows_cut, returned_out))
    rows_all = lax.all_gather(rows_cut, tensor_axes)
    returned = bring(returned_out)
    wide = run_widen(owner_at, weight_parts[:far], owners, mine, shard_width)
    rows_all, wide, weight_parts[far + 1 :] = lax.optimization_barrier(
        (rows_all, wide, weight_parts[far + 1 :])
    )
    grad_mixed, normed_part, matrix, sums = run_pull(
        images_held,
        images,
        cotangent,
        mixed,
        probs,
        routes,
        grad_gates,
        rows_all,
        attended,
        proj,
        packed,
        vectors,
        router_at,
    )
    grad_normed = lax.psum(normed_part, tensor_axes)
    last_parts = [cross(part, far + 1 + s) for s, part in enumerate(weight_parts[far + 1 :])]
    weight_parts[far + 1 :] = last_parts
    normed_part, returned, weight_parts[far] = lax.optimization_barrier(
        (normed_part, returned, weight_parts[far])
    )
    grad_w_in, grad_w_back = wide
    for s in range(far, owners):
        two = weight_parts[s][: 2 * mine * shard_width].astype(f32)
        two = two.reshape(2, mine, shard_width, ff_here)
        start = (owner_at ^ s) * mine
        grad_w_in = lax.dynamic_update_slice_in_dim(grad_w_in, two[0], start, 0)
        grad_w_back = lax.dynamic_update_slice_in_dim(grad_w_back, two[1], start, 0)
    mixed_cut = lax.dynamic_slice_in_dim(mixed, tensor_at * slice_width, slice_width, 2)
    output_cut = run_take_rows(
        images_held, returned, target, probs, routes, mixed_cut, outer, inner, slots
    )
    grad_normed, output_cut, grad_w_in, grad_w_back = lax.optimization_barrier(
        (grad_normed, output_cut, grad_w_in, grad_w_back)
    )
    grad_images, first_sums = run_last(images, grad_normed, grad_mixed, vectors)
    output = lax.all_gather(output_cut, tensor_axes)
    output = output.reshape(tensor, image_count // PAIR, seq_len, PAIR, slice_width)
    output = output.transpose(1, 3, 2, 0, 4).reshape(images.shape)

    pair_sums = [sums[5, :local_width], sums[5, 2 * local_width : 3 * local_width]]
    pair_sums = jnp.tile(jnp.stack(pair_sums), (1, data))
    vector_grads = jnp.concatenate([first_sums[:2], sums[2:5], pair_sums], axis=0)
    high, low = high_low(vector_grads)
    small = jnp.concatenate([matrix, high.T, low.T], axis=1)
    small = swap(small.reshape(groups, shard_width // sources, -1), (DP, EXPERT))
    small = jnp.sum(small.astype(f32), axis=0)
    small = jnp.concatenate(hop_gather(small, EXPERT), axis=0)
    grad_w_qkv = small[:, : 3 * local_width].reshape(shard_width, 3, local_width).transpose(1, 0, 2)
    grad_w_out = small[:, 3 * local_width : router_at].T
    grad_w_router = small[:, router_at : router_at + EXPERTS]
    vector_grads = small[:, router_at + EXPERTS :].T
    vector_grads = vector_grads[:7] + vector_grads[7:]
    grad_w_back = grad_w_back.transpose(0, 2, 1)
    grad_in_bias = jnp.zeros((experts_here, ff_here), f32)
    grad_back_shard = jnp.zeros((experts_here, shard_width), f32)
    for s, part in enumerate(weight_parts):
        start = (owner_at ^ s) * mine
        lines = part[2 * mine * shard_width :].astype(f32)
        line = jnp.sum(lines[: 2 * mine].reshape(mine, 2, ff_here), axis=1)
        grad_in_bias = lax.dynamic_update_slice_in_dim(grad_in_bias, line, start, 0)
        line = lines[2 * mine : 3 * mine]
        line = line[:, :shard_width] + line[:, ff_here // 2 : ff_here // 2 + shard_width]
        grad_back_shard = lax.dynamic_update_slice_in_dim(grad_back_shard, line, start, 0)
    return (
        output,
        grad_images,
        vector_grads[0],
        vector_grads[1],
        grad_w_qkv,
        vector_grads[5:7],
        grad_w_out,
        vector_grads[2],
        vector_grads[3],
        vector_grads[4],
        grad_w_router,
        grad_w_in,
        grad_in_bias,
        grad_w_back,
        grad_back_shard,
    )


def specs(tensor):
    rows = P((DP, EXPERT), None, None)
    vector, square = P(DP), P(tensor, DP)
    qkv, pair, router = P(None, DP, tensor), P(None, tensor), P(DP, None)
    inward, outward = P(EXPERT, DP, tensor), P(EXPERT, tensor, DP)
    params = (vector, vector, qkv, pair, square, vector, vector, vector, router)
    experts = (inward, P(EXPERT, tensor), outward, P(EXPERT, DP))
    taken = (rows, P((DP, EXPERT)), rows, rows, *params, *experts, rows)
    given = (rows, rows, *params, *experts)
    return taken, given


def solution(mesh):
    data, expert, tensor = (mesh.shape[name] for name in (DP, EXPERT, TENSOR))
    inner = FF_PAIR if tensor % FF_PAIR == 0 else 1
    owners = data * inner
    if (EXPERTS // expert) % owners or any(n & (n - 1) for n in (data, expert, tensor)):
        taken, given = specs(TENSOR)
        return jax.shard_map(
            gathered_plan, mesh=mesh, in_specs=taken, out_specs=given, check_vma=False
        )
    devices = mesh.devices.reshape(data, expert, tensor // inner, inner)
    split_mesh = Mesh(devices, (DP, EXPERT, OUTER, INNER))
    taken, given = specs((OUTER, INNER))
    return jax.shard_map(
        moved_plan, mesh=split_mesh, in_specs=taken, out_specs=given, check_vma=False
    )
```
